32 devices in a mesh: batch: 16 (over z, y, x), blk: 2 (over core).
Axes of the slice: x: 2, y: 2, z: 4, core: 2. Of those that a mesh axis runs over, the one named last changes fastest.
Arguments:
- enc_in: bfloat16 [32, 512, 768], P('batch', 'blk'), may hold values from -6 to 6
- dec_in: bfloat16 [32, 768], P('batch'), may hold values from -6 to 6
- lengths: int32 [32], P('batch'), may hold values from 257 to 512, as said below
- cot_enc: bfloat16 [32, 512, 768], P('batch', 'blk'), may hold values from -6 to 6
- cot_dec: bfloat16 [32, 768], P('batch'), may hold values from -6 to 6
- enc_gain_attn: float32 [768], replicated, may hold values from 0.25 to 1.75
- enc_query: bfloat16 [768, 768], replicated, may hold values from -0.109375 to 0.109375
- enc_key: bfloat16 [768, 768], replicated, may hold values from -0.109375 to 0.109375
- enc_value: bfloat16 [768, 768], replicated, may hold values from -0.21875 to 0.21875
- enc_output: bfloat16 [768, 768], replicated, may hold values from -0.625 to 0.625
- relative_bias_table: float32 [32, 12], replicated, may hold values from -4 to 4
- enc_gain_ffn: float32 [768], replicated, may hold values from 0.25 to 1.75
- enc_ff_in: bfloat16 [768, 3072], replicated, may hold values from -0.21875 to 0.21875
- enc_ff_out: bfloat16 [3072, 768], replicated, may hold values from -0.15625 to 0.15625
- enc_gain_final: float32 [768], replicated, may hold values from 0.25 to 1.75
- dec_gain_self: float32 [768], replicated, may hold values from 0.25 to 1.75
- dec_self_value: bfloat16 [768, 768], replicated, may hold values from -0.21875 to 0.21875
- dec_self_output: bfloat16 [768, 768], replicated, may hold values from -0.21875 to 0.21875
- dec_gain_cross: float32 [768], replicated, may hold values from 0.25 to 1.75
- dec_cross_query: bfloat16 [768, 768], replicated, may hold values from -0.109375 to 0.109375
- dec_cross_key: bfloat16 [768, 768], replicated, may hold values from -0.109375 to 0.109375
- dec_cross_value: bfloat16 [768, 768], replicated, may hold values from -0.21875 to 0.21875
- dec_cross_output: bfloat16 [768, 768], replicated, may hold values from -0.625 to 0.625
- dec_gain_ffn: float32 [768], replicated, may hold values from 0.25 to 1.75
- dec_ff_in: bfloat16 [768, 3072], replicated, may hold values from -0.21875 to 0.21875
- dec_ff_out: bfloat16 [3072, 768], replicated, may hold values from -0.15625 to 0.15625
Outputs:
- encoder_output: bfloat16 [32, 512, 768], P('batch', 'blk')
- dec_out: bfloat16 [32, 768], P('batch')
- grad_enc_in: float32 [32, 512, 768], P('batch', 'blk')
- grad_dec_in: float32 [32, 768], P('batch')
- grad_enc_gain_attn: float32 [768], P('batch')
- grad_enc_query: float32 [768, 768], P('batch')
- grad_enc_key: float32 [768, 768], P('batch')
- grad_enc_value: float32 [768, 768], P('batch')
- grad_enc_output: float32 [768, 768], P('batch')
- grad_rel_table: float32 [32, 12], replicated
- grad_enc_gain_ffn: float32 [768], P('batch')
- grad_enc_ff_in: float32 [768, 3072], P('batch')
- grad_enc_ff_out: float32 [3072, 768], P('batch')
- grad_enc_gain_final: float32 [768], P('batch')
- grad_dec_gain_self: float32 [768], P('batch')
- grad_dec_self_value: float32 [768, 768], P('batch')
- grad_dec_self_output: float32 [768, 768], P('batch')
- grad_dec_gain_cross: float32 [768], P('batch')
- grad_dec_cross_query: float32 [768, 768], P('batch')
- grad_dec_cross_key: float32 [768, 768], P('batch')
- grad_dec_cross_value: float32 [768, 768], P('batch')
- grad_dec_cross_output: float32 [768, 768], P('batch')
- grad_dec_gain_ffn: float32 [768], P('batch')
- grad_dec_ff_in: float32 [768, 3072], P('batch')
- grad_dec_ff_out: float32 [3072, 768], P('batch')
The draws below stay inside these ranges and needn't reach their ends.
Inputs may be any that keep to these rules, and one draw needn't show every extreme that they name: `lengths`: every pair is longer than 256 tokens; one pair, drawn from the seed, has length 512.
All inputs are finite; a program needn't handle non-finite values.
Results may differ from the reference program's by a relative error of at most 0.033.
Values may be sent and summed in bfloat16 or wider, within the bound.
No kernel may reach another device: no remote copies, remote signals or barrier semaphores. Data moves between devices by JAX's collectives and lax.ppermute only.
A program may use at most 256 MiB of HBM per device.

```python
import math
import jax
import jax.numpy as jnp
from jax import lax

D = 768
HEADS = 12
FF = 3072
BUCKETS = 32
SEQ = 512
SEQ_DEV = 256
PAIRS = 32


def draw_lengths(key, part):
    key = jax.random.fold_in(key, 11)
    random_key, choice_key = jax.random.split(key)
    random_lengths = jax.random.randint(random_key, (PAIRS,), SEQ_DEV + 1, SEQ + 1)
    chosen = jax.random.randint(choice_key, (), 0, PAIRS)
    is_full = jnp.arange(PAIRS) == chosen
    return jnp.where(is_full, SEQ, random_lengths).astype(jnp.int32)


def block_scale(key, shape, pieces, smallest, top_value):
    def one(axis_at, blocks):
        heights = jax.random.uniform(jax.random.fold_in(jax.random.fold_in(key, 6), axis_at), (blocks,), jnp.float32, smallest / len(pieces), top_value / len(pieces))
        return jnp.repeat(jnp.exp(heights), shape[axis_at] // blocks).reshape((-1,) + (1,) * (len(shape) - axis_at - 1))

    loudness = one(*pieces[0])
    for cut in pieces[1:]:
        loudness = loudness * one(*cut)
    return loudness


def bell_draw(own_key, shape, deviation, most, cuts=(), kind=jnp.bfloat16):
    factor_of = block_scale(own_key, shape, cuts, -0.22, 0.18) if cuts else 1.0
    result = jax.random.normal(own_key, shape, jnp.float32) * deviation * factor_of
    return jnp.minimum(jnp.maximum(result, -most), most).astype(kind)


def setup_inputs(seed: int = 0) -> dict:
    streams_of = jax.random.split(jax.random.key(seed), 27)
    enc_in = bell_draw(streams_of[0], (PAIRS, SEQ, D), 1.0, 6.0, ((0, 16), (1, 2)))
    dec_in = bell_draw(streams_of[1], (PAIRS, D), 1.0, 6.0, ((0, 16),))
    lengths = draw_lengths(jax.random.fold_in(streams_of[26], 71), 0)
    cot_enc = bell_draw(streams_of[3], (PAIRS, SEQ, D), 1.0, 6.0, ((0, 16), (1, 2)))
    cot_dec = bell_draw(streams_of[4], (PAIRS, D), 1.0, 6.0, ((0, 16),))
    enc_gain_attn = jnp.clip(1.0 + 0.15 * jax.random.normal(streams_of[5], (D,), jnp.float32), 0.25, 1.75)
    enc_query = bell_draw(streams_of[6], (D, D), (4 * D) ** -0.5, 0.109375)
    enc_key = bell_draw(streams_of[7], (D, D), (4 * D) ** -0.5, 0.109375)
    enc_value = bell_draw(streams_of[8], (D, D), D ** -0.5, 0.21875)
    enc_output = bell_draw(streams_of[9], (D, D), (D // 8) ** -0.5, 0.625)
    relative_bias_table = bell_draw(streams_of[10], (BUCKETS, HEADS), 1.0, 4.0, (), jnp.float32)
    enc_gain_ffn = jnp.clip(1.0 + 0.15 * jax.random.normal(streams_of[11], (D,), jnp.float32), 0.25, 1.75)
    enc_ff_in = bell_draw(streams_of[12], (D, FF), D ** -0.5, 0.21875)
    enc_ff_out = bell_draw(streams_of[13], (FF, D), (FF // 2) ** -0.5, 0.15625)
    enc_gain_final = jnp.clip(1.0 + 0.15 * jax.random.normal(streams_of[14], (D,), jnp.float32), 0.25, 1.75)
    dec_gain_self = jnp.clip(1.0 + 0.15 * jax.random.normal(streams_of[15], (D,), jnp.float32), 0.25, 1.75)
    dec_self_value = bell_draw(streams_of[16], (D, D), D ** -0.5, 0.21875)
    dec_self_output = bell_draw(streams_of[17], (D, D), D ** -0.5, 0.21875)
    dec_gain_cross = jnp.clip(1.0 + 0.15 * jax.random.normal(streams_of[18], (D,), jnp.float32), 0.25, 1.75)
    dec_cross_query = bell_draw(streams_of[19], (D, D), (4 * D) ** -0.5, 0.109375)
    dec_cross_key = bell_draw(streams_of[20], (D, D), (4 * D) ** -0.5, 0.109375)
    dec_cross_value = bell_draw(streams_of[21], (D, D), D ** -0.5, 0.21875)
    dec_cross_output = bell_draw(streams_of[22], (D, D), (D // 8) ** -0.5, 0.625)
    dec_gain_ffn = jnp.clip(1.0 + 0.15 * jax.random.normal(streams_of[23], (D,), jnp.float32), 0.25, 1.75)
    dec_ff_in = bell_draw(streams_of[24], (D, FF), D ** -0.5, 0.21875)
    dec_ff_out = bell_draw(streams_of[25], (FF, D), (FF // 2) ** -0.5, 0.15625)
    return {"enc_in": enc_in, "dec_in": dec_in, "lengths": lengths, "cot_enc": cot_enc, "cot_dec": cot_dec, "enc_gain_attn": enc_gain_attn, "enc_query": enc_query, "enc_key": enc_key, "enc_value": enc_value, "enc_output": enc_output, "relative_bias_table": relative_bias_table, "enc_gain_ffn": enc_gain_ffn, "enc_ff_in": enc_ff_in, "enc_ff_out": enc_ff_out, "enc_gain_final": enc_gain_final, "dec_gain_self": dec_gain_self, "dec_self_value": dec_self_value, "dec_self_output": dec_self_output, "dec_gain_cross": dec_gain_cross, "dec_cross_query": dec_cross_query, "dec_cross_key": dec_cross_key, "dec_cross_value": dec_cross_value, "dec_cross_output": dec_cross_output, "dec_gain_ffn": dec_gain_ffn, "dec_ff_in": dec_ff_in, "dec_ff_out": dec_ff_out}


@jax.custom_vjp
def low(v):
    return lax.optimization_barrier(v.astype(jnp.bfloat16)).astype(jnp.float32)

@jax.custom_vjp
def low_back(v):
    return v

def low_keep(v):
    return (low(v), None)

def low_pass(kept, grad):
    return (grad,)

def back_keep(v):
    return (v, None)

def back_low(kept, grad):
    return (low(grad),)
low.defvjp(low_keep, low_pass)
low_back.defvjp(back_keep, back_low)
epsilon = 1e-06
masked_score = -1e+30
thresholds = (12, 16, 23, 32, 46, 64, 91)

def bucket_of(offset):
    distance = jnp.abs(offset)
    larger = 8 + sum(((distance >= limit).astype(jnp.int32) for limit in thresholds))
    inner = jnp.where(distance < 8, distance, larger)
    return (jnp.where(offset > 0, 16, 0) + inner).astype(jnp.int32)

def norm_apply(values, gain):
    scale = lax.rsqrt(lax.optimization_barrier(jnp.mean(values * values, axis=-1, keepdims=True)) + epsilon)
    return values * scale * gain

def gelu_tanh(values):
    return jax.nn.gelu(values, approximate=True)

def matmul_high(left, right):
    return jnp.dot(left, right, precision=lax.Precision.HIGHEST)

def softmax_rows(scores):
    row_peak = lax.optimization_barrier(jnp.max(scores, axis=-1, keepdims=True))
    exponent = jnp.exp(scores - row_peak)
    return exponent / lax.optimization_barrier(jnp.sum(exponent, axis=-1, keepdims=True))

def forward(enc_start, dec_start, lengths, params):
    enc_gain_attn, enc_query, enc_key, enc_value, enc_output, relative_bias_table, enc_gain_ffn, enc_ff_in, enc_ff_out, enc_gain_final, dec_gain_self, dec_self_value, dec_self_output, dec_gain_cross, dec_cross_query, dec_cross_key, dec_cross_value, dec_cross_output, dec_gain_ffn, dec_ff_in, dec_ff_out = params
    group_size, seq_all, model_width = enc_start.shape
    head_count = relative_bias_table.shape[1]
    head_dim = model_width // head_count
    highest_precision = lax.Precision.HIGHEST
    positions = jnp.arange(seq_all, dtype=jnp.int32)
    valid = positions[None, :] < lengths[:, None]
    bias_terms = jnp.transpose(relative_bias_table[bucket_of(positions[None, :] - positions[:, None])], (2, 0, 1))
    heads_shape = (group_size, seq_all, head_count, head_dim)
    normed_one = low(norm_apply(enc_start, enc_gain_attn))
    queries = low_back(low(matmul_high(normed_one, enc_query))).reshape(heads_shape)
    keys_all = low_back(low(matmul_high(normed_one, enc_key))).reshape(heads_shape)
    values_all = low_back(low(matmul_high(normed_one, enc_value))).reshape(heads_shape)
    scores = low_back(jnp.einsum('gqhe,gkhe->ghqk', queries, keys_all, precision=highest_precision) + bias_terms[None])
    weights = softmax_rows(jnp.where(valid[:, None, None, :], scores, masked_score))
    context = jnp.einsum('ghqk,gkhe->gqhe', low(weights), values_all, precision=highest_precision)
    context = low_back(low(context)).reshape(group_size, seq_all, model_width)
    after_attn = enc_start + low_back(matmul_high(context, enc_output))
    normed_two = low(norm_apply(after_attn, enc_gain_ffn))
    hidden_pre = low_back(matmul_high(normed_two, enc_ff_in))
    hidden = low(gelu_tanh(hidden_pre))
    enc_result = after_attn + low_back(matmul_high(hidden, enc_ff_out))
    key_source = low(norm_apply(enc_result, enc_gain_final))
    cross_keys = low_back(low(matmul_high(key_source, dec_cross_key))).reshape(heads_shape)
    cross_values = low_back(low(matmul_high(key_source, dec_cross_value))).reshape(heads_shape)
    normed_self = low(norm_apply(dec_start, dec_gain_self))
    self_values = low_back(low(matmul_high(normed_self, dec_self_value)))
    after_self = dec_start + low_back(matmul_high(self_values, dec_self_output))
    normed_cross = low(norm_apply(after_self, dec_gain_cross))
    cross_query = low_back(low(matmul_high(normed_cross, dec_cross_query))).reshape(group_size, head_count, head_dim)
    cross_scores = low_back(jnp.einsum('ghe,gkhe->ghk', cross_query, cross_keys, precision=highest_precision))
    cross_weights = softmax_rows(jnp.where(valid[:, None, :], cross_scores, masked_score))
    cross_mixed = jnp.einsum('ghk,gkhe->ghe', low(cross_weights), cross_values, precision=highest_precision)
    cross_mixed = low_back(low(cross_mixed)).reshape(group_size, model_width)
    after_cross = after_self + low_back(matmul_high(cross_mixed, dec_cross_output))
    normed_ffn = low(norm_apply(after_cross, dec_gain_ffn))
    dec_pre = low_back(matmul_high(normed_ffn, dec_ff_in))
    dec_hidden = low(gelu_tanh(dec_pre))
    dec_result = after_cross + low_back(matmul_high(dec_hidden, dec_ff_out))
    return (enc_result, dec_result)

def reference(enc_in, dec_in, lengths, cot_enc, cot_dec, enc_gain_attn, enc_query, enc_key, enc_value, enc_output, relative_bias_table, enc_gain_ffn, enc_ff_in, enc_ff_out, enc_gain_final, dec_gain_self, dec_self_value, dec_self_output, dec_gain_cross, dec_cross_query, dec_cross_key, dec_cross_value, dec_cross_output, dec_gain_ffn, dec_ff_in, dec_ff_out):
    params = tuple((weight.astype(jnp.float32) for weight in (enc_gain_attn, enc_query, enc_key, enc_value, enc_output, relative_bias_table, enc_gain_ffn, enc_ff_in, enc_ff_out, enc_gain_final, dec_gain_self, dec_self_value, dec_self_output, dec_gain_cross, dec_cross_query, dec_cross_key, dec_cross_value, dec_cross_output, dec_gain_ffn, dec_ff_in, dec_ff_out)))
    group_size = math.gcd(PAIRS, max(1, 4096 // SEQ))
    group_count = PAIRS // group_size

    def grouped(array):
        return array.reshape((group_count, group_size) + array.shape[1:])

    def one_group(totals, inputs):
        enc_part, dec_part, length_part, cot_enc_part, cot_dec_part = inputs

        def apply_layers(enc_start, dec_start, weights):
            return forward(enc_start, dec_start, length_part, weights)
        outputs, pullback = jax.vjp(apply_layers, enc_part.astype(jnp.float32), dec_part.astype(jnp.float32), params)
        enc_grad, dec_grad, weight_grads = pullback((cot_enc_part.astype(jnp.float32), cot_dec_part.astype(jnp.float32)))
        totals = tuple((running + addend for running, addend in zip(totals, weight_grads)))
        return (totals, (outputs[0].astype(jnp.bfloat16), outputs[1].astype(jnp.bfloat16), enc_grad, dec_grad))
    zeros = tuple((jnp.zeros_like(weight) for weight in params))
    totals, stacked = lax.scan(one_group, zeros, (grouped(enc_in), grouped(dec_in), grouped(lengths), grouped(cot_enc), grouped(cot_dec)))
    encoder_output = stacked[0].reshape(PAIRS, SEQ, D)
    dec_out = stacked[1].reshape(PAIRS, D)
    grad_enc_in = stacked[2].reshape(PAIRS, SEQ, D)
    grad_dec_in = stacked[3].reshape(PAIRS, D)
    return (encoder_output, dec_out, grad_enc_in, grad_dec_in, totals[0], totals[1], totals[2], totals[3], totals[4], totals[5], totals[6], totals[7], totals[8], totals[9], totals[10], totals[11], totals[12], totals[13], totals[14], totals[15], totals[16], totals[17], totals[18], totals[19], totals[20])
```

```python
import jax
import jax.numpy as jnp
import numpy as np
from jax import lax
from jax.sharding import PartitionSpec as P

epsilon = 1e-06
masked_score = -1e30
thresholds = (12, 16, 23, 32, 46, 64, 91)
bf16 = jnp.bfloat16
f32 = jnp.float32


def bucket_of(offset):
    distance = jnp.abs(offset)
    larger = 8 + sum(((distance >= limit).astype(jnp.int32) for limit in thresholds))
    inner = jnp.where(distance < 8, distance, larger)
    return jnp.where(offset > 0, 16, 0) + inner


def norm_scale(values):
    return lax.rsqrt(jnp.mean(values * values, axis=-1, keepdims=True) + epsilon)


def norm_apply(values, gain):
    return values * norm_scale(values) * gain


def norm_back(values, gain, upstream):
    scale = norm_scale(values)
    weighted = upstream * gain
    inner = jnp.mean(weighted * values, axis=-1, keepdims=True)
    return scale * weighted - values * (scale * scale * scale * inner)


def gelu_parts(a):
    c0 = 0.7978845608028654
    inner = c0 * (a + 0.044715 * a * a * a)
    t = jnp.tanh(inner)
    half = 0.5 * (1.0 + t)
    slope = half + 0.5 * a * (1.0 - t * t) * c0 * (1.0 + 3 * 0.044715 * a * a)
    return a * half, slope


def dot(left, right, dims=((1,), (0,))):
    return lax.dot_general(left, right, (dims, ((), ())), preferred_element_type=f32)


def dot_t(left, right):
    return dot(left, right, ((1,), (1,)))


def t_dot(left, right):
    return dot(left, right, ((0,), (0,)))


def body(
    enc_in,
    dec_in,
    lengths,
    cot_enc,
    cot_dec,
    enc_gain_attn,
    enc_query,
    enc_key,
    enc_value,
    enc_output,
    relative_bias_table,
    enc_gain_ffn,
    enc_ff_in,
    enc_ff_out,
    enc_gain_final,
    dec_gain_self,
    dec_self_value,
    dec_self_output,
    dec_gain_cross,
    dec_cross_query,
    dec_cross_key,
    dec_cross_value,
    dec_cross_output,
    dec_gain_ffn,
    dec_ff_in,
    dec_ff_out,
):
    pair_count, seq_dev, width = enc_in.shape
    seq_all = 2 * seq_dev
    bucket_count, heads = relative_bias_table.shape
    head_dim = width // heads
    hidden_width = enc_ff_in.shape[1]
    half = width // 2
    cores = lax.axis_size("blk")
    slots = lax.axis_size("batch")
    me = lax.axis_index("blk")
    chip = lax.axis_index("batch")
    stages = slots.bit_length() - 1
    swap = [(0, 1), (1, 0)]

    def across(array):
        return lax.ppermute(array, "blk", swap)

    def whole_pair(array):
        own = lax.dynamic_index_in_dim(array, me, 0, False)
        away = lax.dynamic_index_in_dim(array, 1 - me, 0, False)
        got = across(away)
        return jnp.where(me == 0, jnp.concatenate([own, got]), jnp.concatenate([got, own]))

    def halves(array):
        keep = lax.dynamic_slice_in_dim(array, me * (array.shape[1] // 2), array.shape[1] // 2, 1)
        away = lax.dynamic_slice_in_dim(
            array, (1 - me) * (array.shape[1] // 2), array.shape[1] // 2, 1
        )
        return keep, away

    enc_x = whole_pair(enc_in)
    cot_x = whole_pair(cot_enc)
    dec_x = lax.dynamic_slice_in_dim(dec_in, me, 1, 0).astype(f32)
    cot_d = lax.dynamic_slice_in_dim(cot_dec, me, 1, 0)
    length = lax.dynamic_index_in_dim(lengths, me, 0, False)
    positions = jnp.arange(seq_all, dtype=jnp.int32)
    valid = (positions < length)[None, :]

    def split_heads(array):
        return array.reshape(array.shape[0], heads, head_dim)

    m1 = norm_apply(dec_x, dec_gain_self).astype(bf16)
    sv = dot(m1, dec_self_value).astype(bf16)
    z1 = dec_x + dot(sv, dec_self_output)
    m2 = norm_apply(z1, dec_gain_cross).astype(bf16)
    cq = dot(m2, dec_cross_query).astype(bf16)
    own_head = (
        jnp.arange(width, dtype=jnp.int32)[None, :] // head_dim
        == jnp.arange(heads, dtype=jnp.int32)[:, None]
    )
    zero = jnp.zeros((), bf16)
    key_query = dot_t(jnp.where(own_head, cq, zero), dec_cross_key).astype(bf16)
    hid_up = dot_t(cot_d, dec_ff_out)

    x = enc_x.astype(f32)
    n1 = norm_apply(x, enc_gain_attn).astype(bf16)
    q = split_heads(dot(n1, enc_query).astype(bf16))
    k = split_heads(dot(n1, enc_key).astype(bf16))
    v = split_heads(dot(n1, enc_value).astype(bf16))
    grid = bucket_of(positions[None, :] - positions[:, None])
    one_hot = (jnp.arange(bucket_count, dtype=jnp.int32)[:, None, None] == grid[None]).astype(f32)
    bias = jnp.einsum("vnz,vy->ynz", one_hot, relative_bias_table, precision=lax.Precision.HIGHEST)
    scores = jnp.einsum("qhe,khe->hqk", q, k, preferred_element_type=f32) + bias
    scores = jnp.where(valid[None], scores, masked_score)
    exponent = jnp.exp(scores - jnp.max(scores, axis=-1, keepdims=True))
    weights = exponent / jnp.sum(exponent, axis=-1, keepdims=True)
    low_weights = weights.astype(bf16)
    context = jnp.einsum("hqk,khe->qhe", low_weights, v, preferred_element_type=f32)
    context = context.astype(bf16).reshape(seq_all, width)
    y1 = x + dot(context, enc_output)
    n2 = norm_apply(y1, enc_gain_ffn).astype(bf16)
    a = dot(n2, enc_ff_in)
    gelu, slope = gelu_parts(a)
    hid = gelu.astype(bf16)
    slope = slope.astype(bf16)
    result = y1 + dot(hid, enc_ff_out)
    src = norm_apply(result, enc_gain_final).astype(bf16)
    encoder_output = result.astype(bf16)

    cross = jnp.where(valid, dot_t(key_query, src), masked_score)
    cross = jnp.exp(cross - jnp.max(cross, axis=-1, keepdims=True))
    cross = cross / jnp.sum(cross, axis=-1, keepdims=True)
    low_cross = cross.astype(bf16)
    mix = dot(low_cross, src).astype(bf16)
    cctx = jnp.sum(jnp.where(own_head, dot(mix, dec_cross_value), 0), axis=0, keepdims=True)
    cctx = cctx.astype(bf16)
    z2 = z1 + dot(cctx, dec_cross_output)
    m3 = norm_apply(z2, dec_gain_ffn).astype(bf16)
    b = dot(m3, dec_ff_in)
    dh, dslope = gelu_parts(b)
    dh = dh.astype(bf16)
    dec_result = z2 + dot(dh, dec_ff_out)
    g_b = (dslope * hid_up).astype(bf16)
    gz2 = cot_d.astype(f32) + norm_back(z2, dec_gain_ffn, dot_t(g_b, dec_ff_in))
    gz2_low = gz2.astype(bf16)
    g_cctx = dot_t(gz2_low, dec_cross_output).astype(bf16)
    value_up = dot_t(jnp.where(own_head, g_cctx, zero), dec_cross_value).astype(bf16)
    d_cross = dot_t(value_up, src)
    g_c = cross * (d_cross - jnp.sum(cross * d_cross, axis=-1, keepdims=True))
    g_c = g_c.astype(bf16)
    key_mix = dot(g_c, src).astype(bf16)
    g_cq = jnp.sum(jnp.where(own_head, dot(key_mix, dec_cross_key), 0), axis=0, keepdims=True)
    g_cq = g_cq.astype(bf16)
    gz1 = gz2 + norm_back(z1, dec_gain_cross, dot_t(g_cq, dec_cross_query))
    gz1_low = gz1.astype(bf16)
    g_sv = dot_t(gz1_low, dec_self_output).astype(bf16)
    grad_dec_own = gz1 + norm_back(dec_x, dec_gain_self, dot_t(g_sv, dec_self_value))
    src_up = t_dot(jnp.concatenate([g_c, low_cross]), jnp.concatenate([key_query, value_up]))

    row = jnp.concatenate(
        [m1, sv, m2, cctx, m3, dh, g_sv, gz1_low, g_cq, gz2_low, cq, g_cctx, g_b, cot_d]
        + [key_mix.reshape(1, -1), mix.reshape(1, -1)],
        axis=1,
    )
    table = lax.all_gather(row, ("batch", "blk"), axis=0, tiled=True)

    ge = cot_x.astype(f32) + norm_back(result, enc_gain_final, src_up)
    ge_low = ge.astype(bf16)
    ge_keep, ge_away = halves(ge_low)
    g_a = (slope.astype(f32) * dot_t(ge_low, enc_ff_out)).astype(bf16)
    ga_keep, ga_away = halves(g_a)
    gy1 = ge + norm_back(y1, enc_gain_ffn, dot_t(g_a, enc_ff_in))
    gy1_low = gy1.astype(bf16)
    gy_keep, gy_away = halves(gy1_low)
    g_ctx = split_heads(dot_t(gy1_low, enc_output).astype(bf16))
    prob_up = jnp.einsum("qhe,khe->hqk", g_ctx, v, preferred_element_type=f32)
    delta = jnp.sum(weights * prob_up, axis=-1, keepdims=True)
    g_s = (weights * (prob_up - delta)).astype(bf16)
    table_term = jnp.einsum(
        "tug,cug->tc", one_hot, g_s.astype(f32), precision=lax.Precision.HIGHEST
    )
    g_q = jnp.einsum("hqk,khe->qhe", g_s, k, preferred_element_type=f32).astype(bf16)
    g_k = jnp.einsum("hqk,qhe->khe", g_s, q, preferred_element_type=f32).astype(bf16)
    g_v = jnp.einsum("hqk,qhe->khe", low_weights, g_ctx, preferred_element_type=f32).astype(bf16)
    g_q, g_k, g_v = (part.reshape(seq_all, width) for part in (g_q, g_k, g_v))
    n1_up = dot_t(g_q, enc_query) + dot_t(g_k, enc_key) + dot_t(g_v, enc_value)
    grad_in = gy1 + norm_back(x, enc_gain_attn, n1_up)
    grad_rel_table = lax.psum(table_term, ("batch", "blk"))

    order = list(range(stages))
    crossed = order if stages < 2 else [1, 0] + order[2:]

    def reach(bits):
        masks = []
        for position in range(slots):
            mask = 0
            for stage in range(stages):
                if (position >> (stages - 1 - stage)) & 1:
                    mask |= 1 << bits[stage]
            masks.append(mask)
        return jnp.array(masks, jnp.int32)

    place = chip ^ jnp.where(me == 0, reach(order), reach(crossed))

    def hop(array, stage):
        pairs = []
        for which in range(slots):
            for core in range(2):
                bit = (order, crossed)[core][stage]
                pairs.append((which * 2 + core, (which ^ (1 << bit)) * 2 + core))
        return lax.ppermute(array, ("batch", "blk"), pairs)

    def combine(sums):
        for stage in range(stages):
            rest = sums.shape[0] // 2
            sums = sums[:rest] + hop(sums[rest:], stage)
        return sums[0]

    def weight_sum(left, left_away, keep, away):
        total = t_dot(
            jnp.concatenate([left, left_away]), jnp.concatenate([keep, across(away)])
        ).astype(bf16)
        total = total.reshape(slots, total.shape[0] // slots, total.shape[1])
        total = jnp.take(total, place, axis=0)
        done = combine(total)
        other = across(done)
        return jnp.where(
            me == 0,
            jnp.concatenate([done, other], axis=1),
            jnp.concatenate([other, done], axis=1),
        ).astype(f32)

    hid_away, n2_away, ctx_away, n1_away = (across(part) for part in (hid, n2, context, n1))
    grad_ff_out = weight_sum(hid, hid_away, ge_keep, ge_away)
    grad_ff_in = weight_sum(n2, n2_away, ga_keep, ga_away)
    grad_output = weight_sum(context, ctx_away, gy_keep, gy_away)
    grad_query = weight_sum(n1, n1_away, *halves(g_q))
    grad_key = weight_sum(n1, n1_away, *halves(g_k))
    grad_value = weight_sum(n1, n1_away, *halves(g_v))

    sizes = [width] * 5 + [hidden_width] + [width] * 6 + [hidden_width, width]
    sizes += [heads * width, heads * width]
    offsets = [0] + [int(total) for total in np.cumsum(sizes)]
    (m1s, svs, m2s, cctxs, m3s, dhs, g_svs, gz1s, g_cqs, gz2s, cqs, g_cctxs, g_bs, cots, kms, ms) = (
        table[:, offsets[at] : offsets[at + 1]] for at in range(len(sizes))
    )

    def mine(array, axis):
        size = array.shape[axis] // slots
        return lax.dynamic_slice_in_dim(array, chip * size, size, axis)

    def outer(left, right):
        return t_dot(mine(left, 1), right)

    def outer_heads(left, right):
        left = mine(left.reshape(left.shape[0], heads, width), 2)
        total = jnp.einsum("phd,phe->dhe", left, split_heads(right), preferred_element_type=f32)
        return total.reshape(total.shape[0], width)

    grad_self_value = outer(m1s, g_svs)
    grad_self_output = outer(svs, gz1s)
    grad_cross_query = outer(m2s, g_cqs)
    grad_cross_output = outer(cctxs, gz2s)
    grad_dec_ff_in = outer(m3s, g_bs)
    grad_dec_ff_out = outer(dhs, cots)
    grad_cross_key = outer_heads(kms, cqs)
    grad_cross_value = outer_heads(ms, g_cctxs)

    def gain_grad(gain, *terms):
        total = sum(
            jnp.sum(mine(weight, 0).astype(f32) * gradient, axis=1) for weight, gradient in terms
        )
        return total / mine(gain, 0)

    grad_gain_attn = gain_grad(
        enc_gain_attn, (enc_query, grad_query), (enc_key, grad_key), (enc_value, grad_value)
    )
    grad_gain_ffn = gain_grad(enc_gain_ffn, (enc_ff_in, grad_ff_in))
    grad_gain_final = gain_grad(
        enc_gain_final, (dec_cross_key, grad_cross_key), (dec_cross_value, grad_cross_value)
    )
    grad_gain_self = gain_grad(dec_gain_self, (dec_self_value, grad_self_value))
    grad_gain_cross = gain_grad(dec_gain_cross, (dec_cross_query, grad_cross_query))
    grad_dec_gain_ffn = gain_grad(dec_gain_ffn, (dec_ff_in, grad_dec_ff_in))

    def own_block(array):
        blocks = array.reshape(2, seq_dev, width)
        kept = lax.dynamic_index_in_dim(blocks, me, 0, False)
        got = across(lax.dynamic_index_in_dim(blocks, 1 - me, 0, False))
        return jnp.where(me == 0, jnp.stack([kept, got]), jnp.stack([got, kept]))

    def both_rows(array):
        got = across(array)
        return jnp.where(
            me == 0, jnp.concatenate([array, got]), jnp.concatenate([got, array])
        )

    return (
        own_block(encoder_output),
        both_rows(dec_result.astype(bf16)),
        own_block(grad_in),
        both_rows(grad_dec_own),
        grad_gain_attn,
        grad_query,
        grad_key,
        grad_value,
        grad_output,
        grad_rel_table,
        grad_gain_ffn,
        grad_ff_in,
        grad_ff_out,
        grad_gain_final,
        grad_gain_self,
        grad_self_value,
        grad_self_output,
        grad_gain_cross,
        grad_cross_query,
        grad_cross_key,
        grad_cross_value,
        grad_cross_output,
        grad_dec_gain_ffn,
        grad_dec_ff_in,
        grad_dec_ff_out,
    )


def solution(mesh):
    split = P("batch", "blk", None)
    rows = P("batch", None)
    line = P("batch")
    placed = (split, rows, line, split, rows) + (P(),) * 21
    return jax.shard_map(
        body,
        mesh=mesh,
        in_specs=placed,
        out_specs=(
            (split, rows, split, rows, line, rows, rows, rows, rows, P(), line, rows, rows, line)
            + (line, rows, rows, line, rows, rows, rows, rows, line, rows, rows)
        ),
        check_vma=False,
    )
```

```python
import functools

import jax
import jax.numpy as jnp
from jax import lax
from jax.experimental import pallas as pl
from jax.experimental.pallas import tpu as pltpu
from jax.sharding import PartitionSpec as P

epsilon = 1e-06
masked_score = -1e30
thresholds = (12, 16, 23, 32, 46, 64, 91)
bf16 = jnp.bfloat16
f32 = jnp.float32
tile = 128
chunk = 32
mib = 1 << 20


def bucket_of(offset):
    distance = jnp.abs(offset)
    larger = jnp.full(offset.shape, 8, jnp.int32)
    for limit in thresholds:
        larger = larger + jnp.where(distance >= limit, 1, 0)
    inner = jnp.where(distance < 8, distance, larger)
    return jnp.where(offset > 0, 16, 0) + inner


def norm_scale(values):
    return lax.rsqrt(jnp.mean(values * values, axis=-1, keepdims=True) + epsilon)


def norm_apply(values, gain):
    return values * norm_scale(values) * gain


def norm_back(values, gain, upstream):
    scale = norm_scale(values)
    weighted = upstream * gain
    inner = jnp.mean(weighted * values, axis=-1, keepdims=True)
    return scale * weighted - values * (scale * scale * scale * inner)


def gelu_parts(a):
    root = 0.7978845608028654
    square = a * a
    t = jnp.tanh(root * a * (1.0 + 0.044715 * square))
    half = 0.5 + 0.5 * t
    slope = half + (half * (1.0 - t)) * (a * (root + (3 * 0.044715 * root) * square))
    return a * half, slope


def dot(left, right, dims=((1,), (0,))):
    return lax.dot_general(left, right, (dims, ((), ())), preferred_element_type=f32)


def dot_t(left, right):
    return dot(left, right, ((1,), (1,)))


def t_dot(left, right):
    return dot(left, right, ((0,), (0,)))


def shape(dims, kind):
    return jax.ShapeDtypeStruct(dims, kind)


def whole(array, buffers=None):
    zeros = (0,) * array.ndim
    if buffers is None:
        return pl.BlockSpec(array.shape, lambda *at: zeros)
    return pl.BlockSpec(array.shape, lambda *at: zeros, pipeline_mode=pl.Buffered(buffers))


class Chain:
    def __init__(self):
        self.last = ()

    def run(
        self, kernel, name, grid, args, in_specs, outs, out_specs, scalars=(), scratch=(),
        flops=0, limit=63, also=(),
    ):
        size = sum(a.size * a.dtype.itemsize for a in list(args) + list(outs))
        last = self.last + also
        skip = len(scalars) + len(args)

        def inner(*refs):
            kernel(*refs[:skip], *refs[skip + len(last) :])

        done = pl.pallas_call(
            inner,
            out_shape=outs,
            grid_spec=pltpu.PrefetchScalarGridSpec(
                num_scalar_prefetch=len(scalars),
                grid=grid,
                in_specs=list(in_specs) + [pl.BlockSpec(memory_space=pl.ANY)] * len(last),
                out_specs=out_specs,
                scratch_shapes=scratch,
            ),
            compiler_params=pltpu.CompilerParams(
                vmem_limit_bytes=limit * mib, dimension_semantics=("arbitrary",) * len(grid)
            ),
            cost_estimate=pl.CostEstimate(
                flops=int(4 * flops), bytes_accessed=int(size), transcendentals=0
            ),
            name=name,
        )(*scalars, *args, *last)
        self.last = (done[0],)
        return done


any_space = pl.BlockSpec(memory_space=pl.ANY)
dma = pltpu.SemaphoreType.DMA


def row_of(gain_ref):
    return gain_ref[...].reshape(1, -1)


def fetch(pairs, sems):
    copies = [
        pltpu.make_async_copy(source, target, sems.at[at])
        for at, (source, target) in enumerate(pairs)
    ]
    for copy in copies:
        copy.start()
    return copies


def picked(me, ref):
    rows = ref[...].astype(f32)
    return jnp.where(me == 0, rows[0:1], rows[1:2])


def joined(me, own, got):
    first = jnp.where(me == 0, own, got)
    last = jnp.where(me == 0, got, own)
    return jnp.concatenate([first, last], axis=0)


def encoder_kernel(
    info, lens, gain_ref, table_ref, ffn_ref, final_ref,
    own_any, got_any, wq_any, wk_any, wv_any, wo_any, win_any, wout_any,
    src_ref, low_ref, away_ref, scale_ref,
    n1_any, qt_any, k_any, v_any, e_any, ctx_any, y1_any, n2_any, hid_any, slope_any,
    x_ref, n1_ref, qt_ref, k_ref, v_ref, e_ref, ctx_ref, y1_ref, n2_ref, hid_ref, slope_ref,
    acc_ref, bias_ref, s_ref, wq_ref, wk_ref, wv_ref, wo_ref, win_ref, wout_ref, sems, out_sems, x_sems,
    *, heads, group,
):
    me = info[0]
    seq, width = x_ref.shape
    head_dim = width // heads
    blocks = seq // tile
    parts = win_ref.shape[0]
    wide = group * head_dim
    rounds = heads // group

    loads = []
    for at in range(rounds):
        spot = pl.ds(at * wide, wide)
        for any_ref, ref in ((wq_any, wq_ref), (wk_any, wk_ref), (wv_any, wv_ref)):
            loads.append((any_ref.at[:, spot], ref.at[at]))
    loads.append((wo_any, wo_ref))
    for at in range(parts):
        spot = pl.ds(at * width, width)
        loads.append((win_any.at[:, spot], win_ref.at[at]))
        loads.append((wout_any.at[spot, :], wout_ref.at[at]))
    loads = [
        pltpu.make_async_copy(source, target, sems.at[at])
        for at, (source, target) in enumerate(loads)
    ]
    first = fetch(
        ((own_any.at[me], x_ref.at[pl.ds(me * (seq // 2), seq // 2), :]),
         (got_any.at[me], x_ref.at[pl.ds((1 - me) * (seq // 2), seq // 2), :])), x_sems
    )
    for copy in loads[: 3 * rounds]:
        copy.start()
    saved = []

    def save(source, target):
        copy = pltpu.make_async_copy(source, target, out_sems.at[len(saved)])
        copy.start()
        saved.append(copy)

    tables = jnp.concatenate(
        [table_ref[...], jnp.zeros((table_ref.shape[0], tile - heads), f32)], axis=1
    ).T
    tables = jnp.concatenate(
        [tables, jnp.zeros((tile, tile - table_ref.shape[0]), f32)], axis=1
    )
    rows = lax.broadcasted_iota(jnp.int32, (tile, tile), 0)
    lanes = lax.broadcasted_iota(jnp.int32, (tile, tile), 1)
    kinds = [bucket_of((gap - 1) * tile + rows - lanes) for gap in range(3)]
    for head in range(heads):
        line = jnp.broadcast_to(tables[head : head + 1, :], (tile, tile))
        for gap in range(3):
            bias_ref[head, gap] = jnp.take_along_axis(line, kinds[gap], axis=1)

    for copy in first:
        copy.wait()
    n1_ref[...] = norm_apply(x_ref[...].astype(f32), row_of(gain_ref)).astype(bf16)
    save(n1_ref, n1_any)

    pair_rows = lax.broadcasted_iota(jnp.int32, (2 * head_dim, seq), 0)
    pair_lanes = lax.broadcasted_iota(jnp.int32, (seq, 2 * head_dim), 1)
    key_at = lax.broadcasted_iota(jnp.int32, (seq, 2 * head_dim), 0)
    gone = jnp.where(key_at < lens[me], 0.0, masked_score).astype(bf16)
    ones = jnp.ones((16, seq), bf16)
    vts = {}

    def project(at):
        n1 = n1_ref[...]
        for copy in loads[3 * at : 3 * at + 3]:
            copy.wait()
        for copy in loads[3 * rounds + 3 * at : 3 * rounds + 3 * at + 3]:
            copy.start()
        spot = slice(at * wide, (at + 1) * wide)
        qt_ref[spot, :] = dot(n1, wq_ref[at]).T.astype(bf16)
        k_ref[:, spot] = dot(n1, wk_ref[at]).astype(bf16)
        v = dot(n1, wv_ref[at])
        v_ref[:, spot] = v.astype(bf16)
        vts[at] = v.T.astype(bf16)

    def scores(head):
        pair = slice(head // 2 * 2 * head_dim, (head // 2 + 1) * 2 * head_dim)
        k2, q2 = k_ref[:, pair], qt_ref[pair, :]
        zero = jnp.zeros((), bf16)
        if head % 2 == 0:
            k2 = jnp.where(pair_lanes < head_dim, k2, jnp.where(pair_lanes == head_dim, gone, zero))
            q2 = jnp.where(pair_rows < head_dim, q2, jnp.ones((), bf16))
        else:
            k2 = jnp.where(pair_lanes >= head_dim, k2, jnp.where(pair_lanes == 0, gone, zero))
            q2 = jnp.where(pair_rows >= head_dim, q2, jnp.ones((), bf16))
        s_ref[head % 2] = dot(k2, q2)

    def weigh(head):
        slot = head % 2
        before = tables[head : head + 1, 15:16]
        after = tables[head : head + 1, 31:32]
        for query in range(blocks):
            across = slice(query * tile, (query + 1) * tile)
            tops = None
            for key in range(blocks):
                gap = key - query
                bias = before if gap < -1 else after if gap > 1 else bias_ref[head, gap + 1]
                down = slice(key * tile, (key + 1) * tile)
                value = s_ref[slot, down, across] + bias
                s_ref[slot, down, across] = value
                top = jnp.max(value.reshape(tile // 8, 8, tile), axis=0)
                tops = top if tops is None else jnp.maximum(tops, top)
            peak = jnp.max(tops, axis=0, keepdims=True)
            for key in range(blocks):
                down = slice(key * tile, (key + 1) * tile)
                e_ref[head, down, across] = jnp.exp(s_ref[slot, down, across] - peak).astype(bf16)
        save(e_ref.at[head], e_any.at[head])

    def mix(head):
        at, inner = divmod(head, group)
        vt = vts[at][inner * head_dim : (inner + 1) * head_dim]
        full = dot(jnp.concatenate([vt, ones], axis=0), e_ref[head])
        scale = 1.0 / full[head_dim : head_dim + 1]
        scale_ref[head : head + 1, :] = scale
        ctx_ref[head * head_dim : (head + 1) * head_dim, :] = (full[:head_dim] * scale).astype(bf16)

    project(0)
    scores(0)
    for head in range(heads):
        if head % group == 0 and head // group + 1 < rounds:
            project(head // group + 1)
        if head + 1 < heads:
            scores(head + 1)
        weigh(head)
        mix(head)
    scale_ref[heads:, :] = jnp.zeros((16 - heads, seq), f32)
    save(qt_ref, qt_any)
    save(k_ref, k_any)
    save(v_ref, v_any)
    save(ctx_ref, ctx_any)

    loads[3 * rounds].wait()
    y1 = x_ref[...].astype(f32) + t_dot(ctx_ref[...], wo_ref[...])
    acc_ref[...] = y1
    y1_ref[...] = y1.astype(bf16)
    n2_ref[...] = norm_apply(y1, row_of(ffn_ref)).astype(bf16)
    save(y1_ref, y1_any)
    save(n2_ref, n2_any)
    for at in range(parts):
        spot = pl.ds(at * width, width)
        loads[3 * rounds + 1 + 2 * at].wait()
        value, slope = gelu_parts(dot(n2_ref[...], win_ref[at]))
        hid_ref[at] = value.astype(bf16)
        slope_ref[at] = slope.astype(bf16)
        save(hid_ref.at[at], hid_any.at[:, spot])
        save(slope_ref.at[at], slope_any.at[:, spot])
        loads[3 * rounds + 2 + 2 * at].wait()
        acc_ref[...] += dot(hid_ref[at], wout_ref[at])
    result = acc_ref[...]
    low = result.astype(bf16)
    low_ref[...] = low
    half = seq // 2
    away_ref[...] = jnp.where(me == 0, low[half:], low[:half])
    src_ref[...] = norm_apply(result, row_of(final_ref)).astype(bf16)
    for copy in saved:
        copy.wait()


def encoder(
    chain, info, lens, enc_in, got, gain, wq, wk, wv, table, ffn, final, wo, win, wout, heads, also
):
    pairs, seq_dev, width = enc_in.shape
    seq = 2 * seq_dev
    hidden = win.shape[1]
    group = 4
    rounds = heads // group
    wide = width // rounds
    parts = hidden // width
    act, turned = shape((seq, width), bf16), shape((width, seq), bf16)
    part, tall = shape((seq_dev, width), bf16), shape((seq, hidden), bf16)
    near = (act, act, part, shape((16, seq), f32))
    far = (act, turned, act, act, shape((heads, seq, seq), bf16), turned, act, act, tall, tall)
    small = (gain, table, ffn, final)

    def vmem(dims, kind=bf16):
        return pltpu.VMEM(dims, kind)

    return chain.run(
        functools.partial(encoder_kernel, heads=heads, group=group),
        "encoder_forward",
        (1,),
        small + (enc_in, got, wq, wk, wv, wo, win, wout),
        [whole(a) for a in small] + [any_space] * 8,
        near + far,
        tuple(whole(a) for a in near) + (any_space,) * len(far),
        scalars=(info, lens),
        scratch=(
            vmem((seq, width)), vmem((seq, width)), vmem((width, seq)), vmem((seq, width)),
            vmem((seq, width)), vmem((heads, seq, seq)), vmem((width, seq)), vmem((seq, width)),
            vmem((seq, width)), vmem((parts, seq, width)), vmem((parts, seq, width)),
            vmem((seq, width), f32), vmem((heads, 3, tile, tile), f32), vmem((2, seq, seq), f32),
            vmem((rounds, width, wide)), vmem((rounds, width, wide)), vmem((rounds, width, wide)),
            vmem((width, width)), vmem((parts, width, width)), vmem((parts, width, width)),
            dma((3 * rounds + 1 + 2 * parts,)), dma((7 + heads + 2 * parts,)), dma((2,)),
        ),
        flops=2 * seq * width * (4 * width + 2 * hidden) + 16 * seq * seq * width,
        also=also,
    )


def wide_row(row):
    return jnp.broadcast_to(row.astype(bf16), (16, row.shape[1]))


def row_dot(row, weight):
    return dot(wide_row(row), weight)[0:1]


def row_dot_t(row, weight):
    return dot_t(wide_row(row), weight)[0:1]


def head_mask(width, head_dim):
    rows = lax.broadcasted_iota(jnp.int32, (16, width), 0)
    lanes = lax.broadcasted_iota(jnp.int32, (16, width), 1)
    return (lanes >= rows * head_dim) & (lanes < (rows + 1) * head_dim)


def spread(row, mask):
    return jnp.where(mask, jnp.broadcast_to(row, mask.shape), 0.0).astype(bf16)


def before_kernel(
    info, dec_ref, cot_ref, self_ref, cross_ref, wsv_any, wso_any, wcq_any, wk_any, wout_any,
    state_ref, kq_ref, up_ref, wsv, wso, wcq, wk, wout, sems, *, head_dim,
):
    copies = fetch(
        ((wsv_any, wsv), (wso_any, wso), (wcq_any, wcq), (wk_any, wk), (wout_any, wout)), sems
    )
    x = picked(info[0], dec_ref)
    m1 = norm_apply(x, row_of(self_ref)).astype(bf16).astype(f32)
    copies[0].wait()
    sv = row_dot(m1, wsv[...]).astype(bf16).astype(f32)
    copies[1].wait()
    z1 = x + row_dot(sv, wso[...])
    m2 = norm_apply(z1, row_of(cross_ref)).astype(bf16).astype(f32)
    copies[2].wait()
    cq = row_dot(m2, wcq[...]).astype(bf16).astype(f32)
    copies[3].wait()
    kq_ref[...] = dot_t(spread(cq, head_mask(x.shape[1], head_dim)), wk[...]).astype(bf16)
    copies[4].wait()
    up_ref[...] = row_dot_t(picked(info[0], cot_ref), wout[...])
    for at, row in enumerate((x, m1, sv, z1, m2, cq)):
        state_ref[at : at + 1, :] = row
    state_ref[6:8, :] = jnp.zeros((2, x.shape[1]), f32)


def before(chain, info, dec, cot, gain_self, gain_cross, wsv, wso, wcq, wk, wout, head_dim):
    width, hidden = dec.shape[1], wout.shape[0]
    weights = (wsv, wso, wcq, wk, wout)
    small = (dec, cot, gain_self, gain_cross)
    outs = (shape((8, width), f32), shape((16, width), bf16), shape((1, hidden), f32))
    return chain.run(
        functools.partial(before_kernel, head_dim=head_dim), "decoder_before", (1,),
        small + weights, [whole(a) for a in small] + [any_space] * 5, outs,
        tuple(whole(a) for a in outs), scalars=(info,),
        scratch=tuple(pltpu.VMEM(w.shape, bf16) for w in weights) + (dma((5,)),),
        flops=32 * wout.size,
    )


def cross_kernel(
    info, lens, src_ref, kq_ref, state_ref, up_ref, cot_ref, gain_ref, result_ref,
    own_ref, got_ref, final_ref, wv_any, wco_any, win_any,
    low_ref, away_ref, rows_ref, long_ref, gc_ref, mix_ref, wv, wco, win, sems, *, head_dim,
):
    copies = fetch(((wv_any, wv), (wco_any, wco), (win_any, win)), sems)
    src = src_ref[...]
    seq, width = src.shape
    gain = row_of(gain_ref)
    mask = head_mask(width, head_dim)
    lanes = lax.broadcasted_iota(jnp.int32, (16, seq), 1)
    c = jnp.where(lanes < lens[info[0]], dot_t(kq_ref[...], src), masked_score)
    c = jnp.exp(c - jnp.max(c, axis=-1, keepdims=True))
    c = c * (1.0 / jnp.sum(c, axis=-1, keepdims=True))
    c_low = c.astype(bf16)
    mix = dot(c_low, src).astype(bf16)
    mix_ref[...] = mix
    copies[0].wait()
    cctx = jnp.sum(jnp.where(mask, dot(mix, wv[...]), 0.0), axis=0, keepdims=True)
    cctx = cctx.astype(bf16).astype(f32)
    copies[1].wait()
    z2 = state_ref[3:4, :] + row_dot(cctx, wco[...])
    m3 = norm_apply(z2, gain).astype(bf16).astype(f32)
    copies[2].wait()
    dh, slope = gelu_parts(row_dot(m3, win[...]))
    g_b = (slope * up_ref[...]).astype(bf16).astype(f32)
    cot = picked(info[0], cot_ref)
    gz2 = cot + norm_back(z2, gain, row_dot_t(g_b, win[...]))
    g_cctx = row_dot_t(gz2, wco[...]).astype(bf16).astype(f32)
    up = dot_t(spread(g_cctx, mask), wv[...]).astype(bf16)
    d_c = dot_t(up, src)
    g_c = (c * (d_c - jnp.sum(c * d_c, axis=-1, keepdims=True))).astype(bf16)
    src_up = t_dot(
        jnp.concatenate([g_c, c_low], axis=0), jnp.concatenate([kq_ref[...], up], axis=0)
    )
    cot_x = joined(info[0], own_ref[0], got_ref[0]).astype(f32)
    low = (cot_x + norm_back(result_ref[...].astype(f32), row_of(final_ref), src_up)).astype(bf16)
    low_ref[...] = low
    half = width // 2
    away_ref[...] = jnp.where(info[0] == 0, low[:, half:], low[:, :half])
    gc_ref[...] = g_c
    for at, row in enumerate((cctx, z2, m3, gz2, g_cctx, cot)):
        rows_ref[at : at + 1, :] = row
    rows_ref[6:8, :] = jnp.zeros((2, width), f32)
    long_ref[0:1, :] = dh
    long_ref[1:2, :] = g_b


def cross(chain, info, lens, src, kq, state, up, cot, gain, result, cot_enc, got, final, weights, head_dim):
    seq, width = src.shape
    hidden = up.shape[1]
    small = (src, kq, state, up, cot, gain, result, cot_enc, got, final)
    outs = (
        shape((seq, width), bf16), shape((seq, width // 2), bf16), shape((8, width), f32),
        shape((2, hidden), f32), shape((16, seq), bf16), shape((16, width), bf16),
    )
    specs = [whole(a) for a in small]
    specs[7] = specs[8] = pl.BlockSpec(
        (1,) + cot_enc.shape[1:], lambda i, info, lens: (info[0], 0, 0)
    )
    return chain.run(
        functools.partial(cross_kernel, head_dim=head_dim), "decoder_cross", (1,),
        small + weights, specs + [any_space] * 3, outs, tuple(whole(a) for a in outs),
        scalars=(info, lens),
        scratch=tuple(pltpu.VMEM(w.shape, bf16) for w in weights) + (dma((3,)),),
        flops=64 * weights[2].size,
    )


def after_kernel(
    src_ref, gc_ref, state_ref, rows_ref, long_ref, mix_ref, self_ref, cross_ref,
    wk_any, wcq_any, wso_any, wsv_any, wout_any,
    both_ref, pack_ref, wk, wcq, wso, wsv, wout, pad_ref, sems, *, head_dim, heads,
):
    copies = fetch(
        ((wk_any, wk), (wcq_any, wcq), (wso_any, wso), (wsv_any, wsv), (wout_any, wout)), sems
    )
    x, z1 = state_ref[0:1, :], state_ref[3:4, :]
    z2, gz2 = rows_ref[1:2, :], rows_ref[3:4, :]
    dh, g_b = long_ref[0:1, :], long_ref[1:2, :]
    width = x.shape[1]
    mask = head_mask(width, head_dim)
    mix = dot(gc_ref[...], src_ref[...]).astype(bf16)
    copies[0].wait()
    g_cq = jnp.sum(jnp.where(mask, dot(mix, wk[...]), 0.0), axis=0, keepdims=True)
    g_cq = g_cq.astype(bf16).astype(f32)
    copies[1].wait()
    gz1 = gz2 + norm_back(z1, row_of(cross_ref), row_dot_t(g_cq, wcq[...]))
    copies[2].wait()
    g_sv = row_dot_t(gz1, wso[...]).astype(bf16).astype(f32)
    copies[3].wait()
    both_ref[1:2, :] = gz1 + norm_back(x, row_of(self_ref), row_dot_t(g_sv, wsv[...]))
    copies[4].wait()
    both_ref[0:1, :] = z2 + row_dot(dh, wout[...])
    count = dh.shape[1] // width
    g_bs = [g_b[:, at * width : (at + 1) * width] for at in range(count)]
    dhs = [dh[:, at * width : (at + 1) * width] for at in range(count)]
    right = [g_sv, gz1, g_cq, gz2, state_ref[5:6, :], rows_ref[4:5, :], rows_ref[5:6, :]] + g_bs
    left = [state_ref[1:2, :], state_ref[2:3, :], state_ref[4:5, :], rows_ref[0:1, :], rows_ref[2:3, :]]
    left += dhs
    for at, row in enumerate(right + left):
        pad_ref[at : at + 1, :] = row
    at = len(right + left)
    pad_ref[at : at + heads, :] = mix[:heads].astype(f32)
    pad_ref[at + heads : at + 2 * heads, :] = mix_ref[:heads].astype(f32)
    rest = pad_ref.shape[0] - at - 2 * heads
    pad_ref[at + 2 * heads :, :] = jnp.zeros((rest, width), f32)
    pack_ref[...] = pad_ref[...].astype(bf16)


def pack_rows(width, hidden, heads):
    return -(-(12 + 2 * hidden // width + 2 * heads) // 16) * 16


def after(chain, src, gc, state, rows, long, mix, gain_self, gain_cross, weights, head_dim, heads):
    width = src.shape[1]
    small = (src, gc, state, rows, long, mix, gain_self, gain_cross)
    count = pack_rows(width, long.shape[1], heads)
    outs = (shape((2, width), f32), shape((count, width), bf16))
    return chain.run(
        functools.partial(after_kernel, head_dim=head_dim, heads=heads), "decoder_after", (1,),
        small + weights, [whole(a) for a in small] + [any_space] * 5, outs,
        tuple(whole(a) for a in outs),
        scratch=tuple(pltpu.VMEM(w.shape, bf16) for w in weights)
        + (pltpu.VMEM((count, width), f32), dma((5,))),
        flops=32 * weights[4].size,
    )


def backward_kernel(
    info, gain_ref, low_any, slope_any, wout_any, win_any, y1_any, wo_any,
    *refs,
):
    (low_ref, slope_ref, wout_ref, win_ref, y1_ref, wo_ref, ga_ref, gylow_ref, acc_ref) = refs[-11:-2]
    sems, out_sems = refs[-2:]
    me = info[0]
    parts, seq, width = slope_ref.shape
    part = parts // 2
    away_anys, (keep_any, gylow_any, gyaway_ref, gctx_ref) = refs[:part], refs[part : part + 4]
    chunks = [(1 - me) * part + at for at in range(part)] + [me * part + at for at in range(part)]
    loads = [(low_any, low_ref)]
    for at, chunk_at in enumerate(chunks):
        spot = pl.ds(pl.multiple_of(chunk_at * width, width), width)
        loads.append((wout_any.at[spot, :], wout_ref.at[at]))
        loads.append((slope_any.at[:, spot], slope_ref.at[at]))
        loads.append((win_any.at[:, spot], win_ref.at[at]))
    loads += [(y1_any, y1_ref), (wo_any, wo_ref)]
    loads = fetch(loads, sems)
    saved = []
    loads[0].wait()
    for at in range(parts):
        loads[1 + 3 * at].wait()
        rise = dot_t(low_ref[...], wout_ref[at])
        loads[2 + 3 * at].wait()
        ga_ref[at] = (slope_ref[at].astype(f32) * rise).astype(bf16)
        if at < part:
            target = away_anys[at]
        else:
            target = keep_any.at[:, pl.ds(at % part * width, width)]
        copy = pltpu.make_async_copy(ga_ref.at[at], target, out_sems.at[at])
        copy.start()
        saved.append(copy)
        loads[3 + 3 * at].wait()
        if at == 0:
            acc_ref[...] = dot_t(ga_ref[at], win_ref[at])
        else:
            acc_ref[...] += dot_t(ga_ref[at], win_ref[at])
    loads[-2].wait()
    y1 = y1_ref[...].astype(f32)
    low = (low_ref[...].astype(f32) + norm_back(y1, row_of(gain_ref), acc_ref[...])).astype(bf16)
    gylow_ref[...] = low
    copy = pltpu.make_async_copy(gylow_ref, gylow_any, out_sems.at[parts])
    copy.start()
    saved.append(copy)
    half = width // 2
    gyaway_ref[...] = jnp.where(me == 0, low[:, half:], low[:, :half])
    loads[-1].wait()
    gctx_ref[...] = dot_t(wo_ref[...], low).astype(bf16)
    for copy in saved:
        copy.wait()


def backward(chain, info, low, slope, wout, win, y1, gain, wo):
    seq, width = low.shape
    hidden = win.shape[1]
    parts = hidden // width
    act, tall = shape((seq, width), bf16), shape((seq, hidden // 2), bf16)
    side, turned = shape((seq, width // 2), bf16), shape((width, seq), bf16)

    def vmem(*dims):
        return pltpu.VMEM(dims, bf16)

    return chain.run(
        backward_kernel,
        "feed_forward_back",
        (1,),
        (gain, low, slope, wout, win, y1, wo),
        [whole(gain)] + [any_space] * 6,
        (act,) * (parts // 2) + (tall, act, side, turned),
        (any_space,) * (parts // 2) + (any_space, any_space, whole(side), whole(turned)),
        scalars=(info,),
        scratch=(
            vmem(seq, width), vmem(parts, seq, width), vmem(parts, width, width),
            vmem(parts, width, width), vmem(seq, width), vmem(width, width),
            vmem(parts, seq, width), vmem(seq, width), pltpu.VMEM((seq, width), f32),
            dma((3 + 3 * parts,)), dma((parts + 1,)),
        ),
        flops=2 * seq * width * (width + 2 * hidden),
    )


def attention_back_kernel(
    info, scale_ref, gain_ref, own_ref, got_ref, qt_any, k_any, v_any, ctx_any, gctx_any, e_any,
    wq_any, wk_any, wv_any, gy_any,
    gq_ref, gk_ref, gv_ref, keep_ref, gradkeep_ref, gradaway_ref, table_ref,
    qt_ref, k_ref, v_ref, ctx_ref, gctx_ref, e_ref, wq_ref, wk_ref, wv_ref, gy_ref,
    rise_ref, gs_ref, sums_ref, acc_ref, sems, *, heads,
):
    me = info[0]
    seq, width = k_ref.shape
    head_dim = width // heads
    blocks = seq // tile
    half = width // 2
    side = heads // 2
    pair = 2 * head_dim
    loads = fetch(
        ((k_any, k_ref), (v_any, v_ref), (qt_any, qt_ref), (gctx_any, gctx_ref), (ctx_any, ctx_ref))
        + tuple(
            (e_any.at[(1 - me) * side + at if at < side else me * side + at - side], e_ref.at[at])
            for at in range(heads)
        )
        + ((wq_any, wq_ref), (wk_any, wk_ref), (wv_any, wv_ref), (gy_any, gy_ref)),
        sems,
    )
    for copy in loads[:5]:
        copy.wait()
    pair_lanes = lax.broadcasted_iota(jnp.int32, (seq, pair), 1)
    ones = [
        jnp.where((pair_lanes == start) | (pair_lanes == start + 1), 1.0, 0.0).astype(bf16)
        for start in (head_dim, 0)
    ]
    low_half = pair_lanes < head_dim
    none = jnp.zeros((head_dim - 16, seq), bf16)
    line_rows = lax.broadcasted_iota(jnp.int32, (16, seq), 0)
    sums_ref[...] = jnp.zeros(sums_ref.shape, f32)

    def first_of(at):
        base = (1 - me if at < side else me) * half
        return pl.multiple_of(base + at % side // 2 * pair, pair)

    def prepare(at):
        rows = pl.ds(first_of(at), pair)
        g2 = gctx_ref[rows, :].astype(f32)
        head = lax.div(first_of(at), head_dim)
        g2 = jnp.concatenate(
            [
                g2[:head_dim] * scale_ref[pl.ds(head, 1), :],
                g2[head_dim:] * scale_ref[pl.ds(head + 1, 1), :],
            ],
            axis=0,
        )
        both = g2 * ctx_ref[rows, :].astype(f32)
        g2 = g2.astype(bf16)
        g_ext = []
        for inner in range(2):
            here = slice(inner * head_dim, (inner + 1) * head_dim)
            delta = -jnp.sum(both[here], axis=0, keepdims=True)
            high = delta.astype(bf16).astype(f32)
            extra = jnp.where(line_rows == 0, high, jnp.where(line_rows == 1, delta - high, 0.0))
            extra = extra.astype(bf16)
            if inner == 0:
                g_ext.append(jnp.concatenate([g2[here], extra, none], axis=0))
            else:
                g_ext.append(jnp.concatenate([extra, none, g2[here]], axis=0))
        return g2, g_ext

    pairs = {}

    def rise(at):
        upper = at % 2
        if not upper:
            pairs[at // 2] = prepare(at)
        v2 = v_ref[:, pl.ds(first_of(at), pair)]
        v_ext = jnp.where(low_half, ones[1], v2) if upper else jnp.where(low_half, v2, ones[0])
        rise_ref[upper] = dot(v_ext, pairs[at // 2][1][upper])

    def spread_scores(at):
        slot = at % 2
        near, outer = [], [None, None]
        for sub in range(tile // chunk):
            sums = [None] * 5
            for key in range(blocks):
                start = key * tile + sub * chunk
                down = slice(start, start + chunk)
                for query in range(blocks):
                    across = slice(query * tile, (query + 1) * tile)
                    g = e_ref[at, down, across].astype(f32) * rise_ref[slot, down, across]
                    gs_ref[slot, down, across] = g.astype(bf16)
                    kind = min(max(query - key, -2), 2) + 2
                    sums[kind] = g if sums[kind] is None else sums[kind] + g
            near.append(jnp.concatenate(sums[1:4] + [jnp.zeros((chunk, tile), f32)], axis=1))
            outer = [a if b is None else a + b for a, b in zip((sums[4], sums[0]), outer)]
        folded = jnp.concatenate(near, axis=0)
        lanes = 4 * tile
        while folded.shape[0] > 8:
            rest = folded.shape[0] // 2
            folded = folded[:rest] + pltpu.roll(folded[rest:], lanes - rest, 1)
        rows = lax.broadcasted_iota(jnp.int32, folded.shape, 0)
        for bit in (4, 2, 1):
            moved = pltpu.roll(folded, lanes - bit, 1)
            folded = jnp.where((rows & bit) != 0, moved, folded)
        line = jnp.sum(folded, axis=0, keepdims=True)
        outer = [jnp.sum(part, axis=0, keepdims=True) for part in outer]
        row = (8 if at >= side else 0) + at % side
        sums_ref[row : row + 1, :] = jnp.concatenate([line] + outer, axis=1)

    parts = {}
    rise(0)
    for at in range(heads):
        first = first_of(at)
        upper = at % 2
        if at + 1 < heads:
            rise(at + 1)
        loads[5 + at].wait()
        if not upper:
            turned = k_ref[:, pl.ds(first, pair)].astype(f32).T.astype(bf16)
        spread_scores(at)
        here = slice(upper * head_dim, (upper + 1) * head_dim)
        q_mine = qt_ref[pl.ds(pl.multiple_of(first + upper * head_dim, head_dim), head_dim), :]
        g_q = dot(turned[here], gs_ref[upper])
        g_k = dot_t(q_mine, gs_ref[upper])
        g_v = dot_t(pairs[at // 2][0][here], e_ref[at])
        parts[upper] = (g_q, g_k, g_v)
        if upper:
            for which, gone_ref in enumerate((gq_ref, gk_ref, gv_ref)):
                both = jnp.concatenate([parts[0][which], parts[1][which]], axis=0).T.astype(bf16)
                start = at % side // 2 * pair
                if at < side:
                    gone_ref[:, start : start + pair] = both
                else:
                    keep_ref[:, which * half + start : which * half + start + pair] = both
    for copy in loads[5 + heads :]:
        copy.wait()
    total = None
    for which, (ref, gone_ref) in enumerate(((wq_ref, gq_ref), (wk_ref, gk_ref), (wv_ref, gv_ref))):
        kept = keep_ref[:, which * half : (which + 1) * half]
        for part, base in ((gone_ref[...], (1 - me) * half), (kept, me * half)):
            part = dot_t(part, ref[:, pl.ds(pl.multiple_of(base, half), half)])
            total = part if total is None else total + part
    x = joined(me, own_ref[0], got_ref[0]).astype(f32)
    grad = gy_ref[...].astype(f32) + norm_back(x, row_of(gain_ref), total)
    middle = seq // 2
    gradkeep_ref[...] = jnp.where(me == 0, grad[:middle], grad[middle:])
    gradaway_ref[...] = jnp.where(me == 0, grad[middle:], grad[:middle])
    sums = joined(me, sums_ref[8:], sums_ref[:8])
    spots = lax.broadcasted_iota(jnp.int32, (sums.shape[1], tile), 0)
    offsets = tile - jnp.where(spots < 3 * tile, spots, spots - 4 * tile)
    kinds = jnp.where(spots < 4 * tile, bucket_of(offsets), jnp.where(spots < 5 * tile, 15, 31))
    lanes = lax.broadcasted_iota(jnp.int32, kinds.shape, 1)
    one_hot = jnp.where(kinds == lanes, 1.0, 0.0).astype(f32)
    table = lax.dot_general(
        sums, one_hot, (((1,), (0,)), ((), ())), precision=lax.Precision.HIGHEST,
        preferred_element_type=f32,
    )
    table_ref[:, :tile] = table.astype(bf16)
    table_ref[:, tile:] = jnp.zeros((16, 2 * tile), bf16)


def attention_back(chain, info, scale, gain, enc_in, got, qt, k, v, ctx, gctx, e, wq, wk, wv, gy):
    seq, width = k.shape
    heads = e.shape[0]
    block = pl.BlockSpec((1, seq // 2, width), lambda i, info: (info[0], 0, 0))
    side, part = shape((seq, 3 * width // 2), bf16), shape((seq // 2, width), f32)
    narrow = shape((seq, width // 2), bf16)
    outs = (narrow, narrow, narrow, side, part, part, shape((16, 3 * tile), bf16))
    far = (qt, k, v, ctx, gctx, e, wq, wk, wv, gy)
    return chain.run(
        functools.partial(attention_back_kernel, heads=heads),
        "attention_back",
        (1,),
        (scale, gain, enc_in, got) + far,
        [whole(scale), whole(gain), block, block] + [any_space] * len(far),
        outs,
        tuple(whole(a) for a in outs),
        scalars=(info,),
        scratch=tuple(pltpu.VMEM(a.shape, bf16) for a in far)
        + (
            pltpu.VMEM((2, seq, seq), f32), pltpu.VMEM((2, seq, seq), bf16),
            pltpu.VMEM((16, 6 * tile), f32), pltpu.VMEM((8, tile), f32), dma((9 + heads,)),
        ),
        flops=6 * seq * width * width + 16 * seq * seq * width,
    )


def spot_in(me, relative, stages):
    spot = 0
    for k in range(stages):
        bit = jnp.where(me == 0, k, 1 - k) if k < 2 <= stages else k
        spot = spot | (((relative >> bit) & 1) << (stages - 1 - k))
    return spot


def store(info, base, low, rows, held_ref, slots, line):
    stages = slots.bit_length() - 1
    span = held_ref.shape[0] // slots
    wide = held_ref.shape[1]
    for at in range(low.shape[0] // rows):
        spot = spot_in(info[0], info[1] ^ (base + at), stages)
        for piece in range(low.shape[1] // wide):
            start = pl.multiple_of(spot * span + line + piece * rows, 16)
            held_ref[pl.ds(start, rows), :] = low[
                at * rows : (at + 1) * rows, piece * wide : (piece + 1) * wide
            ]


def release(held_ref, keep_any, send_any, sems, extra=None):
    middle = held_ref.shape[0] // 2
    pairs = [
        (held_ref.at[pl.ds(middle, middle), :], send_any.at[pl.ds(0, middle), :]),
        (held_ref.at[pl.ds(0, middle), :], keep_any),
    ]
    if extra is not None:
        pairs.append((extra, send_any.at[pl.ds(middle, extra.shape[0]), :]))
    for copy in fetch(pairs, sems):
        copy.wait()


def tall_kernel(
    info, r0_ref, r1_ref, l0_any, l1_any, keep_any, send_any, l0_ref, l1_ref, held_ref, sems, out_sems, *, rows, slots
):
    parts, seq, width = l0_ref.shape
    loads = []
    for at in range(parts):
        spot = pl.ds(at * width, width)
        loads += [(l0_any.at[:, spot], l0_ref.at[at]), (l1_any.at[:, spot], l1_ref.at[at])]
    loads = fetch(loads, sems)
    for at in range(parts):
        loads[2 * at].wait()
        loads[2 * at + 1].wait()
        low = (t_dot(l0_ref[at], r0_ref[...]) + t_dot(l1_ref[at], r1_ref[...])).astype(bf16)
        store(info, at * (width // rows), low, rows, held_ref, slots, 0)
    release(held_ref, keep_any, send_any, out_sems)


def tall_grad(chain, info, slots, left, left_got, right, right_got):
    seq, tall = left.shape
    wide = right_got.shape[1]
    rows = tall // slots
    parts = 4
    outs = (shape((slots // 2 * rows, wide), bf16),) * 2
    far = pltpu.VMEM((parts, seq, tall // parts), bf16)
    return chain.run(
        functools.partial(tall_kernel, rows=rows, slots=slots), "grad_ff_out", (1,),
        (right, right_got, left, left_got),
        [
            pl.BlockSpec((seq, wide), lambda i, info: (0, info[0])), whole(right_got),
            any_space, any_space,
        ],
        outs, (any_space, any_space), scalars=(info,),
        scratch=(far, far, pltpu.VMEM((tall, wide), bf16), dma((2 * parts,)), dma((2,))),
        flops=4 * seq * tall * wide,
    )


def mixed_kernel(
    info, n0_any, n1_any, a0_any, c0_any, c1_any, g0_any, g1_any, *refs, rows, slots
):
    steps = len(refs) - 13
    a1_anys, (keep_any, send_any) = refs[:steps], refs[steps : steps + 2]
    n0_ref, n1_ref, a0_ref, a1_ref, c0_ref, c1_ref, g0_ref, g1_ref, held_ref, sems, out_sems = refs[steps + 2 :]
    seq, width = n0_ref.shape
    wide = held_ref.shape[1]
    loads = fetch(
        (
            (n0_any, n0_ref), (a0_any, a0_ref), (n1_any, n1_ref),
            (c0_any, c0_ref), (c1_any, c1_ref),
            (g0_any.at[:, pl.ds(pl.multiple_of(info[0] * wide, wide), wide)], g0_ref),
            (g1_any, g1_ref),
        )
        + tuple((part, a1_ref.at[at]) for at, part in enumerate(a1_anys)),
        sems,
    )
    for copy in loads[:3]:
        copy.wait()
    for at in range(steps):
        spot = slice(at * width, (at + 1) * width)
        loads[7 + at].wait()
        low = t_dot(n0_ref[...], a0_ref[:, spot]) + t_dot(n1_ref[...], a1_ref[at])
        store(info, 0, low.astype(bf16), rows, held_ref, slots, at * (width // wide) * rows)
    for copy in loads[3:7]:
        copy.wait()
    low = (dot(c0_ref[...], g0_ref[...]) + dot(c1_ref[...], g1_ref[...])).astype(bf16)
    store(info, 0, low, rows, held_ref, slots, steps * (width // wide) * rows)
    release(held_ref, keep_any, send_any, out_sems)


def mixed_grad(chain, info, slots, n2, n2_got, ctx, ctx_got, keep, got, gy, gy_got):
    seq, width = n2.shape
    wide = gy_got.shape[1]
    rows = width // slots
    lines = (keep.shape[1] // wide + 1) * rows
    outs = (shape((slots // 2 * lines, wide), bf16),) * 2
    args = (n2, n2_got, keep, ctx, ctx_got, gy, gy_got) + got
    dims = [n2.shape, n2.shape, keep.shape, (len(got),) + n2.shape, ctx.shape, ctx.shape]
    dims += [gy_got.shape, gy_got.shape]
    return chain.run(
        functools.partial(mixed_kernel, rows=rows, slots=slots), "grad_ff_in", (1,), args,
        [any_space] * len(args), outs, (any_space, any_space), scalars=(info,),
        scratch=tuple(pltpu.VMEM(d, bf16) for d in dims + [(slots * lines, wide)])
        + (dma((len(args),)), dma((2,))),
        flops=4 * seq * width * (keep.shape[1] + wide),
    )


def heads_kernel(
    info, table_ref, n0_any, n1_any, g0_any, gq_any, gk_any, gv_any, keep_any, send_any,
    n0_ref, n1_ref, g0_ref, g1_ref, held_ref, sems, out_sems, *, rows, slots,
):
    loads = fetch(
        ((n0_any, n0_ref), (g0_any, g0_ref), (n1_any, n1_ref))
        + tuple(
            (part, g1_ref.at[:, pl.ds(at * held_ref.shape[1], held_ref.shape[1])])
            for at, part in enumerate((gq_any, gk_any, gv_any))
        ),
        sems,
    )
    wide = held_ref.shape[1]
    for copy in loads:
        copy.wait()
    for first, count in ((0, 2), (2, 1)):
        spot = slice(first * wide, (first + count) * wide)
        low = t_dot(n0_ref[...], g0_ref[:, spot]) + t_dot(n1_ref[...], g1_ref[:, spot])
        store(info, 0, low.astype(bf16), rows, held_ref, slots, first * rows)
    release(held_ref, keep_any, send_any, out_sems, table_ref)


def heads_grad(chain, info, slots, n1, n1_got, keep, got, table):
    seq, width = n1.shape
    wide = width // 2
    rows = width // slots
    lines = keep.shape[1] // wide * rows
    outs = (
        shape((slots // 2 * lines, wide), bf16), shape((slots // 2 * lines + 16, wide), bf16),
    )
    args = (n1, n1_got, keep) + got
    dims = (n1.shape, n1.shape, keep.shape, keep.shape)
    return chain.run(
        functools.partial(heads_kernel, rows=rows, slots=slots), "grad_heads", (1,), (table,) + args,
        [whole(table)] + [any_space] * 6, outs, (any_space, any_space), scalars=(info,),
        scratch=tuple(pltpu.VMEM(d, bf16) for d in dims)
        + (pltpu.VMEM((slots * lines, wide), bf16), dma((6,)), dma((3,))),
        flops=4 * seq * width * keep.shape[1],
    )


def stage_kernel(*refs, half, table):
    keep_ref, got_ref = refs[:2]
    outs = refs[3:] if table else refs[2:]
    outs[0][:half, :] = keep_ref[:half, :] + got_ref[:half, :]
    if len(outs) > 1:
        outs[1][:half, :] = keep_ref[half:, :] + got_ref[half : 2 * half, :]
    if table:
        total = refs[2][...] + got_ref[keep_ref.shape[0] :, :]
        if len(outs) > 1:
            outs[1][half:, :] = total
            outs[2][...] = total
        else:
            outs[0][half:, :] = total


def stage(chain, keep, got, last, table=None):
    count, wide = keep.shape
    extra = 0 if table is None else table.shape[0]
    args = (keep, got) if table is None else (keep, got, table)
    half = count if last else count // 2
    outs = (shape((half + extra, wide), bf16),)
    if not last:
        outs = (shape((half, wide), bf16), shape((half + extra, wide), bf16))
        outs += () if table is None else (shape(table.shape, bf16),)
    return chain.run(
        functools.partial(stage_kernel, half=half, table=table is not None), "sum_stage", (1,),
        args, [whole(a) for a in args], outs, tuple(whole(a) for a in outs),
    )


def gain_of(weight, grad):
    return jnp.sum(weight[...].astype(f32) * grad, axis=1, keepdims=True)


def gain_line(total, gain_ref, chip):
    rows = total.shape[0]
    turned = jnp.broadcast_to(total, (rows, tile)).T[0:1]
    gain = row_of(gain_ref)
    width = gain.shape[1]
    mine = pltpu.roll(gain, lax.rem(width - chip * rows, width), 1)[:, :rows]
    return (turned / mine).reshape(rows)


def decoder_kernel(
    info, own_ref, got_ref, wsv_ref, wcq_ref, win_ref, wk_ref, wv_ref,
    gself_ref, gcross_ref, gffn_ref, gfinal_ref,
    sv_ref, so_ref, cq_ref, co_ref, in_ref, out_ref, ck_ref, cv_ref,
    dself_ref, dcross_ref, dffn_ref, dfinal_ref, all_ref, *, rows, heads,
):
    chip = info[1]
    count, lines, width = all_ref.shape
    head_dim = width // heads
    tall, hidden = out_ref.shape[0], in_ref.shape[1]
    many = hidden // width
    all_ref[: count // 2] = own_ref[...].astype(f32)
    all_ref[count // 2 :] = got_ref[...].astype(f32)

    def factor(at):
        return all_ref[:, at, :].astype(bf16)

    r = [factor(at) for at in range(7)]
    r_hid = jnp.concatenate([factor(7 + at) for at in range(many)], axis=1)
    first = 7 + many
    at_rows = lax.broadcasted_iota(jnp.int32, (width, tile), 0)
    at_lanes = lax.broadcasted_iota(jnp.int32, (width, tile), 1)
    choose = jnp.where((at_rows == chip * rows + at_lanes) & (at_lanes < rows), 1.0, 0.0).astype(bf16)
    names = [first + at for at in range(5)] + [first + 5 + many + at for at in range(2 * heads)]
    mine = dot(jnp.concatenate([factor(at) for at in names], axis=0), choose).astype(bf16)
    l = [mine[at * count : (at + 1) * count] for at in range(len(names))]
    l_hid = None
    wide = -(-tall // tile) * tile
    hid_rows = lax.broadcasted_iota(jnp.int32, (width, wide), 0)
    hid_lanes = lax.broadcasted_iota(jnp.int32, (width, wide), 1)
    for at in range(many):
        here = (hid_rows + at * width == chip * tall + hid_lanes) & (hid_lanes < tall)
        part = dot(factor(first + 5 + at), jnp.where(here, 1.0, 0.0).astype(bf16))
        l_hid = part if l_hid is None else l_hid + part
    l_hid = l_hid.astype(bf16)
    sv_ref[...] = t_dot(l[0], r[0])[:rows]
    dself_ref[...] = gain_line(gain_of(wsv_ref, sv_ref[...]), gself_ref, chip)
    so_ref[...] = t_dot(l[1], r[1])[:rows]
    cq_ref[...] = t_dot(l[2], r[2])[:rows]
    dcross_ref[...] = gain_line(gain_of(wcq_ref, cq_ref[...]), gcross_ref, chip)
    co_ref[...] = t_dot(l[3], r[3])[:rows]
    in_ref[...] = t_dot(l[4], r_hid)[:rows]
    dffn_ref[...] = gain_line(gain_of(win_ref, in_ref[...]), gffn_ref, chip)
    out_ref[...] = t_dot(l_hid, r[6])[:tall]
    for head in range(heads):
        spot = slice(head * head_dim, (head + 1) * head_dim)
        ck_ref[:, spot] = t_dot(l[5 + head], r[4][:, spot])[:rows]
        cv_ref[:, spot] = t_dot(l[5 + heads + head], r[5][:, spot])[:rows]
    total = gain_of(wk_ref, ck_ref[...]) + gain_of(wv_ref, cv_ref[...])
    dfinal_ref[...] = gain_line(total, gfinal_ref, chip)


def decoder_grads(chain, info, own, got, weights, gains, rows, heads):
    width, hidden = weights[0].shape[0], weights[2].shape[1]
    tall = hidden * rows // width
    line = shape((rows,), f32)
    flat = shape((rows, width), f32)
    outs = (flat, flat, flat, flat, shape((rows, hidden), f32), shape((tall, width), f32), flat, flat)
    outs += (line,) * 4

    def sliced(array):
        return pl.BlockSpec((rows, array.shape[1]), lambda i, info: (info[1], 0))

    return chain.run(
        functools.partial(decoder_kernel, rows=rows, heads=heads), "decoder_grads",
        (1,), (own, got) + weights + gains,
        [whole(own), whole(got)] + [sliced(a) for a in weights] + [whole(a) for a in gains],
        outs, tuple(whole(a) for a in outs), scalars=(info,),
        scratch=(pltpu.VMEM((2 * own.shape[0],) + own.shape[1:], f32),),
    )


def sides(me, own_ref, got_ref, first, rows):
    own, got = own_ref[first : first + rows, :], got_ref[first : first + rows, :]
    low = jnp.where(me == 0, own, got).astype(f32)
    high = jnp.where(me == 0, got, own).astype(f32)
    return low, high


def finish_kernel(
    info, out_ref, out_got, mix_ref, mix_got, win_ref, gain_ref,
    keep_ref, away_ref, grad_ref, grad_got, row_ref, row_got,
    fout_ref, fin_ref, o_ref, dffn_ref, enc_ref, back_ref, dec_ref, decback_ref, *, rows, steps,
):
    me = info[0]
    wide = out_ref.shape[1]
    low, high = sides(me, out_ref, out_got, 0, out_ref.shape[0])
    fout_ref[:, :wide] = low
    fout_ref[:, wide:] = high
    for at in range(steps):
        low, high = sides(me, mix_ref, mix_got, at * rows, rows)
        fin_ref[:, at * wide : (at + 1) * wide] = low
        fin_ref[:, (steps + at) * wide : (steps + at + 1) * wide] = high
    low, high = sides(me, mix_ref, mix_got, steps * rows, rows)
    o_ref[:, :wide] = low
    o_ref[:, wide:] = high
    dffn_ref[...] = gain_line(gain_of(win_ref, fin_ref[...]), gain_ref, info[1])
    enc_ref[me] = keep_ref[...]
    enc_ref[1 - me] = away_ref[...]
    back_ref[me] = grad_ref[...]
    back_ref[1 - me] = grad_got[...]
    rows_two = lax.broadcasted_iota(jnp.int32, (2, row_ref.shape[1]), 0)
    both = jnp.where(rows_two == me, row_ref[0:1], row_got[0:1])
    dec_ref[...] = both.astype(bf16)
    decback_ref[...] = jnp.where(rows_two == me, row_ref[1:2], row_got[1:2])


def finish(chain, info, out, out_got, mix, mix_got, win, gain, keep, away, grad, grad_got, row, row_got, rows):
    width, hidden = win.shape
    wide = out.shape[1]
    half = away.shape[0]
    args = (out, out_got, mix, mix_got, win, gain, keep, away, grad, grad_got, row, row_got)
    outs = (
        shape((out.shape[0], width), f32), shape((rows, hidden), f32), shape((rows, width), f32),
        shape((rows,), f32), shape((2, half, width), bf16), shape((2, half, width), f32),
        shape((2, width), bf16), shape((2, width), f32),
    )
    specs = [whole(a) for a in args]
    specs[4] = pl.BlockSpec((rows, hidden), lambda i, info: (info[1], 0))
    specs[6] = pl.BlockSpec((half, width), lambda i, info: (info[0], 0))
    return chain.run(
        functools.partial(finish_kernel, rows=rows, steps=hidden // 2 // wide), "finish_most", (1,),
        args, specs, outs, tuple(whole(a) for a in outs), scalars=(info,),
    )


def last_kernel(
    info, sum_ref, got_ref, wq_ref, wk_ref, wv_ref, gain_ref,
    q_ref, k_ref, v_ref, d_ref, table_ref, *, rows, heads,
):
    me = info[0]
    wide = sum_ref.shape[1]
    outs = (q_ref, k_ref, v_ref)
    for at, ref in enumerate(outs):
        low, high = sides(me, sum_ref, got_ref, at * rows, rows)
        ref[:, :wide] = low
        ref[:, wide:] = high
    total = sum(gain_of(w, ref[...]) for w, ref in zip((wq_ref, wk_ref, wv_ref), outs))
    d_ref[...] = gain_line(total, gain_ref, info[1])
    first = 3 * rows
    table = sum_ref[first:, :tile].astype(f32) + got_ref[first:, :tile].astype(f32)
    turned = table.T[: table_ref.shape[0]]
    part = heads // 2
    table_ref[:, :part] = turned[:, :part]
    table_ref[:, part:] = turned[:, 8 : 8 + part]


def last(chain, info, done, got, wq, wk, wv, gain, rows, buckets, heads):
    width = wq.shape[0]
    flat = shape((rows, width), f32)
    args = (done, got, wq, wk, wv, gain)
    outs = (flat, flat, flat, shape((rows,), f32), shape((buckets, heads), f32))
    specs = [whole(a) for a in args]
    for at in (2, 3, 4):
        specs[at] = pl.BlockSpec((rows, args[at].shape[1]), lambda i, info: (info[1], 0))
    return chain.run(
        functools.partial(last_kernel, rows=rows, heads=heads), "finish_last", (1,), args, specs,
        outs, tuple(whole(a) for a in outs), scalars=(info,),
    )


def plain_grad(me, place, pieces, tall):
    parts = []
    for left, left_got, right, right_got, offset in pieces:
        wide = right_got.shape[1]
        keep = lax.dynamic_slice_in_dim(right, me * wide, wide, 1) if offset else right
        total = t_dot(
            jnp.concatenate([left, left_got]), jnp.concatenate([keep, right_got])
        ).astype(bf16)
        slots = place.shape[0]
        if tall:
            parts.append(total.reshape(slots, -1, wide))
        else:
            half = left.shape[1] // 2
            for at in range(0, wide, half):
                parts.append(total[:, at : at + half].reshape(slots, -1, half))
    total = jnp.concatenate(parts, axis=1)
    order = jnp.zeros_like(place).at[place].set(jnp.arange(place.shape[0], dtype=jnp.int32))
    return jnp.take(total, order, axis=0)


def plain_sides(me, done, got):
    low = jnp.where(me == 0, done, got).astype(f32)
    high = jnp.where(me == 0, got, done).astype(f32)
    return low, high


def body(
    enc_in,
    dec_in,
    lengths,
    cot_enc,
    cot_dec,
    enc_gain_attn,
    enc_query,
    enc_key,
    enc_value,
    enc_output,
    relative_bias_table,
    enc_gain_ffn,
    enc_ff_in,
    enc_ff_out,
    enc_gain_final,
    dec_gain_self,
    dec_self_value,
    dec_self_output,
    dec_gain_cross,
    dec_cross_query,
    dec_cross_key,
    dec_cross_value,
    dec_cross_output,
    dec_gain_ffn,
    dec_ff_in,
    dec_ff_out,
):
    pair_count, seq_dev, width = enc_in.shape
    seq_all = 2 * seq_dev
    bucket_count, heads = relative_bias_table.shape
    head_dim = width // heads
    hidden = enc_ff_in.shape[1]
    slots = lax.axis_size("batch")
    me = lax.axis_index("blk")
    chip = lax.axis_index("batch")
    stages = slots.bit_length() - 1
    rows = width // slots
    aligned = rows % 16 == 0
    chain = Chain()

    def across(array):
        return lax.ppermute(array, "blk", [(0, 1), (1, 0)])

    info = jnp.stack([me, chip]).astype(jnp.int32)
    order = list(range(stages))
    crossed = order if stages < 2 else [1, 0] + order[2:]
    def hop(array, step):
        pairs = []
        for which in range(slots):
            for core in range(2):
                bit = (order, crossed)[core][step]
                pairs.append((which * 2 + core, (which ^ (1 << bit)) * 2 + core))
        return lax.ppermute(array, ("batch", "blk"), pairs)

    class Sum:
        def __init__(self, keep, send, table=None):
            self.keep, self.table, self.at = keep, table, 0
            self.got = hop(send, 0)

        def step(self):
            if self.at == stages:
                return
            self.at += 1
            last = self.at == stages
            if aligned:
                outs = list(stage(chain, self.keep, self.got, last, self.table))
            else:
                total = self.keep + self.got
                half = total.shape[0] // 2
                outs = [total] if last else [total[:half], total[half:]]
            self.keep = outs[0]
            if self.table is not None and len(outs) == 3:
                self.table = outs[2]
            if last:
                self.done = self.keep
                self.other = across(self.done)
            else:
                self.got = hop(outs[1], self.at)

        def rest(self):
            while self.at < stages:
                self.step()

    def plain_sum(pieces, tall):
        relative = chip ^ jnp.arange(slots, dtype=jnp.int32)
        total = plain_grad(me, spot_in(me, relative, stages).astype(jnp.int32), pieces, tall)
        total = total.reshape(-1, total.shape[-1])
        half = total.shape[0] // 2
        return Sum(total[:half], total[half:])

    enc_got = across(enc_in)
    cot_got = across(cot_enc)
    state, key_query, hid_up = before(
        chain, info, dec_in, cot_dec, dec_gain_self, dec_gain_cross, dec_self_value,
        dec_self_output, dec_cross_query, dec_cross_key, dec_ff_out, head_dim,
    )

    (
        src, result_low, out_away, scale, n1, q_turned, k, v, weights, context, y1, n2, hid, slope
    ) = encoder(
        chain, info, lengths, enc_in, enc_got, enc_gain_attn, enc_query, enc_key, enc_value,
        relative_bias_table, enc_gain_ffn, enc_gain_final, enc_output, enc_ff_in, enc_ff_out, heads,
        (cot_got,),
    )
    hid_got, n2_got, ctx_got, n1_got = (across(part) for part in (hid, n2, context, n1))
    out_got = across(out_away)

    ge_low, ge_away, dec_lines, dec_long, g_c, mix = cross(
        chain, info, lengths, src, key_query, state, hid_up, cot_dec, dec_gain_ffn, result_low,
        cot_enc, cot_got, enc_gain_final, (dec_cross_value, dec_cross_output, dec_ff_in), head_dim,
    )
    ge_got = across(ge_away)
    dec_rows, packed = after(
        chain, src, g_c, state, dec_lines, dec_long, mix, dec_gain_self, dec_gain_cross,
        (dec_cross_key, dec_cross_query, dec_self_output, dec_self_value, dec_ff_out),
        head_dim, heads,
    )
    dec_got = across(dec_rows)
    gathered = lax.all_gather(packed, "batch", axis=0, tiled=True)
    gathered_got = across(gathered)

    if aligned:
        sum_out = Sum(*tall_grad(chain, info, slots, hid, hid_got, ge_low, ge_got))
    else:
        sum_out = plain_sum([(hid, hid_got, ge_low, ge_got, True)], True)
    *ga_away, ga_keep, gy_low, gy_away, g_ctx = backward(
        chain, info, ge_low, slope, enc_ff_out, enc_ff_in, y1, enc_gain_ffn, enc_output
    )
    ga_got, gy_got = tuple(across(part) for part in ga_away), across(gy_away)
    sum_out.step()
    if aligned:
        sum_mix = Sum(
            *mixed_grad(
                chain, info, slots, n2, n2_got, context, ctx_got, ga_keep, ga_got, gy_low, gy_got
            )
        )
    else:
        sum_mix = plain_sum(
            [(n2, n2_got, ga_keep, jnp.concatenate(ga_got, axis=1), False), (context.T, ctx_got.T, gy_low, gy_got, True)], False
        )
    *g_away, g_keep, grad_keep, grad_away, table_term = attention_back(
        chain, info, scale, enc_gain_attn, enc_in, enc_got, q_turned, k, v, context, g_ctx, weights,
        enc_query, enc_key, enc_value, gy_low,
    )
    g_got = tuple(across(part) for part in g_away)
    grad_got = across(grad_away)
    sum_out.step()
    sum_mix.step()
    if aligned:
        sum_heads = Sum(
            *heads_grad(chain, info, slots, n1, n1_got, g_keep, g_got, table_term), table_term
        )
    else:
        sum_heads = plain_sum([(n1, n1_got, g_keep, jnp.concatenate(g_got, axis=1), False)], False)
        table_sum = lax.psum(table_term.astype(f32), ("batch", "blk"))
    sum_out.step()
    sum_mix.step()
    sum_heads.step()

    lines = packed.shape[0]
    gathered = gathered.reshape(slots, lines, width)
    gathered_got = gathered_got.reshape(slots, lines, width)
    dec_weights = (dec_self_value, dec_cross_query, dec_ff_in, dec_cross_key, dec_cross_value)
    dec_gains = (dec_gain_self, dec_gain_cross, dec_gain_ffn, enc_gain_final)

    def mine(array):
        return lax.dynamic_slice_in_dim(array, chip * (array.shape[0] // slots), array.shape[0] // slots, 0)

    if aligned:
        dec_outs = decoder_grads(
            chain, info, gathered, gathered_got, dec_weights, dec_gains, rows, heads
        )
        (grad_self_value, grad_self_output, grad_cross_query, grad_cross_output) = dec_outs[:4]
        (grad_dec_ff_in, grad_dec_ff_out, grad_cross_key, grad_cross_value) = dec_outs[4:8]
        gain_self, gain_cross, gain_dec_ffn, gain_final = dec_outs[8:]
    else:
        table = jnp.concatenate([gathered, gathered_got]).astype(bf16)
        count = hidden // width
        tall = hidden // slots
        r = [table[:, at] for at in range(7)]
        r_hid = table[:, 7 : 7 + count].reshape(-1, hidden)
        first = 7 + count
        chosen = lax.dynamic_slice_in_dim(table[:, first:], chip * rows, rows, 2)
        l = [chosen[:, at] for at in range(5)]
        l_hid = table[:, first + 5 : first + 5 + count].reshape(-1, hidden)
        l_hid = lax.dynamic_slice_in_dim(l_hid, chip * tall, tall, 1)
        grad_self_value, grad_self_output = t_dot(l[0], r[0]), t_dot(l[1], r[1])
        grad_cross_query, grad_cross_output = t_dot(l[2], r[2]), t_dot(l[3], r[3])
        grad_dec_ff_in = t_dot(l[4], r_hid)
        grad_dec_ff_out = t_dot(l_hid, r[6])
        many = chosen[:, 5 + count : 5 + count + 2 * heads].reshape(-1, 2, heads, rows)
        grad_cross_key, grad_cross_value = (
            jnp.einsum(
                "phd,phe->dhe", many[:, at], r[4 + at].reshape(-1, heads, head_dim),
                preferred_element_type=f32,
            ).reshape(rows, width)
            for at in range(2)
        )

        def gain_plain(gain, *terms):
            return sum(jnp.sum(mine(w).astype(f32) * g, axis=1) for w, g in terms) / mine(gain)

        gain_self = gain_plain(dec_gain_self, (dec_self_value, grad_self_value))
        gain_cross = gain_plain(dec_gain_cross, (dec_cross_query, grad_cross_query))
        gain_dec_ffn = gain_plain(dec_gain_ffn, (dec_ff_in, grad_dec_ff_in))
        gain_final = gain_plain(
            enc_gain_final, (dec_cross_key, grad_cross_key), (dec_cross_value, grad_cross_value)
        )

    sum_out.rest()
    sum_mix.step()
    sum_heads.step()
    sum_mix.rest()
    sum_heads.step()
    if aligned:
        (grad_ff_out, grad_ff_in, grad_output, gain_ffn, encoder_output, grad_in, dec_out, grad_dec) = finish(
            chain, info, sum_out.done, sum_out.other, sum_mix.done, sum_mix.other, enc_ff_in,
            enc_gain_ffn, result_low, out_got, grad_keep, grad_got, dec_rows, dec_got, rows,
        )
        sum_heads.rest()
        grad_query, grad_key, grad_value, gain_attn, grad_rel_table = last(
            chain, info, sum_heads.done, sum_heads.other, enc_query, enc_key, enc_value,
            enc_gain_attn, rows, bucket_count, heads,
        )
    else:
        sum_heads.rest()
        grad_ff_out = jnp.concatenate(plain_sides(me, sum_out.done, sum_out.other), axis=1)
        low, high = plain_sides(me, sum_mix.done, sum_mix.other)

        def pick(side, at):
            return side[at * rows : (at + 1) * rows]

        grad_ff_in = jnp.concatenate(
            [pick(side, at) for side in (low, high) for at in range(low.shape[0] // rows - 1)], axis=1
        )
        spot = low.shape[0] // rows - 1
        grad_output = jnp.concatenate([pick(low, spot), pick(high, spot)], axis=1)
        low, high = plain_sides(me, sum_heads.done, sum_heads.other)
        grad_query, grad_key, grad_value = (
            jnp.concatenate([pick(low, at), pick(high, at)], axis=1) for at in range(3)
        )
        gain_ffn = gain_plain(enc_gain_ffn, (enc_ff_in, grad_ff_in))
        gain_attn = gain_plain(
            enc_gain_attn, (enc_query, grad_query), (enc_key, grad_key), (enc_value, grad_value)
        )
        turned = table_sum.T[:bucket_count]
        grad_rel_table = jnp.concatenate([turned[:, : heads // 2], turned[:, 8 : 8 + heads // 2]], axis=1)

        def stacked(own, got):
            return jnp.where(me == 0, jnp.stack([own, got]), jnp.stack([got, own]))

        out_keep = lax.dynamic_slice_in_dim(result_low, me * seq_dev, seq_dev, 0)
        encoder_output, grad_in = stacked(out_keep, out_got), stacked(grad_keep, grad_got)
        dec_out = stacked(dec_rows[0], dec_got[0]).astype(bf16)
        grad_dec = stacked(dec_rows[1], dec_got[1])

    return (
        encoder_output,
        dec_out,
        grad_in,
        grad_dec,
        gain_attn,
        grad_query,
        grad_key,
        grad_value,
        grad_output,
        grad_rel_table,
        gain_ffn,
        grad_ff_in,
        grad_ff_out,
        gain_final,
        gain_self,
        grad_self_value,
        grad_self_output,
        gain_cross,
        grad_cross_query,
        grad_cross_key,
        grad_cross_value,
        grad_cross_output,
        gain_dec_ffn,
        grad_dec_ff_in,
        grad_dec_ff_out,
    )


def solution(mesh):
    split = P("batch", "blk", None)
    rows = P("batch", None)
    line = P("batch")
    placed = (split, rows, line, split, rows) + (P(),) * 21
    return jax.shard_map(
        body,
        mesh=mesh,
        in_specs=placed,
        out_specs=(
            (split, rows, split, rows, line, rows, rows, rows, rows, P(), line, rows, rows, line)
            + (line, rows, rows, line, rows, rows, rows, rows, line, rows, rows)
        ),
        check_vma=False,
    )
```

```python
import functools

import jax
import jax.numpy as jnp
from jax import lax
from jax.experimental import pallas as pl
from jax.experimental.pallas import tpu as pltpu
from jax.sharding import PartitionSpec as P

epsilon = 1e-06
masked_score = -1e30
thresholds = (12, 16, 23, 32, 46, 64, 91)
bf16 = jnp.bfloat16
f32 = jnp.float32
tile = 128
chunk = 32
mib = 1 << 20


def bucket_of(offset):
    distance = jnp.abs(offset)
    larger = jnp.full(offset.shape, 8, jnp.int32)
    for limit in thresholds:
        larger = larger + jnp.where(distance >= limit, 1, 0)
    inner = jnp.where(distance < 8, distance, larger)
    return jnp.where(offset > 0, 16, 0) + inner


def norm_scale(values):
    return lax.rsqrt(jnp.mean(values * values, axis=-1, keepdims=True) + epsilon)


def norm_apply(values, gain):
    return values * norm_scale(values) * gain


def norm_back(values, gain, upstream):
    scale = norm_scale(values)
    weighted = upstream * gain
    inner = jnp.mean(weighted * values, axis=-1, keepdims=True)
    return scale * weighted - values * (scale * scale * scale * inner)


def gelu_parts(a):
    root = 0.7978845608028654
    square = a * a
    t = jnp.tanh(root * a * (1.0 + 0.044715 * square))
    half = 0.5 + 0.5 * t
    slope = half + (half * (1.0 - t)) * (a * (root + (3 * 0.044715 * root) * square))
    return a * half, slope


def dot(left, right, dims=((1,), (0,))):
    return lax.dot_general(left, right, (dims, ((), ())), preferred_element_type=f32)


def dot_t(left, right):
    return dot(left, right, ((1,), (1,)))


def t_dot(left, right):
    return dot(left, right, ((0,), (0,)))


def shape(dims, kind):
    return jax.ShapeDtypeStruct(dims, kind)


def whole(array, buffers=None):
    zeros = (0,) * array.ndim
    if buffers is None:
        return pl.BlockSpec(array.shape, lambda *at: zeros)
    return pl.BlockSpec(array.shape, lambda *at: zeros, pipeline_mode=pl.Buffered(buffers))


class Chain:
    def __init__(self):
        self.last = ()

    def run(
        self, kernel, name, grid, args, in_specs, outs, out_specs, scalars=(), scratch=(),
        flops=0, limit=63, also=(),
    ):
        size = sum(a.size * a.dtype.itemsize for a in list(args) + list(outs))
        last = self.last + also
        skip = len(scalars) + len(args)

        def inner(*refs):
            kernel(*refs[:skip], *refs[skip + len(last) :])

        done = pl.pallas_call(
            inner,
            out_shape=outs,
            grid_spec=pltpu.PrefetchScalarGridSpec(
                num_scalar_prefetch=len(scalars),
                grid=grid,
                in_specs=list(in_specs) + [pl.BlockSpec(memory_space=pl.ANY)] * len(last),
                out_specs=out_specs,
                scratch_shapes=scratch,
            ),
            compiler_params=pltpu.CompilerParams(
                vmem_limit_bytes=limit * mib, dimension_semantics=("arbitrary",) * len(grid)
            ),
            cost_estimate=pl.CostEstimate(
                flops=int(4 * flops), bytes_accessed=int(size), transcendentals=0
            ),
            name=name,
        )(*scalars, *args, *last)
        self.last = (done[0],)
        return done


any_space = pl.BlockSpec(memory_space=pl.ANY)
dma = pltpu.SemaphoreType.DMA


def row_of(gain_ref):
    return gain_ref[...].reshape(1, -1)


def fetch(pairs, sems, first=None):
    copies = [
        pltpu.make_async_copy(source, target, sems.at[at])
        for at, (source, target) in enumerate(pairs)
    ]
    for copy in copies[:first]:
        copy.start()
    return copies


def picked(me, ref):
    rows = ref[...].astype(f32)
    return jnp.where(me == 0, rows[0:1], rows[1:2])


def joined(me, own, got):
    first = jnp.where(me == 0, own, got)
    last = jnp.where(me == 0, got, own)
    return jnp.concatenate([first, last], axis=0)


def encoder_kernel(
    info, lens, gain_ref, table_ref, ffn_ref, final_ref,
    own_any, got_any, wq_any, wk_any, wv_any, wo_any, win_any, wout_any,
    src_ref, low_ref, away_ref, scale_ref,
    n1_any, qt_any, k_any, v_any, e_any, ctx_any, y1_any, n2_any, hid_any, slope_any,
    x_ref, n1_ref, qt_ref, k_ref, v_ref, e_ref, ctx_ref, y1_ref, n2_ref, hid_ref, slope_ref,
    acc_ref, bias_ref, s_ref, wq_ref, wk_ref, wv_ref, wo_ref, win_ref, wout_ref, sems, out_sems, x_sems,
    *, heads, group,
):
    me = info[0]
    seq, width = x_ref.shape
    head_dim = width // heads
    blocks = seq // tile
    parts = win_ref.shape[0]
    wide = group * head_dim
    rounds = heads // group

    loads = []
    for at in range(rounds):
        spot = pl.ds(at * wide, wide)
        for any_ref, ref in ((wq_any, wq_ref), (wk_any, wk_ref), (wv_any, wv_ref)):
            loads.append((any_ref.at[:, spot], ref.at[at]))
    loads.append((wo_any, wo_ref))
    for at in range(parts):
        spot = pl.ds(at * width, width)
        loads.append((win_any.at[:, spot], win_ref.at[at]))
        loads.append((wout_any.at[spot, :], wout_ref.at[at]))
    loads = [
        pltpu.make_async_copy(source, target, sems.at[at])
        for at, (source, target) in enumerate(loads)
    ]
    first = fetch(
        ((own_any.at[me], x_ref.at[pl.ds(me * (seq // 2), seq // 2), :]),
         (got_any.at[me], x_ref.at[pl.ds((1 - me) * (seq // 2), seq // 2), :])), x_sems
    )
    for copy in loads[: 3 * rounds]:
        copy.start()
    saved = []

    def save(source, target):
        copy = pltpu.make_async_copy(source, target, out_sems.at[len(saved)])
        copy.start()
        saved.append(copy)

    tables = jnp.concatenate(
        [table_ref[...], jnp.zeros((heads, tile - table_ref.shape[1]), f32)], axis=1
    )
    rows = lax.broadcasted_iota(jnp.int32, (tile, tile), 0)
    lanes = lax.broadcasted_iota(jnp.int32, (tile, tile), 1)
    kinds = [bucket_of((gap - 1) * tile + rows - lanes) for gap in range(3)]
    for head in range(heads):
        line = jnp.broadcast_to(tables[head : head + 1, :], (tile, tile))
        for gap in range(3):
            bias_ref[head, gap] = jnp.take_along_axis(line, kinds[gap], axis=1)

    for copy in first:
        copy.wait()
    n1_ref[...] = norm_apply(x_ref[...].astype(f32), row_of(gain_ref)).astype(bf16)
    save(n1_ref, n1_any)

    pair_rows = lax.broadcasted_iota(jnp.int32, (2 * head_dim, seq), 0)
    pair_lanes = lax.broadcasted_iota(jnp.int32, (seq, 2 * head_dim), 1)
    key_at = lax.broadcasted_iota(jnp.int32, (seq, 2 * head_dim), 0)
    gone = jnp.where(key_at < lens[me], 0.0, masked_score).astype(bf16)
    ones = jnp.ones((16, seq), bf16)
    vts = {}

    def project(at):
        n1 = n1_ref[...]
        for copy in loads[3 * at : 3 * at + 3]:
            copy.wait()
        for copy in loads[3 * rounds + 3 * at : 3 * rounds + 3 * at + 3]:
            copy.start()
        spot = slice(at * wide, (at + 1) * wide)
        qt_ref[spot, :] = dot(n1, wq_ref[at]).T.astype(bf16)
        k_ref[:, spot] = dot(n1, wk_ref[at]).astype(bf16)
        v = dot(n1, wv_ref[at])
        v_ref[:, spot] = v.astype(bf16)
        vts[at] = v.T.astype(bf16)

    def scores(head):
        pair = slice(head // 2 * 2 * head_dim, (head // 2 + 1) * 2 * head_dim)
        k2, q2 = k_ref[:, pair], qt_ref[pair, :]
        zero = jnp.zeros((), bf16)
        if head % 2 == 0:
            k2 = jnp.where(pair_lanes < head_dim, k2, jnp.where(pair_lanes == head_dim, gone, zero))
            q2 = jnp.where(pair_rows < head_dim, q2, jnp.ones((), bf16))
        else:
            k2 = jnp.where(pair_lanes >= head_dim, k2, jnp.where(pair_lanes == 0, gone, zero))
            q2 = jnp.where(pair_rows >= head_dim, q2, jnp.ones((), bf16))
        s_ref[head % 2] = dot(k2, q2)

    def weigh(head):
        slot = head % 2
        before = tables[head : head + 1, 15:16]
        after = tables[head : head + 1, 31:32]
        for query in range(blocks):
            across = slice(query * tile, (query + 1) * tile)
            tops = None
            for key in range(blocks):
                gap = key - query
                bias = before if gap < -1 else after if gap > 1 else bias_ref[head, gap + 1]
                down = slice(key * tile, (key + 1) * tile)
                value = s_ref[slot, down, across] + bias
                s_ref[slot, down, across] = value
                top = jnp.max(value.reshape(tile // 8, 8, tile), axis=0)
                tops = top if tops is None else jnp.maximum(tops, top)
            peak = jnp.max(tops, axis=0, keepdims=True)
            for key in range(blocks):
                down = slice(key * tile, (key + 1) * tile)
                e_ref[head, down, across] = jnp.exp(s_ref[slot, down, across] - peak).astype(bf16)
        save(e_ref.at[head], e_any.at[head])

    def mix(head):
        at, inner = divmod(head, group)
        vt = vts[at][inner * head_dim : (inner + 1) * head_dim]
        full = dot(jnp.concatenate([vt, ones], axis=0), e_ref[head])
        scale = 1.0 / full[head_dim : head_dim + 1]
        scale_ref[head : head + 1, :] = scale
        ctx_ref[head * head_dim : (head + 1) * head_dim, :] = (full[:head_dim] * scale).astype(bf16)

    project(0)
    scores(0)
    for head in range(heads):
        if head % group == 0 and head // group + 1 < rounds:
            project(head // group + 1)
        if head + 1 < heads:
            scores(head + 1)
        weigh(head)
        mix(head)
    scale_ref[heads:, :] = jnp.zeros((16 - heads, seq), f32)
    save(qt_ref, qt_any)
    save(k_ref, k_any)
    save(v_ref, v_any)
    save(ctx_ref, ctx_any)

    loads[3 * rounds].wait()
    y1 = x_ref[...].astype(f32) + t_dot(ctx_ref[...], wo_ref[...])
    acc_ref[...] = y1
    y1_ref[...] = y1.astype(bf16)
    n2_ref[...] = norm_apply(y1, row_of(ffn_ref)).astype(bf16)
    save(y1_ref, y1_any)
    save(n2_ref, n2_any)
    for at in range(parts):
        spot = pl.ds(at * width, width)
        loads[3 * rounds + 1 + 2 * at].wait()
        value, slope = gelu_parts(dot(n2_ref[...], win_ref[at]))
        hid_ref[at] = value.astype(bf16)
        slope_ref[at] = slope.astype(bf16)
        save(hid_ref.at[at], hid_any.at[:, spot])
        save(slope_ref.at[at], slope_any.at[:, spot])
        loads[3 * rounds + 2 + 2 * at].wait()
        acc_ref[...] += dot(hid_ref[at], wout_ref[at])
    result = acc_ref[...]
    low = result.astype(bf16)
    low_ref[...] = low
    half = seq // 2
    away_ref[...] = jnp.where(me == 0, low[half:], low[:half])
    src_ref[...] = norm_apply(result, row_of(final_ref)).astype(bf16)
    for copy in saved:
        copy.wait()


def encoder(
    chain, info, lens, enc_in, got, gain, wq, wk, wv, table, ffn, final, wo, win, wout, heads, also
):
    pairs, seq_dev, width = enc_in.shape
    seq = 2 * seq_dev
    hidden = win.shape[1]
    group = 4
    rounds = heads // group
    wide = width // rounds
    parts = hidden // width
    act, turned = shape((seq, width), bf16), shape((width, seq), bf16)
    part, tall = shape((seq_dev, width), bf16), shape((seq, hidden), bf16)
    near = (act, act, part, shape((16, seq), f32))
    far = (act, turned, act, act, shape((heads, seq, seq), bf16), turned, act, act, tall, tall)
    small = (gain, table, ffn, final)

    def vmem(dims, kind=bf16):
        return pltpu.VMEM(dims, kind)

    return chain.run(
        functools.partial(encoder_kernel, heads=heads, group=group),
        "encoder_forward",
        (1,),
        small + (enc_in, got, wq, wk, wv, wo, win, wout),
        [whole(a) for a in small] + [any_space] * 8,
        near + far,
        tuple(whole(a) for a in near) + (any_space,) * len(far),
        scalars=(info, lens),
        scratch=(
            vmem((seq, width)), vmem((seq, width)), vmem((width, seq)), vmem((seq, width)),
            vmem((seq, width)), vmem((heads, seq, seq)), vmem((width, seq)), vmem((seq, width)),
            vmem((seq, width)), vmem((parts, seq, width)), vmem((parts, seq, width)),
            vmem((seq, width), f32), vmem((heads, 3, tile, tile), f32), vmem((2, seq, seq), f32),
            vmem((rounds, width, wide)), vmem((rounds, width, wide)), vmem((rounds, width, wide)),
            vmem((width, width)), vmem((parts, width, width)), vmem((parts, width, width)),
            dma((3 * rounds + 1 + 2 * parts,)), dma((7 + heads + 2 * parts,)), dma((2,)),
        ),
        flops=2 * seq * width * (4 * width + 2 * hidden) + 16 * seq * seq * width,
        also=also,
    )


def wide_row(row):
    return jnp.broadcast_to(row.astype(bf16), (16, row.shape[1]))


def row_dot(row, weight):
    return dot(wide_row(row), weight)[0:1]


def row_dot_t(row, weight):
    return dot_t(wide_row(row), weight)[0:1]


def head_mask(width, head_dim):
    rows = lax.broadcasted_iota(jnp.int32, (16, width), 0)
    lanes = lax.broadcasted_iota(jnp.int32, (16, width), 1)
    return (lanes >= rows * head_dim) & (lanes < (rows + 1) * head_dim)


def spread(row, mask):
    return jnp.where(mask, jnp.broadcast_to(row, mask.shape), 0.0).astype(bf16)


def before_kernel(
    info, dec_ref, cot_ref, self_ref, cross_ref, wsv_any, wso_any, wcq_any, wk_any, wout_any,
    state_ref, kq_ref, up_ref, wsv, wso, wcq, wk, wout, sems, *, head_dim,
):
    copies = fetch(
        ((wsv_any, wsv), (wso_any, wso), (wcq_any, wcq), (wk_any, wk), (wout_any, wout)), sems
    )
    x = picked(info[0], dec_ref)
    m1 = norm_apply(x, row_of(self_ref)).astype(bf16).astype(f32)
    copies[0].wait()
    sv = row_dot(m1, wsv[...]).astype(bf16).astype(f32)
    copies[1].wait()
    z1 = x + row_dot(sv, wso[...])
    m2 = norm_apply(z1, row_of(cross_ref)).astype(bf16).astype(f32)
    copies[2].wait()
    cq = row_dot(m2, wcq[...]).astype(bf16).astype(f32)
    copies[3].wait()
    kq_ref[...] = dot_t(spread(cq, head_mask(x.shape[1], head_dim)), wk[...]).astype(bf16)
    copies[4].wait()
    up_ref[...] = row_dot_t(picked(info[0], cot_ref), wout[...])
    for at, row in enumerate((x, m1, sv, z1, m2, cq)):
        state_ref[at : at + 1, :] = row
    state_ref[6:8, :] = jnp.zeros((2, x.shape[1]), f32)


def before(chain, info, dec, cot, gain_self, gain_cross, wsv, wso, wcq, wk, wout, head_dim):
    width, hidden = dec.shape[1], wout.shape[0]
    weights = (wsv, wso, wcq, wk, wout)
    small = (dec, cot, gain_self, gain_cross)
    outs = (shape((8, width), f32), shape((16, width), bf16), shape((1, hidden), f32))
    return chain.run(
        functools.partial(before_kernel, head_dim=head_dim), "decoder_before", (1,),
        small + weights, [whole(a) for a in small] + [any_space] * 5, outs,
        tuple(whole(a) for a in outs), scalars=(info,),
        scratch=tuple(pltpu.VMEM(w.shape, bf16) for w in weights) + (dma((5,)),),
        flops=32 * wout.size,
    )


def cross_kernel(
    info, lens, src_ref, kq_ref, state_ref, up_ref, cot_ref, gain_ref, result_ref,
    own_ref, got_ref, final_ref, wv_any, wco_any, win_any,
    low_ref, away_ref, rows_ref, long_ref, gc_ref, mix_ref, wv, wco, win, sems, *, head_dim,
):
    copies = fetch(((wv_any, wv), (wco_any, wco), (win_any, win)), sems)
    src = src_ref[...]
    seq, width = src.shape
    gain = row_of(gain_ref)
    mask = head_mask(width, head_dim)
    lanes = lax.broadcasted_iota(jnp.int32, (16, seq), 1)
    c = jnp.where(lanes < lens[info[0]], dot_t(kq_ref[...], src), masked_score)
    c = jnp.exp(c - jnp.max(c, axis=-1, keepdims=True))
    c = c * (1.0 / jnp.sum(c, axis=-1, keepdims=True))
    c_low = c.astype(bf16)
    mix = dot(c_low, src).astype(bf16)
    mix_ref[...] = mix
    copies[0].wait()
    cctx = jnp.sum(jnp.where(mask, dot(mix, wv[...]), 0.0), axis=0, keepdims=True)
    cctx = cctx.astype(bf16).astype(f32)
    copies[1].wait()
    z2 = state_ref[3:4, :] + row_dot(cctx, wco[...])
    m3 = norm_apply(z2, gain).astype(bf16).astype(f32)
    copies[2].wait()
    dh, slope = gelu_parts(row_dot(m3, win[...]))
    g_b = (slope * up_ref[...]).astype(bf16).astype(f32)
    cot = picked(info[0], cot_ref)
    gz2 = cot + norm_back(z2, gain, row_dot_t(g_b, win[...]))
    g_cctx = row_dot_t(gz2, wco[...]).astype(bf16).astype(f32)
    up = dot_t(spread(g_cctx, mask), wv[...]).astype(bf16)
    d_c = dot_t(up, src)
    g_c = (c * (d_c - jnp.sum(c * d_c, axis=-1, keepdims=True))).astype(bf16)
    src_up = t_dot(
        jnp.concatenate([g_c, c_low], axis=0), jnp.concatenate([kq_ref[...], up], axis=0)
    )
    cot_x = joined(info[0], own_ref[0], got_ref[0]).astype(f32)
    low = (cot_x + norm_back(result_ref[...].astype(f32), row_of(final_ref), src_up)).astype(bf16)
    low_ref[...] = low
    half = width // 2
    away_ref[...] = jnp.where(info[0] == 0, low[:, half:], low[:, :half])
    gc_ref[...] = g_c
    for at, row in enumerate((cctx, z2, m3, gz2, g_cctx, cot)):
        rows_ref[at : at + 1, :] = row
    rows_ref[6:8, :] = jnp.zeros((2, width), f32)
    long_ref[0:1, :] = dh
    long_ref[1:2, :] = g_b


def cross(chain, info, lens, src, kq, state, up, cot, gain, result, cot_enc, got, final, weights, head_dim):
    seq, width = src.shape
    hidden = up.shape[1]
    small = (src, kq, state, up, cot, gain, result, cot_enc, got, final)
    outs = (
        shape((seq, width), bf16), shape((seq, width // 2), bf16), shape((8, width), f32),
        shape((2, hidden), f32), shape((16, seq), bf16), shape((16, width), bf16),
    )
    specs = [whole(a) for a in small]
    specs[7] = specs[8] = pl.BlockSpec(
        (1,) + cot_enc.shape[1:], lambda i, info, lens: (info[0], 0, 0)
    )
    return chain.run(
        functools.partial(cross_kernel, head_dim=head_dim), "decoder_cross", (1,),
        small + weights, specs + [any_space] * 3, outs, tuple(whole(a) for a in outs),
        scalars=(info, lens),
        scratch=tuple(pltpu.VMEM(w.shape, bf16) for w in weights) + (dma((3,)),),
        flops=64 * weights[2].size,
    )


def after_kernel(
    info, src_ref, gc_ref, state_ref, rows_ref, long_ref, mix_ref, self_ref, cross_ref,
    wk_any, wcq_any, wso_any, wsv_any, wout_any, both_ref, *refs, head_dim, heads, slots,
):
    packs = 3 if slots else 1
    wk, wcq, wso, wsv, wout, pad_ref, sems = refs[packs : packs + 7]
    refs = refs[:packs] + refs[packs + 7 :]
    copies = fetch(
        ((wk_any, wk), (wcq_any, wcq), (wso_any, wso), (wsv_any, wsv), (wout_any, wout)), sems
    )
    x, z1 = state_ref[0:1, :], state_ref[3:4, :]
    z2, gz2 = rows_ref[1:2, :], rows_ref[3:4, :]
    dh, g_b = long_ref[0:1, :], long_ref[1:2, :]
    width = x.shape[1]
    mask = head_mask(width, head_dim)
    mix = dot(gc_ref[...], src_ref[...]).astype(bf16)
    copies[0].wait()
    g_cq = jnp.sum(jnp.where(mask, dot(mix, wk[...]), 0.0), axis=0, keepdims=True)
    g_cq = g_cq.astype(bf16).astype(f32)
    copies[1].wait()
    gz1 = gz2 + norm_back(z1, row_of(cross_ref), row_dot_t(g_cq, wcq[...]))
    copies[2].wait()
    g_sv = row_dot_t(gz1, wso[...]).astype(bf16).astype(f32)
    copies[3].wait()
    both_ref[1:2, :] = gz1 + norm_back(x, row_of(self_ref), row_dot_t(g_sv, wsv[...]))
    copies[4].wait()
    both_ref[0:1, :] = z2 + row_dot(dh, wout[...])
    count = dh.shape[1] // width
    g_bs = [g_b[:, at * width : (at + 1) * width] for at in range(count)]
    dhs = [dh[:, at * width : (at + 1) * width] for at in range(count)]
    right = [g_sv, gz1, g_cq, gz2, state_ref[5:6, :], rows_ref[4:5, :], rows_ref[5:6, :]] + g_bs
    left = [state_ref[1:2, :], state_ref[2:3, :], state_ref[4:5, :], rows_ref[0:1, :], rows_ref[2:3, :]]
    pad_ref[...] = jnp.zeros(pad_ref.shape, f32)
    for first, group in ((0, right), (16, left), (48, dhs)):
        for at, row in enumerate(group):
            pad_ref[first + at : first + at + 1, :] = row
    pad_ref[24 : 24 + heads, :] = mix[:heads].astype(f32)
    pad_ref[24 + heads : 24 + 2 * heads, :] = mix_ref[:heads].astype(f32)
    if not slots:
        refs[0][...] = pad_ref[...].astype(bf16)
        return
    send_ref, keep_ref, right_ref, held_ref = refs
    half = width // 2
    both = jnp.concatenate([pad_ref[:16, :half], pad_ref[:16, half:]], axis=0).astype(bf16)
    right_ref[...] = both
    stages = slots.bit_length() - 1
    rows, tall = width // slots, dh.shape[1] // slots
    per = width // tall
    many = pad_ref[16:48, :]
    two = lax.broadcasted_iota(jnp.int32, (16, tile), 0)
    for slot in range(slots):
        mine = pltpu.roll(many, (width - slot * rows) % width, 1)[:, :tile]
        hid = pad_ref[48 + slot // per : 49 + slot // per, :]
        hid = pltpu.roll(hid, (width - slot % per * tall) % width, 1)
        hid = jnp.where(two == 0, hid[:, :tile], jnp.where(two == 1, hid[:, tile : 2 * tile], 0.0))
        spot = spot_in(info[0], info[1] ^ slot, stages)
        held_ref[pl.ds(pl.multiple_of(spot * 16, 16), 16), :] = jnp.concatenate(
            [mine[:16], mine[16:], hid], axis=1
        ).astype(bf16)
    middle = slots // 2 * 16
    keep_ref[...] = held_ref[:middle, :]
    send_ref[:middle, :] = held_ref[middle:, :]
    send_ref[middle:, :] = both


def after(
    chain, info, src, gc, state, rows, long, mix, gain_self, gain_cross, weights, head_dim, heads, slots
):
    width = src.shape[1]
    small = (src, gc, state, rows, long, mix, gain_self, gain_cross)
    half = slots // 2 * 16
    if slots:
        outs = tuple(shape((lines, width // 2), bf16) for lines in (half + 32, half, 32))
    else:
        outs = (shape((64, width), bf16),)
    outs = (shape((2, width), f32),) + outs
    return chain.run(
        functools.partial(after_kernel, head_dim=head_dim, heads=heads, slots=slots),
        "decoder_after", (1,),
        small + weights, [whole(a) for a in small] + [any_space] * 5, outs,
        tuple(whole(a) for a in outs), scalars=(info,),
        scratch=tuple(pltpu.VMEM(w.shape, bf16) for w in weights)
        + (pltpu.VMEM((64, width), f32), dma((5,)))
        + ((pltpu.VMEM((2 * half, width // 2), bf16),) if slots else ()),
        flops=32 * weights[4].size,
    )


def backward_kernel(
    info, gain_ref, low_any, slope_any, wout_any, win_any, y1_any, wo_any,
    *refs,
):
    (low_ref, slope_ref, wout_ref, win_ref, y1_ref, wo_ref, ga_ref, gylow_ref, acc_ref) = refs[-11:-2]
    sems, out_sems = refs[-2:]
    me = info[0]
    parts, seq, width = slope_ref.shape
    part = parts // 2
    away_anys, (keep_any, gylow_any, gyaway_ref, gctx_ref) = refs[:part], refs[part : part + 4]
    chunks = [(1 - me) * part + at for at in range(part)] + [me * part + at for at in range(part)]
    loads = [(low_any, low_ref)]
    for at, chunk_at in enumerate(chunks):
        spot = pl.ds(pl.multiple_of(chunk_at * width, width), width)
        loads.append((wout_any.at[spot, :], wout_ref.at[at]))
        loads.append((slope_any.at[:, spot], slope_ref.at[at]))
        loads.append((win_any.at[:, spot], win_ref.at[at]))
    loads += [(y1_any, y1_ref), (wo_any, wo_ref)]
    loads = fetch(loads, sems, 4)
    saved = []
    loads[0].wait()
    for at in range(parts):
        for copy in loads[4 + 3 * at : 7 + 3 * at]:
            copy.start()
        loads[1 + 3 * at].wait()
        rise = dot_t(low_ref[...], wout_ref[at])
        loads[2 + 3 * at].wait()
        ga_ref[at] = (slope_ref[at].astype(f32) * rise).astype(bf16)
        if at < part:
            target = away_anys[at]
        else:
            target = keep_any.at[:, pl.ds(at % part * width, width)]
        copy = pltpu.make_async_copy(ga_ref.at[at], target, out_sems.at[at])
        copy.start()
        saved.append(copy)
        loads[3 + 3 * at].wait()
        if at == 0:
            acc_ref[...] = dot_t(ga_ref[at], win_ref[at])
        else:
            acc_ref[...] += dot_t(ga_ref[at], win_ref[at])
    loads[-2].wait()
    y1 = y1_ref[...].astype(f32)
    low = (low_ref[...].astype(f32) + norm_back(y1, row_of(gain_ref), acc_ref[...])).astype(bf16)
    gylow_ref[...] = low
    copy = pltpu.make_async_copy(gylow_ref, gylow_any, out_sems.at[parts])
    copy.start()
    saved.append(copy)
    half = width // 2
    gyaway_ref[...] = jnp.where(me == 0, low[:, half:], low[:, :half])
    loads[-1].wait()
    gctx_ref[...] = dot_t(wo_ref[...], low).astype(bf16)
    for copy in saved:
        copy.wait()


def backward(chain, info, low, slope, wout, win, y1, gain, wo):
    seq, width = low.shape
    hidden = win.shape[1]
    parts = hidden // width
    act, tall = shape((seq, width), bf16), shape((seq, hidden // 2), bf16)
    side, turned = shape((seq, width // 2), bf16), shape((width, seq), bf16)

    def vmem(*dims):
        return pltpu.VMEM(dims, bf16)

    return chain.run(
        backward_kernel,
        "feed_forward_back",
        (1,),
        (gain, low, slope, wout, win, y1, wo),
        [whole(gain)] + [any_space] * 6,
        (act,) * (parts // 2) + (tall, act, side, turned),
        (any_space,) * (parts // 2) + (any_space, any_space, whole(side), whole(turned)),
        scalars=(info,),
        scratch=(
            vmem(seq, width), vmem(parts, seq, width), vmem(parts, width, width),
            vmem(parts, width, width), vmem(seq, width), vmem(width, width),
            vmem(parts, seq, width), vmem(seq, width), pltpu.VMEM((seq, width), f32),
            dma((3 + 3 * parts,)), dma((parts + 1,)),
        ),
        flops=2 * seq * width * (width + 2 * hidden),
    )


def attention_back_kernel(
    info, scale_ref, gain_ref, own_ref, got_ref, qt_any, k_any, v_any, ctx_any, gctx_any, e_any,
    wq_any, wk_any, wv_any, gy_any,
    gq_ref, gk_ref, gv_ref, keep_ref, gradkeep_ref, gradaway_ref, table_ref,
    qt_ref, k_ref, v_ref, ctx_ref, gctx_ref, e_ref, wq_ref, wk_ref, wv_ref, gy_ref,
    rise_ref, gs_ref, sums_ref, acc_ref, sems, *, heads,
):
    me = info[0]
    seq, width = k_ref.shape
    head_dim = width // heads
    blocks = seq // tile
    half = width // 2
    side = heads // 2
    pair = 2 * head_dim
    loads = fetch(
        ((k_any, k_ref), (v_any, v_ref), (qt_any, qt_ref), (gctx_any, gctx_ref), (ctx_any, ctx_ref))
        + tuple(
            (e_any.at[(1 - me) * side + at if at < side else me * side + at - side], e_ref.at[at])
            for at in range(heads)
        )
        + ((wq_any, wq_ref), (wk_any, wk_ref), (wv_any, wv_ref), (gy_any, gy_ref)),
        sems,
        7,
    )
    for copy in loads[:5]:
        copy.wait()
    pair_lanes = lax.broadcasted_iota(jnp.int32, (seq, pair), 1)
    ones = [
        jnp.where((pair_lanes == start) | (pair_lanes == start + 1), 1.0, 0.0).astype(bf16)
        for start in (head_dim, 0)
    ]
    low_half = pair_lanes < head_dim
    none = jnp.zeros((head_dim - 16, seq), bf16)
    line_rows = lax.broadcasted_iota(jnp.int32, (16, seq), 0)
    sums_ref[...] = jnp.zeros(sums_ref.shape, f32)

    def first_of(at):
        base = (1 - me if at < side else me) * half
        return pl.multiple_of(base + at % side // 2 * pair, pair)

    def prepare(at):
        rows = pl.ds(first_of(at), pair)
        g2 = gctx_ref[rows, :].astype(f32)
        head = lax.div(first_of(at), head_dim)
        g2 = jnp.concatenate(
            [
                g2[:head_dim] * scale_ref[pl.ds(head, 1), :],
                g2[head_dim:] * scale_ref[pl.ds(head + 1, 1), :],
            ],
            axis=0,
        )
        both = g2 * ctx_ref[rows, :].astype(f32)
        g2 = g2.astype(bf16)
        g_ext = []
        for inner in range(2):
            here = slice(inner * head_dim, (inner + 1) * head_dim)
            delta = -jnp.sum(both[here], axis=0, keepdims=True)
            high = delta.astype(bf16).astype(f32)
            extra = jnp.where(line_rows == 0, high, jnp.where(line_rows == 1, delta - high, 0.0))
            extra = extra.astype(bf16)
            if inner == 0:
                g_ext.append(jnp.concatenate([g2[here], extra, none], axis=0))
            else:
                g_ext.append(jnp.concatenate([extra, none, g2[here]], axis=0))
        return g2, g_ext

    pairs = {}

    def rise(at):
        upper = at % 2
        if not upper:
            pairs[at // 2] = prepare(at)
        v2 = v_ref[:, pl.ds(first_of(at), pair)]
        v_ext = jnp.where(low_half, ones[1], v2) if upper else jnp.where(low_half, v2, ones[0])
        rise_ref[upper] = dot(v_ext, pairs[at // 2][1][upper])

    def spread_scores(at):
        slot = at % 2
        near, outer = [], [None, None]
        for sub in range(tile // chunk):
            sums = [None] * 5
            for key in range(blocks):
                start = key * tile + sub * chunk
                down = slice(start, start + chunk)
                for query in range(blocks):
                    across = slice(query * tile, (query + 1) * tile)
                    g = e_ref[at, down, across].astype(f32) * rise_ref[slot, down, across]
                    gs_ref[slot, down, across] = g.astype(bf16)
                    kind = min(max(query - key, -2), 2) + 2
                    sums[kind] = g if sums[kind] is None else sums[kind] + g
            near.append(jnp.concatenate(sums[1:4] + [jnp.zeros((chunk, tile), f32)], axis=1))
            outer = [a if b is None else a + b for a, b in zip((sums[4], sums[0]), outer)]
        folded = jnp.concatenate(near, axis=0)
        lanes = 4 * tile
        while folded.shape[0] > 8:
            rest = folded.shape[0] // 2
            folded = folded[:rest] + pltpu.roll(folded[rest:], lanes - rest, 1)
        rows = lax.broadcasted_iota(jnp.int32, folded.shape, 0)
        for bit in (4, 2, 1):
            moved = pltpu.roll(folded, lanes - bit, 1)
            folded = jnp.where((rows & bit) != 0, moved, folded)
        line = jnp.sum(folded, axis=0, keepdims=True)
        outer = [jnp.sum(part, axis=0, keepdims=True) for part in outer]
        row = (8 if at >= side else 0) + at % side
        sums_ref[row : row + 1, :] = jnp.concatenate([line] + outer, axis=1)

    parts = {}
    rise(0)
    for at in range(heads):
        first = first_of(at)
        upper = at % 2
        if at + 1 < heads:
            rise(at + 1)
        for copy in loads[7 + at : 8 + at] + (loads[7 + heads :] if at == heads - 1 else []):
            copy.start()
        loads[5 + at].wait()
        if not upper:
            turned = k_ref[:, pl.ds(first, pair)].astype(f32).T.astype(bf16)
        spread_scores(at)
        here = slice(upper * head_dim, (upper + 1) * head_dim)
        q_mine = qt_ref[pl.ds(pl.multiple_of(first + upper * head_dim, head_dim), head_dim), :]
        g_q = dot(turned[here], gs_ref[upper])
        g_k = dot_t(q_mine, gs_ref[upper])
        g_v = dot_t(pairs[at // 2][0][here], e_ref[at])
        parts[upper] = (g_q, g_k, g_v)
        if upper:
            for which, gone_ref in enumerate((gq_ref, gk_ref, gv_ref)):
                both = jnp.concatenate([parts[0][which], parts[1][which]], axis=0).T.astype(bf16)
                start = at % side // 2 * pair
                if at < side:
                    gone_ref[:, start : start + pair] = both
                else:
                    keep_ref[:, which * half + start : which * half + start + pair] = both
    for copy in loads[5 + heads :]:
        copy.wait()
    total = None
    for which, (ref, gone_ref) in enumerate(((wq_ref, gq_ref), (wk_ref, gk_ref), (wv_ref, gv_ref))):
        kept = keep_ref[:, which * half : (which + 1) * half]
        for part, base in ((gone_ref[...], (1 - me) * half), (kept, me * half)):
            part = dot_t(part, ref[:, pl.ds(pl.multiple_of(base, half), half)])
            total = part if total is None else total + part
    x = joined(me, own_ref[0], got_ref[0]).astype(f32)
    grad = gy_ref[...].astype(f32) + norm_back(x, row_of(gain_ref), total)
    middle = seq // 2
    gradkeep_ref[...] = jnp.where(me == 0, grad[:middle], grad[middle:])
    gradaway_ref[...] = jnp.where(me == 0, grad[middle:], grad[:middle])
    sums = joined(me, sums_ref[8:], sums_ref[:8])
    spots = lax.broadcasted_iota(jnp.int32, (sums.shape[1], tile), 0)
    offsets = tile - jnp.where(spots < 3 * tile, spots, spots - 4 * tile)
    kinds = jnp.where(spots < 4 * tile, bucket_of(offsets), jnp.where(spots < 5 * tile, 15, 31))
    lanes = lax.broadcasted_iota(jnp.int32, kinds.shape, 1)
    one_hot = jnp.where(kinds == lanes, 1.0, 0.0).astype(f32)
    table = lax.dot_general(
        sums, one_hot, (((1,), (0,)), ((), ())), precision=lax.Precision.HIGHEST,
        preferred_element_type=f32,
    )
    table_ref[:, :tile] = table.astype(bf16)
    table_ref[:, tile:] = jnp.zeros((16, 2 * tile), bf16)


def attention_back(chain, info, scale, gain, enc_in, got, qt, k, v, ctx, gctx, e, wq, wk, wv, gy):
    seq, width = k.shape
    heads = e.shape[0]
    block = pl.BlockSpec((1, seq // 2, width), lambda i, info: (info[0], 0, 0))
    side, part = shape((seq, 3 * width // 2), bf16), shape((seq // 2, width), f32)
    narrow = shape((seq, width // 2), bf16)
    outs = (narrow, narrow, narrow, side, part, part, shape((16, 3 * tile), bf16))
    far = (qt, k, v, ctx, gctx, e, wq, wk, wv, gy)
    return chain.run(
        functools.partial(attention_back_kernel, heads=heads),
        "attention_back",
        (1,),
        (scale, gain, enc_in, got) + far,
        [whole(scale), whole(gain), block, block] + [any_space] * len(far),
        outs,
        tuple(whole(a) for a in outs),
        scalars=(info,),
        scratch=tuple(pltpu.VMEM(a.shape, bf16) for a in far)
        + (
            pltpu.VMEM((2, seq, seq), f32), pltpu.VMEM((2, seq, seq), bf16),
            pltpu.VMEM((16, 6 * tile), f32), pltpu.VMEM((8, tile), f32), dma((9 + heads,)),
        ),
        flops=6 * seq * width * width + 16 * seq * seq * width,
    )


def spot_in(me, relative, stages):
    spot = 0
    for k in range(stages):
        bit = jnp.where(me == 0, k, 1 - k) if k < 2 <= stages else k
        spot = spot | (((relative >> bit) & 1) << (stages - 1 - k))
    return spot


def store(info, base, low, rows, held_ref, slots, line):
    stages = slots.bit_length() - 1
    span = held_ref.shape[0] // slots
    wide = held_ref.shape[1]
    for at in range(low.shape[0] // rows):
        spot = spot_in(info[0], info[1] ^ (base + at), stages)
        for piece in range(low.shape[1] // wide):
            start = pl.multiple_of(spot * span + line + piece * rows, 16)
            held_ref[pl.ds(start, rows), :] = low[
                at * rows : (at + 1) * rows, piece * wide : (piece + 1) * wide
            ]


def release(held_ref, keep_any, send_any, sems, extra=None):
    middle = held_ref.shape[0] // 2
    pairs = [
        (held_ref.at[pl.ds(middle, middle), :], send_any.at[pl.ds(0, middle), :]),
        (held_ref.at[pl.ds(0, middle), :], keep_any),
    ]
    if extra is not None:
        pairs.append((extra, send_any.at[pl.ds(middle, extra.shape[0]), :]))
    for copy in fetch(pairs, sems):
        copy.wait()


def tall_kernel(
    info, r0_ref, r1_ref, extra_ref, l0_any, l1_any, keep_any, send_any, l0_ref, l1_ref, held_ref, sems, out_sems, *, rows, slots
):
    parts, seq, width = l0_ref.shape
    loads = []
    for at in range(parts):
        spot = pl.ds(at * width, width)
        loads += [(l0_any.at[:, spot], l0_ref.at[at]), (l1_any.at[:, spot], l1_ref.at[at])]
    loads = fetch(loads, sems, 4)
    for at in range(parts):
        loads[2 * at].wait()
        loads[2 * at + 1].wait()
        for copy in loads[2 * at + 4 : 2 * at + 6]:
            copy.start()
        low = (t_dot(l0_ref[at], r0_ref[...]) + t_dot(l1_ref[at], r1_ref[...])).astype(bf16)
        store(info, at * (width // rows), low, rows, held_ref, slots, 0)
    release(held_ref, keep_any, send_any, out_sems, extra_ref)


def tall_grad(chain, info, slots, left, left_got, right, right_got, extra):
    seq, tall = left.shape
    wide = right_got.shape[1]
    rows = tall // slots
    parts = 4
    middle = slots // 2 * rows
    outs = (shape((middle, wide), bf16), shape((middle + extra.shape[0], wide), bf16))
    far = pltpu.VMEM((parts, seq, tall // parts), bf16)
    return chain.run(
        functools.partial(tall_kernel, rows=rows, slots=slots), "grad_ff_out", (1,),
        (right, right_got, extra, left, left_got),
        [
            pl.BlockSpec((seq, wide), lambda i, info: (0, info[0])), whole(right_got), whole(extra),
            any_space, any_space,
        ],
        outs, (any_space, any_space), scalars=(info,),
        scratch=(far, far, pltpu.VMEM((tall, wide), bf16), dma((2 * parts,)), dma((3,))),
        flops=4 * seq * tall * wide,
    )


def mixed_kernel(
    info, n0_any, n1_any, a0_any, c0_any, c1_any, g0_any, g1_any, *refs, rows, slots
):
    steps = len(refs) - 13
    a1_anys, (keep_any, send_any) = refs[:steps], refs[steps : steps + 2]
    n0_ref, n1_ref, a0_ref, a1_ref, c0_ref, c1_ref, g0_ref, g1_ref, held_ref, sems, out_sems = refs[steps + 2 :]
    seq, width = n0_ref.shape
    wide = held_ref.shape[1]
    loads = fetch(
        (
            (n0_any, n0_ref), (a0_any, a0_ref), (n1_any, n1_ref),
            (c0_any, c0_ref), (c1_any, c1_ref),
            (g0_any.at[:, pl.ds(pl.multiple_of(info[0] * wide, wide), wide)], g0_ref),
            (g1_any, g1_ref),
        )
        + tuple((part, a1_ref.at[at]) for at, part in enumerate(a1_anys)),
        sems,
    )
    for copy in loads[:3]:
        copy.wait()
    for at in range(steps):
        spot = slice(at * width, (at + 1) * width)
        loads[7 + at].wait()
        low = t_dot(n0_ref[...], a0_ref[:, spot]) + t_dot(n1_ref[...], a1_ref[at])
        store(info, 0, low.astype(bf16), rows, held_ref, slots, at * (width // wide) * rows)
    for copy in loads[3:7]:
        copy.wait()
    low = (dot(c0_ref[...], g0_ref[...]) + dot(c1_ref[...], g1_ref[...])).astype(bf16)
    store(info, 0, low, rows, held_ref, slots, steps * (width // wide) * rows)
    release(held_ref, keep_any, send_any, out_sems)


def mixed_grad(chain, info, slots, n2, n2_got, ctx, ctx_got, keep, got, gy, gy_got):
    seq, width = n2.shape
    wide = gy_got.shape[1]
    rows = width // slots
    lines = (keep.shape[1] // wide + 1) * rows
    outs = (shape((slots // 2 * lines, wide), bf16),) * 2
    args = (n2, n2_got, keep, ctx, ctx_got, gy, gy_got) + got
    dims = [n2.shape, n2.shape, keep.shape, (len(got),) + n2.shape, ctx.shape, ctx.shape]
    dims += [gy_got.shape, gy_got.shape]
    return chain.run(
        functools.partial(mixed_kernel, rows=rows, slots=slots), "grad_ff_in", (1,), args,
        [any_space] * len(args), outs, (any_space, any_space), scalars=(info,),
        scratch=tuple(pltpu.VMEM(d, bf16) for d in dims + [(slots * lines, wide)])
        + (dma((len(args),)), dma((2,))),
        flops=4 * seq * width * (keep.shape[1] + wide),
    )


def heads_kernel(
    info, table_ref, n0_any, n1_any, g0_any, gq_any, gk_any, gv_any, keep_any, send_any,
    n0_ref, n1_ref, g0_ref, g1_ref, held_ref, sems, out_sems, *, rows, slots,
):
    loads = fetch(
        ((n0_any, n0_ref), (g0_any, g0_ref), (n1_any, n1_ref))
        + tuple(
            (part, g1_ref.at[:, pl.ds(at * held_ref.shape[1], held_ref.shape[1])])
            for at, part in enumerate((gq_any, gk_any, gv_any))
        ),
        sems,
    )
    wide = held_ref.shape[1]
    for copy in loads:
        copy.wait()
    for first, count in ((0, 2), (2, 1)):
        spot = slice(first * wide, (first + count) * wide)
        low = t_dot(n0_ref[...], g0_ref[:, spot]) + t_dot(n1_ref[...], g1_ref[:, spot])
        store(info, 0, low.astype(bf16), rows, held_ref, slots, first * rows)
    release(held_ref, keep_any, send_any, out_sems, table_ref)


def heads_grad(chain, info, slots, n1, n1_got, keep, got, table):
    seq, width = n1.shape
    wide = width // 2
    rows = width // slots
    lines = keep.shape[1] // wide * rows
    outs = (
        shape((slots // 2 * lines, wide), bf16), shape((slots // 2 * lines + 16, wide), bf16),
    )
    args = (n1, n1_got, keep) + got
    dims = (n1.shape, n1.shape, keep.shape, keep.shape)
    return chain.run(
        functools.partial(heads_kernel, rows=rows, slots=slots), "grad_heads", (1,), (table,) + args,
        [whole(table)] + [any_space] * 6, outs, (any_space, any_space), scalars=(info,),
        scratch=tuple(pltpu.VMEM(d, bf16) for d in dims)
        + (pltpu.VMEM((slots * lines, wide), bf16), dma((6,)), dma((3,))),
        flops=4 * seq * width * keep.shape[1],
    )


def stage_kernel(*refs, half, table):
    keep_ref, got_ref = refs[:2]
    outs = refs[3:] if table else refs[2:]
    outs[0][:half, :] = keep_ref[:half, :] + got_ref[:half, :]
    if len(outs) > 1:
        outs[1][:half, :] = keep_ref[half:, :] + got_ref[half : 2 * half, :]
    if table:
        total = refs[2][...] + got_ref[keep_ref.shape[0] :, :]
        if len(outs) > 1:
            outs[1][half:, :] = total
            outs[2][...] = total
        else:
            outs[0][half:, :] = total


def stage(chain, keep, got, last, table=None, flops=0):
    count, wide = keep.shape
    extra = 0 if table is None else table.shape[0]
    args = (keep, got) if table is None else (keep, got, table)
    half = count if last else count // 2
    outs = (shape((half + extra, wide), bf16),)
    if not last:
        outs = (shape((half, wide), bf16), shape((half + extra, wide), bf16))
        outs += () if table is None else (shape(table.shape, bf16),)
    return chain.run(
        functools.partial(stage_kernel, half=half, table=table is not None), "sum_stage", (1,),
        args, [whole(a) for a in args], outs, tuple(whole(a) for a in outs), limit=24, flops=flops,
    )


def factor_stage_kernel(keep_ref, got_ref, left_ref, right_ref, *refs, slots, pairs, rows):
    half = slots // 2
    block = 16 * pairs
    after = slots * rows
    got_right = after + slots * block
    if slots == 1:
        done_ref, = refs
        done_ref[:rows, :] = keep_ref[...] + got_ref[:rows, :]
        done_ref[rows : rows + block, :] = left_ref[...]
        done_ref[rows + block : rows + 2 * block, :] = got_ref[after:got_right, :]
        done_ref[rows + 2 * block : rows + 4 * block, :] = right_ref[...]
        done_ref[rows + 4 * block :, :] = got_ref[got_right:, :]
        return
    keep_out, send_out, left_out, right_out = refs
    middle = half * rows
    keep_out[...] = keep_ref[:middle, :] + got_ref[:middle, :]
    send_out[:middle, :] = keep_ref[middle:, :] + got_ref[middle:after, :]
    for slot in range(slots):
        target, first = (left_out, 0) if slot < half else (send_out, middle)
        first += slot % half * 2 * block
        target[first : first + block, :] = left_ref[slot * block : (slot + 1) * block, :]
        target[first + block : first + 2 * block, :] = got_ref[
            after + slot * block : after + (slot + 1) * block, :
        ]
    right_out[: 2 * block, :] = right_ref[...]
    right_out[2 * block :, :] = got_ref[got_right:, :]
    first = middle + half * 2 * block
    send_out[first : first + 2 * block, :] = right_ref[...]
    send_out[first + 2 * block :, :] = got_ref[got_right:, :]


def factor_stage(chain, keep, got, left, right):
    wide = keep.shape[1]
    pairs = right.shape[0] // 32
    slots = left.shape[0] // (16 * pairs)
    rows = keep.shape[0] // slots
    if slots == 1:
        lines = (rows + 96 * pairs,)
    else:
        half = slots // 2
        lines = (half * rows, half * rows + 32 * half * pairs + 64 * pairs, 32 * half * pairs, 64 * pairs)
    outs = tuple(shape((count, wide), bf16) for count in lines)
    args = (keep, got, left, right)
    return chain.run(
        functools.partial(factor_stage_kernel, slots=slots, pairs=pairs, rows=rows), "sum_stage",
        (1,), args, [whole(a) for a in args], outs, tuple(whole(a) for a in outs), limit=24,
    )


def gain_of(weight, grad):
    return jnp.sum(weight[...].astype(f32) * grad, axis=1, keepdims=True)


def gain_line(total, gain_ref, chip):
    rows = total.shape[0]
    turned = jnp.broadcast_to(total, (rows, tile)).T[0:1]
    gain = row_of(gain_ref)
    width = gain.shape[1]
    mine = pltpu.roll(gain, lax.rem(width - chip * rows, width), 1)[:, :rows]
    return (turned / mine).reshape(rows)


def decoder_kernel(
    info, own_ref, got_ref, wsv_ref, wcq_ref, win_ref, wk_ref, wv_ref,
    gself_ref, gcross_ref, gffn_ref, gfinal_ref,
    sv_ref, so_ref, cq_ref, co_ref, in_ref, out_ref, ck_ref, cv_ref,
    dself_ref, dcross_ref, dffn_ref, dfinal_ref, left_ref, right_ref, *, heads,
):
    chip = info[1]
    count = left_ref.shape[0]
    each = count // 2
    tall, width = out_ref.shape
    rows, hidden = in_ref.shape
    head_dim = width // heads
    half = width // 2
    middle = tall + 16 * each
    for at, ref in enumerate((own_ref, got_ref)):
        here = slice(at * each, (at + 1) * each)
        left_ref[here] = ref[tall:middle, :].astype(f32).reshape(each, 16, half)
        right_ref[here] = ref[middle:, :].astype(f32).reshape(each, 32, half)

    def right(at):
        return jnp.concatenate([right_ref[:, at, :], right_ref[:, 16 + at, :]], axis=1).astype(bf16)

    def left(at):
        lane = at // 16 * tile
        return left_ref[:, at % 16, lane : lane + tile].astype(bf16)[:, :rows]

    r = [right(at) for at in range(7)]
    r_hid = jnp.concatenate([right(7 + at) for at in range(hidden // width)], axis=1)
    l_hid = jnp.concatenate(
        [left_ref[:, 0, 2 * tile :], left_ref[:, 1, 2 * tile :]], axis=1
    ).astype(bf16)[:, :tall]
    sv_ref[...] = t_dot(left(0), r[0])
    dself_ref[...] = gain_line(gain_of(wsv_ref, sv_ref[...]), gself_ref, chip)
    so_ref[...] = t_dot(left(1), r[1])
    cq_ref[...] = t_dot(left(2), r[2])
    dcross_ref[...] = gain_line(gain_of(wcq_ref, cq_ref[...]), gcross_ref, chip)
    co_ref[...] = t_dot(left(3), r[3])
    in_ref[...] = t_dot(left(4), r_hid)
    dffn_ref[...] = gain_line(gain_of(win_ref, in_ref[...]), gffn_ref, chip)
    out_ref[...] = t_dot(l_hid, r[6])
    for head in range(heads):
        spot = slice(head * head_dim, (head + 1) * head_dim)
        ck_ref[:, spot] = t_dot(left(8 + head), r[4][:, spot])
        cv_ref[:, spot] = t_dot(left(8 + heads + head), r[5][:, spot])
    total = gain_of(wk_ref, ck_ref[...]) + gain_of(wv_ref, cv_ref[...])
    dfinal_ref[...] = gain_line(total, gfinal_ref, chip)


def decoder_grads(chain, info, own, got, weights, gains, rows, heads):
    width, hidden = weights[0].shape[0], weights[2].shape[1]
    tall = hidden * rows // width
    each = (own.shape[0] - tall) // 48
    line = shape((rows,), f32)
    flat = shape((rows, width), f32)
    outs = (flat, flat, flat, flat, shape((rows, hidden), f32), shape((tall, width), f32), flat, flat)
    outs += (line,) * 4

    def sliced(array):
        return pl.BlockSpec((rows, array.shape[1]), lambda i, info: (info[1], 0))

    return chain.run(
        functools.partial(decoder_kernel, heads=heads), "decoder_grads",
        (1,), (own, got) + weights + gains,
        [whole(own), whole(got)] + [sliced(a) for a in weights] + [whole(a) for a in gains],
        outs, tuple(whole(a) for a in outs), scalars=(info,), limit=40, flops=2 * 10**9,
        scratch=(
            pltpu.VMEM((2 * each, 16, width // 2), f32), pltpu.VMEM((2 * each, 32, width // 2), f32),
        ),
    )


def sides(me, own_ref, got_ref, first, rows):
    own, got = own_ref[first : first + rows, :], got_ref[first : first + rows, :]
    low = jnp.where(me == 0, own, got).astype(f32)
    high = jnp.where(me == 0, got, own).astype(f32)
    return low, high


def finish_kernel(
    info, out_ref, out_got, keep_ref, away_ref, grad_ref, grad_got, row_ref, row_got,
    fout_ref, enc_ref, back_ref, dec_ref, decback_ref,
):
    me = info[0]
    wide = out_ref.shape[1]
    low, high = sides(me, out_ref, out_got, 0, fout_ref.shape[0])
    fout_ref[:, :wide] = low
    fout_ref[:, wide:] = high
    enc_ref[me] = keep_ref[...]
    enc_ref[1 - me] = away_ref[...]
    back_ref[me] = grad_ref[...]
    back_ref[1 - me] = grad_got[...]
    rows_two = lax.broadcasted_iota(jnp.int32, (2, row_ref.shape[1]), 0)
    both = jnp.where(rows_two == me, row_ref[0:1], row_got[0:1])
    dec_ref[...] = both.astype(bf16)
    decback_ref[...] = jnp.where(rows_two == me, row_ref[1:2], row_got[1:2])


def finish(chain, info, tall, out, out_got, keep, away, grad, grad_got, row, row_got):
    width = keep.shape[1]
    half = away.shape[0]
    args = (out, out_got, keep, away, grad, grad_got, row, row_got)
    outs = (
        shape((tall, width), f32), shape((2, half, width), bf16),
        shape((2, half, width), f32), shape((2, width), bf16), shape((2, width), f32),
    )
    specs = [whole(a) for a in args]
    specs[0] = specs[1] = pl.BlockSpec((tall, out.shape[1]), lambda i, info: (0, 0))
    specs[2] = pl.BlockSpec((half, width), lambda i, info: (info[0], 0))
    return chain.run(
        finish_kernel, "finish_activations", (1,),
        args, specs, outs, tuple(whole(a) for a in outs), scalars=(info,), limit=40,
    )


def finish_mix_kernel(
    info, mix_ref, mix_got, win_ref, gain_ref, fin_ref, o_ref, dffn_ref, *, rows, steps
):
    me = info[0]
    wide = mix_ref.shape[1]
    for at in range(steps):
        low, high = sides(me, mix_ref, mix_got, at * rows, rows)
        fin_ref[:, at * wide : (at + 1) * wide] = low
        fin_ref[:, (steps + at) * wide : (steps + at + 1) * wide] = high
    low, high = sides(me, mix_ref, mix_got, steps * rows, rows)
    o_ref[:, :wide] = low
    o_ref[:, wide:] = high
    dffn_ref[...] = gain_line(gain_of(win_ref, fin_ref[...]), gain_ref, info[1])


def finish_mix(chain, info, mix, mix_got, win, gain, rows):
    width, hidden = win.shape
    args = (mix, mix_got, win, gain)
    outs = (shape((rows, hidden), f32), shape((rows, width), f32), shape((rows,), f32))
    specs = [whole(a) for a in args]
    specs[2] = pl.BlockSpec((rows, hidden), lambda i, info: (info[1], 0))
    return chain.run(
        functools.partial(finish_mix_kernel, rows=rows, steps=hidden // 2 // mix.shape[1]),
        "finish_mixed", (1,),
        args, specs, outs, tuple(whole(a) for a in outs), scalars=(info,), limit=40,
    )


def last_kernel(
    info, sum_ref, got_ref, wq_ref, wk_ref, wv_ref, gain_ref,
    q_ref, k_ref, v_ref, d_ref, table_ref, *, rows, heads,
):
    me = info[0]
    wide = sum_ref.shape[1]
    outs = (q_ref, k_ref, v_ref)
    for at, ref in enumerate(outs):
        low, high = sides(me, sum_ref, got_ref, at * rows, rows)
        ref[:, :wide] = low
        ref[:, wide:] = high
    total = sum(gain_of(w, ref[...]) for w, ref in zip((wq_ref, wk_ref, wv_ref), outs))
    d_ref[...] = gain_line(total, gain_ref, info[1])
    first = 3 * rows
    table = sum_ref[first:, :tile].astype(f32) + got_ref[first:, :tile].astype(f32)
    part = heads // 2
    table_ref[:part, :] = table[:part, : table_ref.shape[1]]
    table_ref[part:, :] = table[8 : 8 + part, : table_ref.shape[1]]


def last(chain, info, done, got, wq, wk, wv, gain, rows, buckets, heads):
    width = wq.shape[0]
    flat = shape((rows, width), f32)
    args = (done, got, wq, wk, wv, gain)
    outs = (flat, flat, flat, shape((rows,), f32), shape((heads, buckets), f32))
    specs = [whole(a) for a in args]
    for at in (2, 3, 4):
        specs[at] = pl.BlockSpec((rows, args[at].shape[1]), lambda i, info: (info[1], 0))
    return chain.run(
        functools.partial(last_kernel, rows=rows, heads=heads), "finish_last", (1,), args, specs,
        outs, tuple(whole(a) for a in outs), scalars=(info,), limit=40,
    )


def plain_grad(me, place, pieces, tall):
    parts = []
    for left, left_got, right, right_got, offset in pieces:
        wide = right_got.shape[1]
        keep = lax.dynamic_slice_in_dim(right, me * wide, wide, 1) if offset else right
        total = t_dot(
            jnp.concatenate([left, left_got]), jnp.concatenate([keep, right_got])
        ).astype(bf16)
        slots = place.shape[0]
        if tall:
            parts.append(total.reshape(slots, -1, wide))
        else:
            half = left.shape[1] // 2
            for at in range(0, wide, half):
                parts.append(total[:, at : at + half].reshape(slots, -1, half))
    total = jnp.concatenate(parts, axis=1)
    order = jnp.zeros_like(place).at[place].set(jnp.arange(place.shape[0], dtype=jnp.int32))
    return jnp.take(total, order, axis=0)


def plain_sides(me, done, got):
    low = jnp.where(me == 0, done, got).astype(f32)
    high = jnp.where(me == 0, got, done).astype(f32)
    return low, high


def body(
    enc_in,
    dec_in,
    lengths,
    cot_enc,
    cot_dec,
    enc_gain_attn,
    enc_query,
    enc_key,
    enc_value,
    enc_output,
    relative_bias_table,
    enc_gain_ffn,
    enc_ff_in,
    enc_ff_out,
    enc_gain_final,
    dec_gain_self,
    dec_self_value,
    dec_self_output,
    dec_gain_cross,
    dec_cross_query,
    dec_cross_key,
    dec_cross_value,
    dec_cross_output,
    dec_gain_ffn,
    dec_ff_in,
    dec_ff_out,
):
    pair_count, seq_dev, width = enc_in.shape
    seq_all = 2 * seq_dev
    bucket_count, heads = relative_bias_table.shape
    head_dim = width // heads
    hidden = enc_ff_in.shape[1]
    slots = lax.axis_size("batch")
    me = lax.axis_index("blk")
    chip = lax.axis_index("batch")
    stages = slots.bit_length() - 1
    rows = width // slots
    aligned = rows % 16 == 0
    chain = Chain()

    def across(array):
        return lax.ppermute(array, "blk", [(0, 1), (1, 0)])

    info = jnp.stack([me, chip]).astype(jnp.int32)
    order = list(range(stages))
    crossed = order if stages < 2 else [1, 0] + order[2:]
    def hop(array, step):
        pairs = []
        for which in range(slots):
            for core in range(2):
                bit = (order, crossed)[core][step]
                pairs.append((which * 2 + core, (which ^ (1 << bit)) * 2 + core))
        return lax.ppermute(array, ("batch", "blk"), pairs)

    class Sum:
        def __init__(self, keep, send, table=None, flops=0, factors=None):
            self.keep, self.table, self.at, self.flops = keep, table, 0, flops
            self.factors = factors
            self.got = hop(send, 0)

        def step(self):
            if self.at == stages:
                return
            self.at += 1
            last = self.at == stages
            if self.factors is not None:
                outs = factor_stage(chain, self.keep, self.got, *self.factors)
                self.factors = outs[2:]
            elif aligned:
                outs = list(stage(chain, self.keep, self.got, last, self.table, self.flops))
            else:
                total = self.keep + self.got
                half = total.shape[0] // 2
                outs = [total] if last else [total[:half], total[half:]]
            self.keep = outs[0]
            if self.table is not None and len(outs) == 3 and self.factors is None:
                self.table = outs[2]
            if last:
                self.done = self.keep
                self.other = across(self.done)
            else:
                self.got = hop(outs[1], self.at)

        def rest(self):
            while self.at < stages:
                self.step()

    def plain_sum(pieces, tall):
        relative = chip ^ jnp.arange(slots, dtype=jnp.int32)
        total = plain_grad(me, spot_in(me, relative, stages).astype(jnp.int32), pieces, tall)
        total = total.reshape(-1, total.shape[-1])
        half = total.shape[0] // 2
        return Sum(total[:half], total[half:])

    enc_got = across(enc_in)
    cot_got = across(cot_enc)
    state, key_query, hid_up = before(
        chain, info, dec_in, cot_dec, dec_gain_self, dec_gain_cross, dec_self_value,
        dec_self_output, dec_cross_query, dec_cross_key, dec_ff_out, head_dim,
    )

    (
        src, result_low, out_away, scale, n1, q_turned, k, v, weights, context, y1, n2, hid, slope
    ) = encoder(
        chain, info, lengths, enc_in, enc_got, enc_gain_attn, enc_query, enc_key, enc_value,
        relative_bias_table.T, enc_gain_ffn, enc_gain_final, enc_output, enc_ff_in, enc_ff_out, heads,
        (cot_got,),
    )
    hid_got, n2_got, ctx_got, n1_got = (across(part) for part in (hid, n2, context, n1))
    out_got = across(out_away)

    ge_low, ge_away, dec_lines, dec_long, g_c, mix = cross(
        chain, info, lengths, src, key_query, state, hid_up, cot_dec, dec_gain_ffn, result_low,
        cot_enc, cot_got, enc_gain_final, (dec_cross_value, dec_cross_output, dec_ff_in), head_dim,
    )
    ge_got = across(ge_away)
    dec_rows, *packed = after(
        chain, info, src, g_c, state, dec_lines, dec_long, mix, dec_gain_self, dec_gain_cross,
        (dec_cross_key, dec_cross_query, dec_self_output, dec_self_value, dec_ff_out),
        head_dim, heads, slots if aligned else 0,
    )
    dec_got = across(dec_rows)

    if aligned:
        left_send, left_keep, right = packed
        sum_out = Sum(
            *tall_grad(chain, info, slots, hid, hid_got, ge_low, ge_got, left_send),
            factors=(left_keep, right),
        )
    else:
        sum_out = plain_sum([(hid, hid_got, ge_low, ge_got, True)], True)
    *ga_away, ga_keep, gy_low, gy_away, g_ctx = backward(
        chain, info, ge_low, slope, enc_ff_out, enc_ff_in, y1, enc_gain_ffn, enc_output
    )
    ga_got, gy_got = tuple(across(part) for part in ga_away), across(gy_away)
    sum_out.step()
    if aligned:
        sum_mix = Sum(
            *mixed_grad(
                chain, info, slots, n2, n2_got, context, ctx_got, ga_keep, ga_got, gy_low, gy_got
            ),
            flops=5 * 10**9,
        )
    else:
        sum_mix = plain_sum(
            [(n2, n2_got, ga_keep, jnp.concatenate(ga_got, axis=1), False), (context.T, ctx_got.T, gy_low, gy_got, True)], False
        )
    sum_out.step()
    *g_away, g_keep, grad_keep, grad_away, table_term = attention_back(
        chain, info, scale, enc_gain_attn, enc_in, enc_got, q_turned, k, v, context, g_ctx, weights,
        enc_query, enc_key, enc_value, gy_low,
    )
    g_got = tuple(across(part) for part in g_away)
    grad_got = across(grad_away)
    sum_out.step()
    sum_mix.step()
    if aligned:
        sum_heads = Sum(
            *heads_grad(chain, info, slots, n1, n1_got, g_keep, g_got, table_term), table_term
        )
    else:
        sum_heads = plain_sum([(n1, n1_got, g_keep, jnp.concatenate(g_got, axis=1), False)], False)
        table_sum = lax.psum(table_term.astype(f32), ("batch", "blk"))

    dec_weights = (dec_self_value, dec_cross_query, dec_ff_in, dec_cross_key, dec_cross_value)
    dec_gains = (dec_gain_self, dec_gain_cross, dec_gain_ffn, enc_gain_final)

    def mine(array):
        return lax.dynamic_slice_in_dim(array, chip * (array.shape[0] // slots), array.shape[0] // slots, 0)

    sum_mix.step()
    sum_heads.step()
    sum_out.rest()
    if aligned:
        sum_mix.step()
        sum_heads.step()
        grad_ff_out, encoder_output, grad_in, dec_out, grad_dec = finish(
            chain, info, hidden // slots, sum_out.done, sum_out.other, result_low, out_got, grad_keep,
            grad_got, dec_rows, dec_got,
        )
        sum_mix.rest()
        sum_heads.step()
        dec_outs = decoder_grads(
            chain, info, sum_out.done, sum_out.other, dec_weights, dec_gains, rows, heads
        )
        (grad_self_value, grad_self_output, grad_cross_query, grad_cross_output) = dec_outs[:4]
        (grad_dec_ff_in, grad_dec_ff_out, grad_cross_key, grad_cross_value) = dec_outs[4:8]
        gain_self, gain_cross, gain_dec_ffn, gain_final = dec_outs[8:]
        grad_ff_in, grad_output, gain_ffn = finish_mix(
            chain, info, sum_mix.done, sum_mix.other, enc_ff_in, enc_gain_ffn, rows
        )
        sum_heads.rest()
        grad_query, grad_key, grad_value, gain_attn, grad_rel_table = last(
            chain, info, sum_heads.done, sum_heads.other, enc_query, enc_key, enc_value,
            enc_gain_attn, rows, bucket_count, heads,
        )
        grad_rel_table = grad_rel_table.T
    else:
        sum_mix.rest()
        sum_heads.rest()
        table = lax.all_gather(packed[0], ("batch", "blk"), axis=0, tiled=False)
        count = hidden // width
        tall = hidden // slots
        r = [table[:, at] for at in range(7)]
        r_hid = table[:, 7 : 7 + count].reshape(-1, hidden)
        chosen = lax.dynamic_slice_in_dim(table[:, 16:48], chip * rows, rows, 2)
        l = [chosen[:, at] for at in range(5)]
        l_hid = table[:, 48 : 48 + count].reshape(-1, hidden)
        l_hid = lax.dynamic_slice_in_dim(l_hid, chip * tall, tall, 1)
        grad_self_value, grad_self_output = t_dot(l[0], r[0]), t_dot(l[1], r[1])
        grad_cross_query, grad_cross_output = t_dot(l[2], r[2]), t_dot(l[3], r[3])
        grad_dec_ff_in = t_dot(l[4], r_hid)
        grad_dec_ff_out = t_dot(l_hid, r[6])
        many = chosen[:, 8 : 8 + 2 * heads].reshape(-1, 2, heads, rows)
        grad_cross_key, grad_cross_value = (
            jnp.einsum(
                "phd,phe->dhe", many[:, at], r[4 + at].reshape(-1, heads, head_dim),
                preferred_element_type=f32,
            ).reshape(rows, width)
            for at in range(2)
        )

        def gain_plain(gain, *terms):
            return sum(jnp.sum(mine(w).astype(f32) * g, axis=1) for w, g in terms) / mine(gain)

        gain_self = gain_plain(dec_gain_self, (dec_self_value, grad_self_value))
        gain_cross = gain_plain(dec_gain_cross, (dec_cross_query, grad_cross_query))
        gain_dec_ffn = gain_plain(dec_gain_ffn, (dec_ff_in, grad_dec_ff_in))
        gain_final = gain_plain(
            enc_gain_final, (dec_cross_key, grad_cross_key), (dec_cross_value, grad_cross_value)
        )
        sum_mix.rest()
        sum_heads.rest()
        grad_ff_out = jnp.concatenate(plain_sides(me, sum_out.done, sum_out.other), axis=1)
        low, high = plain_sides(me, sum_mix.done, sum_mix.other)

        def pick(side, at):
            return side[at * rows : (at + 1) * rows]

        grad_ff_in = jnp.concatenate(
            [pick(side, at) for side in (low, high) for at in range(low.shape[0] // rows - 1)], axis=1
        )
        spot = low.shape[0] // rows - 1
        grad_output = jnp.concatenate([pick(low, spot), pick(high, spot)], axis=1)
        low, high = plain_sides(me, sum_heads.done, sum_heads.other)
        grad_query, grad_key, grad_value = (
            jnp.concatenate([pick(low, at), pick(high, at)], axis=1) for at in range(3)
        )
        gain_ffn = gain_plain(enc_gain_ffn, (enc_ff_in, grad_ff_in))
        gain_attn = gain_plain(
            enc_gain_attn, (enc_query, grad_query), (enc_key, grad_key), (enc_value, grad_value)
        )
        turned = table_sum.T[:bucket_count]
        grad_rel_table = jnp.concatenate([turned[:, : heads // 2], turned[:, 8 : 8 + heads // 2]], axis=1)

        def stacked(own, got):
            return jnp.where(me == 0, jnp.stack([own, got]), jnp.stack([got, own]))

        out_keep = lax.dynamic_slice_in_dim(result_low, me * seq_dev, seq_dev, 0)
        encoder_output, grad_in = stacked(out_keep, out_got), stacked(grad_keep, grad_got)
        dec_out = stacked(dec_rows[0], dec_got[0]).astype(bf16)
        grad_dec = stacked(dec_rows[1], dec_got[1])

    return (
        encoder_output,
        dec_out,
        grad_in,
        grad_dec,
        gain_attn,
        grad_query,
        grad_key,
        grad_value,
        grad_output,
        grad_rel_table,
        gain_ffn,
        grad_ff_in,
        grad_ff_out,
        gain_final,
        gain_self,
        grad_self_value,
        grad_self_output,
        gain_cross,
        grad_cross_query,
        grad_cross_key,
        grad_cross_value,
        grad_cross_output,
        gain_dec_ffn,
        grad_dec_ff_in,
        grad_dec_ff_out,
    )


def solution(mesh):
    split = P("batch", "blk", None)
    rows = P("batch", None)
    line = P("batch")
    placed = (split, rows, line, split, rows) + (P(),) * 21
    return jax.shard_map(
        body,
        mesh=mesh,
        in_specs=placed,
        out_specs=(
            (split, rows, split, rows, line, rows, rows, rows, rows, P(), line, rows, rows, line)
            + (line, rows, rows, line, rows, rows, rows, rows, line, rows, rows)
        ),
        check_vma=False,
    )
```

```python
import functools

import jax
import jax.numpy as jnp
from jax import lax
from jax.experimental import pallas as pl
from jax.experimental.pallas import tpu as pltpu
from jax.sharding import PartitionSpec as P

epsilon = 1e-06
masked_score = -1e30
thresholds = (12, 16, 23, 32, 46, 64, 91)
bf16 = jnp.bfloat16
f32 = jnp.float32
tile = 128
chunk = 32
mib = 1 << 20
large = 5 * 10**9


def bucket_of(offset):
    distance = jnp.abs(offset)
    larger = jnp.full(offset.shape, 8, jnp.int32)
    for limit in thresholds:
        larger = larger + jnp.where(distance >= limit, 1, 0)
    inner = jnp.where(distance < 8, distance, larger)
    return jnp.where(offset > 0, 16, 0) + inner


def norm_scale(values):
    return lax.rsqrt(jnp.mean(values * values, axis=-1, keepdims=True) + epsilon)


def norm_apply(values, gain):
    return values * norm_scale(values) * gain


def norm_back(values, gain, upstream):
    scale = norm_scale(values)
    weighted = upstream * gain
    inner = jnp.mean(weighted * values, axis=-1, keepdims=True)
    return scale * weighted - values * (scale * scale * scale * inner)


def gelu_parts(a):
    root = 0.7978845608028654
    square = a * a
    t = jnp.tanh(root * a * (1.0 + 0.044715 * square))
    half = 0.5 + 0.5 * t
    slope = half + (half * (1.0 - t)) * (a * (root + (3 * 0.044715 * root) * square))
    return a * half, slope


def dot(left, right, dims=((1,), (0,))):
    return lax.dot_general(left, right, (dims, ((), ())), preferred_element_type=f32)


def dot_t(left, right):
    return dot(left, right, ((1,), (1,)))


def t_dot(left, right):
    return dot(left, right, ((0,), (0,)))


def shape(dims, kind):
    return jax.ShapeDtypeStruct(dims, kind)


def whole(array, buffers=None):
    zeros = (0,) * array.ndim
    if buffers is None:
        return pl.BlockSpec(array.shape, lambda *at: zeros)
    return pl.BlockSpec(array.shape, lambda *at: zeros, pipeline_mode=pl.Buffered(buffers))


class Chain:
    def __init__(self):
        self.last = ()

    def run(
        self, kernel, name, grid, args, in_specs, outs, out_specs, scalars=(), scratch=(),
        flops=0, limit=64, also=(),
    ):
        size = sum(a.size * a.dtype.itemsize for a in list(args) + list(outs))
        last = self.last + also
        skip = len(scalars) + len(args)

        def inner(*refs):
            kernel(*refs[:skip], *refs[skip + len(last) :])

        done = pl.pallas_call(
            inner,
            out_shape=outs,
            grid_spec=pltpu.PrefetchScalarGridSpec(
                num_scalar_prefetch=len(scalars),
                grid=grid,
                in_specs=list(in_specs) + [pl.BlockSpec(memory_space=pl.ANY)] * len(last),
                out_specs=out_specs,
                scratch_shapes=scratch,
            ),
            compiler_params=pltpu.CompilerParams(
                vmem_limit_bytes=limit * mib, dimension_semantics=("arbitrary",) * len(grid)
            ),
            cost_estimate=pl.CostEstimate(
                flops=int(4 * flops), bytes_accessed=int(size), transcendentals=0
            ),
            name=name,
        )(*scalars, *args, *last)
        self.last = (done[0],)
        return done


any_space = pl.BlockSpec(memory_space=pl.ANY)
dma = pltpu.SemaphoreType.DMA


def row_of(gain_ref):
    return gain_ref[...].reshape(1, -1)


def fetch(pairs, sems, first=None):
    copies = [
        pltpu.make_async_copy(source, target, sems.at[at])
        for at, (source, target) in enumerate(pairs)
    ]
    for copy in copies[:first]:
        copy.start()
    return copies


def picked(me, ref):
    rows = ref[...].astype(f32)
    return jnp.where(me == 0, rows[0:1], rows[1:2])


def joined(me, own, got):
    first = jnp.where(me == 0, own, got)
    last = jnp.where(me == 0, got, own)
    return jnp.concatenate([first, last], axis=0)


def wide_row(row):
    return jnp.broadcast_to(row.astype(bf16), (16, row.shape[1]))


def row_dot(row, weight):
    return dot(wide_row(row), weight)[0:1]


def row_dot_t(row, weight):
    return dot_t(wide_row(row), weight)[0:1]


def head_mask(width, head_dim):
    rows = lax.broadcasted_iota(jnp.int32, (16, width), 0)
    lanes = lax.broadcasted_iota(jnp.int32, (16, width), 1)
    return (lanes >= rows * head_dim) & (lanes < (rows + 1) * head_dim)


def spread(row, mask):
    return jnp.where(mask, jnp.broadcast_to(row, mask.shape), 0.0).astype(bf16)


def encoder_kernel(
    info, lens, gain_ref, table_ref, ffn_ref, final_ref,
    kq_ref, state_ref, cot_ref, dec_gain_ref,
    own_any, got_any, wq_any, wk_any, wv_any, wo_any, win_any, wout_any,
    cot_own_any, cot_got_any, dec_wv_any, dec_wco_any, dec_win_any, dec_wout_any,
    low_ref, away_ref, scale_ref, ge_ref, geaway_ref, rows_ref, long_ref, keymix_ref, mix_ref,
    n1_any, qt_any, k_any, v_any, e_any, ctx_any, y1_any, n2_any, hid_any, slope_any,
    x_ref, n1_ref, qt_ref, k_ref, v_ref, e_ref, ctx_ref, y1_ref, n2_ref, hid_ref, slope_ref,
    acc_ref, bias_ref, s_ref, wq_ref, wk_ref, wv_ref, wo_ref, win_ref, wout_ref, cot_x_ref,
    dec_wv, dec_wco, dec_win, dec_wout, sems, out_sems, x_sems, dec_sems, up_sems,
    *, heads, group,
):
    me = info[0]
    seq, width = x_ref.shape
    head_dim = width // heads
    blocks = seq // tile
    parts = win_ref.shape[0]
    wide = group * head_dim
    rounds = heads // group

    loads = []
    for at in range(rounds):
        spot = pl.ds(at * wide, wide)
        for any_ref, ref in ((wq_any, wq_ref), (wk_any, wk_ref), (wv_any, wv_ref)):
            loads.append((any_ref.at[:, spot], ref.at[at]))
    loads.append((wo_any, wo_ref))
    for at in range(parts):
        spot = pl.ds(at * width, width)
        loads.append((win_any.at[:, spot], win_ref.at[at]))
        loads.append((wout_any.at[spot, :], wout_ref.at[at]))
    loads = [
        pltpu.make_async_copy(source, target, sems.at[at])
        for at, (source, target) in enumerate(loads)
    ]
    first = fetch(
        ((own_any.at[me], x_ref.at[pl.ds(me * (seq // 2), seq // 2), :]),
         (got_any.at[me], x_ref.at[pl.ds((1 - me) * (seq // 2), seq // 2), :])), x_sems
    )
    for copy in loads[: 3 * rounds]:
        copy.start()
    saved = []

    def save(source, target):
        copy = pltpu.make_async_copy(source, target, out_sems.at[len(saved)])
        copy.start()
        saved.append(copy)

    tables = jnp.concatenate(
        [table_ref[...], jnp.zeros((heads, tile - table_ref.shape[1]), f32)], axis=1
    )
    rows = lax.broadcasted_iota(jnp.int32, (tile, tile), 0)
    lanes = lax.broadcasted_iota(jnp.int32, (tile, tile), 1)
    kinds = [bucket_of((gap - 1) * tile + rows - lanes) for gap in range(3)]
    for head in range(heads):
        line = jnp.broadcast_to(tables[head : head + 1, :], (tile, tile))
        for gap in range(3):
            bias_ref[head, gap] = jnp.take_along_axis(line, kinds[gap], axis=1)

    for copy in first:
        copy.wait()
    n1_ref[...] = norm_apply(x_ref[...].astype(f32), row_of(gain_ref)).astype(bf16)
    save(n1_ref, n1_any)

    pair_rows = lax.broadcasted_iota(jnp.int32, (2 * head_dim, seq), 0)
    pair_lanes = lax.broadcasted_iota(jnp.int32, (seq, 2 * head_dim), 1)
    key_at = lax.broadcasted_iota(jnp.int32, (seq, 2 * head_dim), 0)
    gone = jnp.where(key_at < lens[me], 0.0, masked_score).astype(bf16)
    ones = jnp.ones((16, seq), bf16)
    vts = {}

    def project(at):
        n1 = n1_ref[...]
        for copy in loads[3 * at : 3 * at + 3]:
            copy.wait()
        for copy in loads[3 * rounds + 3 * at : 3 * rounds + 3 * at + 3]:
            copy.start()
        spot = slice(at * wide, (at + 1) * wide)
        qt_ref[spot, :] = dot(n1, wq_ref[at]).T.astype(bf16)
        k_ref[:, spot] = dot(n1, wk_ref[at]).astype(bf16)
        v = dot(n1, wv_ref[at])
        v_ref[:, spot] = v.astype(bf16)
        vts[at] = v.T.astype(bf16)

    def scores(head):
        pair = slice(head // 2 * 2 * head_dim, (head // 2 + 1) * 2 * head_dim)
        k2, q2 = k_ref[:, pair], qt_ref[pair, :]
        zero = jnp.zeros((), bf16)
        if head % 2 == 0:
            k2 = jnp.where(pair_lanes < head_dim, k2, jnp.where(pair_lanes == head_dim, gone, zero))
            q2 = jnp.where(pair_rows < head_dim, q2, jnp.ones((), bf16))
        else:
            k2 = jnp.where(pair_lanes >= head_dim, k2, jnp.where(pair_lanes == 0, gone, zero))
            q2 = jnp.where(pair_rows >= head_dim, q2, jnp.ones((), bf16))
        middle = seq // 2
        s_ref[head % 2, :, :middle] = dot(k2, q2[:, :middle])
        yield
        s_ref[head % 2, :, middle:] = dot(k2, q2[:, middle:])
        yield

    def weigh(head):
        slot = head % 2
        before = tables[head : head + 1, 15:16]
        after = tables[head : head + 1, 31:32]
        for query in range(blocks):
            yield
            across = slice(query * tile, (query + 1) * tile)
            tops = None
            for key in range(blocks):
                gap = key - query
                bias = before if gap < -1 else after if gap > 1 else bias_ref[head, gap + 1]
                down = slice(key * tile, (key + 1) * tile)
                value = s_ref[slot, down, across] + bias
                s_ref[slot, down, across] = value
                top = jnp.max(value.reshape(tile // 8, 8, tile), axis=0)
                tops = top if tops is None else jnp.maximum(tops, top)
            peak = jnp.max(tops, axis=0, keepdims=True)
            for key in range(blocks):
                down = slice(key * tile, (key + 1) * tile)
                e_ref[head, down, across] = jnp.exp(s_ref[slot, down, across] - peak).astype(bf16)
        save(e_ref.at[head], e_any.at[head])

    def mix(head):
        at, inner = divmod(head, group)
        vt = vts[at][inner * head_dim : (inner + 1) * head_dim]
        full = dot(jnp.concatenate([vt, ones], axis=0), e_ref[head])
        scale = 1.0 / full[head_dim : head_dim + 1]
        scale_ref[head : head + 1, :] = scale
        ctx_ref[head * head_dim : (head + 1) * head_dim, :] = (full[:head_dim] * scale).astype(bf16)

    project(0)
    wide_loads = fetch(
        tuple((dec_wout_any.at[pl.ds(at * width, width), :], dec_wout.at[at]) for at in range(parts)),
        up_sems,
    )
    cot = picked(me, cot_ref)
    ups = []
    for _ in scores(0):
        pass
    for head in range(heads):
        if head % group == 0 and head // group + 1 < rounds:
            project(head // group + 1)
        ahead = scores(head + 1) if head + 1 < heads else iter(())
        for step, _ in enumerate(weigh(head)):
            if step == 1 and head:
                mix(head - 1)
            elif step > 1:
                next(ahead, None)
        for _ in ahead:
            pass
        if head % 2 and len(ups) < parts:
            wide_loads[len(ups)].wait()
            ups.append(row_dot_t(cot, dec_wout[len(ups)]))
    mix(heads - 1)
    scale_ref[heads:, :] = jnp.zeros((16 - heads, seq), f32)
    save(qt_ref, qt_any)
    save(k_ref, k_any)
    save(v_ref, v_any)
    save(ctx_ref, ctx_any)

    loads[3 * rounds].wait()
    y1 = x_ref[...].astype(f32) + t_dot(ctx_ref[...], wo_ref[...])
    acc_ref[...] = y1
    y1_ref[...] = y1.astype(bf16)
    n2_ref[...] = norm_apply(y1, row_of(ffn_ref)).astype(bf16)
    save(y1_ref, y1_any)
    save(n2_ref, n2_any)
    for at in range(parts):
        spot = pl.ds(at * width, width)
        loads[3 * rounds + 1 + 2 * at].wait()
        if at == 1:
            late = fetch(
                (
                    (dec_wv_any, dec_wv), (dec_wco_any, dec_wco), (dec_win_any, dec_win),
                    (cot_own_any.at[me], cot_x_ref.at[pl.ds(me * (seq // 2), seq // 2), :]),
                    (cot_got_any.at[me], cot_x_ref.at[pl.ds((1 - me) * (seq // 2), seq // 2), :]),
                ),
                dec_sems,
            )
        value, slope = gelu_parts(dot(n2_ref[...], win_ref[at]))
        hid_ref[at] = value.astype(bf16)
        slope_ref[at] = slope.astype(bf16)
        save(hid_ref.at[at], hid_any.at[:, spot])
        save(slope_ref.at[at], slope_any.at[:, spot])
        loads[3 * rounds + 2 + 2 * at].wait()
        acc_ref[...] += dot(hid_ref[at], wout_ref[at])
    result = acc_ref[...]
    low = result.astype(bf16)
    low_ref[...] = low
    half = seq // 2
    away_ref[...] = jnp.where(me == 0, low[half:], low[:half])
    src = norm_apply(result, row_of(final_ref)).astype(bf16)

    gain = row_of(dec_gain_ref)
    mask = head_mask(width, head_dim)
    lanes = lax.broadcasted_iota(jnp.int32, (16, seq), 1)
    c = jnp.where(lanes < lens[me], dot_t(kq_ref[...], src), masked_score)
    c = jnp.exp(c - jnp.max(c, axis=-1, keepdims=True))
    c = c * (1.0 / jnp.sum(c, axis=-1, keepdims=True))
    c_low = c.astype(bf16)
    mixed = dot(c_low, src).astype(bf16)
    mix_ref[...] = mixed
    late[0].wait()
    cctx = jnp.sum(jnp.where(mask, dot(mixed, dec_wv[...]), 0.0), axis=0, keepdims=True)
    cctx = cctx.astype(bf16).astype(f32)
    late[1].wait()
    z2 = state_ref[3:4, :] + row_dot(cctx, dec_wco[...])
    m3 = norm_apply(z2, gain).astype(bf16).astype(f32)
    late[2].wait()
    dh, slope = gelu_parts(row_dot(m3, dec_win[...]))
    g_b = (slope * jnp.concatenate(ups, axis=1)).astype(bf16).astype(f32)
    gz2 = cot + norm_back(z2, gain, row_dot_t(g_b, dec_win[...]))
    g_cctx = row_dot_t(gz2, dec_wco[...]).astype(bf16).astype(f32)
    up = dot_t(spread(g_cctx, mask), dec_wv[...]).astype(bf16)
    d_c = dot_t(up, src)
    g_c = (c * (d_c - jnp.sum(c * d_c, axis=-1, keepdims=True))).astype(bf16)
    src_up = t_dot(
        jnp.concatenate([g_c, c_low], axis=0), jnp.concatenate([kq_ref[...], up], axis=0)
    )
    late[3].wait()
    late[4].wait()
    back = norm_back(acc_ref[...], row_of(final_ref), src_up)
    ge = (cot_x_ref[...].astype(f32) + back).astype(bf16)
    ge_ref[...] = ge
    middle = width // 2
    geaway_ref[...] = jnp.where(me == 0, ge[:, middle:], ge[:, :middle])
    keymix_ref[...] = dot(g_c, src).astype(bf16)
    for at, row in enumerate((cctx, z2, m3, gz2, g_cctx, cot)):
        rows_ref[at : at + 1, :] = row
    rows_ref[6:8, :] = jnp.zeros((2, width), f32)
    long_ref[0:1, :] = dh
    long_ref[1:2, :] = g_b
    for copy in saved:
        copy.wait()


def encoder(
    chain, info, lens, enc_in, got, gain, wq, wk, wv, table, ffn, final, wo, win, wout, heads,
    cot_enc, cot_got, decoder, dec_weights,
):
    pairs, seq_dev, width = enc_in.shape
    seq = 2 * seq_dev
    hidden = win.shape[1]
    group = 4
    rounds = heads // group
    wide = width // rounds
    parts = hidden // width
    act, turned = shape((seq, width), bf16), shape((width, seq), bf16)
    part, tall = shape((seq_dev, width), bf16), shape((seq, hidden), bf16)
    few, hat = shape((16, width), bf16), shape((seq, width // 2), bf16)
    near = (act, part, shape((16, seq), f32), act, hat)
    near += (shape((8, width), f32), shape((2, hidden), f32), few, few)
    far = (act, turned, act, act, shape((heads, seq, seq), bf16), turned, act, act, tall, tall)
    small = (gain, table, ffn, final) + decoder

    def vmem(dims, kind=bf16):
        return pltpu.VMEM(dims, kind)

    return chain.run(
        functools.partial(encoder_kernel, heads=heads, group=group),
        "encoder_forward",
        (1,),
        small + (enc_in, got, wq, wk, wv, wo, win, wout, cot_enc, cot_got) + dec_weights,
        [whole(a) for a in small] + [any_space] * 14,
        near + far,
        tuple(whole(a) for a in near) + (any_space,) * len(far),
        scalars=(info, lens),
        scratch=(
            vmem((seq, width)), vmem((seq, width)), vmem((width, seq)), vmem((seq, width)),
            vmem((seq, width)), vmem((heads, seq, seq)), vmem((width, seq)), vmem((seq, width)),
            vmem((seq, width)), vmem((parts, seq, width)), vmem((parts, seq, width)),
            vmem((seq, width), f32), vmem((heads, 3, tile, tile), f32), vmem((2, seq, seq), f32),
            vmem((rounds, width, wide)), vmem((rounds, width, wide)), vmem((rounds, width, wide)),
            vmem((width, width)), vmem((parts, width, width)), vmem((parts, width, width)),
            vmem((seq, width)),
        )
        + tuple(vmem(w.shape) for w in dec_weights[:3])
        + (
            vmem((parts, width, width)),
            dma((3 * rounds + 1 + 2 * parts,)), dma((7 + heads + 2 * parts,)), dma((2,)), dma((5,)), dma((parts,)),
        ),
        flops=2 * seq * width * (4 * width + 2 * hidden) + 16 * seq * seq * width,
    )


def before_kernel(
    info, dec_ref, self_ref, cross_ref, wsv_any, wso_any, wcq_any, wk_any,
    state_ref, kq_ref, wsv, wso, wcq, wk, sems, *, head_dim,
):
    copies = fetch(((wsv_any, wsv), (wso_any, wso), (wcq_any, wcq), (wk_any, wk)), sems)
    x = picked(info[0], dec_ref)
    m1 = norm_apply(x, row_of(self_ref)).astype(bf16).astype(f32)
    copies[0].wait()
    sv = row_dot(m1, wsv[...]).astype(bf16).astype(f32)
    copies[1].wait()
    z1 = x + row_dot(sv, wso[...])
    m2 = norm_apply(z1, row_of(cross_ref)).astype(bf16).astype(f32)
    copies[2].wait()
    cq = row_dot(m2, wcq[...]).astype(bf16).astype(f32)
    copies[3].wait()
    kq_ref[...] = dot_t(spread(cq, head_mask(x.shape[1], head_dim)), wk[...]).astype(bf16)
    for at, row in enumerate((x, m1, sv, z1, m2, cq)):
        state_ref[at : at + 1, :] = row
    state_ref[6:8, :] = jnp.zeros((2, x.shape[1]), f32)


def before(chain, info, dec, gain_self, gain_cross, wsv, wso, wcq, wk, head_dim):
    width = dec.shape[1]
    weights = (wsv, wso, wcq, wk)
    small = (dec, gain_self, gain_cross)
    outs = (shape((8, width), f32), shape((16, width), bf16))
    return chain.run(
        functools.partial(before_kernel, head_dim=head_dim), "decoder_before", (1,),
        small + weights, [whole(a) for a in small] + [any_space] * 4, outs,
        tuple(whole(a) for a in outs), scalars=(info,),
        scratch=tuple(pltpu.VMEM(w.shape, bf16) for w in weights) + (dma((4,)),),
        flops=64 * wk.size,
    )


def after_kernel(
    info, keymix_ref, state_ref, rows_ref, long_ref, mix_ref, self_ref, cross_ref,
    wk_any, wcq_any, wso_any, wsv_any, wout_any, both_ref, *refs, head_dim, heads, slots,
):
    packs = 3 if slots else 1
    wk, wcq, wso, wsv, wout, pad_ref, sems = refs[packs : packs + 7]
    refs = refs[:packs] + refs[packs + 7 :]
    width = state_ref.shape[1]
    pieces = [pl.ds(at, width) for at in range(0, wout.shape[0], width)]
    copies = fetch(
        ((wk_any, wk), (wcq_any, wcq), (wso_any, wso), (wsv_any, wsv))
        + tuple((wout_any.at[piece, :], wout.at[piece, :]) for piece in pieces),
        sems,
        4,
    )
    x, z1 = state_ref[0:1, :], state_ref[3:4, :]
    z2, gz2 = rows_ref[1:2, :], rows_ref[3:4, :]
    dh, g_b = long_ref[0:1, :], long_ref[1:2, :]
    width = x.shape[1]
    mask = head_mask(width, head_dim)
    mix = keymix_ref[...]
    copies[0].wait()
    for copy in copies[4:]:
        copy.start()
    g_cq = jnp.sum(jnp.where(mask, dot(mix, wk[...]), 0.0), axis=0, keepdims=True)
    g_cq = g_cq.astype(bf16).astype(f32)
    copies[1].wait()
    gz1 = gz2 + norm_back(z1, row_of(cross_ref), row_dot_t(g_cq, wcq[...]))
    count = dh.shape[1] // width
    g_bs = [g_b[:, at * width : (at + 1) * width] for at in range(count)]
    dhs = [dh[:, at * width : (at + 1) * width] for at in range(count)]
    right = [gz1, g_cq, gz2, rows_ref[4:5, :]] + g_bs
    left = [state_ref[1:2, :], state_ref[2:3, :], state_ref[4:5, :], rows_ref[0:1, :], rows_ref[2:3, :]]
    pad_ref[...] = jnp.zeros(pad_ref.shape, f32)
    for first, group in ((0, right), (16, left), (48, dhs)):
        for at, row in enumerate(group):
            pad_ref[first + at : first + at + 1, :] = row
    pad_ref[24 : 24 + heads, :] = mix[:heads].astype(f32)
    pad_ref[24 + heads : 24 + 2 * heads, :] = mix_ref[:heads].astype(f32)
    if not slots:
        pad_ref[8:9, :] = state_ref[5:6, :]
        pad_ref[9:10, :] = rows_ref[5:6, :]
        refs[0][...] = pad_ref[...].astype(bf16)
    else:
        send_factors(info, pad_ref, state_ref[5:6, :], rows_ref[5:6, :], refs, slots, width, count * width)
    copies[2].wait()
    g_sv = row_dot_t(gz1, wso[...]).astype(bf16).astype(f32)
    copies[3].wait()
    both_ref[1:2, :] = gz1 + norm_back(x, row_of(self_ref), row_dot_t(g_sv, wsv[...]))
    total = z2
    for at, piece in enumerate(pieces):
        copies[4 + at].wait()
        total = total + row_dot(dhs[at], wout[piece, :])
    both_ref[0:1, :] = total


def send_factors(info, pad_ref, query, cot, refs, slots, width, hidden):
    send_ref, keep_ref, right_ref, held_ref = refs
    half = width // 2
    both = jnp.concatenate([pad_ref[:8, :half], pad_ref[:8, half:]], axis=0).astype(bf16)
    right_ref[...] = both
    stages = slots.bit_length() - 1
    rows, tall = width // slots, hidden // slots
    per = width // tall
    many = pad_ref[16:48, :]
    two = lax.broadcasted_iota(jnp.int32, (16, tile), 0)
    count = width // tile
    fixed = jnp.zeros((16, tile), f32)
    for first, row in ((2, query), (2 + count, cot)):
        for at in range(count):
            fixed = jnp.where(two == first + at, row[:, at * tile : (at + 1) * tile], fixed)
    for slot in range(slots):
        mine = pltpu.roll(many, (width - slot * rows) % width, 1)[:, :tile]
        hid = pad_ref[48 + slot // per : 49 + slot // per, :]
        hid = pltpu.roll(hid, (width - slot % per * tall) % width, 1)
        hid = jnp.where(two == 0, hid[:, :tile], jnp.where(two == 1, hid[:, tile : 2 * tile], fixed))
        spot = spot_in(info[0], info[1] ^ slot, stages)
        held_ref[pl.ds(pl.multiple_of(spot * 16, 16), 16), :] = jnp.concatenate(
            [mine[:16], mine[16:], hid], axis=1
        ).astype(bf16)
    middle = slots // 2 * 16
    keep_ref[...] = held_ref[:middle, :]
    send_ref[:middle, :] = held_ref[middle:, :]
    send_ref[middle:, :] = both


def after(
    chain, info, key_mix, state, rows, long, mix, gain_self, gain_cross, weights, head_dim, heads, slots
):
    width = key_mix.shape[1]
    small = (key_mix, state, rows, long, mix, gain_self, gain_cross)
    half = slots // 2 * 16
    if slots:
        outs = tuple(shape((lines, width // 2), bf16) for lines in (half + 16, half, 16))
    else:
        outs = (shape((64, width), bf16),)
    outs = (shape((2, width), f32),) + outs
    return chain.run(
        functools.partial(after_kernel, head_dim=head_dim, heads=heads, slots=slots),
        "decoder_after", (1,),
        small + weights, [whole(a) for a in small] + [any_space] * 5, outs,
        tuple(whole(a) for a in outs), scalars=(info,),
        scratch=tuple(pltpu.VMEM(w.shape, bf16) for w in weights)
        + (pltpu.VMEM((64, width), f32), dma((4 + long.shape[1] // width,)))
        + ((pltpu.VMEM((2 * half, width // 2), bf16),) if slots else ()),
        flops=32 * weights[4].size,
    )


def backward_kernel(
    info, gain_ref, low_any, slope_any, wout_any, win_any, y1_any, wo_any,
    *refs,
):
    (low_ref, slope_ref, wout_ref, win_ref, y1_ref, wo_ref, ga_ref, gylow_ref, acc_ref) = refs[-11:-2]
    sems, out_sems = refs[-2:]
    me = info[0]
    parts, seq, width = slope_ref.shape
    part = parts // 2
    away_anys, (keep_any, gylow_any, gyaway_ref, gctx_ref) = refs[:part], refs[part : part + 4]
    chunks = [(1 - me) * part + at for at in range(part)] + [me * part + at for at in range(part)]
    loads = [(low_any, low_ref)]
    for at, chunk_at in enumerate(chunks):
        spot = pl.ds(pl.multiple_of(chunk_at * width, width), width)
        loads.append((wout_any.at[spot, :], wout_ref.at[at]))
        loads.append((slope_any.at[:, spot], slope_ref.at[at]))
        loads.append((win_any.at[:, spot], win_ref.at[at]))
    loads += [(y1_any, y1_ref), (wo_any, wo_ref)]
    loads = fetch(loads, sems, 7)
    saved = []
    loads[0].wait()
    for at in range(parts):
        for copy in loads[7 + 3 * at : 10 + 3 * at]:
            copy.start()
        loads[1 + 3 * at].wait()
        rise = dot_t(low_ref[...], wout_ref[at])
        loads[2 + 3 * at].wait()
        ga_ref[at] = (slope_ref[at].astype(f32) * rise).astype(bf16)
        if at < part:
            target = away_anys[at]
        else:
            target = keep_any.at[:, pl.ds(at % part * width, width)]
        copy = pltpu.make_async_copy(ga_ref.at[at], target, out_sems.at[at])
        copy.start()
        saved.append(copy)
        loads[3 + 3 * at].wait()
        if at == 0:
            acc_ref[...] = dot_t(ga_ref[at], win_ref[at])
        else:
            acc_ref[...] += dot_t(ga_ref[at], win_ref[at])
    loads[-2].wait()
    y1 = y1_ref[...].astype(f32)
    low = (low_ref[...].astype(f32) + norm_back(y1, row_of(gain_ref), acc_ref[...])).astype(bf16)
    gylow_ref[...] = low
    copy = pltpu.make_async_copy(gylow_ref, gylow_any, out_sems.at[parts])
    copy.start()
    saved.append(copy)
    half = width // 2
    gyaway_ref[...] = jnp.where(me == 0, low[:, half:], low[:, :half])
    loads[-1].wait()
    gctx_ref[...] = dot_t(wo_ref[...], low).astype(bf16)
    for copy in saved:
        copy.wait()


def backward(chain, info, low, slope, wout, win, y1, gain, wo):
    seq, width = low.shape
    hidden = win.shape[1]
    parts = hidden // width
    act, tall = shape((seq, width), bf16), shape((seq, hidden // 2), bf16)
    side, turned = shape((seq, width // 2), bf16), shape((width, seq), bf16)

    def vmem(*dims):
        return pltpu.VMEM(dims, bf16)

    return chain.run(
        backward_kernel,
        "feed_forward_back",
        (1,),
        (gain, low, slope, wout, win, y1, wo),
        [whole(gain)] + [any_space] * 6,
        (act,) * (parts // 2) + (tall, act, side, turned),
        (any_space,) * (parts // 2) + (any_space, any_space, whole(side), whole(turned)),
        scalars=(info,),
        scratch=(
            vmem(seq, width), vmem(parts, seq, width), vmem(parts, width, width),
            vmem(parts, width, width), vmem(seq, width), vmem(width, width),
            vmem(parts, seq, width), vmem(seq, width), pltpu.VMEM((seq, width), f32),
            dma((3 + 3 * parts,)), dma((parts + 1,)),
        ),
        flops=2 * seq * width * (width + 2 * hidden),
    )


def attention_back_kernel(
    info, scale_ref, gain_ref, own_ref, got_ref, qt_any, k_any, v_any, ctx_any, gctx_any, e_any,
    wq_any, wk_any, wv_any, gy_any,
    gq_ref, gk_ref, gv_ref, keep_ref, gradkeep_ref, gradaway_ref, table_ref,
    qt_ref, k_ref, v_ref, ctx_ref, gctx_ref, e_ref, wq_ref, wk_ref, wv_ref, gy_ref,
    rise_ref, gs_ref, sums_ref, all_ref, sems, *, heads,
):
    me = info[0]
    seq, width = k_ref.shape
    head_dim = width // heads
    blocks = seq // tile
    half = width // 2
    side = heads // 2
    pair = 2 * head_dim
    loads = fetch(
        ((k_any, k_ref), (v_any, v_ref), (qt_any, qt_ref), (gctx_any, gctx_ref), (ctx_any, ctx_ref))
        + tuple(
            (e_any.at[(1 - me) * side + at if at < side else me * side + at - side], e_ref.at[at])
            for at in range(heads)
        )
        + ((wq_any, wq_ref), (wk_any, wk_ref), (wv_any, wv_ref), (gy_any, gy_ref)),
        sems,
        11,
    )
    for copy in loads[:5]:
        copy.wait()
    pair_lanes = lax.broadcasted_iota(jnp.int32, (seq, pair), 1)
    ones = [
        jnp.where((pair_lanes == start) | (pair_lanes == start + 1), 1.0, 0.0).astype(bf16)
        for start in (head_dim, 0)
    ]
    low_half = pair_lanes < head_dim
    none = jnp.zeros((head_dim - 16, seq), bf16)
    line_rows = lax.broadcasted_iota(jnp.int32, (16, seq), 0)
    sums_ref[...] = jnp.zeros(sums_ref.shape, f32)

    def first_of(at):
        base = (1 - me if at < side else me) * half
        return pl.multiple_of(base + at % side // 2 * pair, pair)

    def prepare(at):
        rows = pl.ds(first_of(at), pair)
        g2 = gctx_ref[rows, :].astype(f32)
        head = lax.div(first_of(at), head_dim)
        g2 = jnp.concatenate(
            [
                g2[:head_dim] * scale_ref[pl.ds(head, 1), :],
                g2[head_dim:] * scale_ref[pl.ds(head + 1, 1), :],
            ],
            axis=0,
        )
        both = g2 * ctx_ref[rows, :].astype(f32)
        g2 = g2.astype(bf16)
        g_ext = []
        for inner in range(2):
            here = slice(inner * head_dim, (inner + 1) * head_dim)
            delta = -jnp.sum(both[here], axis=0, keepdims=True)
            high = delta.astype(bf16).astype(f32)
            extra = jnp.where(line_rows == 0, high, jnp.where(line_rows == 1, delta - high, 0.0))
            extra = extra.astype(bf16)
            if inner == 0:
                g_ext.append(jnp.concatenate([g2[here], extra, none], axis=0))
            else:
                g_ext.append(jnp.concatenate([extra, none, g2[here]], axis=0))
        return g2, g_ext

    pairs = {}

    def rise(at):
        upper = at % 2
        if not upper:
            pairs[at // 2] = prepare(at)
        v2 = v_ref[:, pl.ds(first_of(at), pair)]
        v_ext = jnp.where(low_half, ones[1], v2) if upper else jnp.where(low_half, v2, ones[0])
        rise_ref[upper] = dot(v_ext, pairs[at // 2][1][upper])

    def spread_scores(at):
        slot = at % 2
        near, outer = [], [None, None]
        for sub in range(tile // chunk):
            sums = [None] * 5
            for key in range(blocks):
                start = key * tile + sub * chunk
                down = slice(start, start + chunk)
                for query in range(blocks):
                    across = slice(query * tile, (query + 1) * tile)
                    g = e_ref[at, down, across].astype(f32) * rise_ref[slot, down, across]
                    gs_ref[slot, down, across] = g.astype(bf16)
                    kind = min(max(query - key, -2), 2) + 2
                    sums[kind] = g if sums[kind] is None else sums[kind] + g
            near.append(jnp.concatenate(sums[1:4] + [jnp.zeros((chunk, tile), f32)], axis=1))
            outer = [a if b is None else a + b for a, b in zip((sums[4], sums[0]), outer)]
            yield
        folded = jnp.concatenate(near, axis=0)
        lanes = 4 * tile
        while folded.shape[0] > 8:
            rest = folded.shape[0] // 2
            folded = folded[:rest] + pltpu.roll(folded[rest:], lanes - rest, 1)
        rows = lax.broadcasted_iota(jnp.int32, folded.shape, 0)
        for bit in (4, 2, 1):
            moved = pltpu.roll(folded, lanes - bit, 1)
            folded = jnp.where((rows & bit) != 0, moved, folded)
        line = jnp.sum(folded, axis=0, keepdims=True)
        outer = [jnp.sum(part, axis=0, keepdims=True) for part in outer]
        row = (8 if at >= side else 0) + at % side
        sums_ref[row : row + 1, :] = jnp.concatenate([line] + outer, axis=1)

    parts = {}
    rise(0)
    turned = {}

    def close(at):
        if at < 0:
            yield from [None] * 4
            return
        first = first_of(at)
        upper = at % 2
        here = slice(upper * head_dim, (upper + 1) * head_dim)
        q_mine = qt_ref[pl.ds(pl.multiple_of(first + upper * head_dim, head_dim), head_dim), :]
        g_q = dot(turned[at // 2][here], gs_ref[upper])
        yield
        g_k = dot_t(q_mine, gs_ref[upper])
        yield
        g_v = dot_t(pairs[at // 2][0][here], e_ref[at])
        yield
        parts[upper] = (g_q, g_k, g_v)
        if upper:
            for which, gone_ref in enumerate((gq_ref, gk_ref, gv_ref)):
                both = jnp.concatenate([parts[0][which], parts[1][which]], axis=0).astype(bf16).T
                all_ref[which, :, pl.ds(first, pair)] = both
                start = at % side // 2 * pair
                if at < side:
                    gone_ref[:, start : start + pair] = both
                else:
                    keep_ref[:, which * half + start : which * half + start + pair] = both
        yield

    for at in range(heads + 1):
        last_head = close(at - 1)
        if at == heads:
            for _ in last_head:
                pass
            break
        for copy in loads[11 + at : 12 + at]:
            copy.start()
        if at % 2 == 0:
            turned[at // 2] = k_ref[:, pl.ds(first_of(at), pair)].T
        loads[5 + at].wait()
        for step, _ in enumerate(spread_scores(at)):
            next(last_head)
            if step == 1 and at + 1 < heads:
                rise(at + 1)
    for copy in loads[5 + heads :]:
        copy.wait()
    total = None
    for which, ref in enumerate((wq_ref, wk_ref, wv_ref)):
        part = dot_t(all_ref[which], ref[...])
        total = part if total is None else total + part
    x = joined(me, own_ref[0], got_ref[0]).astype(f32)
    grad = gy_ref[...].astype(f32) + norm_back(x, row_of(gain_ref), total)
    middle = seq // 2
    gradkeep_ref[...] = jnp.where(me == 0, grad[:middle], grad[middle:])
    gradaway_ref[...] = jnp.where(me == 0, grad[middle:], grad[:middle])
    sums = joined(me, sums_ref[8:], sums_ref[:8])
    spots = lax.broadcasted_iota(jnp.int32, (sums.shape[1], tile), 0)
    offsets = tile - jnp.where(spots < 3 * tile, spots, spots - 4 * tile)
    kinds = jnp.where(spots < 4 * tile, bucket_of(offsets), jnp.where(spots < 5 * tile, 15, 31))
    lanes = lax.broadcasted_iota(jnp.int32, kinds.shape, 1)
    one_hot = jnp.where(kinds == lanes, 1.0, 0.0).astype(f32)
    table = lax.dot_general(
        sums, one_hot, (((1,), (0,)), ((), ())), precision=lax.Precision.HIGHEST,
        preferred_element_type=f32,
    )
    table_ref[:, :tile] = table.astype(bf16)
    table_ref[:, tile:] = jnp.zeros((16, 2 * tile), bf16)


def attention_back(chain, info, scale, gain, enc_in, got, qt, k, v, ctx, gctx, e, wq, wk, wv, gy):
    seq, width = k.shape
    heads = e.shape[0]
    block = pl.BlockSpec((1, seq // 2, width), lambda i, info: (info[0], 0, 0))
    side, part = shape((seq, 3 * width // 2), bf16), shape((seq // 2, width), f32)
    narrow = shape((seq, width // 2), bf16)
    outs = (narrow, narrow, narrow, side, part, part, shape((16, 3 * tile), bf16))
    far = (qt, k, v, ctx, gctx, e, wq, wk, wv, gy)
    return chain.run(
        functools.partial(attention_back_kernel, heads=heads),
        "attention_back",
        (1,),
        (scale, gain, enc_in, got) + far,
        [whole(scale), whole(gain), block, block] + [any_space] * len(far),
        outs,
        tuple(whole(a) for a in outs),
        scalars=(info,),
        scratch=tuple(pltpu.VMEM(a.shape, bf16) for a in far)
        + (
            pltpu.VMEM((2, seq, seq), f32), pltpu.VMEM((2, seq, seq), bf16),
            pltpu.VMEM((16, 6 * tile), f32), pltpu.VMEM((3, seq, width), bf16), dma((9 + heads,)),
        ),
        flops=6 * seq * width * width + 16 * seq * seq * width,
    )


def spot_in(me, relative, stages):
    spot = 0
    for k in range(stages):
        bit = jnp.where(me == 0, k, 1 - k) if k < 2 <= stages else k
        spot = spot | (((relative >> bit) & 1) << (stages - 1 - k))
    return spot


def store(info, base, low, rows, held_ref, slots, line):
    stages = slots.bit_length() - 1
    span = held_ref.shape[0] // slots
    wide = held_ref.shape[1]
    for at in range(low.shape[0] // rows):
        spot = spot_in(info[0], info[1] ^ (base + at), stages)
        for piece in range(low.shape[1] // wide):
            start = pl.multiple_of(spot * span + line + piece * rows, 16)
            held_ref[pl.ds(start, rows), :] = low[
                at * rows : (at + 1) * rows, piece * wide : (piece + 1) * wide
            ]


def release(held_ref, keep_any, send_any, sems, extra=None):
    middle = held_ref.shape[0] // 2
    pairs = [
        (held_ref.at[pl.ds(middle, middle), :], send_any.at[pl.ds(0, middle), :]),
        (held_ref.at[pl.ds(0, middle), :], keep_any),
    ]
    if extra is not None:
        pairs.append((extra, send_any.at[pl.ds(middle, extra.shape[0]), :]))
    for copy in fetch(pairs, sems):
        copy.wait()


def tall_kernel(
    info, r0_any, r1_any, extra_any, l0_any, l1_any, keep_any, send_any,
    r0_ref, r1_ref, extra_ref, l0_ref, l1_ref, held_ref, sems, out_sems, *, rows, slots
):
    parts, seq, width = l0_ref.shape
    wide = r0_ref.shape[1]
    loads = [
        (r0_any.at[:, pl.ds(pl.multiple_of(info[0] * wide, wide), wide)], r0_ref), (r1_any, r1_ref)
    ]
    for at in range(parts):
        spot = pl.ds(at * width, width)
        loads += [(l0_any.at[:, spot], l0_ref.at[at]), (l1_any.at[:, spot], l1_ref.at[at])]
    loads.append((extra_any, extra_ref))
    loads = fetch(loads, sems, 6)
    loads[0].wait()
    loads[1].wait()
    for at in range(parts):
        loads[2 * at + 2].wait()
        loads[2 * at + 3].wait()
        for copy in loads[2 * at + 6 : 2 * at + 8 + at // (parts - 2)]:
            copy.start()
        low = (t_dot(l0_ref[at], r0_ref[...]) + t_dot(l1_ref[at], r1_ref[...])).astype(bf16)
        store(info, at * (width // rows), low, rows, held_ref, slots, 0)
    loads[-1].wait()
    release(held_ref, keep_any, send_any, out_sems, extra_ref)


def tall_grad(chain, info, slots, left, left_got, right, right_got, extra):
    seq, tall = left.shape
    wide = right_got.shape[1]
    rows = tall // slots
    parts = 4
    middle = slots // 2 * rows
    outs = (shape((middle, wide), bf16), shape((middle + extra.shape[0], wide), bf16))
    far = pltpu.VMEM((parts, seq, tall // parts), bf16)
    return chain.run(
        functools.partial(tall_kernel, rows=rows, slots=slots), "grad_ff_out", (1,),
        (right, right_got, extra, left, left_got),
        [any_space] * 5,
        outs, (any_space, any_space), scalars=(info,),
        scratch=(
            pltpu.VMEM(right_got.shape, bf16), pltpu.VMEM(right_got.shape, bf16),
            pltpu.VMEM(extra.shape, bf16), far, far, pltpu.VMEM((tall, wide), bf16),
            dma((2 * parts + 3,)), dma((3,)),
        ),
        flops=4 * seq * tall * wide,
    )


def mixed_kernel(
    info, n0_any, n1_any, a0_any, c0_any, c1_any, g0_any, g1_any, *refs, rows, slots
):
    steps = len(refs) - 13
    a1_anys, (keep_any, send_any) = refs[:steps], refs[steps : steps + 2]
    n0_ref, n1_ref, a0_ref, a1_ref, c0_ref, c1_ref, g0_ref, g1_ref, held_ref, sems, out_sems = refs[steps + 2 :]
    seq, width = n0_ref.shape
    wide = held_ref.shape[1]
    loads = fetch(
        (
            (n0_any, n0_ref), (a0_any, a0_ref), (n1_any, n1_ref),
            (c0_any, c0_ref), (c1_any, c1_ref),
            (g0_any.at[:, pl.ds(pl.multiple_of(info[0] * wide, wide), wide)], g0_ref),
            (g1_any, g1_ref),
        )
        + tuple((part, a1_ref.at[at]) for at, part in enumerate(a1_anys)),
        sems,
    )
    for copy in loads[:3]:
        copy.wait()
    for at in range(steps):
        spot = slice(at * width, (at + 1) * width)
        loads[7 + at].wait()
        low = t_dot(n0_ref[...], a0_ref[:, spot]) + t_dot(n1_ref[...], a1_ref[at])
        store(info, 0, low.astype(bf16), rows, held_ref, slots, at * (width // wide) * rows)
    for copy in loads[3:7]:
        copy.wait()
    low = (dot(c0_ref[...], g0_ref[...]) + dot(c1_ref[...], g1_ref[...])).astype(bf16)
    store(info, 0, low, rows, held_ref, slots, steps * (width // wide) * rows)
    release(held_ref, keep_any, send_any, out_sems)


def mixed_grad(chain, info, slots, n2, n2_got, ctx, ctx_got, keep, got, gy, gy_got):
    seq, width = n2.shape
    wide = gy_got.shape[1]
    rows = width // slots
    lines = (keep.shape[1] // wide + 1) * rows
    outs = (shape((slots // 2 * lines, wide), bf16),) * 2
    args = (n2, n2_got, keep, ctx, ctx_got, gy, gy_got) + got
    dims = [n2.shape, n2.shape, keep.shape, (len(got),) + n2.shape, ctx.shape, ctx.shape]
    dims += [gy_got.shape, gy_got.shape]
    return chain.run(
        functools.partial(mixed_kernel, rows=rows, slots=slots), "grad_ff_in", (1,), args,
        [any_space] * len(args), outs, (any_space, any_space), scalars=(info,),
        scratch=tuple(pltpu.VMEM(d, bf16) for d in dims + [(slots * lines, wide)])
        + (dma((len(args),)), dma((2,))),
        flops=4 * seq * width * (keep.shape[1] + wide),
    )


def heads_kernel(
    info, table_ref, n0_any, n1_any, g0_any, gq_any, gk_any, gv_any, keep_any, send_any,
    n0_ref, n1_ref, g0_ref, g1_ref, held_ref, sems, out_sems, *, rows, slots,
):
    loads = fetch(
        ((n0_any, n0_ref), (g0_any, g0_ref), (n1_any, n1_ref))
        + tuple(
            (part, g1_ref.at[:, pl.ds(at * held_ref.shape[1], held_ref.shape[1])])
            for at, part in enumerate((gq_any, gk_any, gv_any))
        ),
        sems,
    )
    wide = held_ref.shape[1]
    for copy in loads:
        copy.wait()
    for first, count in ((0, 2), (2, 1)):
        spot = slice(first * wide, (first + count) * wide)
        low = t_dot(n0_ref[...], g0_ref[:, spot]) + t_dot(n1_ref[...], g1_ref[:, spot])
        store(info, 0, low.astype(bf16), rows, held_ref, slots, first * rows)
    release(held_ref, keep_any, send_any, out_sems, table_ref)


def heads_grad(chain, info, slots, n1, n1_got, keep, got, table):
    seq, width = n1.shape
    wide = width // 2
    rows = width // slots
    lines = keep.shape[1] // wide * rows
    outs = (
        shape((slots // 2 * lines, wide), bf16), shape((slots // 2 * lines + 16, wide), bf16),
    )
    args = (n1, n1_got, keep) + got
    dims = (n1.shape, n1.shape, keep.shape, keep.shape)
    return chain.run(
        functools.partial(heads_kernel, rows=rows, slots=slots), "grad_heads", (1,), (table,) + args,
        [whole(table)] + [any_space] * 6, outs, (any_space, any_space), scalars=(info,),
        scratch=tuple(pltpu.VMEM(d, bf16) for d in dims)
        + (pltpu.VMEM((slots * lines, wide), bf16), dma((6,)), dma((3,))),
        flops=4 * seq * width * keep.shape[1],
    )


def stage_kernel(*refs, half, table):
    keep_ref, got_ref = refs[:2]
    outs = refs[3:] if table else refs[2:]
    outs[0][:half, :] = keep_ref[:half, :] + got_ref[:half, :]
    if len(outs) > 1:
        outs[1][:half, :] = keep_ref[half:, :] + got_ref[half : 2 * half, :]
    if table:
        total = refs[2][...] + got_ref[keep_ref.shape[0] :, :]
        if len(outs) > 1:
            outs[1][half:, :] = total
            outs[2][...] = total
        else:
            outs[0][half:, :] = total


def stage(chain, keep, got, last, table, flops, limit):
    count, wide = keep.shape
    extra = 0 if table is None else table.shape[0]
    args = (keep, got) if table is None else (keep, got, table)
    half = count if last else count // 2
    outs = (shape((half + extra, wide), bf16),)
    if not last:
        outs = (shape((half, wide), bf16), shape((half + extra, wide), bf16))
        outs += () if table is None else (shape(table.shape, bf16),)
    return chain.run(
        functools.partial(stage_kernel, half=half, table=table is not None), "sum_stage", (1,),
        args, [whole(a) for a in args], outs, tuple(whole(a) for a in outs), limit=limit, flops=flops,
    )


def factor_stage_kernel(keep_ref, got_ref, left_ref, right_ref, *refs, slots, pairs, rows):
    half = slots // 2
    block = 16 * pairs
    after = slots * rows
    got_right = after + slots * block
    if slots == 1:
        done_ref, = refs
        done_ref[:rows, :] = keep_ref[...] + got_ref[:rows, :]
        done_ref[rows : rows + block, :] = left_ref[...]
        done_ref[rows + block : rows + 2 * block, :] = got_ref[after:got_right, :]
        done_ref[rows + 2 * block : rows + 3 * block, :] = right_ref[...]
        done_ref[rows + 3 * block :, :] = got_ref[got_right:, :]
        return
    keep_out, send_out, left_out, right_out = refs
    middle = half * rows
    keep_out[...] = keep_ref[:middle, :] + got_ref[:middle, :]
    send_out[:middle, :] = keep_ref[middle:, :] + got_ref[middle:after, :]
    for slot in range(slots):
        target, first = (left_out, 0) if slot < half else (send_out, middle)
        first += slot % half * 2 * block
        target[first : first + block, :] = left_ref[slot * block : (slot + 1) * block, :]
        target[first + block : first + 2 * block, :] = got_ref[
            after + slot * block : after + (slot + 1) * block, :
        ]
    right_out[:block, :] = right_ref[...]
    right_out[block:, :] = got_ref[got_right:, :]
    first = middle + half * 2 * block
    send_out[first : first + block, :] = right_ref[...]
    send_out[first + block :, :] = got_ref[got_right:, :]


def factor_stage(chain, keep, got, left, right, limit, flops):
    wide = keep.shape[1]
    pairs = right.shape[0] // 16
    slots = left.shape[0] // (16 * pairs)
    rows = keep.shape[0] // slots
    if slots == 1:
        lines = (rows + 64 * pairs,)
    else:
        half = slots // 2
        lines = (half * rows, half * rows + 32 * half * pairs + 32 * pairs, 32 * half * pairs, 32 * pairs)
    outs = tuple(shape((count, wide), bf16) for count in lines)
    args = (keep, got, left, right)
    return chain.run(
        functools.partial(factor_stage_kernel, slots=slots, pairs=pairs, rows=rows), "sum_stage",
        (1,), args, [whole(a) for a in args], outs, tuple(whole(a) for a in outs), limit=limit,
        flops=flops,
    )


def gain_of(weight, grad):
    return jnp.sum(weight[...].astype(f32) * grad, axis=1, keepdims=True)


def gain_line(total, gain_ref, chip):
    rows = total.shape[0]
    turned = jnp.broadcast_to(total, (rows, tile)).T[0:1]
    gain = row_of(gain_ref)
    width = gain.shape[1]
    mine = pltpu.roll(gain, lax.rem(width - chip * rows, width), 1)[:, :rows]
    return (turned / mine).reshape(rows)


def decoder_kernel(
    info, own_ref, got_ref, wso_ref, wsv_ref, wcq_ref, win_ref, wk_ref, wv_ref,
    gself_ref, gcross_ref, gffn_ref, gfinal_ref,
    sv_ref, so_ref, cq_ref, co_ref, in_ref, out_ref, ck_ref, cv_ref,
    dself_ref, dcross_ref, dffn_ref, dfinal_ref, left_ref, right_ref, *, heads,
):
    chip = info[1]
    count = left_ref.shape[0]
    each = count // 2
    tall, width = out_ref.shape
    rows, hidden = in_ref.shape
    head_dim = width // heads
    half = width // 2
    middle = tall + 16 * each
    for at, ref in enumerate((own_ref, got_ref)):
        here = slice(at * each, (at + 1) * each)
        left_ref[here] = ref[tall:middle, :].astype(f32).reshape(each, 16, half)
        right_ref[here] = ref[middle:, :].astype(f32).reshape(each, 16, half)

    def right(at):
        return jnp.concatenate([right_ref[:, at, :], right_ref[:, 8 + at, :]], axis=1).astype(bf16)

    def left(at):
        lane = at // 16 * tile
        return left_ref[:, at % 16, lane : lane + tile].astype(bf16)[:, :rows]

    pieces = width // tile
    early = [
        jnp.concatenate(
            [left_ref[:, 2 + which * pieces + at, 2 * tile :] for at in range(pieces)], axis=1
        ).astype(bf16)
        for which in range(2)
    ]
    r_z1, r_cq, r_z2, r_cctx = [right(at) for at in range(4)]
    r_sv = dot_t(r_z1, wso_ref[...]).astype(bf16)
    r = [r_sv, r_z1, r_cq, r_z2, early[0], r_cctx, early[1]]
    r_hid = jnp.concatenate([right(4 + at) for at in range(hidden // width)], axis=1)
    l_hid = jnp.concatenate(
        [left_ref[:, 0, 2 * tile :], left_ref[:, 1, 2 * tile :]], axis=1
    ).astype(bf16)[:, :tall]
    sv_ref[...] = t_dot(left(0), r[0])
    dself_ref[...] = gain_line(gain_of(wsv_ref, sv_ref[...]), gself_ref, chip)
    so_ref[...] = t_dot(left(1), r[1])
    cq_ref[...] = t_dot(left(2), r[2])
    dcross_ref[...] = gain_line(gain_of(wcq_ref, cq_ref[...]), gcross_ref, chip)
    co_ref[...] = t_dot(left(3), r[3])
    in_ref[...] = t_dot(left(4), r_hid)
    dffn_ref[...] = gain_line(gain_of(win_ref, in_ref[...]), gffn_ref, chip)
    out_ref[...] = t_dot(l_hid, r[6])
    for head in range(heads):
        spot = slice(head * head_dim, (head + 1) * head_dim)
        ck_ref[:, spot] = t_dot(left(8 + head), r[4][:, spot])
        cv_ref[:, spot] = t_dot(left(8 + heads + head), r[5][:, spot])
    total = gain_of(wk_ref, ck_ref[...]) + gain_of(wv_ref, cv_ref[...])
    dfinal_ref[...] = gain_line(total, gfinal_ref, chip)


def decoder_grads(chain, info, own, got, wso, weights, gains, rows, heads):
    width, hidden = weights[0].shape[0], weights[2].shape[1]
    tall = hidden * rows // width
    each = (own.shape[0] - tall) // 32
    line = shape((rows,), f32)
    flat = shape((rows, width), f32)
    outs = (flat, flat, flat, flat, shape((rows, hidden), f32), shape((tall, width), f32), flat, flat)
    outs += (line,) * 4

    def sliced(array):
        return pl.BlockSpec((rows, array.shape[1]), lambda i, info: (info[1], 0))

    return chain.run(
        functools.partial(decoder_kernel, heads=heads), "decoder_grads",
        (1,), (own, got, wso) + weights + gains,
        [whole(own), whole(got), whole(wso)] + [sliced(a) for a in weights] + [whole(a) for a in gains],
        outs, tuple(whole(a) for a in outs), scalars=(info,), limit=40,
        scratch=(
            pltpu.VMEM((2 * each, 16, width // 2), f32), pltpu.VMEM((2 * each, 16, width // 2), f32),
        ),
    )


def sides(me, own_ref, got_ref, first, rows):
    own, got = own_ref[first : first + rows, :], got_ref[first : first + rows, :]
    low = jnp.where(me == 0, own, got).astype(f32)
    high = jnp.where(me == 0, got, own).astype(f32)
    return low, high


def finish_kernel(
    info, out_ref, out_got, keep_ref, away_ref, grad_ref, grad_got, row_ref, row_got,
    fout_ref, enc_ref, back_ref, dec_ref, decback_ref,
):
    me = info[0]
    wide = out_ref.shape[1]
    low, high = sides(me, out_ref, out_got, 0, fout_ref.shape[0])
    fout_ref[:, :wide] = low
    fout_ref[:, wide:] = high
    enc_ref[me] = keep_ref[...]
    enc_ref[1 - me] = away_ref[...]
    back_ref[me] = grad_ref[...]
    back_ref[1 - me] = grad_got[...]
    rows_two = lax.broadcasted_iota(jnp.int32, (2, row_ref.shape[1]), 0)
    both = jnp.where(rows_two == me, row_ref[0:1], row_got[0:1])
    dec_ref[...] = both.astype(bf16)
    decback_ref[...] = jnp.where(rows_two == me, row_ref[1:2], row_got[1:2])


def finish(chain, info, tall, out, out_got, keep, away, grad, grad_got, row, row_got):
    width = keep.shape[1]
    half = away.shape[0]
    args = (out, out_got, keep, away, grad, grad_got, row, row_got)
    outs = (
        shape((tall, width), f32), shape((2, half, width), bf16),
        shape((2, half, width), f32), shape((2, width), bf16), shape((2, width), f32),
    )
    specs = [whole(a) for a in args]
    specs[0] = specs[1] = pl.BlockSpec((tall, out.shape[1]), lambda i, info: (0, 0))
    specs[2] = pl.BlockSpec((half, width), lambda i, info: (info[0], 0))
    return chain.run(
        finish_kernel, "finish_activations", (1,),
        args, specs, outs, tuple(whole(a) for a in outs), scalars=(info,), limit=40,
    )


def finish_mix_kernel(
    info, mix_ref, mix_got, win_ref, gain_ref, fin_ref, o_ref, dffn_ref, *, rows, steps
):
    me = info[0]
    wide = mix_ref.shape[1]
    for at in range(steps):
        low, high = sides(me, mix_ref, mix_got, at * rows, rows)
        fin_ref[:, at * wide : (at + 1) * wide] = low
        fin_ref[:, (steps + at) * wide : (steps + at + 1) * wide] = high
    low, high = sides(me, mix_ref, mix_got, steps * rows, rows)
    o_ref[:, :wide] = low
    o_ref[:, wide:] = high
    dffn_ref[...] = gain_line(gain_of(win_ref, fin_ref[...]), gain_ref, info[1])


def finish_mix(chain, info, mix, mix_got, win, gain, rows):
    width, hidden = win.shape
    args = (mix, mix_got, win, gain)
    outs = (shape((rows, hidden), f32), shape((rows, width), f32), shape((rows,), f32))
    specs = [whole(a) for a in args]
    specs[2] = pl.BlockSpec((rows, hidden), lambda i, info: (info[1], 0))
    return chain.run(
        functools.partial(finish_mix_kernel, rows=rows, steps=hidden // 2 // mix.shape[1]),
        "finish_mixed", (1,),
        args, specs, outs, tuple(whole(a) for a in outs), scalars=(info,), limit=40,
    )


def last_kernel(
    info, sum_ref, got_ref, wq_ref, wk_ref, wv_ref, gain_ref,
    q_ref, k_ref, v_ref, d_ref, table_ref, *, rows, heads,
):
    me = info[0]
    wide = sum_ref.shape[1]
    outs = (q_ref, k_ref, v_ref)
    for at, ref in enumerate(outs):
        low, high = sides(me, sum_ref, got_ref, at * rows, rows)
        ref[:, :wide] = low
        ref[:, wide:] = high
    total = sum(gain_of(w, ref[...]) for w, ref in zip((wq_ref, wk_ref, wv_ref), outs))
    d_ref[...] = gain_line(total, gain_ref, info[1])
    first = 3 * rows
    table = sum_ref[first:, :tile].astype(f32) + got_ref[first:, :tile].astype(f32)
    part = heads // 2
    table_ref[:part, :] = table[:part, : table_ref.shape[1]]
    table_ref[part:, :] = table[8 : 8 + part, : table_ref.shape[1]]


def last(chain, info, done, got, wq, wk, wv, gain, rows, buckets, heads):
    width = wq.shape[0]
    flat = shape((rows, width), f32)
    args = (done, got, wq, wk, wv, gain)
    outs = (flat, flat, flat, shape((rows,), f32), shape((heads, buckets), f32))
    specs = [whole(a) for a in args]
    for at in (2, 3, 4):
        specs[at] = pl.BlockSpec((rows, args[at].shape[1]), lambda i, info: (info[1], 0))
    return chain.run(
        functools.partial(last_kernel, rows=rows, heads=heads), "finish_last", (1,), args, specs,
        outs, tuple(whole(a) for a in outs), scalars=(info,), limit=40,
    )


def plain_grad(me, place, pieces, tall):
    parts = []
    for left, left_got, right, right_got, offset in pieces:
        wide = right_got.shape[1]
        keep = lax.dynamic_slice_in_dim(right, me * wide, wide, 1) if offset else right
        total = t_dot(
            jnp.concatenate([left, left_got]), jnp.concatenate([keep, right_got])
        ).astype(bf16)
        slots = place.shape[0]
        if tall:
            parts.append(total.reshape(slots, -1, wide))
        else:
            half = left.shape[1] // 2
            for at in range(0, wide, half):
                parts.append(total[:, at : at + half].reshape(slots, -1, half))
    total = jnp.concatenate(parts, axis=1)
    order = jnp.zeros_like(place).at[place].set(jnp.arange(place.shape[0], dtype=jnp.int32))
    return jnp.take(total, order, axis=0)


def plain_sides(me, done, got):
    low = jnp.where(me == 0, done, got).astype(f32)
    high = jnp.where(me == 0, got, done).astype(f32)
    return low, high


def body(
    enc_in,
    dec_in,
    lengths,
    cot_enc,
    cot_dec,
    enc_gain_attn,
    enc_query,
    enc_key,
    enc_value,
    enc_output,
    relative_bias_table,
    enc_gain_ffn,
    enc_ff_in,
    enc_ff_out,
    enc_gain_final,
    dec_gain_self,
    dec_self_value,
    dec_self_output,
    dec_gain_cross,
    dec_cross_query,
    dec_cross_key,
    dec_cross_value,
    dec_cross_output,
    dec_gain_ffn,
    dec_ff_in,
    dec_ff_out,
):
    pair_count, seq_dev, width = enc_in.shape
    seq_all = 2 * seq_dev
    bucket_count, heads = relative_bias_table.shape
    head_dim = width // heads
    hidden = enc_ff_in.shape[1]
    slots = lax.axis_size("batch")
    me = lax.axis_index("blk")
    chip = lax.axis_index("batch")
    stages = slots.bit_length() - 1
    rows = width // slots
    aligned = rows % 16 == 0
    chain = Chain()

    def across(array):
        return lax.ppermute(array, "blk", [(0, 1), (1, 0)])

    info = jnp.stack([me, chip]).astype(jnp.int32)
    order = list(range(stages))
    crossed = order if stages < 2 else [1, 0] + order[2:]
    def hop(array, step):
        pairs = []
        for which in range(slots):
            for core in range(2):
                bit = (order, crossed)[core][step]
                pairs.append((which * 2 + core, (which ^ (1 << bit)) * 2 + core))
        return lax.ppermute(array, ("batch", "blk"), pairs)

    class Sum:
        def __init__(self, keep, send, table=None, factors=None):
            self.keep, self.table, self.at = keep, table, 0
            self.factors = factors
            self.got = hop(send, 0)

        def step(self, limit=24, flops=0):
            if self.at == stages:
                return
            self.at += 1
            last = self.at == stages
            if self.factors is not None:
                outs = factor_stage(chain, self.keep, self.got, *self.factors, limit, flops)
                self.factors = outs[2:]
            elif aligned:
                outs = list(stage(chain, self.keep, self.got, last, self.table, flops, limit))
            else:
                total = self.keep + self.got
                half = total.shape[0] // 2
                outs = [total] if last else [total[:half], total[half:]]
            self.keep = outs[0]
            if self.table is not None and len(outs) == 3 and self.factors is None:
                self.table = outs[2]
            if last:
                self.done = self.keep
                self.other = across(self.done)
            else:
                self.got = hop(outs[1], self.at)

        def rest(self):
            while self.at < stages:
                self.step()

    def plain_sum(pieces, tall):
        relative = chip ^ jnp.arange(slots, dtype=jnp.int32)
        total = plain_grad(me, spot_in(me, relative, stages).astype(jnp.int32), pieces, tall)
        total = total.reshape(-1, total.shape[-1])
        half = total.shape[0] // 2
        return Sum(total[:half], total[half:])

    enc_got = across(enc_in)
    cot_got = across(cot_enc)
    state, key_query = before(
        chain, info, dec_in, dec_gain_self, dec_gain_cross, dec_self_value, dec_self_output,
        dec_cross_query, dec_cross_key, head_dim,
    )

    (
        result_low, out_away, scale, ge_low, ge_away, dec_lines, dec_long, key_mix, mix,
        n1, q_turned, k, v, weights, context, y1, n2, hid, slope,
    ) = encoder(
        chain, info, lengths, enc_in, enc_got, enc_gain_attn, enc_query, enc_key, enc_value,
        relative_bias_table.T, enc_gain_ffn, enc_gain_final, enc_output, enc_ff_in, enc_ff_out, heads,
        cot_enc, cot_got, (key_query, state, cot_dec, dec_gain_ffn),
        (dec_cross_value, dec_cross_output, dec_ff_in, dec_ff_out),
    )
    ge_got = across(ge_away)
    hid_got, n2_got, ctx_got, n1_got = (across(part) for part in (hid, n2, context, n1))
    out_got = across(out_away)

    dec_rows, *packed = after(
        chain, info, key_mix, state, dec_lines, dec_long, mix, dec_gain_self, dec_gain_cross,
        (dec_cross_key, dec_cross_query, dec_self_output, dec_self_value, dec_ff_out),
        head_dim, heads, slots if aligned else 0,
    )
    dec_got = across(dec_rows)

    if aligned:
        left_send, left_keep, right = packed
        sum_out = Sum(
            *tall_grad(chain, info, slots, hid, hid_got, ge_low, ge_got, left_send),
            factors=(left_keep, right),
        )
    else:
        sum_out = plain_sum([(hid, hid_got, ge_low, ge_got, True)], True)
    *ga_away, ga_keep, gy_low, gy_away, g_ctx = backward(
        chain, info, ge_low, slope, enc_ff_out, enc_ff_in, y1, enc_gain_ffn, enc_output
    )
    ga_got, gy_got = tuple(across(part) for part in ga_away), across(gy_away)
    sum_out.step(64)
    if aligned:
        sum_mix = Sum(
            *mixed_grad(
                chain, info, slots, n2, n2_got, context, ctx_got, ga_keep, ga_got, gy_low, gy_got
            ),
        )
    else:
        sum_mix = plain_sum(
            [(n2, n2_got, ga_keep, jnp.concatenate(ga_got, axis=1), False), (context.T, ctx_got.T, gy_low, gy_got, True)], False
        )
    sum_out.step(64)
    *g_away, g_keep, grad_keep, grad_away, table_term = attention_back(
        chain, info, scale, enc_gain_attn, enc_in, enc_got, q_turned, k, v, context, g_ctx, weights,
        enc_query, enc_key, enc_value, gy_low,
    )
    g_got = tuple(across(part) for part in g_away)
    grad_got = across(grad_away)
    sum_out.step(64)
    sum_mix.step(64, large)
    if aligned:
        sum_heads = Sum(
            *heads_grad(chain, info, slots, n1, n1_got, g_keep, g_got, table_term), table_term
        )
    else:
        sum_heads = plain_sum([(n1, n1_got, g_keep, jnp.concatenate(g_got, axis=1), False)], False)
        table_sum = lax.psum(table_term.astype(f32), ("batch", "blk"))

    dec_weights = (dec_self_value, dec_cross_query, dec_ff_in, dec_cross_key, dec_cross_value)
    dec_gains = (dec_gain_self, dec_gain_cross, dec_gain_ffn, enc_gain_final)

    def mine(array):
        return lax.dynamic_slice_in_dim(array, chip * (array.shape[0] // slots), array.shape[0] // slots, 0)

    sum_mix.step()
    sum_out.step(24, large)
    sum_heads.step()
    sum_out.rest()
    if aligned:
        sum_mix.step(24, large)
        sum_heads.step()
        grad_ff_out, encoder_output, grad_in, dec_out, grad_dec = finish(
            chain, info, hidden // slots, sum_out.done, sum_out.other, result_low, out_got, grad_keep,
            grad_got, dec_rows, dec_got,
        )
        sum_mix.step(24, large)
        sum_heads.step()
        dec_outs = decoder_grads(
            chain, info, sum_out.done, sum_out.other, dec_self_output, dec_weights, dec_gains, rows, heads
        )
        (grad_self_value, grad_self_output, grad_cross_query, grad_cross_output) = dec_outs[:4]
        (grad_dec_ff_in, grad_dec_ff_out, grad_cross_key, grad_cross_value) = dec_outs[4:8]
        gain_self, gain_cross, gain_dec_ffn, gain_final = dec_outs[8:]
        grad_ff_in, grad_output, gain_ffn = finish_mix(
            chain, info, sum_mix.done, sum_mix.other, enc_ff_in, enc_gain_ffn, rows
        )
        sum_heads.rest()
        grad_query, grad_key, grad_value, gain_attn, grad_rel_table = last(
            chain, info, sum_heads.done, sum_heads.other, enc_query, enc_key, enc_value,
            enc_gain_attn, rows, bucket_count, heads,
        )
        grad_rel_table = grad_rel_table.T
    else:
        sum_mix.rest()
        sum_heads.rest()
        table = lax.all_gather(packed[0], ("batch", "blk"), axis=0, tiled=False)
        count = hidden // width
        tall = hidden // slots
        r = [table[:, at] for at in range(4)]
        r = [dot_t(r[0], dec_self_output).astype(bf16)] + r[:3] + [table[:, 8], r[3], table[:, 9]]
        r_hid = table[:, 4 : 4 + count].reshape(-1, hidden)
        chosen = lax.dynamic_slice_in_dim(table[:, 16:48], chip * rows, rows, 2)
        l = [chosen[:, at] for at in range(5)]
        l_hid = table[:, 48 : 48 + count].reshape(-1, hidden)
        l_hid = lax.dynamic_slice_in_dim(l_hid, chip * tall, tall, 1)
        grad_self_value, grad_self_output = t_dot(l[0], r[0]), t_dot(l[1], r[1])
        grad_cross_query, grad_cross_output = t_dot(l[2], r[2]), t_dot(l[3], r[3])
        grad_dec_ff_in = t_dot(l[4], r_hid)
        grad_dec_ff_out = t_dot(l_hid, r[6])
        many = chosen[:, 8 : 8 + 2 * heads].reshape(-1, 2, heads, rows)
        grad_cross_key, grad_cross_value = (
            jnp.einsum(
                "phd,phe->dhe", many[:, at], r[4 + at].reshape(-1, heads, head_dim),
                preferred_element_type=f32,
            ).reshape(rows, width)
            for at in range(2)
        )

        def gain_plain(gain, *terms):
            return sum(jnp.sum(mine(w).astype(f32) * g, axis=1) for w, g in terms) / mine(gain)

        gain_self = gain_plain(dec_gain_self, (dec_self_value, grad_self_value))
        gain_cross = gain_plain(dec_gain_cross, (dec_cross_query, grad_cross_query))
        gain_dec_ffn = gain_plain(dec_gain_ffn, (dec_ff_in, grad_dec_ff_in))
        gain_final = gain_plain(
            enc_gain_final, (dec_cross_key, grad_cross_key), (dec_cross_value, grad_cross_value)
        )
        sum_mix.rest()
        sum_heads.rest()
        grad_ff_out = jnp.concatenate(plain_sides(me, sum_out.done, sum_out.other), axis=1)
        low, high = plain_sides(me, sum_mix.done, sum_mix.other)

        def pick(side, at):
            return side[at * rows : (at + 1) * rows]

        grad_ff_in = jnp.concatenate(
            [pick(side, at) for side in (low, high) for at in range(low.shape[0] // rows - 1)], axis=1
        )
        spot = low.shape[0] // rows - 1
        grad_output = jnp.concatenate([pick(low, spot), pick(high, spot)], axis=1)
        low, high = plain_sides(me, sum_heads.done, sum_heads.other)
        grad_query, grad_key, grad_value = (
            jnp.concatenate([pick(low, at), pick(high, at)], axis=1) for at in range(3)
        )
        gain_ffn = gain_plain(enc_gain_ffn, (enc_ff_in, grad_ff_in))
        gain_attn = gain_plain(
            enc_gain_attn, (enc_query, grad_query), (enc_key, grad_key), (enc_value, grad_value)
        )
        turned = table_sum.T[:bucket_count]
        grad_rel_table = jnp.concatenate([turned[:, : heads // 2], turned[:, 8 : 8 + heads // 2]], axis=1)

        def stacked(own, got):
            return jnp.where(me == 0, jnp.stack([own, got]), jnp.stack([got, own]))

        out_keep = lax.dynamic_slice_in_dim(result_low, me * seq_dev, seq_dev, 0)
        encoder_output, grad_in = stacked(out_keep, out_got), stacked(grad_keep, grad_got)
        dec_out = stacked(dec_rows[0], dec_got[0]).astype(bf16)
        grad_dec = stacked(dec_rows[1], dec_got[1])

    return (
        encoder_output,
        dec_out,
        grad_in,
        grad_dec,
        gain_attn,
        grad_query,
        grad_key,
        grad_value,
        grad_output,
        grad_rel_table,
        gain_ffn,
        grad_ff_in,
        grad_ff_out,
        gain_final,
        gain_self,
        grad_self_value,
        grad_self_output,
        gain_cross,
        grad_cross_query,
        grad_cross_key,
        grad_cross_value,
        grad_cross_output,
        gain_dec_ffn,
        grad_dec_ff_in,
        grad_dec_ff_out,
    )


def solution(mesh):
    split = P("batch", "blk", None)
    rows = P("batch", None)
    line = P("batch")
    placed = (split, rows, line, split, rows) + (P(),) * 21
    return jax.shard_map(
        body,
        mesh=mesh,
        in_specs=placed,
        out_specs=(
            (split, rows, split, rows, line, rows, rows, rows, rows, P(), line, rows, rows, line)
            + (line, rows, rows, line, rows, rows, rows, rows, line, rows, rows)
        ),
        check_vma=False,
    )
```

```python
import functools

import jax
import jax.numpy as jnp
from jax import lax
from jax.experimental import pallas as pl
from jax.experimental.pallas import tpu as pltpu
from jax.sharding import PartitionSpec as P

epsilon = 1e-06
masked_score = -1e30
thresholds = (12, 16, 23, 32, 46, 64, 91)
bf16 = jnp.bfloat16
f32 = jnp.float32
tile = 128
chunk = 32
mib = 1 << 20
large = 5 * 10**9


def bucket_of(offset):
    distance = jnp.abs(offset)
    larger = jnp.full(offset.shape, 8, jnp.int32)
    for limit in thresholds:
        larger = larger + jnp.where(distance >= limit, 1, 0)
    inner = jnp.where(distance < 8, distance, larger)
    return jnp.where(offset > 0, 16, 0) + inner


def norm_scale(values):
    return lax.rsqrt(jnp.mean(values * values, axis=-1, keepdims=True) + epsilon)


def norm_apply(values, gain):
    return values * norm_scale(values) * gain


def norm_back(values, gain, upstream):
    scale = norm_scale(values)
    weighted = upstream * gain
    inner = jnp.mean(weighted * values, axis=-1, keepdims=True)
    return scale * weighted - values * (scale * scale * scale * inner)


def gelu_parts(a):
    root = 0.7978845608028654
    square = a * a
    t = jnp.tanh(root * a * (1.0 + 0.044715 * square))
    half = 0.5 + 0.5 * t
    slope = half + (half * (1.0 - t)) * (a * (root + (3 * 0.044715 * root) * square))
    return a * half, slope


def dot(left, right, dims=((1,), (0,))):
    return lax.dot_general(left, right, (dims, ((), ())), preferred_element_type=f32)


def dot_t(left, right):
    return dot(left, right, ((1,), (1,)))


def t_dot(left, right):
    return dot(left, right, ((0,), (0,)))


def shape(dims, kind):
    return jax.ShapeDtypeStruct(dims, kind)


def whole(array, buffers=None):
    zeros = (0,) * array.ndim
    if buffers is None:
        return pl.BlockSpec(array.shape, lambda *at: zeros)
    return pl.BlockSpec(array.shape, lambda *at: zeros, pipeline_mode=pl.Buffered(buffers))


class Chain:
    def __init__(self):
        self.last = ()

    def run(
        self, kernel, name, grid, args, in_specs, outs, out_specs, scalars=(), scratch=(),
        flops=0, limit=64, also=(), free=False,
    ):
        size = 0 if free else sum(a.size * a.dtype.itemsize for a in list(args) + list(outs))
        last = self.last + also
        skip = len(scalars) + len(args)

        def inner(*refs):
            kernel(*refs[:skip], *refs[skip + len(last) :])

        done = pl.pallas_call(
            inner,
            out_shape=outs,
            grid_spec=pltpu.PrefetchScalarGridSpec(
                num_scalar_prefetch=len(scalars),
                grid=grid,
                in_specs=list(in_specs) + [pl.BlockSpec(memory_space=pl.ANY)] * len(last),
                out_specs=out_specs,
                scratch_shapes=scratch,
            ),
            compiler_params=pltpu.CompilerParams(
                vmem_limit_bytes=limit * mib, dimension_semantics=("arbitrary",) * len(grid)
            ),
            cost_estimate=pl.CostEstimate(
                flops=int(4 * flops), bytes_accessed=int(size), transcendentals=0
            ),
            name=name,
        )(*scalars, *args, *last)
        self.last = (done[0],)
        return done


any_space = pl.BlockSpec(memory_space=pl.ANY)
dma = pltpu.SemaphoreType.DMA


def row_of(gain_ref):
    return gain_ref[...].reshape(1, -1)


def fetch(pairs, sems, first=None):
    copies = [
        pltpu.make_async_copy(source, target, sems.at[at])
        for at, (source, target) in enumerate(pairs)
    ]
    for copy in copies[:first]:
        copy.start()
    return copies


def picked(me, ref):
    rows = ref[...].astype(f32)
    return jnp.where(me == 0, rows[0:1], rows[1:2])


def joined(me, own, got):
    first = jnp.where(me == 0, own, got)
    last = jnp.where(me == 0, got, own)
    return jnp.concatenate([first, last], axis=0)


def wide_row(row):
    return jnp.broadcast_to(row.astype(bf16), (16, row.shape[1]))


def row_dot(row, weight):
    return dot(wide_row(row), weight)[0:1]


def row_dot_t(row, weight):
    return dot_t(wide_row(row), weight)[0:1]


def head_mask(width, head_dim):
    rows = lax.broadcasted_iota(jnp.int32, (16, width), 0)
    lanes = lax.broadcasted_iota(jnp.int32, (16, width), 1)
    return (lanes >= rows * head_dim) & (lanes < (rows + 1) * head_dim)


def spread(row, mask):
    return jnp.where(mask, jnp.broadcast_to(row, mask.shape), 0.0).astype(bf16)


def encoder_kernel(
    info, lens, gain_ref, table_ref, ffn_ref, final_ref,
    kq_ref, state_ref, cot_ref, dec_gain_ref,
    own_any, got_any, wq_any, wk_any, wv_any, wo_any, win_any, wout_any,
    cot_own_any, cot_got_any, dec_wv_any, dec_wco_any, dec_win_any, dec_wout_any,
    scale_ref, ge_ref, geaway_ref, rows_ref, long_ref, keymix_ref, mix_ref,
    n1_any, qt_any, k_any, v_any, e_any, ctx_any, y1_any, n2_any, hid_any, slope_any, low_any, away_any,
    x_ref, n1_ref, qt_ref, k_ref, v_ref, e_ref, ctx_ref, y1_ref, n2_ref, hid_ref, slope_ref,
    acc_ref, low_ref, away_ref, bias_ref, s_ref, wq_ref, wk_ref, wv_ref, wo_ref, win_ref, wout_ref, cot_x_ref,
    dec_wv, dec_wco, dec_win, dec_wout, sems, out_sems, x_sems, dec_sems, up_sems,
    *, heads, group,
):
    me = info[0]
    seq, width = x_ref.shape
    head_dim = width // heads
    blocks = seq // tile
    parts, _, piece = win_ref.shape
    many = parts * piece // width
    wide = group * head_dim
    rounds = heads // group

    loads = []
    for at in range(rounds):
        spot = pl.ds(at * wide, wide)
        for any_ref, ref in ((wq_any, wq_ref), (wk_any, wk_ref), (wv_any, wv_ref)):
            loads.append((any_ref.at[:, spot], ref.at[at]))
    loads.append((wo_any, wo_ref))
    for at in range(parts):
        spot = pl.ds(at * piece, piece)
        loads.append((win_any.at[:, spot], win_ref.at[at]))
        loads.append((wout_any.at[spot, :], wout_ref.at[at]))
    loads = [
        pltpu.make_async_copy(source, target, sems.at[at])
        for at, (source, target) in enumerate(loads)
    ]
    first = fetch(
        ((own_any.at[me], x_ref.at[pl.ds(me * (seq // 2), seq // 2), :]),
         (got_any.at[me], x_ref.at[pl.ds((1 - me) * (seq // 2), seq // 2), :])), x_sems
    )
    for copy in loads[: 3 * rounds]:
        copy.start()
    saved = []

    def save(source, target):
        copy = pltpu.make_async_copy(source, target, out_sems.at[len(saved)])
        copy.start()
        saved.append(copy)

    tables = jnp.concatenate(
        [table_ref[...], jnp.zeros((heads, tile - table_ref.shape[1]), f32)], axis=1
    )
    rows = lax.broadcasted_iota(jnp.int32, (tile, tile), 0)
    lanes = lax.broadcasted_iota(jnp.int32, (tile, tile), 1)
    kinds = [bucket_of((gap - 1) * tile + rows - lanes) for gap in range(3)]
    for head in range(heads):
        line = jnp.broadcast_to(tables[head : head + 1, :], (tile, tile))
        for gap in range(3):
            bias_ref[head, gap] = jnp.take_along_axis(line, kinds[gap], axis=1)

    for copy in first:
        copy.wait()
    n1_ref[...] = norm_apply(x_ref[...].astype(f32), row_of(gain_ref)).astype(bf16)
    save(n1_ref, n1_any)

    pair_rows = lax.broadcasted_iota(jnp.int32, (2 * head_dim, seq), 0)
    pair_lanes = lax.broadcasted_iota(jnp.int32, (seq, 2 * head_dim), 1)
    key_at = lax.broadcasted_iota(jnp.int32, (seq, 2 * head_dim), 0)
    gone = jnp.where(key_at < lens[me], 0.0, masked_score).astype(bf16)
    ones = jnp.ones((16, seq), bf16)
    vts = {}

    def project(at):
        n1 = n1_ref[...]
        for copy in loads[3 * at : 3 * at + 3]:
            copy.wait()
        for copy in loads[3 * rounds + 3 * at : 3 * rounds + 3 * at + 3]:
            copy.start()
        spot = slice(at * wide, (at + 1) * wide)
        qt_ref[spot, :] = dot(n1, wq_ref[at]).T.astype(bf16)
        k_ref[:, spot] = dot(n1, wk_ref[at]).astype(bf16)
        v = dot(n1, wv_ref[at])
        v_ref[:, spot] = v.astype(bf16)
        vts[at] = v.T.astype(bf16)

    def scores(head):
        pair = slice(head // 2 * 2 * head_dim, (head // 2 + 1) * 2 * head_dim)
        k2, q2 = k_ref[:, pair], qt_ref[pair, :]
        zero = jnp.zeros((), bf16)
        if head % 2 == 0:
            k2 = jnp.where(pair_lanes < head_dim, k2, jnp.where(pair_lanes == head_dim, gone, zero))
            q2 = jnp.where(pair_rows < head_dim, q2, jnp.ones((), bf16))
        else:
            k2 = jnp.where(pair_lanes >= head_dim, k2, jnp.where(pair_lanes == 0, gone, zero))
            q2 = jnp.where(pair_rows >= head_dim, q2, jnp.ones((), bf16))
        middle = seq // 2
        s_ref[head % 2, :, :middle] = dot(k2, q2[:, :middle])
        yield
        s_ref[head % 2, :, middle:] = dot(k2, q2[:, middle:])
        yield

    def weigh(head):
        slot = head % 2
        before = tables[head : head + 1, 15:16]
        after = tables[head : head + 1, 31:32]
        for query in range(blocks):
            yield
            across = slice(query * tile, (query + 1) * tile)
            tops = None
            for key in range(blocks):
                gap = key - query
                bias = before if gap < -1 else after if gap > 1 else bias_ref[head, gap + 1]
                down = slice(key * tile, (key + 1) * tile)
                value = s_ref[slot, down, across] + bias
                s_ref[slot, down, across] = value
                top = jnp.max(value.reshape(tile // 8, 8, tile), axis=0)
                tops = top if tops is None else jnp.maximum(tops, top)
            peak = jnp.max(tops, axis=0, keepdims=True)
            for key in range(blocks):
                down = slice(key * tile, (key + 1) * tile)
                e_ref[head, down, across] = jnp.exp(s_ref[slot, down, across] - peak).astype(bf16)
        save(e_ref.at[head], e_any.at[head])

    def mix(head):
        at, inner = divmod(head, group)
        vt = vts[at][inner * head_dim : (inner + 1) * head_dim]
        full = dot(jnp.concatenate([vt, ones], axis=0), e_ref[head])
        scale = 1.0 / full[head_dim : head_dim + 1]
        scale_ref[head : head + 1, :] = scale
        ctx_ref[head * head_dim : (head + 1) * head_dim, :] = (full[:head_dim] * scale).astype(bf16)

    project(0)
    wide_loads = fetch(
        tuple((dec_wout_any.at[pl.ds(at * width, width), :], dec_wout.at[at]) for at in range(many)),
        up_sems,
    )
    cot = picked(me, cot_ref)
    ups = []
    for _ in scores(0):
        pass
    for head in range(heads):
        if head % group == 0 and head // group + 1 < rounds:
            project(head // group + 1)
        ahead = scores(head + 1) if head + 1 < heads else iter(())
        for step, _ in enumerate(weigh(head)):
            if step == 1 and head:
                mix(head - 1)
            elif step > 1:
                next(ahead, None)
        for _ in ahead:
            pass
        if head % 2 and len(ups) < many:
            wide_loads[len(ups)].wait()
            ups.append(row_dot_t(cot, dec_wout[len(ups)]))
    mix(heads - 1)
    scale_ref[heads:, :] = jnp.zeros((16 - heads, seq), f32)
    save(qt_ref, qt_any)
    save(k_ref, k_any)
    save(v_ref, v_any)
    save(ctx_ref, ctx_any)

    loads[3 * rounds].wait()
    y1 = x_ref[...].astype(f32) + t_dot(ctx_ref[...], wo_ref[...])
    acc_ref[...] = y1
    y1_ref[...] = y1.astype(bf16)
    n2_ref[...] = norm_apply(y1, row_of(ffn_ref)).astype(bf16)
    save(y1_ref, y1_any)
    save(n2_ref, n2_any)
    for at in range(parts):
        spot = pl.ds(at * piece, piece)
        loads[3 * rounds + 1 + 2 * at].wait()
        if at == 1:
            late = fetch(
                (
                    (dec_wv_any, dec_wv), (dec_wco_any, dec_wco), (dec_win_any, dec_win),
                    (cot_own_any.at[me], cot_x_ref.at[pl.ds(me * (seq // 2), seq // 2), :]),
                    (cot_got_any.at[me], cot_x_ref.at[pl.ds((1 - me) * (seq // 2), seq // 2), :]),
                ),
                dec_sems,
            )
        value, slope = gelu_parts(dot(n2_ref[...], win_ref[at]))
        hid_ref[at] = value.astype(bf16)
        slope_ref[at] = slope.astype(bf16)
        save(hid_ref.at[at], hid_any.at[:, spot])
        save(slope_ref.at[at], slope_any.at[:, spot])
        loads[3 * rounds + 2 + 2 * at].wait()
        acc_ref[...] += dot(hid_ref[at], wout_ref[at])
    result = acc_ref[...]
    low = result.astype(bf16)
    low_ref[...] = low
    half = seq // 2
    away_ref[...] = jnp.where(me == 0, low[half:], low[:half])
    save(away_ref, away_any)
    save(low_ref, low_any)
    src = norm_apply(result, row_of(final_ref)).astype(bf16)

    gain = row_of(dec_gain_ref)
    mask = head_mask(width, head_dim)
    lanes = lax.broadcasted_iota(jnp.int32, (16, seq), 1)
    c = jnp.where(lanes < lens[me], dot_t(kq_ref[...], src), masked_score)
    c = jnp.exp(c - jnp.max(c, axis=-1, keepdims=True))
    c = c * (1.0 / jnp.sum(c, axis=-1, keepdims=True))
    c_low = c.astype(bf16)
    mixed = dot(c_low, src).astype(bf16)
    mix_ref[...] = mixed
    late[0].wait()
    cctx = jnp.sum(jnp.where(mask, dot(mixed, dec_wv[...]), 0.0), axis=0, keepdims=True)
    cctx = cctx.astype(bf16).astype(f32)
    late[1].wait()
    z2 = state_ref[3:4, :] + row_dot(cctx, dec_wco[...])
    m3 = norm_apply(z2, gain).astype(bf16).astype(f32)
    late[2].wait()
    dh, slope = gelu_parts(row_dot(m3, dec_win[...]))
    g_b = (slope * jnp.concatenate(ups, axis=1)).astype(bf16).astype(f32)
    gz2 = cot + norm_back(z2, gain, row_dot_t(g_b, dec_win[...]))
    g_cctx = row_dot_t(gz2, dec_wco[...]).astype(bf16).astype(f32)
    up = dot_t(spread(g_cctx, mask), dec_wv[...]).astype(bf16)
    d_c = dot_t(up, src)
    g_c = (c * (d_c - jnp.sum(c * d_c, axis=-1, keepdims=True))).astype(bf16)
    src_up = t_dot(
        jnp.concatenate([g_c, c_low], axis=0), jnp.concatenate([kq_ref[...], up], axis=0)
    )
    late[3].wait()
    late[4].wait()
    back = norm_back(acc_ref[...], row_of(final_ref), src_up)
    ge = (cot_x_ref[...].astype(f32) + back).astype(bf16)
    ge_ref[...] = ge
    middle = width // 2
    geaway_ref[...] = jnp.where(me == 0, ge[:, middle:], ge[:, :middle])
    keymix_ref[...] = dot(g_c, src).astype(bf16)
    for at, row in enumerate((cctx, z2, m3, gz2, g_cctx, cot)):
        rows_ref[at : at + 1, :] = row
    rows_ref[6:8, :] = jnp.zeros((2, width), f32)
    long_ref[0:1, :] = dh
    long_ref[1:2, :] = g_b
    for copy in saved:
        copy.wait()


def encoder(
    chain, info, lens, enc_in, got, gain, wq, wk, wv, table, ffn, final, wo, win, wout, heads,
    cot_enc, cot_got, decoder, dec_weights,
):
    pairs, seq_dev, width = enc_in.shape
    seq = 2 * seq_dev
    hidden = win.shape[1]
    group = 4
    rounds = heads // group
    wide = width // rounds
    piece = 2 * width
    parts, many = hidden // piece, hidden // width
    act, turned = shape((seq, width), bf16), shape((width, seq), bf16)
    part, tall = shape((seq_dev, width), bf16), shape((seq, hidden), bf16)
    few, hat = shape((16, width), bf16), shape((seq, width // 2), bf16)
    near = (shape((16, seq), f32), act, hat)
    near += (shape((8, width), f32), shape((2, hidden), f32), few, few)
    far = (act, turned, act, act, shape((heads, seq, seq), bf16), turned, act, act, tall, tall, act, part)
    small = (gain, table, ffn, final) + decoder

    def vmem(dims, kind=bf16):
        return pltpu.VMEM(dims, kind)

    return chain.run(
        functools.partial(encoder_kernel, heads=heads, group=group),
        "encoder_forward",
        (1,),
        small + (enc_in, got, wq, wk, wv, wo, win, wout, cot_enc, cot_got) + dec_weights,
        [whole(a) for a in small] + [any_space] * 14,
        near + far,
        tuple(whole(a) for a in near) + (any_space,) * len(far),
        scalars=(info, lens),
        scratch=(
            vmem((seq, width)), vmem((seq, width)), vmem((width, seq)), vmem((seq, width)),
            vmem((seq, width)), vmem((heads, seq, seq)), vmem((width, seq)), vmem((seq, width)),
            vmem((seq, width)), vmem((parts, seq, piece)), vmem((parts, seq, piece)),
            vmem((seq, width), f32), vmem((seq, width)), vmem((seq_dev, width)),
            vmem((heads, 3, tile, tile), f32), vmem((2, seq, seq), f32),
            vmem((rounds, width, wide)), vmem((rounds, width, wide)), vmem((rounds, width, wide)),
            vmem((width, width)), vmem((parts, width, piece)), vmem((parts, piece, width)),
            vmem((seq, width)),
        )
        + tuple(vmem(w.shape) for w in dec_weights[:3])
        + (
            vmem((many, width, width)),
            dma((3 * rounds + 1 + 2 * parts,)), dma((9 + heads + 2 * parts,)), dma((2,)), dma((5,)), dma((many,)),
        ),
        flops=2 * seq * width * (4 * width + 2 * hidden) + 16 * seq * seq * width,
    )


def before_kernel(
    info, dec_ref, self_ref, cross_ref, wsv_any, wso_any, wcq_any, wk_any,
    state_ref, kq_ref, wsv, wso, wcq, wk, sems, *, head_dim,
):
    copies = fetch(((wsv_any, wsv), (wso_any, wso), (wcq_any, wcq), (wk_any, wk)), sems)
    x = picked(info[0], dec_ref)
    m1 = norm_apply(x, row_of(self_ref)).astype(bf16).astype(f32)
    copies[0].wait()
    sv = row_dot(m1, wsv[...]).astype(bf16).astype(f32)
    copies[1].wait()
    z1 = x + row_dot(sv, wso[...])
    m2 = norm_apply(z1, row_of(cross_ref)).astype(bf16).astype(f32)
    copies[2].wait()
    cq = row_dot(m2, wcq[...]).astype(bf16).astype(f32)
    copies[3].wait()
    kq_ref[...] = dot_t(spread(cq, head_mask(x.shape[1], head_dim)), wk[...]).astype(bf16)
    for at, row in enumerate((x, m1, sv, z1, m2, cq)):
        state_ref[at : at + 1, :] = row
    state_ref[6:8, :] = jnp.zeros((2, x.shape[1]), f32)


def before(chain, info, dec, gain_self, gain_cross, wsv, wso, wcq, wk, head_dim):
    width = dec.shape[1]
    weights = (wsv, wso, wcq, wk)
    small = (dec, gain_self, gain_cross)
    outs = (shape((8, width), f32), shape((16, width), bf16))
    return chain.run(
        functools.partial(before_kernel, head_dim=head_dim), "decoder_before", (1,),
        small + weights, [whole(a) for a in small] + [any_space] * 4, outs,
        tuple(whole(a) for a in outs), scalars=(info,),
        scratch=tuple(pltpu.VMEM(w.shape, bf16) for w in weights) + (dma((4,)),),
        flops=64 * wk.size,
    )


def after_kernel(
    info, keymix_ref, state_ref, rows_ref, long_ref, mix_ref, self_ref, cross_ref,
    wk_any, wcq_any, wso_any, wsv_any, wout_any, both_ref, *refs, head_dim, heads, slots,
):
    packs = 3 if slots else 1
    wk, wcq, wso, wsv, wout, pad_ref, sems = refs[packs : packs + 7]
    refs = refs[:packs] + refs[packs + 7 :]
    width = state_ref.shape[1]
    pieces = [pl.ds(at, width) for at in range(0, wout.shape[0], width)]
    copies = fetch(
        ((wk_any, wk), (wcq_any, wcq), (wso_any, wso), (wsv_any, wsv))
        + tuple((wout_any.at[piece, :], wout.at[piece, :]) for piece in pieces),
        sems,
        4,
    )
    x, z1 = state_ref[0:1, :], state_ref[3:4, :]
    z2, gz2 = rows_ref[1:2, :], rows_ref[3:4, :]
    dh, g_b = long_ref[0:1, :], long_ref[1:2, :]
    width = x.shape[1]
    mask = head_mask(width, head_dim)
    mix = keymix_ref[...]
    copies[0].wait()
    for copy in copies[4:]:
        copy.start()
    g_cq = jnp.sum(jnp.where(mask, dot(mix, wk[...]), 0.0), axis=0, keepdims=True)
    g_cq = g_cq.astype(bf16).astype(f32)
    copies[1].wait()
    gz1 = gz2 + norm_back(z1, row_of(cross_ref), row_dot_t(g_cq, wcq[...]))
    count = dh.shape[1] // width
    g_bs = [g_b[:, at * width : (at + 1) * width] for at in range(count)]
    dhs = [dh[:, at * width : (at + 1) * width] for at in range(count)]
    right = [gz1, g_cq, gz2, rows_ref[4:5, :]] + g_bs
    left = [state_ref[1:2, :], state_ref[2:3, :], state_ref[4:5, :], rows_ref[0:1, :], rows_ref[2:3, :]]
    pad_ref[...] = jnp.zeros(pad_ref.shape, f32)
    for first, group in ((0, right), (16, left), (48, dhs)):
        for at, row in enumerate(group):
            pad_ref[first + at : first + at + 1, :] = row
    pad_ref[24 : 24 + heads, :] = mix[:heads].astype(f32)
    pad_ref[24 + heads : 24 + 2 * heads, :] = mix_ref[:heads].astype(f32)
    if not slots:
        pad_ref[8:9, :] = state_ref[5:6, :]
        pad_ref[9:10, :] = rows_ref[5:6, :]
        refs[0][...] = pad_ref[...].astype(bf16)
    else:
        send_factors(info, pad_ref, state_ref[5:6, :], rows_ref[5:6, :], refs, slots, width, count * width)
    copies[2].wait()
    g_sv = row_dot_t(gz1, wso[...]).astype(bf16).astype(f32)
    copies[3].wait()
    both_ref[1:2, :] = gz1 + norm_back(x, row_of(self_ref), row_dot_t(g_sv, wsv[...]))
    total = z2
    for at, piece in enumerate(pieces):
        copies[4 + at].wait()
        total = total + row_dot(dhs[at], wout[piece, :])
    both_ref[0:1, :] = total


def send_factors(info, pad_ref, query, cot, refs, slots, width, hidden):
    send_ref, keep_ref, right_ref, held_ref = refs
    half = width // 2
    both = jnp.concatenate([pad_ref[:8, :half], pad_ref[:8, half:]], axis=0).astype(bf16)
    right_ref[...] = both
    stages = slots.bit_length() - 1
    rows, tall = width // slots, hidden // slots
    per = width // tall
    many = pad_ref[16:48, :]
    two = lax.broadcasted_iota(jnp.int32, (16, tile), 0)
    count = width // tile
    fixed = jnp.zeros((16, tile), f32)
    for first, row in ((2, query), (2 + count, cot)):
        for at in range(count):
            fixed = jnp.where(two == first + at, row[:, at * tile : (at + 1) * tile], fixed)
    for slot in range(slots):
        mine = pltpu.roll(many, (width - slot * rows) % width, 1)[:, :tile]
        hid = pad_ref[48 + slot // per : 49 + slot // per, :]
        hid = pltpu.roll(hid, (width - slot % per * tall) % width, 1)
        hid = jnp.where(two == 0, hid[:, :tile], jnp.where(two == 1, hid[:, tile : 2 * tile], fixed))
        spot = spot_in(info[0], info[1] ^ slot, stages)
        held_ref[pl.ds(pl.multiple_of(spot * 16, 16), 16), :] = jnp.concatenate(
            [mine[:16], mine[16:], hid], axis=1
        ).astype(bf16)
    middle = slots // 2 * 16
    keep_ref[...] = held_ref[:middle, :]
    send_ref[:middle, :] = held_ref[middle:, :]
    send_ref[middle:, :] = both


def after(
    chain, info, key_mix, state, rows, long, mix, gain_self, gain_cross, weights, head_dim, heads, slots
):
    width = key_mix.shape[1]
    small = (key_mix, state, rows, long, mix, gain_self, gain_cross)
    half = slots // 2 * 16
    if slots:
        outs = tuple(shape((lines, width // 2), bf16) for lines in (half + 16, half, 16))
    else:
        outs = (shape((64, width), bf16),)
    outs = (shape((2, width), f32),) + outs
    return chain.run(
        functools.partial(after_kernel, head_dim=head_dim, heads=heads, slots=slots),
        "decoder_after", (1,),
        small + weights, [whole(a) for a in small] + [any_space] * 5, outs,
        tuple(whole(a) for a in outs), scalars=(info,),
        scratch=tuple(pltpu.VMEM(w.shape, bf16) for w in weights)
        + (pltpu.VMEM((64, width), f32), dma((4 + long.shape[1] // width,)))
        + ((pltpu.VMEM((2 * half, width // 2), bf16),) if slots else ()),
        flops=32 * weights[4].size,
    )


def backward_kernel(
    info, gain_ref, low_any, slope_any, wout_any, win_any, y1_any, wo_any,
    *refs,
):
    (low_ref, slope_ref, wout_ref, win_ref, y1_ref, wo_ref, ga_ref, gylow_ref, acc_ref) = refs[-11:-2]
    sems, out_sems = refs[-2:]
    me = info[0]
    parts, seq, width = slope_ref.shape
    part = parts // 2
    away_anys, (keep_any, gylow_any, gyaway_ref, gctx_ref) = refs[:part], refs[part : part + 4]
    chunks = [(1 - me) * part + at for at in range(part)] + [me * part + at for at in range(part)]
    loads = [(low_any, low_ref)]
    for at, chunk_at in enumerate(chunks):
        spot = pl.ds(pl.multiple_of(chunk_at * width, width), width)
        loads.append((wout_any.at[spot, :], wout_ref.at[at]))
        loads.append((slope_any.at[:, spot], slope_ref.at[at]))
        loads.append((win_any.at[:, spot], win_ref.at[at]))
    loads += [(y1_any, y1_ref), (wo_any, wo_ref)]
    loads = fetch(loads, sems, 7)
    saved = []
    loads[0].wait()
    for at in range(parts):
        for copy in loads[7 + 3 * at : 10 + 3 * at]:
            copy.start()
        loads[1 + 3 * at].wait()
        rise = dot_t(low_ref[...], wout_ref[at])
        loads[2 + 3 * at].wait()
        ga_ref[at] = (slope_ref[at].astype(f32) * rise).astype(bf16)
        if at < part:
            target = away_anys[at]
        else:
            target = keep_any.at[:, pl.ds(at % part * width, width)]
        copy = pltpu.make_async_copy(ga_ref.at[at], target, out_sems.at[at])
        copy.start()
        saved.append(copy)
        loads[3 + 3 * at].wait()
        if at == 0:
            acc_ref[...] = dot_t(ga_ref[at], win_ref[at])
        else:
            acc_ref[...] += dot_t(ga_ref[at], win_ref[at])
    loads[-2].wait()
    y1 = y1_ref[...].astype(f32)
    low = (low_ref[...].astype(f32) + norm_back(y1, row_of(gain_ref), acc_ref[...])).astype(bf16)
    gylow_ref[...] = low
    copy = pltpu.make_async_copy(gylow_ref, gylow_any, out_sems.at[parts])
    copy.start()
    saved.append(copy)
    half = width // 2
    gyaway_ref[...] = jnp.where(me == 0, low[:, half:], low[:, :half])
    loads[-1].wait()
    gctx_ref[...] = dot_t(wo_ref[...], low).astype(bf16)
    for copy in saved:
        copy.wait()


def backward(chain, info, low, slope, wout, win, y1, gain, wo):
    seq, width = low.shape
    hidden = win.shape[1]
    parts = hidden // width
    act, tall = shape((seq, width), bf16), shape((seq, hidden // 2), bf16)
    side, turned = shape((seq, width // 2), bf16), shape((width, seq), bf16)

    def vmem(*dims):
        return pltpu.VMEM(dims, bf16)

    return chain.run(
        backward_kernel,
        "feed_forward_back",
        (1,),
        (gain, low, slope, wout, win, y1, wo),
        [whole(gain)] + [any_space] * 6,
        (act,) * (parts // 2) + (tall, act, side, turned),
        (any_space,) * (parts // 2) + (any_space, any_space, whole(side), whole(turned)),
        scalars=(info,),
        scratch=(
            vmem(seq, width), vmem(parts, seq, width), vmem(parts, width, width),
            vmem(parts, width, width), vmem(seq, width), vmem(width, width),
            vmem(parts, seq, width), vmem(seq, width), pltpu.VMEM((seq, width), f32),
            dma((3 + 3 * parts,)), dma((parts + 1,)),
        ),
        flops=2 * seq * width * (width + 2 * hidden),
    )


def attention_back_kernel(
    info, scale_ref, gain_ref, own_ref, got_ref, qt_any, k_any, v_any, ctx_any, gctx_any, e_any,
    wq_any, wk_any, wv_any, gy_any,
    gradkeep_ref, gradaway_ref, table_ref, gq_any, gk_any, gv_any, keep_any,
    gq_ref, gk_ref, gv_ref, keep_ref, qt_ref, k_ref, v_ref, ctx_ref, gctx_ref, e_ref, wq_ref, wk_ref, wv_ref, gy_ref,
    rise_ref, gs_ref, sums_ref, all_ref, sems, out_sems, *, heads,
):
    me = info[0]
    seq, width = k_ref.shape
    head_dim = width // heads
    blocks = seq // tile
    half = width // 2
    side = heads // 2
    pair = 2 * head_dim
    loads = fetch(
        ((k_any, k_ref), (v_any, v_ref), (qt_any, qt_ref), (gctx_any, gctx_ref), (ctx_any, ctx_ref))
        + tuple(
            (e_any.at[(1 - me) * side + at if at < side else me * side + at - side], e_ref.at[at])
            for at in range(heads)
        )
        + ((wq_any, wq_ref), (wk_any, wk_ref), (wv_any, wv_ref), (gy_any, gy_ref)),
        sems,
        11,
    )
    for copy in loads[:5]:
        copy.wait()
    pair_lanes = lax.broadcasted_iota(jnp.int32, (seq, pair), 1)
    ones = [
        jnp.where((pair_lanes == start) | (pair_lanes == start + 1), 1.0, 0.0).astype(bf16)
        for start in (head_dim, 0)
    ]
    low_half = pair_lanes < head_dim
    none = jnp.zeros((head_dim - 16, seq), bf16)
    line_rows = lax.broadcasted_iota(jnp.int32, (16, seq), 0)
    sums_ref[...] = jnp.zeros(sums_ref.shape, f32)

    def first_of(at):
        base = (1 - me if at < side else me) * half
        return pl.multiple_of(base + at % side // 2 * pair, pair)

    def prepare(at):
        rows = pl.ds(first_of(at), pair)
        g2 = gctx_ref[rows, :].astype(f32)
        head = lax.div(first_of(at), head_dim)
        g2 = jnp.concatenate(
            [
                g2[:head_dim] * scale_ref[pl.ds(head, 1), :],
                g2[head_dim:] * scale_ref[pl.ds(head + 1, 1), :],
            ],
            axis=0,
        )
        both = g2 * ctx_ref[rows, :].astype(f32)
        g2 = g2.astype(bf16)
        g_ext = []
        for inner in range(2):
            here = slice(inner * head_dim, (inner + 1) * head_dim)
            delta = -jnp.sum(both[here], axis=0, keepdims=True)
            high = delta.astype(bf16).astype(f32)
            extra = jnp.where(line_rows == 0, high, jnp.where(line_rows == 1, delta - high, 0.0))
            extra = extra.astype(bf16)
            if inner == 0:
                g_ext.append(jnp.concatenate([g2[here], extra, none], axis=0))
            else:
                g_ext.append(jnp.concatenate([extra, none, g2[here]], axis=0))
        return g2, g_ext

    pairs = {}

    def rise(at):
        upper = at % 2
        if not upper:
            pairs[at // 2] = prepare(at)
        v2 = v_ref[:, pl.ds(first_of(at), pair)]
        v_ext = jnp.where(low_half, ones[1], v2) if upper else jnp.where(low_half, v2, ones[0])
        rise_ref[upper] = dot(v_ext, pairs[at // 2][1][upper])

    def spread_scores(at):
        slot = at % 2
        near, outer = [], [None, None]
        for sub in range(tile // chunk):
            sums = [None] * 5
            for key in range(blocks):
                start = key * tile + sub * chunk
                down = slice(start, start + chunk)
                for query in range(blocks):
                    across = slice(query * tile, (query + 1) * tile)
                    g = e_ref[at, down, across].astype(f32) * rise_ref[slot, down, across]
                    gs_ref[slot, down, across] = g.astype(bf16)
                    kind = min(max(query - key, -2), 2) + 2
                    sums[kind] = g if sums[kind] is None else sums[kind] + g
            near.append(jnp.concatenate(sums[1:4] + [jnp.zeros((chunk, tile), f32)], axis=1))
            outer = [a if b is None else a + b for a, b in zip((sums[4], sums[0]), outer)]
            yield
        folded = jnp.concatenate(near, axis=0)
        lanes = 4 * tile
        while folded.shape[0] > 8:
            rest = folded.shape[0] // 2
            folded = folded[:rest] + pltpu.roll(folded[rest:], lanes - rest, 1)
        rows = lax.broadcasted_iota(jnp.int32, folded.shape, 0)
        for bit in (4, 2, 1):
            moved = pltpu.roll(folded, lanes - bit, 1)
            folded = jnp.where((rows & bit) != 0, moved, folded)
        line = jnp.sum(folded, axis=0, keepdims=True)
        outer = [jnp.sum(part, axis=0, keepdims=True) for part in outer]
        row = (8 if at >= side else 0) + at % side
        sums_ref[row : row + 1, :] = jnp.concatenate([line] + outer, axis=1)

    parts = {}
    rise(0)
    turned = {}

    def close(at):
        if at < 0:
            yield from [None] * 4
            return
        first = first_of(at)
        upper = at % 2
        here = slice(upper * head_dim, (upper + 1) * head_dim)
        q_mine = qt_ref[pl.ds(pl.multiple_of(first + upper * head_dim, head_dim), head_dim), :]
        g_q = dot(turned[at // 2][here], gs_ref[upper])
        yield
        g_k = dot_t(q_mine, gs_ref[upper])
        yield
        g_v = dot_t(pairs[at // 2][0][here], e_ref[at])
        yield
        parts[upper] = (g_q, g_k, g_v)
        if upper:
            for which, gone_ref in enumerate((gq_ref, gk_ref, gv_ref)):
                both = jnp.concatenate([parts[0][which], parts[1][which]], axis=0).astype(bf16).T
                all_ref[which, :, pl.ds(first, pair)] = both
                start = at % side // 2 * pair
                if at < side:
                    gone_ref[:, start : start + pair] = both
                else:
                    keep_ref[:, which * half + start : which * half + start + pair] = both
        yield

    for at in range(heads + 1):
        last_head = close(at - 1)
        if at == heads:
            for _ in last_head:
                pass
            break
        for copy in loads[11 + at : 12 + at]:
            copy.start()
        if at % 2 == 0:
            turned[at // 2] = k_ref[:, pl.ds(first_of(at), pair)].T
        loads[5 + at].wait()
        for step, _ in enumerate(spread_scores(at)):
            next(last_head)
            if step == 1 and at + 1 < heads:
                rise(at + 1)
    gone = fetch(
        ((gq_ref, gq_any), (gk_ref, gk_any), (gv_ref, gv_any), (keep_ref, keep_any)), out_sems
    )
    for copy in loads[5 + heads :]:
        copy.wait()
    total = None
    for which, ref in enumerate((wq_ref, wk_ref, wv_ref)):
        part = dot_t(all_ref[which], ref[...])
        total = part if total is None else total + part
    x = joined(me, own_ref[0], got_ref[0]).astype(f32)
    grad = gy_ref[...].astype(f32) + norm_back(x, row_of(gain_ref), total)
    middle = seq // 2
    gradkeep_ref[...] = jnp.where(me == 0, grad[:middle], grad[middle:])
    gradaway_ref[...] = jnp.where(me == 0, grad[middle:], grad[:middle])
    sums = joined(me, sums_ref[8:], sums_ref[:8])
    spots = lax.broadcasted_iota(jnp.int32, (sums.shape[1], tile), 0)
    offsets = tile - jnp.where(spots < 3 * tile, spots, spots - 4 * tile)
    kinds = jnp.where(spots < 4 * tile, bucket_of(offsets), jnp.where(spots < 5 * tile, 15, 31))
    lanes = lax.broadcasted_iota(jnp.int32, kinds.shape, 1)
    one_hot = jnp.where(kinds == lanes, 1.0, 0.0).astype(f32)
    table = lax.dot_general(
        sums, one_hot, (((1,), (0,)), ((), ())), precision=lax.Precision.HIGHEST,
        preferred_element_type=f32,
    )
    table_ref[:, :tile] = table.astype(bf16)
    table_ref[:, tile:] = jnp.zeros((16, 2 * tile), bf16)
    for copy in gone:
        copy.wait()


def attention_back(chain, info, scale, gain, enc_in, got, qt, k, v, ctx, gctx, e, wq, wk, wv, gy):
    seq, width = k.shape
    heads = e.shape[0]
    block = pl.BlockSpec((1, seq // 2, width), lambda i, info: (info[0], 0, 0))
    side, part = shape((seq, 3 * width // 2), bf16), shape((seq // 2, width), f32)
    narrow = shape((seq, width // 2), bf16)
    near = (part, part, shape((16, 3 * tile), bf16))
    leaving = (narrow, narrow, narrow, side)
    far = (qt, k, v, ctx, gctx, e, wq, wk, wv, gy)
    return chain.run(
        functools.partial(attention_back_kernel, heads=heads),
        "attention_back",
        (1,),
        (scale, gain, enc_in, got) + far,
        [whole(scale), whole(gain), block, block] + [any_space] * len(far),
        near + leaving,
        tuple(whole(a) for a in near) + (any_space,) * 4,
        scalars=(info,),
        scratch=tuple(pltpu.VMEM(a.shape, bf16) for a in leaving + far)
        + (
            pltpu.VMEM((2, seq, seq), f32), pltpu.VMEM((2, seq, seq), bf16),
            pltpu.VMEM((16, 6 * tile), f32), pltpu.VMEM((3, seq, width), bf16), dma((9 + heads,)), dma((4,)),
        ),
        flops=6 * seq * width * width + 16 * seq * seq * width,
    )


def spot_in(me, relative, stages):
    spot = 0
    for k in range(stages):
        bit = jnp.where(me == 0, k, 1 - k) if k < 2 <= stages else k
        spot = spot | (((relative >> bit) & 1) << (stages - 1 - k))
    return spot


def store(info, base, low, rows, held_ref, slots, line):
    stages = slots.bit_length() - 1
    span = held_ref.shape[0] // slots
    wide = held_ref.shape[1]
    for at in range(low.shape[0] // rows):
        spot = spot_in(info[0], info[1] ^ (base + at), stages)
        for piece in range(low.shape[1] // wide):
            start = pl.multiple_of(spot * span + line + piece * rows, 16)
            held_ref[pl.ds(start, rows), :] = low[
                at * rows : (at + 1) * rows, piece * wide : (piece + 1) * wide
            ]


def release(held_ref, keep_any, send_any, sems, extra=None):
    middle = held_ref.shape[0] // 2
    pairs = [
        (held_ref.at[pl.ds(middle, middle), :], send_any.at[pl.ds(0, middle), :]),
        (held_ref.at[pl.ds(0, middle), :], keep_any),
    ]
    if extra is not None:
        pairs.append((extra, send_any.at[pl.ds(middle, extra.shape[0]), :]))
    for copy in fetch(pairs, sems):
        copy.wait()


def tall_kernel(
    info, r0_any, r1_any, extra_any, l0_any, l1_any, keep_any, send_any,
    r0_ref, r1_ref, extra_ref, l0_ref, l1_ref, held_ref, sems, out_sems, *, rows, slots
):
    parts, seq, width = l0_ref.shape
    wide = r0_ref.shape[1]
    loads = [
        (r0_any.at[:, pl.ds(pl.multiple_of(info[0] * wide, wide), wide)], r0_ref), (r1_any, r1_ref)
    ]
    for at in range(parts):
        spot = pl.ds(at * width, width)
        loads += [(l0_any.at[:, spot], l0_ref.at[at]), (l1_any.at[:, spot], l1_ref.at[at])]
    loads.append((extra_any, extra_ref))
    loads = fetch(loads, sems, 6)
    loads[0].wait()
    loads[1].wait()
    for at in range(parts):
        loads[2 * at + 2].wait()
        loads[2 * at + 3].wait()
        for copy in loads[2 * at + 6 : 2 * at + 8 + at // (parts - 2)]:
            copy.start()
        low = (t_dot(l0_ref[at], r0_ref[...]) + t_dot(l1_ref[at], r1_ref[...])).astype(bf16)
        store(info, at * (width // rows), low, rows, held_ref, slots, 0)
    loads[-1].wait()
    release(held_ref, keep_any, send_any, out_sems, extra_ref)


def tall_grad(chain, info, slots, left, left_got, right, right_got, extra):
    seq, tall = left.shape
    wide = right_got.shape[1]
    rows = tall // slots
    parts = 4
    middle = slots // 2 * rows
    outs = (shape((middle, wide), bf16), shape((middle + extra.shape[0], wide), bf16))
    far = pltpu.VMEM((parts, seq, tall // parts), bf16)
    return chain.run(
        functools.partial(tall_kernel, rows=rows, slots=slots), "grad_ff_out", (1,),
        (right, right_got, extra, left, left_got),
        [any_space] * 5,
        outs, (any_space, any_space), scalars=(info,),
        scratch=(
            pltpu.VMEM(right_got.shape, bf16), pltpu.VMEM(right_got.shape, bf16),
            pltpu.VMEM(extra.shape, bf16), far, far, pltpu.VMEM((tall, wide), bf16),
            dma((2 * parts + 3,)), dma((3,)),
        ),
        flops=4 * seq * tall * wide,
    )


def mixed_kernel(
    info, n0_any, n1_any, a0_any, c0_any, c1_any, g0_any, g1_any, *refs, rows, slots
):
    steps = len(refs) - 13
    a1_anys, (keep_any, send_any) = refs[:steps], refs[steps : steps + 2]
    n0_ref, n1_ref, a0_ref, a1_ref, c0_ref, c1_ref, g0_ref, g1_ref, held_ref, sems, out_sems = refs[steps + 2 :]
    seq, width = n0_ref.shape
    wide = held_ref.shape[1]
    loads = fetch(
        (
            (n0_any, n0_ref), (a0_any, a0_ref), (n1_any, n1_ref),
            (c0_any, c0_ref), (c1_any, c1_ref),
            (g0_any.at[:, pl.ds(pl.multiple_of(info[0] * wide, wide), wide)], g0_ref),
            (g1_any, g1_ref),
        )
        + tuple((part, a1_ref.at[at]) for at, part in enumerate(a1_anys)),
        sems,
        2,
    )
    loads[0].wait()
    loads[1].wait()
    for at in (2, *range(7, 7 + steps), 3, 4, 5, 6):
        loads[at].start()
    lines = width // wide * rows
    middle = slots // 2
    span = held_ref.shape[0] // slots
    held = held_ref.reshape(slots, span, wide)
    saved = []

    def leave(at, first, count):
        here = pl.ds(first, count)
        for which, (target, start) in enumerate(((send_any, middle), (keep_any, 0))):
            copy = pltpu.make_async_copy(
                held.at[pl.ds(start, middle), here, :],
                target.at[:, here, :],
                out_sems.at[2 * at + which],
            )
            copy.start()
            saved.append(copy)

    for at in range(steps):
        spot = slice(at * width, (at + 1) * width)
        low = t_dot(n0_ref[...], a0_ref[:, spot])
        if at == 0:
            loads[2].wait()
        loads[7 + at].wait()
        low = low + t_dot(n1_ref[...], a1_ref[at])
        store(info, 0, low.astype(bf16), rows, held_ref, slots, at * lines)
        leave(at, at * lines, lines)
    for copy in loads[3:7]:
        copy.wait()
    low = (dot(c0_ref[...], g0_ref[...]) + dot(c1_ref[...], g1_ref[...])).astype(bf16)
    store(info, 0, low, rows, held_ref, slots, steps * lines)
    leave(steps, steps * lines, rows)
    for copy in saved:
        copy.wait()


def mixed_grad(chain, info, slots, n2, n2_got, ctx, ctx_got, keep, got, gy, gy_got):
    seq, width = n2.shape
    wide = gy_got.shape[1]
    rows = width // slots
    lines = (keep.shape[1] // wide + 1) * rows
    outs = (shape((slots // 2, lines, wide), bf16),) * 2
    args = (n2, n2_got, keep, ctx, ctx_got, gy, gy_got) + got
    dims = [n2.shape, n2.shape, keep.shape, (len(got),) + n2.shape, ctx.shape, ctx.shape]
    dims += [gy_got.shape, gy_got.shape]
    done = chain.run(
        functools.partial(mixed_kernel, rows=rows, slots=slots), "grad_ff_in", (1,), args,
        [any_space] * len(args), outs, (any_space, any_space), scalars=(info,),
        scratch=tuple(pltpu.VMEM(d, bf16) for d in dims + [(slots * lines, wide)])
        + (dma((len(args),)), dma((2 * len(got) + 2,))),
        flops=4 * seq * width * (keep.shape[1] + wide),
    )
    return tuple(part.reshape(-1, wide) for part in done)


def heads_kernel(
    info, table_ref, n0_any, n1_any, g0_any, gq_any, gk_any, gv_any, keep_any, send_any,
    n0_ref, n1_ref, g0_ref, g1_ref, held_ref, sems, out_sems, *, rows, slots,
):
    loads = fetch(
        ((n0_any, n0_ref), (g0_any, g0_ref), (n1_any, n1_ref))
        + tuple(
            (part, g1_ref.at[:, pl.ds(at * held_ref.shape[1], held_ref.shape[1])])
            for at, part in enumerate((gq_any, gk_any, gv_any))
        ),
        sems,
    )
    wide = held_ref.shape[1]
    for copy in loads:
        copy.wait()
    for first, count in ((0, 2), (2, 1)):
        spot = slice(first * wide, (first + count) * wide)
        low = t_dot(n0_ref[...], g0_ref[:, spot]) + t_dot(n1_ref[...], g1_ref[:, spot])
        store(info, 0, low.astype(bf16), rows, held_ref, slots, first * rows)
    release(held_ref, keep_any, send_any, out_sems, table_ref)


def heads_grad(chain, info, slots, n1, n1_got, keep, got, table):
    seq, width = n1.shape
    wide = width // 2
    rows = width // slots
    lines = keep.shape[1] // wide * rows
    outs = (
        shape((slots // 2 * lines, wide), bf16), shape((slots // 2 * lines + 16, wide), bf16),
    )
    args = (n1, n1_got, keep) + got
    dims = (n1.shape, n1.shape, keep.shape, keep.shape)
    return chain.run(
        functools.partial(heads_kernel, rows=rows, slots=slots), "grad_heads", (1,), (table,) + args,
        [whole(table)] + [any_space] * 6, outs, (any_space, any_space), scalars=(info,),
        scratch=tuple(pltpu.VMEM(d, bf16) for d in dims)
        + (pltpu.VMEM((slots * lines, wide), bf16), dma((6,)), dma((3,))),
        flops=4 * seq * width * keep.shape[1],
    )


def stage_kernel(*refs, half, table):
    keep_ref, got_ref = refs[:2]
    outs = refs[3:] if table else refs[2:]
    outs[0][:half, :] = keep_ref[:half, :] + got_ref[:half, :]
    if len(outs) > 1:
        outs[1][:half, :] = keep_ref[half:, :] + got_ref[half : 2 * half, :]
    if table:
        total = refs[2][...] + got_ref[keep_ref.shape[0] :, :]
        if len(outs) > 1:
            outs[1][half:, :] = total
            outs[2][...] = total
        else:
            outs[0][half:, :] = total


def stage(chain, keep, got, last, table, flops, limit):
    count, wide = keep.shape
    extra = 0 if table is None else table.shape[0]
    args = (keep, got) if table is None else (keep, got, table)
    half = count if last else count // 2
    outs = (shape((half + extra, wide), bf16),)
    if not last:
        outs = (shape((half, wide), bf16), shape((half + extra, wide), bf16))
        outs += () if table is None else (shape(table.shape, bf16),)
    return chain.run(
        functools.partial(stage_kernel, half=half, table=table is not None), "sum_stage", (1,),
        args, [whole(a) for a in args], outs, tuple(whole(a) for a in outs), limit=limit, flops=flops,
    )


def split_kernel(*refs, rows, table):
    keep_ref, got_ref = refs[:2]
    outs = refs[3:] if table else refs[2:]
    for at in range(4):
        here = slice(at * rows, (at + 1) * rows)
        outs[at][:rows, :] = keep_ref[here, :] + got_ref[here, :]
    if table:
        total = refs[2][...] + got_ref[4 * rows :, :]
        for out in outs[1:4]:
            out[rows:, :] = total
        outs[4][...] = total


def split(chain, keep, got, table, limit, flops):
    rows, wide = keep.shape[0] // 4, keep.shape[1]
    extra = 0 if table is None else table.shape[0]
    args = (keep, got) if table is None else (keep, got, table)
    outs = (shape((rows, wide), bf16),) + (shape((rows + extra, wide), bf16),) * 3
    outs += () if table is None else (shape(table.shape, bf16),)
    return chain.run(
        functools.partial(split_kernel, rows=rows, table=table is not None), "sum_split", (1,),
        args, [whole(a) for a in args], outs, tuple(whole(a) for a in outs), limit=limit, flops=flops,
    )


def four_kernel(*refs, rows, table):
    keep_ref, *got = refs[:4]
    done_ref = refs[-1]
    total = keep_ref[...].astype(f32)
    for ref in got:
        total = total + ref[:rows, :].astype(f32)
    done_ref[:rows, :] = total.astype(bf16)
    if table:
        total = refs[4][...].astype(f32)
        for ref in got:
            total = total + ref[rows:, :].astype(f32)
        done_ref[rows:, :] = total.astype(bf16)


def four(chain, keep, got, table, limit, flops):
    args = (keep,) + got + (() if table is None else (table,))
    outs = (shape(got[0].shape, bf16),)
    return chain.run(
        functools.partial(four_kernel, rows=keep.shape[0], table=table is not None), "sum_four", (1,),
        args, [whole(a) for a in args], outs, tuple(whole(a) for a in outs), limit=limit, flops=flops,
    )


def factor_stage_kernel(keep_ref, got_ref, left_ref, right_ref, *refs, slots, pairs, rows):
    half = slots // 2
    block = 16 * pairs
    after = slots * rows
    got_right = after + slots * block
    if slots == 1:
        done_ref, = refs
        done_ref[:rows, :] = keep_ref[...] + got_ref[:rows, :]
        done_ref[rows : rows + block, :] = left_ref[...]
        done_ref[rows + block : rows + 2 * block, :] = got_ref[after:got_right, :]
        done_ref[rows + 2 * block : rows + 3 * block, :] = right_ref[...]
        done_ref[rows + 3 * block :, :] = got_ref[got_right:, :]
        return
    keep_out, send_out, left_out, right_out = refs
    middle = half * rows
    keep_out[...] = keep_ref[:middle, :] + got_ref[:middle, :]
    send_out[:middle, :] = keep_ref[middle:, :] + got_ref[middle:after, :]
    for slot in range(slots):
        target, first = (left_out, 0) if slot < half else (send_out, middle)
        first += slot % half * 2 * block
        target[first : first + block, :] = left_ref[slot * block : (slot + 1) * block, :]
        target[first + block : first + 2 * block, :] = got_ref[
            after + slot * block : after + (slot + 1) * block, :
        ]
    right_out[:block, :] = right_ref[...]
    right_out[block:, :] = got_ref[got_right:, :]
    first = middle + half * 2 * block
    send_out[first : first + block, :] = right_ref[...]
    send_out[first + block :, :] = got_ref[got_right:, :]


def factor_stage(chain, keep, got, left, right, limit, flops):
    wide = keep.shape[1]
    pairs = right.shape[0] // 16
    slots = left.shape[0] // (16 * pairs)
    rows = keep.shape[0] // slots
    if slots == 1:
        lines = (rows + 64 * pairs,)
    else:
        half = slots // 2
        lines = (half * rows, half * rows + 32 * half * pairs + 32 * pairs, 32 * half * pairs, 32 * pairs)
    outs = tuple(shape((count, wide), bf16) for count in lines)
    args = (keep, got, left, right)
    return chain.run(
        functools.partial(factor_stage_kernel, slots=slots, pairs=pairs, rows=rows), "sum_stage",
        (1,), args, [whole(a) for a in args], outs, tuple(whole(a) for a in outs), limit=limit,
        flops=flops,
    )


def gain_of(weight, grad):
    return jnp.sum(weight[...].astype(f32) * grad, axis=1, keepdims=True)


def gain_line(total, gain_ref, chip):
    rows = total.shape[0]
    turned = jnp.broadcast_to(total, (rows, tile)).T[0:1]
    gain = row_of(gain_ref)
    width = gain.shape[1]
    mine = pltpu.roll(gain, lax.rem(width - chip * rows, width), 1)[:, :rows]
    return (turned / mine).reshape(rows)


def decoder_kernel(
    info, own_ref, got_ref, wso_ref, wsv_ref, wcq_ref, win_ref, wk_ref, wv_ref,
    gself_ref, gcross_ref, gffn_ref, gfinal_ref,
    sv_ref, so_ref, cq_ref, co_ref, in_ref, out_ref, ck_ref, cv_ref,
    dself_ref, dcross_ref, dffn_ref, dfinal_ref, left_ref, right_ref, *, heads,
):
    chip = info[1]
    count = left_ref.shape[0]
    each = count // 2
    tall, width = out_ref.shape
    rows, hidden = in_ref.shape
    head_dim = width // heads
    half = width // 2
    middle = tall + 16 * each
    for at, ref in enumerate((own_ref, got_ref)):
        here = slice(at * each, (at + 1) * each)
        left_ref[here] = ref[tall:middle, :].astype(f32).reshape(each, 16, half)
        right_ref[here] = ref[middle:, :].astype(f32).reshape(each, 16, half)

    def right(at):
        return jnp.concatenate([right_ref[:, at, :], right_ref[:, 8 + at, :]], axis=1).astype(bf16)

    def left(at):
        lane = at // 16 * tile
        return left_ref[:, at % 16, lane : lane + tile].astype(bf16)[:, :rows]

    pieces = width // tile
    early = [
        jnp.concatenate(
            [left_ref[:, 2 + which * pieces + at, 2 * tile :] for at in range(pieces)], axis=1
        ).astype(bf16)
        for which in range(2)
    ]
    r_z1, r_cq, r_z2, r_cctx = [right(at) for at in range(4)]
    r_sv = dot_t(r_z1, wso_ref[...]).astype(bf16)
    r = [r_sv, r_z1, r_cq, r_z2, early[0], r_cctx, early[1]]
    r_hid = jnp.concatenate([right(4 + at) for at in range(hidden // width)], axis=1)
    l_hid = jnp.concatenate(
        [left_ref[:, 0, 2 * tile :], left_ref[:, 1, 2 * tile :]], axis=1
    ).astype(bf16)[:, :tall]
    sv_ref[...] = t_dot(left(0), r[0])
    dself_ref[...] = gain_line(gain_of(wsv_ref, sv_ref[...]), gself_ref, chip)
    so_ref[...] = t_dot(left(1), r[1])
    cq_ref[...] = t_dot(left(2), r[2])
    dcross_ref[...] = gain_line(gain_of(wcq_ref, cq_ref[...]), gcross_ref, chip)
    co_ref[...] = t_dot(left(3), r[3])
    in_ref[...] = t_dot(left(4), r_hid)
    dffn_ref[...] = gain_line(gain_of(win_ref, in_ref[...]), gffn_ref, chip)
    out_ref[...] = t_dot(l_hid, r[6])
    for head in range(heads):
        spot = slice(head * head_dim, (head + 1) * head_dim)
        ck_ref[:, spot] = t_dot(left(8 + head), r[4][:, spot])
        cv_ref[:, spot] = t_dot(left(8 + heads + head), r[5][:, spot])
    total = gain_of(wk_ref, ck_ref[...]) + gain_of(wv_ref, cv_ref[...])
    dfinal_ref[...] = gain_line(total, gfinal_ref, chip)


def decoder_grads(chain, info, own, got, wso, weights, gains, rows, heads):
    width, hidden = weights[0].shape[0], weights[2].shape[1]
    tall = hidden * rows // width
    each = (own.shape[0] - tall) // 32
    line = shape((rows,), f32)
    flat = shape((rows, width), f32)
    outs = (flat, flat, flat, flat, shape((rows, hidden), f32), shape((tall, width), f32), flat, flat)
    outs += (line,) * 4

    def sliced(array):
        return pl.BlockSpec((rows, array.shape[1]), lambda i, info: (info[1], 0))

    return chain.run(
        functools.partial(decoder_kernel, heads=heads), "decoder_grads",
        (1,), (own, got, wso) + weights + gains,
        [whole(own), whole(got), whole(wso)] + [sliced(a) for a in weights] + [whole(a) for a in gains],
        outs, tuple(whole(a) for a in outs), scalars=(info,), limit=40, free=True,
        scratch=(
            pltpu.VMEM((2 * each, 16, width // 2), f32), pltpu.VMEM((2 * each, 16, width // 2), f32),
        ),
    )


def sides(me, own_ref, got_ref, first, rows):
    own, got = own_ref[first : first + rows, :], got_ref[first : first + rows, :]
    low = jnp.where(me == 0, own, got).astype(f32)
    high = jnp.where(me == 0, got, own).astype(f32)
    return low, high


def finish_kernel(
    info, out_ref, out_got, keep_ref, away_ref, grad_ref, grad_got, row_ref, row_got,
    fout_ref, enc_ref, back_ref, dec_ref, decback_ref,
):
    me = info[0]
    wide = out_ref.shape[1]
    low, high = sides(me, out_ref, out_got, 0, fout_ref.shape[0])
    fout_ref[:, :wide] = low
    fout_ref[:, wide:] = high
    enc_ref[me] = keep_ref[...]
    enc_ref[1 - me] = away_ref[...]
    back_ref[me] = grad_ref[...]
    back_ref[1 - me] = grad_got[...]
    rows_two = lax.broadcasted_iota(jnp.int32, (2, row_ref.shape[1]), 0)
    both = jnp.where(rows_two == me, row_ref[0:1], row_got[0:1])
    dec_ref[...] = both.astype(bf16)
    decback_ref[...] = jnp.where(rows_two == me, row_ref[1:2], row_got[1:2])


def finish(chain, info, tall, out, out_got, keep, away, grad, grad_got, row, row_got):
    width = keep.shape[1]
    half = away.shape[0]
    args = (out, out_got, keep, away, grad, grad_got, row, row_got)
    outs = (
        shape((tall, width), f32), shape((2, half, width), bf16),
        shape((2, half, width), f32), shape((2, width), bf16), shape((2, width), f32),
    )
    specs = [whole(a) for a in args]
    specs[0] = specs[1] = pl.BlockSpec((tall, out.shape[1]), lambda i, info: (0, 0))
    specs[2] = pl.BlockSpec((half, width), lambda i, info: (info[0], 0))
    return chain.run(
        finish_kernel, "finish_activations", (1,),
        args, specs, outs, tuple(whole(a) for a in outs), scalars=(info,), limit=40, free=True,
    )


def finish_mix_kernel(
    info, mix_ref, mix_got, win_ref, gain_ref, fin_ref, o_ref, dffn_ref, *, rows, steps
):
    me = info[0]
    wide = mix_ref.shape[1]
    for at in range(steps):
        low, high = sides(me, mix_ref, mix_got, at * rows, rows)
        fin_ref[:, at * wide : (at + 1) * wide] = low
        fin_ref[:, (steps + at) * wide : (steps + at + 1) * wide] = high
    low, high = sides(me, mix_ref, mix_got, steps * rows, rows)
    o_ref[:, :wide] = low
    o_ref[:, wide:] = high
    dffn_ref[...] = gain_line(gain_of(win_ref, fin_ref[...]), gain_ref, info[1])


def finish_mix(chain, info, mix, mix_got, win, gain, rows):
    width, hidden = win.shape
    args = (mix, mix_got, win, gain)
    outs = (shape((rows, hidden), f32), shape((rows, width), f32), shape((rows,), f32))
    specs = [whole(a) for a in args]
    specs[2] = pl.BlockSpec((rows, hidden), lambda i, info: (info[1], 0))
    return chain.run(
        functools.partial(finish_mix_kernel, rows=rows, steps=hidden // 2 // mix.shape[1]),
        "finish_mixed", (1,),
        args, specs, outs, tuple(whole(a) for a in outs), scalars=(info,), limit=40, free=True,
    )


def last_kernel(
    info, sum_ref, got_ref, wq_ref, wk_ref, wv_ref, gain_ref,
    q_ref, k_ref, v_ref, d_ref, table_ref, *, rows, heads,
):
    me = info[0]
    wide = sum_ref.shape[1]
    outs = (q_ref, k_ref, v_ref)
    for at, ref in enumerate(outs):
        low, high = sides(me, sum_ref, got_ref, at * rows, rows)
        ref[:, :wide] = low
        ref[:, wide:] = high
    total = sum(gain_of(w, ref[...]) for w, ref in zip((wq_ref, wk_ref, wv_ref), outs))
    d_ref[...] = gain_line(total, gain_ref, info[1])
    first = 3 * rows
    table = sum_ref[first:, :tile].astype(f32) + got_ref[first:, :tile].astype(f32)
    part = heads // 2
    table_ref[:part, :] = table[:part, : table_ref.shape[1]]
    table_ref[part:, :] = table[8 : 8 + part, : table_ref.shape[1]]


def last(chain, info, done, got, wq, wk, wv, gain, rows, buckets, heads):
    width = wq.shape[0]
    flat = shape((rows, width), f32)
    args = (done, got, wq, wk, wv, gain)
    outs = (flat, flat, flat, shape((rows,), f32), shape((heads, buckets), f32))
    specs = [whole(a) for a in args]
    for at in (2, 3, 4):
        specs[at] = pl.BlockSpec((rows, args[at].shape[1]), lambda i, info: (info[1], 0))
    return chain.run(
        functools.partial(last_kernel, rows=rows, heads=heads), "finish_last", (1,), args, specs,
        outs, tuple(whole(a) for a in outs), scalars=(info,), limit=40, free=True,
    )


def plain_grad(me, place, pieces, tall):
    parts = []
    for left, left_got, right, right_got, offset in pieces:
        wide = right_got.shape[1]
        keep = lax.dynamic_slice_in_dim(right, me * wide, wide, 1) if offset else right
        total = t_dot(
            jnp.concatenate([left, left_got]), jnp.concatenate([keep, right_got])
        ).astype(bf16)
        slots = place.shape[0]
        if tall:
            parts.append(total.reshape(slots, -1, wide))
        else:
            half = left.shape[1] // 2
            for at in range(0, wide, half):
                parts.append(total[:, at : at + half].reshape(slots, -1, half))
    total = jnp.concatenate(parts, axis=1)
    order = jnp.zeros_like(place).at[place].set(jnp.arange(place.shape[0], dtype=jnp.int32))
    return jnp.take(total, order, axis=0)


def plain_sides(me, done, got):
    low = jnp.where(me == 0, done, got).astype(f32)
    high = jnp.where(me == 0, got, done).astype(f32)
    return low, high


def body(
    enc_in,
    dec_in,
    lengths,
    cot_enc,
    cot_dec,
    enc_gain_attn,
    enc_query,
    enc_key,
    enc_value,
    enc_output,
    relative_bias_table,
    enc_gain_ffn,
    enc_ff_in,
    enc_ff_out,
    enc_gain_final,
    dec_gain_self,
    dec_self_value,
    dec_self_output,
    dec_gain_cross,
    dec_cross_query,
    dec_cross_key,
    dec_cross_value,
    dec_cross_output,
    dec_gain_ffn,
    dec_ff_in,
    dec_ff_out,
):
    pair_count, seq_dev, width = enc_in.shape
    seq_all = 2 * seq_dev
    bucket_count, heads = relative_bias_table.shape
    head_dim = width // heads
    hidden = enc_ff_in.shape[1]
    slots = lax.axis_size("batch")
    me = lax.axis_index("blk")
    chip = lax.axis_index("batch")
    stages = slots.bit_length() - 1
    rows = width // slots
    aligned = rows % 16 == 0
    chain = Chain()

    def across(array):
        return lax.ppermute(array, "blk", [(0, 1), (1, 0)])

    info = jnp.stack([me, chip]).astype(jnp.int32)
    order = list(range(stages))
    crossed = order if stages < 2 else [1, 0] + order[2:]
    def hop(array, *steps):
        pairs = []
        for which in range(slots):
            for core in range(2):
                mask = sum(1 << (order, crossed)[core][step] for step in steps)
                pairs.append((which * 2 + core, (which ^ mask) * 2 + core))
        return lax.ppermute(array, ("batch", "blk"), pairs)

    class Sum:
        def __init__(self, keep, send, table=None, factors=None):
            self.keep, self.table, self.at = keep, table, 0
            self.direct = aligned and table is not None and stages >= 4
            self.total = stages - 1 if self.direct else stages
            self.factors = factors
            self.got = hop(send, 0)

        def step(self, limit=24, flops=0):
            if self.at == self.total:
                return
            self.at += 1
            last = self.at == self.total
            apart = self.direct and self.at == stages - 2
            if self.factors is not None:
                outs = factor_stage(chain, self.keep, self.got, *self.factors, limit, flops)
                self.factors = outs[2:]
            elif apart:
                outs = split(chain, self.keep, self.got, self.table, limit, flops)
            elif last and self.direct:
                outs = four(chain, self.keep, self.got, self.table, limit, flops)
            elif aligned:
                outs = list(stage(chain, self.keep, self.got, last, self.table, flops, limit))
            else:
                total = self.keep + self.got
                half = total.shape[0] // 2
                outs = [total] if last else [total[:half], total[half:]]
            self.keep = outs[0]
            if self.table is not None and not last and aligned:
                self.table = outs[-1]
            if last:
                self.done = self.keep
                self.other = across(self.done)
            elif apart:
                first, then = self.at, self.at + 1
                self.got = (hop(outs[1], then), hop(outs[2], first), hop(outs[3], first, then))
            else:
                self.got = hop(outs[1], self.at)

        def rest(self):
            while self.at < self.total:
                self.step()

    def plain_sum(pieces, tall):
        relative = chip ^ jnp.arange(slots, dtype=jnp.int32)
        total = plain_grad(me, spot_in(me, relative, stages).astype(jnp.int32), pieces, tall)
        total = total.reshape(-1, total.shape[-1])
        half = total.shape[0] // 2
        return Sum(total[:half], total[half:])

    enc_got = across(enc_in)
    cot_got = across(cot_enc)
    state, key_query = before(
        chain, info, dec_in, dec_gain_self, dec_gain_cross, dec_self_value, dec_self_output,
        dec_cross_query, dec_cross_key, head_dim,
    )

    (
        scale, ge_low, ge_away, dec_lines, dec_long, key_mix, mix,
        n1, q_turned, k, v, weights, context, y1, n2, hid, slope, result_low, out_away,
    ) = encoder(
        chain, info, lengths, enc_in, enc_got, enc_gain_attn, enc_query, enc_key, enc_value,
        relative_bias_table.T, enc_gain_ffn, enc_gain_final, enc_output, enc_ff_in, enc_ff_out, heads,
        cot_enc, cot_got, (key_query, state, cot_dec, dec_gain_ffn),
        (dec_cross_value, dec_cross_output, dec_ff_in, dec_ff_out),
    )
    ge_got = across(ge_away)
    hid_got, n2_got, ctx_got, n1_got = (across(part) for part in (hid, n2, context, n1))
    out_got = across(out_away)

    dec_rows, *packed = after(
        chain, info, key_mix, state, dec_lines, dec_long, mix, dec_gain_self, dec_gain_cross,
        (dec_cross_key, dec_cross_query, dec_self_output, dec_self_value, dec_ff_out),
        head_dim, heads, slots if aligned else 0,
    )
    dec_got = across(dec_rows)

    if aligned:
        left_send, left_keep, right = packed
        sum_out = Sum(
            *tall_grad(chain, info, slots, hid, hid_got, ge_low, ge_got, left_send),
            factors=(left_keep, right),
        )
    else:
        sum_out = plain_sum([(hid, hid_got, ge_low, ge_got, True)], True)
    *ga_away, ga_keep, gy_low, gy_away, g_ctx = backward(
        chain, info, ge_low, slope, enc_ff_out, enc_ff_in, y1, enc_gain_ffn, enc_output
    )
    ga_got, gy_got = tuple(across(part) for part in ga_away), across(gy_away)
    sum_out.step(64)
    if aligned:
        sum_mix = Sum(
            *mixed_grad(
                chain, info, slots, n2, n2_got, context, ctx_got, ga_keep, ga_got, gy_low, gy_got
            ),
        )
    else:
        sum_mix = plain_sum(
            [(n2, n2_got, ga_keep, jnp.concatenate(ga_got, axis=1), False), (context.T, ctx_got.T, gy_low, gy_got, True)], False
        )
    sum_out.step(64)
    grad_keep, grad_away, table_term, *g_away, g_keep = attention_back(
        chain, info, scale, enc_gain_attn, enc_in, enc_got, q_turned, k, v, context, g_ctx, weights,
        enc_query, enc_key, enc_value, gy_low,
    )
    g_got = tuple(across(part) for part in g_away)
    grad_got = across(grad_away)
    sum_out.step(64)
    sum_mix.step(64, large)
    if aligned:
        sum_heads = Sum(
            *heads_grad(chain, info, slots, n1, n1_got, g_keep, g_got, table_term), table_term
        )
    else:
        sum_heads = plain_sum([(n1, n1_got, g_keep, jnp.concatenate(g_got, axis=1), False)], False)
        table_sum = lax.psum(table_term.astype(f32), ("batch", "blk"))

    dec_weights = (dec_self_value, dec_cross_query, dec_ff_in, dec_cross_key, dec_cross_value)
    dec_gains = (dec_gain_self, dec_gain_cross, dec_gain_ffn, enc_gain_final)

    def mine(array):
        return lax.dynamic_slice_in_dim(array, chip * (array.shape[0] // slots), array.shape[0] // slots, 0)

    sum_mix.step()
    sum_out.step(24, large)
    sum_heads.step()
    sum_out.rest()
    if aligned:
        sum_mix.step(24, large)
        sum_heads.step()
        grad_ff_out, encoder_output, grad_in, dec_out, grad_dec = finish(
            chain, info, hidden // slots, sum_out.done, sum_out.other, result_low, out_got, grad_keep,
            grad_got, dec_rows, dec_got,
        )
        dec_outs = decoder_grads(
            chain, info, sum_out.done, sum_out.other, dec_self_output, dec_weights, dec_gains, rows, heads
        )
        (grad_self_value, grad_self_output, grad_cross_query, grad_cross_output) = dec_outs[:4]
        (grad_dec_ff_in, grad_dec_ff_out, grad_cross_key, grad_cross_value) = dec_outs[4:8]
        gain_self, gain_cross, gain_dec_ffn, gain_final = dec_outs[8:]
        sum_heads.rest()
        sum_mix.rest()
        grad_ff_in, grad_output, gain_ffn = finish_mix(
            chain, info, sum_mix.done, sum_mix.other, enc_ff_in, enc_gain_ffn, rows
        )
        sum_heads.rest()
        grad_query, grad_key, grad_value, gain_attn, grad_rel_table = last(
            chain, info, sum_heads.done, sum_heads.other, enc_query, enc_key, enc_value,
            enc_gain_attn, rows, bucket_count, heads,
        )
        grad_rel_table = grad_rel_table.T
    else:
        sum_mix.rest()
        sum_heads.rest()
        table = lax.all_gather(packed[0], ("batch", "blk"), axis=0, tiled=False)
        count = hidden // width
        tall = hidden // slots
        r = [table[:, at] for at in range(4)]
        r = [dot_t(r[0], dec_self_output).astype(bf16)] + r[:3] + [table[:, 8], r[3], table[:, 9]]
        r_hid = table[:, 4 : 4 + count].reshape(-1, hidden)
        chosen = lax.dynamic_slice_in_dim(table[:, 16:48], chip * rows, rows, 2)
        l = [chosen[:, at] for at in range(5)]
        l_hid = table[:, 48 : 48 + count].reshape(-1, hidden)
        l_hid = lax.dynamic_slice_in_dim(l_hid, chip * tall, tall, 1)
        grad_self_value, grad_self_output = t_dot(l[0], r[0]), t_dot(l[1], r[1])
        grad_cross_query, grad_cross_output = t_dot(l[2], r[2]), t_dot(l[3], r[3])
        grad_dec_ff_in = t_dot(l[4], r_hid)
        grad_dec_ff_out = t_dot(l_hid, r[6])
        many = chosen[:, 8 : 8 + 2 * heads].reshape(-1, 2, heads, rows)
        grad_cross_key, grad_cross_value = (
            jnp.einsum(
                "phd,phe->dhe", many[:, at], r[4 + at].reshape(-1, heads, head_dim),
                preferred_element_type=f32,
            ).reshape(rows, width)
            for at in range(2)
        )

        def gain_plain(gain, *terms):
            return sum(jnp.sum(mine(w).astype(f32) * g, axis=1) for w, g in terms) / mine(gain)

        gain_self = gain_plain(dec_gain_self, (dec_self_value, grad_self_value))
        gain_cross = gain_plain(dec_gain_cross, (dec_cross_query, grad_cross_query))
        gain_dec_ffn = gain_plain(dec_gain_ffn, (dec_ff_in, grad_dec_ff_in))
        gain_final = gain_plain(
            enc_gain_final, (dec_cross_key, grad_cross_key), (dec_cross_value, grad_cross_value)
        )
        sum_mix.rest()
        sum_heads.rest()
        grad_ff_out = jnp.concatenate(plain_sides(me, sum_out.done, sum_out.other), axis=1)
        low, high = plain_sides(me, sum_mix.done, sum_mix.other)

        def pick(side, at):
            return side[at * rows : (at + 1) * rows]

        grad_ff_in = jnp.concatenate(
            [pick(side, at) for side in (low, high) for at in range(low.shape[0] // rows - 1)], axis=1
        )
        spot = low.shape[0] // rows - 1
        grad_output = jnp.concatenate([pick(low, spot), pick(high, spot)], axis=1)
        low, high = plain_sides(me, sum_heads.done, sum_heads.other)
        grad_query, grad_key, grad_value = (
            jnp.concatenate([pick(low, at), pick(high, at)], axis=1) for at in range(3)
        )
        gain_ffn = gain_plain(enc_gain_ffn, (enc_ff_in, grad_ff_in))
        gain_attn = gain_plain(
            enc_gain_attn, (enc_query, grad_query), (enc_key, grad_key), (enc_value, grad_value)
        )
        turned = table_sum.T[:bucket_count]
        grad_rel_table = jnp.concatenate([turned[:, : heads // 2], turned[:, 8 : 8 + heads // 2]], axis=1)

        def stacked(own, got):
            return jnp.where(me == 0, jnp.stack([own, got]), jnp.stack([got, own]))

        out_keep = lax.dynamic_slice_in_dim(result_low, me * seq_dev, seq_dev, 0)
        encoder_output, grad_in = stacked(out_keep, out_got), stacked(grad_keep, grad_got)
        dec_out = stacked(dec_rows[0], dec_got[0]).astype(bf16)
        grad_dec = stacked(dec_rows[1], dec_got[1])

    return (
        encoder_output,
        dec_out,
        grad_in,
        grad_dec,
        gain_attn,
        grad_query,
        grad_key,
        grad_value,
        grad_output,
        grad_rel_table,
        gain_ffn,
        grad_ff_in,
        grad_ff_out,
        gain_final,
        gain_self,
        grad_self_value,
        grad_self_output,
        gain_cross,
        grad_cross_query,
        grad_cross_key,
        grad_cross_value,
        grad_cross_output,
        gain_dec_ffn,
        grad_dec_ff_in,
        grad_dec_ff_out,
    )


def solution(mesh):
    split = P("batch", "blk", None)
    rows = P("batch", None)
    line = P("batch")
    placed = (split, rows, line, split, rows) + (P(),) * 21
    return jax.shard_map(
        body,
        mesh=mesh,
        in_specs=placed,
        out_specs=(
            (split, rows, split, rows, line, rows, rows, rows, rows, P(), line, rows, rows, line)
            + (line, rows, rows, line, rows, rows, rows, rows, line, rows, rows)
        ),
        check_vma=False,
    )
```

```python
import functools

import jax
import jax.numpy as jnp
from jax import lax
from jax.experimental import pallas as pl
from jax.experimental.pallas import tpu as pltpu
from jax.sharding import PartitionSpec as P

epsilon = 1e-06
masked_score = -1e30
thresholds = (12, 16, 23, 32, 46, 64, 91)
bf16 = jnp.bfloat16
f32 = jnp.float32
tile = 128
chunk = 32
mib = 1 << 20
large = 5 * 10**9


def bucket_of(offset):
    distance = jnp.abs(offset)
    larger = jnp.full(offset.shape, 8, jnp.int32)
    for limit in thresholds:
        larger = larger + jnp.where(distance >= limit, 1, 0)
    inner = jnp.where(distance < 8, distance, larger)
    return jnp.where(offset > 0, 16, 0) + inner


def norm_scale(values):
    return lax.rsqrt(jnp.mean(values * values, axis=-1, keepdims=True) + epsilon)


def norm_apply(values, gain):
    return values * norm_scale(values) * gain


def norm_back(values, gain, upstream):
    scale = norm_scale(values)
    weighted = upstream * gain
    inner = jnp.mean(weighted * values, axis=-1, keepdims=True)
    return scale * weighted - values * (scale * scale * scale * inner)


def gelu_parts(a):
    root = 0.7978845608028654
    square = a * a
    t = jnp.tanh(root * a * (1.0 + 0.044715 * square))
    half = 0.5 + 0.5 * t
    slope = half + (half * (1.0 - t)) * (a * (root + (3 * 0.044715 * root) * square))
    return a * half, slope


def dot(left, right, dims=((1,), (0,))):
    return lax.dot_general(left, right, (dims, ((), ())), preferred_element_type=f32)


def dot_t(left, right):
    return dot(left, right, ((1,), (1,)))


def t_dot(left, right):
    return dot(left, right, ((0,), (0,)))


def shape(dims, kind):
    return jax.ShapeDtypeStruct(dims, kind)


def whole(array, buffers=None):
    zeros = (0,) * array.ndim
    if buffers is None:
        return pl.BlockSpec(array.shape, lambda *at: zeros)
    return pl.BlockSpec(array.shape, lambda *at: zeros, pipeline_mode=pl.Buffered(buffers))


class Chain:
    def __init__(self):
        self.last = ()

    def run(
        self, kernel, name, grid, args, in_specs, outs, out_specs, scalars=(), scratch=(),
        flops=0, limit=64, also=(), free=False,
    ):
        size = 0 if free else sum(a.size * a.dtype.itemsize for a in list(args) + list(outs))
        last = self.last + also
        skip = len(scalars) + len(args)

        def inner(*refs):
            kernel(*refs[:skip], *refs[skip + len(last) :])

        done = pl.pallas_call(
            inner,
            out_shape=outs,
            grid_spec=pltpu.PrefetchScalarGridSpec(
                num_scalar_prefetch=len(scalars),
                grid=grid,
                in_specs=list(in_specs) + [pl.BlockSpec(memory_space=pl.ANY)] * len(last),
                out_specs=out_specs,
                scratch_shapes=scratch,
            ),
            compiler_params=pltpu.CompilerParams(
                vmem_limit_bytes=limit * mib, dimension_semantics=("arbitrary",) * len(grid)
            ),
            cost_estimate=pl.CostEstimate(
                flops=int(4 * flops), bytes_accessed=int(size), transcendentals=0
            ),
            name=name,
        )(*scalars, *args, *last)
        self.last = (done[0],)
        return done


any_space = pl.BlockSpec(memory_space=pl.ANY)
dma = pltpu.SemaphoreType.DMA


def row_of(gain_ref):
    return gain_ref[...].reshape(1, -1)


def fetch(pairs, sems, first=None):
    copies = [
        pltpu.make_async_copy(source, target, sems.at[at])
        for at, (source, target) in enumerate(pairs)
    ]
    for copy in copies[:first]:
        copy.start()
    return copies


def picked(me, ref):
    rows = ref[...].astype(f32)
    return jnp.where(me == 0, rows[0:1], rows[1:2])


def joined(me, own, got):
    first = jnp.where(me == 0, own, got)
    last = jnp.where(me == 0, got, own)
    return jnp.concatenate([first, last], axis=0)


def wide_row(row):
    return jnp.broadcast_to(row.astype(bf16), (16, row.shape[1]))


def row_dot(row, weight):
    return dot(wide_row(row), weight)[0:1]


def row_dot_t(row, weight):
    return dot_t(wide_row(row), weight)[0:1]


def head_mask(width, head_dim):
    rows = lax.broadcasted_iota(jnp.int32, (16, width), 0)
    lanes = lax.broadcasted_iota(jnp.int32, (16, width), 1)
    return (lanes >= rows * head_dim) & (lanes < (rows + 1) * head_dim)


def spread(row, mask):
    return jnp.where(mask, jnp.broadcast_to(row, mask.shape), 0.0).astype(bf16)


def encoder_kernel(
    info, lens, gain_ref, table_ref, ffn_ref, final_ref,
    kq_ref, state_ref, cot_ref, dec_gain_ref,
    own_any, got_any, wq_any, wk_any, wv_any, wo_any, win_any, wout_any,
    cot_own_any, cot_got_any, dec_wv_any, dec_wco_any, dec_win_any, dec_wout_any,
    scale_ref, ge_ref, geaway_ref, rows_ref, long_ref, keymix_ref, mix_ref,
    n1_any, qt_any, k_any, v_any, e_any, ctx_any, y1_any, n2_any, hid_any, slope_any, low_any, away_any,
    x_ref, n1_ref, qt_ref, k_ref, v_ref, e_ref, ctx_ref, y1_ref, n2_ref, hid_ref, slope_ref,
    acc_ref, low_ref, away_ref, bias_ref, s_ref, wq_ref, wk_ref, wv_ref, wo_ref, win_ref, wout_ref, cot_x_ref,
    dec_wv, dec_wco, dec_win, dec_wout, sems, out_sems, x_sems, dec_sems, up_sems,
    *, heads, group,
):
    me = info[0]
    seq, width = x_ref.shape
    head_dim = width // heads
    blocks = seq // tile
    parts, _, piece = win_ref.shape
    many = parts * piece // width
    wide = group * head_dim
    rounds = heads // group

    loads = []
    for at in range(rounds):
        spot = pl.ds(at * wide, wide)
        for any_ref, ref in ((wq_any, wq_ref), (wk_any, wk_ref), (wv_any, wv_ref)):
            loads.append((any_ref.at[:, spot], ref.at[at]))
    loads.append((wo_any, wo_ref))
    for at in range(parts):
        spot = pl.ds(at * piece, piece)
        loads.append((win_any.at[:, spot], win_ref.at[at]))
        loads.append((wout_any.at[spot, :], wout_ref.at[at]))
    loads = [
        pltpu.make_async_copy(source, target, sems.at[at])
        for at, (source, target) in enumerate(loads)
    ]
    first = fetch(
        ((own_any.at[me], x_ref.at[pl.ds(me * (seq // 2), seq // 2), :]),
         (got_any.at[me], x_ref.at[pl.ds((1 - me) * (seq // 2), seq // 2), :])), x_sems
    )
    for copy in loads[: 3 * rounds]:
        copy.start()
    saved = []

    def save(source, target):
        copy = pltpu.make_async_copy(source, target, out_sems.at[len(saved)])
        copy.start()
        saved.append(copy)

    tables = jnp.concatenate(
        [table_ref[...], jnp.zeros((heads, tile - table_ref.shape[1]), f32)], axis=1
    )
    rows = lax.broadcasted_iota(jnp.int32, (tile, tile), 0)
    lanes = lax.broadcasted_iota(jnp.int32, (tile, tile), 1)
    kinds = [bucket_of((gap - 1) * tile + rows - lanes) for gap in range(3)]
    for head in range(heads):
        line = jnp.broadcast_to(tables[head : head + 1, :], (tile, tile))
        for gap in range(3):
            bias_ref[head, gap] = jnp.take_along_axis(line, kinds[gap], axis=1)

    for copy in first:
        copy.wait()
    n1_ref[...] = norm_apply(x_ref[...].astype(f32), row_of(gain_ref)).astype(bf16)
    save(n1_ref, n1_any)

    pair_rows = lax.broadcasted_iota(jnp.int32, (2 * head_dim, seq), 0)
    pair_lanes = lax.broadcasted_iota(jnp.int32, (seq, 2 * head_dim), 1)
    key_at = lax.broadcasted_iota(jnp.int32, (seq, 2 * head_dim), 0)
    gone = jnp.where(key_at < lens[me], 0.0, masked_score).astype(bf16)
    ones = jnp.ones((16, seq), bf16)
    vts = {}

    def project(at):
        n1 = n1_ref[...]
        for copy in loads[3 * at : 3 * at + 3]:
            copy.wait()
        for copy in loads[3 * rounds + 3 * at : 3 * rounds + 3 * at + 3]:
            copy.start()
        spot = slice(at * wide, (at + 1) * wide)
        qt_ref[spot, :] = dot(n1, wq_ref[at]).T.astype(bf16)
        k_ref[:, spot] = dot(n1, wk_ref[at]).astype(bf16)
        v = dot(n1, wv_ref[at])
        v_ref[:, spot] = v.astype(bf16)
        vts[at] = v.T.astype(bf16)

    def scores(head):
        pair = slice(head // 2 * 2 * head_dim, (head // 2 + 1) * 2 * head_dim)
        k2, q2 = k_ref[:, pair], qt_ref[pair, :]
        zero = jnp.zeros((), bf16)
        if head % 2 == 0:
            k2 = jnp.where(pair_lanes < head_dim, k2, jnp.where(pair_lanes == head_dim, gone, zero))
            q2 = jnp.where(pair_rows < head_dim, q2, jnp.ones((), bf16))
        else:
            k2 = jnp.where(pair_lanes >= head_dim, k2, jnp.where(pair_lanes == 0, gone, zero))
            q2 = jnp.where(pair_rows >= head_dim, q2, jnp.ones((), bf16))
        middle = seq // 2
        s_ref[head % 2, :, :middle] = dot(k2, q2[:, :middle])
        yield
        s_ref[head % 2, :, middle:] = dot(k2, q2[:, middle:])
        yield

    def weigh(head):
        slot = head % 2
        before = tables[head : head + 1, 15:16]
        after = tables[head : head + 1, 31:32]
        for query in range(blocks):
            yield
            across = slice(query * tile, (query + 1) * tile)
            tops = None
            for key in range(blocks):
                gap = key - query
                bias = before if gap < -1 else after if gap > 1 else bias_ref[head, gap + 1]
                down = slice(key * tile, (key + 1) * tile)
                value = s_ref[slot, down, across] + bias
                s_ref[slot, down, across] = value
                top = jnp.max(value.reshape(tile // 8, 8, tile), axis=0)
                tops = top if tops is None else jnp.maximum(tops, top)
            peak = jnp.max(tops, axis=0, keepdims=True)
            for key in range(blocks):
                down = slice(key * tile, (key + 1) * tile)
                e_ref[head, down, across] = jnp.exp(s_ref[slot, down, across] - peak).astype(bf16)
        save(e_ref.at[head], e_any.at[head])

    def mix(head):
        at, inner = divmod(head, group)
        vt = vts[at][inner * head_dim : (inner + 1) * head_dim]
        full = dot(jnp.concatenate([vt, ones], axis=0), e_ref[head])
        scale = 1.0 / full[head_dim : head_dim + 1]
        scale_ref[head : head + 1, :] = scale
        ctx_ref[head * head_dim : (head + 1) * head_dim, :] = (full[:head_dim] * scale).astype(bf16)

    project(0)
    wide_loads = fetch(
        tuple((dec_wout_any.at[pl.ds(at * width, width), :], dec_wout.at[at]) for at in range(many)),
        up_sems,
    )
    cot = picked(me, cot_ref)
    ups = []
    for _ in scores(0):
        pass
    for head in range(heads):
        if head % group == 0 and head // group + 1 < rounds:
            project(head // group + 1)
        ahead = scores(head + 1) if head + 1 < heads else iter(())
        for step, _ in enumerate(weigh(head)):
            if step == 1 and head:
                mix(head - 1)
            elif step > 1:
                next(ahead, None)
        for _ in ahead:
            pass
        if head % 2 and len(ups) < many:
            wide_loads[len(ups)].wait()
            ups.append(row_dot_t(cot, dec_wout[len(ups)]))
    mix(heads - 1)
    scale_ref[heads:, :] = jnp.zeros((16 - heads, seq), f32)
    save(qt_ref, qt_any)
    save(k_ref, k_any)
    save(v_ref, v_any)
    save(ctx_ref, ctx_any)

    loads[3 * rounds].wait()
    y1 = x_ref[...].astype(f32) + t_dot(ctx_ref[...], wo_ref[...])
    acc_ref[...] = y1
    y1_ref[...] = y1.astype(bf16)
    n2_ref[...] = norm_apply(y1, row_of(ffn_ref)).astype(bf16)
    save(y1_ref, y1_any)
    save(n2_ref, n2_any)
    for at in range(parts):
        spot = pl.ds(at * piece, piece)
        loads[3 * rounds + 1 + 2 * at].wait()
        if at == 1:
            late = fetch(
                (
                    (dec_wv_any, dec_wv), (dec_wco_any, dec_wco), (dec_win_any, dec_win),
                    (cot_own_any.at[me], cot_x_ref.at[pl.ds(me * (seq // 2), seq // 2), :]),
                    (cot_got_any.at[me], cot_x_ref.at[pl.ds((1 - me) * (seq // 2), seq // 2), :]),
                ),
                dec_sems,
            )
        value, slope = gelu_parts(dot(n2_ref[...], win_ref[at]))
        hid_ref[at] = value.astype(bf16)
        slope_ref[at] = slope.astype(bf16)
        save(hid_ref.at[at], hid_any.at[:, spot])
        save(slope_ref.at[at], slope_any.at[:, spot])
        loads[3 * rounds + 2 + 2 * at].wait()
        acc_ref[...] += dot(hid_ref[at], wout_ref[at])
    result = acc_ref[...]
    low = result.astype(bf16)
    low_ref[...] = low
    half = seq // 2
    away_ref[...] = jnp.where(me == 0, low[half:], low[:half])
    save(away_ref, away_any)
    save(low_ref, low_any)
    src = norm_apply(result, row_of(final_ref)).astype(bf16)

    gain = row_of(dec_gain_ref)
    mask = head_mask(width, head_dim)
    lanes = lax.broadcasted_iota(jnp.int32, (16, seq), 1)
    c = jnp.where(lanes < lens[me], dot_t(kq_ref[...], src), masked_score)
    c = jnp.exp(c - jnp.max(c, axis=-1, keepdims=True))
    c = c * (1.0 / jnp.sum(c, axis=-1, keepdims=True))
    c_low = c.astype(bf16)
    mixed = dot(c_low, src).astype(bf16)
    mix_ref[...] = mixed
    late[0].wait()
    cctx = jnp.sum(jnp.where(mask, dot(mixed, dec_wv[...]), 0.0), axis=0, keepdims=True)
    cctx = cctx.astype(bf16).astype(f32)
    late[1].wait()
    z2 = state_ref[3:4, :] + row_dot(cctx, dec_wco[...])
    m3 = norm_apply(z2, gain).astype(bf16).astype(f32)
    late[2].wait()
    dh, slope = gelu_parts(row_dot(m3, dec_win[...]))
    g_b = (slope * jnp.concatenate(ups, axis=1)).astype(bf16).astype(f32)
    gz2 = cot + norm_back(z2, gain, row_dot_t(g_b, dec_win[...]))
    g_cctx = row_dot_t(gz2, dec_wco[...]).astype(bf16).astype(f32)
    up = dot_t(spread(g_cctx, mask), dec_wv[...]).astype(bf16)
    d_c = dot_t(up, src)
    g_c = (c * (d_c - jnp.sum(c * d_c, axis=-1, keepdims=True))).astype(bf16)
    src_up = t_dot(
        jnp.concatenate([g_c, c_low], axis=0), jnp.concatenate([kq_ref[...], up], axis=0)
    )
    late[3].wait()
    late[4].wait()
    back = norm_back(acc_ref[...], row_of(final_ref), src_up)
    ge = (cot_x_ref[...].astype(f32) + back).astype(bf16)
    ge_ref[...] = ge
    middle = width // 2
    geaway_ref[...] = jnp.where(me == 0, ge[:, middle:], ge[:, :middle])
    keymix_ref[...] = dot(g_c, src).astype(bf16)
    for at, row in enumerate((cctx, z2, m3, gz2, g_cctx, cot)):
        rows_ref[at : at + 1, :] = row
    rows_ref[6:8, :] = jnp.zeros((2, width), f32)
    long_ref[0:1, :] = dh
    long_ref[1:2, :] = g_b
    for copy in saved:
        copy.wait()


def encoder(
    chain, info, lens, enc_in, got, gain, wq, wk, wv, table, ffn, final, wo, win, wout, heads,
    cot_enc, cot_got, decoder, dec_weights,
):
    pairs, seq_dev, width = enc_in.shape
    seq = 2 * seq_dev
    hidden = win.shape[1]
    group = 4
    rounds = heads // group
    wide = width // rounds
    piece = 2 * width
    parts, many = hidden // piece, hidden // width
    act, turned = shape((seq, width), bf16), shape((width, seq), bf16)
    part, tall = shape((seq_dev, width), bf16), shape((seq, hidden), bf16)
    few, hat = shape((16, width), bf16), shape((seq, width // 2), bf16)
    near = (shape((16, seq), f32), act, hat)
    near += (shape((8, width), f32), shape((2, hidden), f32), few, few)
    far = (act, turned, act, act, shape((heads, seq, seq), bf16), turned, act, act, tall, tall, act, part)
    small = (gain, table, ffn, final) + decoder

    def vmem(dims, kind=bf16):
        return pltpu.VMEM(dims, kind)

    return chain.run(
        functools.partial(encoder_kernel, heads=heads, group=group),
        "encoder_forward",
        (1,),
        small + (enc_in, got, wq, wk, wv, wo, win, wout, cot_enc, cot_got) + dec_weights,
        [whole(a) for a in small] + [any_space] * 14,
        near + far,
        tuple(whole(a) for a in near) + (any_space,) * len(far),
        scalars=(info, lens),
        scratch=(
            vmem((seq, width)), vmem((seq, width)), vmem((width, seq)), vmem((seq, width)),
            vmem((seq, width)), vmem((heads, seq, seq)), vmem((width, seq)), vmem((seq, width)),
            vmem((seq, width)), vmem((parts, seq, piece)), vmem((parts, seq, piece)),
            vmem((seq, width), f32), vmem((seq, width)), vmem((seq_dev, width)),
            vmem((heads, 3, tile, tile), f32), vmem((2, seq, seq), f32),
            vmem((rounds, width, wide)), vmem((rounds, width, wide)), vmem((rounds, width, wide)),
            vmem((width, width)), vmem((parts, width, piece)), vmem((parts, piece, width)),
            vmem((seq, width)),
        )
        + tuple(vmem(w.shape) for w in dec_weights[:3])
        + (
            vmem((many, width, width)),
            dma((3 * rounds + 1 + 2 * parts,)), dma((9 + heads + 2 * parts,)), dma((2,)), dma((5,)), dma((many,)),
        ),
        flops=2 * seq * width * (4 * width + 2 * hidden) + 16 * seq * seq * width,
    )


def before_kernel(
    info, dec_ref, self_ref, cross_ref, wsv_any, wso_any, wcq_any, wk_any,
    state_ref, kq_ref, wsv, wso, wcq, wk, sems, *, head_dim,
):
    copies = fetch(((wsv_any, wsv), (wso_any, wso), (wcq_any, wcq), (wk_any, wk)), sems)
    x = picked(info[0], dec_ref)
    m1 = norm_apply(x, row_of(self_ref)).astype(bf16).astype(f32)
    copies[0].wait()
    sv = row_dot(m1, wsv[...]).astype(bf16).astype(f32)
    copies[1].wait()
    z1 = x + row_dot(sv, wso[...])
    m2 = norm_apply(z1, row_of(cross_ref)).astype(bf16).astype(f32)
    copies[2].wait()
    cq = row_dot(m2, wcq[...]).astype(bf16).astype(f32)
    copies[3].wait()
    kq_ref[...] = dot_t(spread(cq, head_mask(x.shape[1], head_dim)), wk[...]).astype(bf16)
    for at, row in enumerate((x, m1, sv, z1, m2, cq)):
        state_ref[at : at + 1, :] = row
    state_ref[6:8, :] = jnp.zeros((2, x.shape[1]), f32)


def before(chain, info, dec, gain_self, gain_cross, wsv, wso, wcq, wk, head_dim):
    width = dec.shape[1]
    weights = (wsv, wso, wcq, wk)
    small = (dec, gain_self, gain_cross)
    outs = (shape((8, width), f32), shape((16, width), bf16))
    return chain.run(
        functools.partial(before_kernel, head_dim=head_dim), "decoder_before", (1,),
        small + weights, [whole(a) for a in small] + [any_space] * 4, outs,
        tuple(whole(a) for a in outs), scalars=(info,),
        scratch=tuple(pltpu.VMEM(w.shape, bf16) for w in weights) + (dma((4,)),),
        flops=64 * wk.size,
    )


def after_kernel(
    info, keymix_ref, state_ref, rows_ref, long_ref, mix_ref, self_ref, cross_ref,
    wk_any, wcq_any, wso_any, wsv_any, wout_any, both_ref, *refs, head_dim, heads, slots,
):
    packs = 3 if slots else 1
    wk, wcq, wso, wsv, wout, pad_ref, sems = refs[packs : packs + 7]
    refs = refs[:packs] + refs[packs + 7 :]
    width = state_ref.shape[1]
    pieces = [pl.ds(at, width) for at in range(0, wout.shape[0], width)]
    copies = fetch(
        ((wk_any, wk), (wcq_any, wcq), (wso_any, wso), (wsv_any, wsv))
        + tuple((wout_any.at[piece, :], wout.at[piece, :]) for piece in pieces),
        sems,
        4,
    )
    x, z1 = state_ref[0:1, :], state_ref[3:4, :]
    z2, gz2 = rows_ref[1:2, :], rows_ref[3:4, :]
    dh, g_b = long_ref[0:1, :], long_ref[1:2, :]
    width = x.shape[1]
    mask = head_mask(width, head_dim)
    mix = keymix_ref[...]
    copies[0].wait()
    for copy in copies[4:]:
        copy.start()
    g_cq = jnp.sum(jnp.where(mask, dot(mix, wk[...]), 0.0), axis=0, keepdims=True)
    g_cq = g_cq.astype(bf16).astype(f32)
    copies[1].wait()
    gz1 = gz2 + norm_back(z1, row_of(cross_ref), row_dot_t(g_cq, wcq[...]))
    count = dh.shape[1] // width
    g_bs = [g_b[:, at * width : (at + 1) * width] for at in range(count)]
    dhs = [dh[:, at * width : (at + 1) * width] for at in range(count)]
    right = [gz1, g_cq, gz2, rows_ref[4:5, :]] + g_bs
    left = [state_ref[1:2, :], state_ref[2:3, :], state_ref[4:5, :], rows_ref[0:1, :], rows_ref[2:3, :]]
    pad_ref[...] = jnp.zeros(pad_ref.shape, f32)
    for first, group in ((0, right), (16, left), (48, dhs)):
        for at, row in enumerate(group):
            pad_ref[first + at : first + at + 1, :] = row
    pad_ref[24 : 24 + heads, :] = mix[:heads].astype(f32)
    pad_ref[24 + heads : 24 + 2 * heads, :] = mix_ref[:heads].astype(f32)
    if not slots:
        pad_ref[8:9, :] = state_ref[5:6, :]
        pad_ref[9:10, :] = rows_ref[5:6, :]
        refs[0][...] = pad_ref[...].astype(bf16)
    else:
        send_factors(info, pad_ref, state_ref[5:6, :], rows_ref[5:6, :], refs, slots, width, count * width)
    copies[2].wait()
    g_sv = row_dot_t(gz1, wso[...]).astype(bf16).astype(f32)
    copies[3].wait()
    both_ref[1:2, :] = gz1 + norm_back(x, row_of(self_ref), row_dot_t(g_sv, wsv[...]))
    total = z2
    for at, piece in enumerate(pieces):
        copies[4 + at].wait()
        total = total + row_dot(dhs[at], wout[piece, :])
    both_ref[0:1, :] = total


def send_factors(info, pad_ref, query, cot, refs, slots, width, hidden):
    send_ref, keep_ref, right_ref, held_ref = refs
    half = width // 2
    both = jnp.concatenate([pad_ref[:8, :half], pad_ref[:8, half:]], axis=0).astype(bf16)
    right_ref[...] = both
    stages = slots.bit_length() - 1
    rows, tall = width // slots, hidden // slots
    per = width // tall
    many = pad_ref[16:48, :]
    two = lax.broadcasted_iota(jnp.int32, (16, tile), 0)
    count = width // tile
    fixed = jnp.zeros((16, tile), f32)
    for first, row in ((2, query), (2 + count, cot)):
        for at in range(count):
            fixed = jnp.where(two == first + at, row[:, at * tile : (at + 1) * tile], fixed)
    for slot in range(slots):
        mine = pltpu.roll(many, (width - slot * rows) % width, 1)[:, :tile]
        hid = pad_ref[48 + slot // per : 49 + slot // per, :]
        hid = pltpu.roll(hid, (width - slot % per * tall) % width, 1)
        hid = jnp.where(two == 0, hid[:, :tile], jnp.where(two == 1, hid[:, tile : 2 * tile], fixed))
        spot = spot_in(info[0], info[1] ^ slot, stages)
        held_ref[pl.ds(pl.multiple_of(spot * 16, 16), 16), :] = jnp.concatenate(
            [mine[:16], mine[16:], hid], axis=1
        ).astype(bf16)
    middle = slots // 2 * 16
    keep_ref[...] = held_ref[:middle, :]
    send_ref[:middle, :] = held_ref[middle:, :]
    send_ref[middle:, :] = both


def after(
    chain, info, key_mix, state, rows, long, mix, gain_self, gain_cross, weights, head_dim, heads, slots
):
    width = key_mix.shape[1]
    small = (key_mix, state, rows, long, mix, gain_self, gain_cross)
    half = slots // 2 * 16
    if slots:
        outs = tuple(shape((lines, width // 2), bf16) for lines in (half + 16, half, 16))
    else:
        outs = (shape((64, width), bf16),)
    outs = (shape((2, width), f32),) + outs
    return chain.run(
        functools.partial(after_kernel, head_dim=head_dim, heads=heads, slots=slots),
        "decoder_after", (1,),
        small + weights, [whole(a) for a in small] + [any_space] * 5, outs,
        tuple(whole(a) for a in outs), scalars=(info,),
        scratch=tuple(pltpu.VMEM(w.shape, bf16) for w in weights)
        + (pltpu.VMEM((64, width), f32), dma((4 + long.shape[1] // width,)))
        + ((pltpu.VMEM((2 * half, width // 2), bf16),) if slots else ()),
        flops=32 * weights[4].size,
    )


def backward_kernel(
    info, gain_ref, low_any, slope_any, wout_any, win_any, y1_any, wo_any,
    *refs,
):
    (low_ref, slope_ref, wout_ref, win_ref, y1_ref, wo_ref, ga_ref, gylow_ref, acc_ref) = refs[-11:-2]
    sems, out_sems = refs[-2:]
    me = info[0]
    parts, seq, width = slope_ref.shape
    part = parts // 2
    away_anys, (keep_any, gylow_any, gyaway_ref, gctx_ref) = refs[:part], refs[part : part + 4]
    chunks = [(1 - me) * part + at for at in range(part)] + [me * part + at for at in range(part)]
    loads = [(low_any, low_ref)]
    for at, chunk_at in enumerate(chunks):
        spot = pl.ds(pl.multiple_of(chunk_at * width, width), width)
        loads.append((wout_any.at[spot, :], wout_ref.at[at]))
        loads.append((slope_any.at[:, spot], slope_ref.at[at]))
        loads.append((win_any.at[:, spot], win_ref.at[at]))
    loads += [(y1_any, y1_ref), (wo_any, wo_ref)]
    loads = fetch(loads, sems, 7)
    saved = []
    loads[0].wait()
    for at in range(parts):
        for copy in loads[7 + 3 * at : 10 + 3 * at]:
            copy.start()
        loads[1 + 3 * at].wait()
        rise = dot_t(low_ref[...], wout_ref[at])
        loads[2 + 3 * at].wait()
        ga_ref[at] = (slope_ref[at].astype(f32) * rise).astype(bf16)
        if at < part:
            target = away_anys[at]
        else:
            target = keep_any.at[:, pl.ds(at % part * width, width)]
        copy = pltpu.make_async_copy(ga_ref.at[at], target, out_sems.at[at])
        copy.start()
        saved.append(copy)
        loads[3 + 3 * at].wait()
        if at == 0:
            acc_ref[...] = dot_t(ga_ref[at], win_ref[at])
        else:
            acc_ref[...] += dot_t(ga_ref[at], win_ref[at])
    loads[-2].wait()
    y1 = y1_ref[...].astype(f32)
    low = (low_ref[...].astype(f32) + norm_back(y1, row_of(gain_ref), acc_ref[...])).astype(bf16)
    gylow_ref[...] = low
    copy = pltpu.make_async_copy(gylow_ref, gylow_any, out_sems.at[parts])
    copy.start()
    saved.append(copy)
    half = width // 2
    gyaway_ref[...] = jnp.where(me == 0, low[:, half:], low[:, :half])
    loads[-1].wait()
    gctx_ref[...] = dot_t(wo_ref[...], low).astype(bf16)
    for copy in saved:
        copy.wait()


def backward(chain, info, low, slope, wout, win, y1, gain, wo):
    seq, width = low.shape
    hidden = win.shape[1]
    parts = hidden // width
    act, tall = shape((seq, width), bf16), shape((seq, hidden // 2), bf16)
    side, turned = shape((seq, width // 2), bf16), shape((width, seq), bf16)

    def vmem(*dims):
        return pltpu.VMEM(dims, bf16)

    return chain.run(
        backward_kernel,
        "feed_forward_back",
        (1,),
        (gain, low, slope, wout, win, y1, wo),
        [whole(gain)] + [any_space] * 6,
        (act,) * (parts // 2) + (tall, act, side, turned),
        (any_space,) * (parts // 2) + (any_space, any_space, whole(side), whole(turned)),
        scalars=(info,),
        scratch=(
            vmem(seq, width), vmem(parts, seq, width), vmem(parts, width, width),
            vmem(parts, width, width), vmem(seq, width), vmem(width, width),
            vmem(parts, seq, width), vmem(seq, width), pltpu.VMEM((seq, width), f32),
            dma((3 + 3 * parts,)), dma((parts + 1,)),
        ),
        flops=2 * seq * width * (width + 2 * hidden),
    )


def attention_back_kernel(
    info, scale_ref, gain_ref, own_ref, got_ref, qt_any, k_any, v_any, ctx_any, gctx_any, e_any,
    wq_any, wk_any, wv_any, gy_any,
    gradkeep_ref, gradaway_ref, table_ref, gq_any, gk_any, gv_any, keep_any,
    gq_ref, gk_ref, gv_ref, keep_ref, qt_ref, k_ref, v_ref, ctx_ref, gctx_ref, e_ref, wq_ref, wk_ref, wv_ref, gy_ref,
    rise_ref, gs_ref, sums_ref, all_ref, sems, out_sems, *, heads,
):
    me = info[0]
    seq, width = k_ref.shape
    head_dim = width // heads
    blocks = seq // tile
    half = width // 2
    side = heads // 2
    pair = 2 * head_dim
    loads = fetch(
        ((k_any, k_ref), (v_any, v_ref), (qt_any, qt_ref), (gctx_any, gctx_ref), (ctx_any, ctx_ref))
        + tuple(
            (e_any.at[(1 - me) * side + at if at < side else me * side + at - side], e_ref.at[at])
            for at in range(heads)
        )
        + ((wq_any, wq_ref), (wk_any, wk_ref), (wv_any, wv_ref), (gy_any, gy_ref)),
        sems,
        11,
    )
    for copy in loads[:5]:
        copy.wait()
    pair_lanes = lax.broadcasted_iota(jnp.int32, (seq, pair), 1)
    ones = [
        jnp.where((pair_lanes == start) | (pair_lanes == start + 1), 1.0, 0.0).astype(bf16)
        for start in (head_dim, 0)
    ]
    low_half = pair_lanes < head_dim
    none = jnp.zeros((head_dim - 16, seq), bf16)
    line_rows = lax.broadcasted_iota(jnp.int32, (16, seq), 0)
    sums_ref[...] = jnp.zeros(sums_ref.shape, f32)

    def first_of(at):
        base = (1 - me if at < side else me) * half
        return pl.multiple_of(base + at % side // 2 * pair, pair)

    def prepare(at):
        rows = pl.ds(first_of(at), pair)
        g2 = gctx_ref[rows, :].astype(f32)
        head = lax.div(first_of(at), head_dim)
        g2 = jnp.concatenate(
            [
                g2[:head_dim] * scale_ref[pl.ds(head, 1), :],
                g2[head_dim:] * scale_ref[pl.ds(head + 1, 1), :],
            ],
            axis=0,
        )
        both = g2 * ctx_ref[rows, :].astype(f32)
        g2 = g2.astype(bf16)
        g_ext = []
        for inner in range(2):
            here = slice(inner * head_dim, (inner + 1) * head_dim)
            delta = -jnp.sum(both[here], axis=0, keepdims=True)
            high = delta.astype(bf16).astype(f32)
            extra = jnp.where(line_rows == 0, high, jnp.where(line_rows == 1, delta - high, 0.0))
            extra = extra.astype(bf16)
            if inner == 0:
                g_ext.append(jnp.concatenate([g2[here], extra, none], axis=0))
            else:
                g_ext.append(jnp.concatenate([extra, none, g2[here]], axis=0))
        return g2, g_ext

    pairs = {}

    def rise(at):
        upper = at % 2
        if not upper:
            pairs[at // 2] = prepare(at)
        v2 = v_ref[:, pl.ds(first_of(at), pair)]
        v_ext = jnp.where(low_half, ones[1], v2) if upper else jnp.where(low_half, v2, ones[0])
        rise_ref[upper] = dot(v_ext, pairs[at // 2][1][upper])

    def spread_scores(at):
        slot = at % 2
        near, outer = [], [None, None]
        for sub in range(tile // chunk):
            sums = [None] * 5
            for key in range(blocks):
                start = key * tile + sub * chunk
                down = slice(start, start + chunk)
                for query in range(blocks):
                    across = slice(query * tile, (query + 1) * tile)
                    g = e_ref[at, down, across].astype(f32) * rise_ref[slot, down, across]
                    gs_ref[slot, down, across] = g.astype(bf16)
                    kind = min(max(query - key, -2), 2) + 2
                    sums[kind] = g if sums[kind] is None else sums[kind] + g
            near.append(jnp.concatenate(sums[1:4] + [jnp.zeros((chunk, tile), f32)], axis=1))
            outer = [a if b is None else a + b for a, b in zip((sums[4], sums[0]), outer)]
            yield
        folded = jnp.concatenate(near, axis=0)
        lanes = 4 * tile
        while folded.shape[0] > 8:
            rest = folded.shape[0] // 2
            folded = folded[:rest] + pltpu.roll(folded[rest:], lanes - rest, 1)
        rows = lax.broadcasted_iota(jnp.int32, folded.shape, 0)
        for bit in (4, 2, 1):
            moved = pltpu.roll(folded, lanes - bit, 1)
            folded = jnp.where((rows & bit) != 0, moved, folded)
        line = jnp.sum(folded, axis=0, keepdims=True)
        outer = [jnp.sum(part, axis=0, keepdims=True) for part in outer]
        row = (8 if at >= side else 0) + at % side
        sums_ref[row : row + 1, :] = jnp.concatenate([line] + outer, axis=1)

    parts = {}
    rise(0)
    turned = {}

    def close(at):
        if at < 0:
            yield from [None] * 4
            return
        first = first_of(at)
        upper = at % 2
        here = slice(upper * head_dim, (upper + 1) * head_dim)
        q_mine = qt_ref[pl.ds(pl.multiple_of(first + upper * head_dim, head_dim), head_dim), :]
        g_q = dot(turned[at // 2][here], gs_ref[upper])
        yield
        g_k = dot_t(q_mine, gs_ref[upper])
        yield
        g_v = dot_t(pairs[at // 2][0][here], e_ref[at])
        yield
        parts[upper] = (g_q, g_k, g_v)
        if upper:
            for which, gone_ref in enumerate((gq_ref, gk_ref, gv_ref)):
                both = jnp.concatenate([parts[0][which], parts[1][which]], axis=0).astype(bf16).T
                all_ref[which, :, pl.ds(first, pair)] = both
                start = at % side // 2 * pair
                if at < side:
                    gone_ref[:, start : start + pair] = both
                else:
                    keep_ref[:, which * half + start : which * half + start + pair] = both
        yield

    for at in range(heads + 1):
        last_head = close(at - 1)
        if at == heads:
            for _ in last_head:
                pass
            break
        for copy in loads[11 + at : 12 + at]:
            copy.start()
        if at % 2 == 0:
            turned[at // 2] = k_ref[:, pl.ds(first_of(at), pair)].T
        loads[5 + at].wait()
        for step, _ in enumerate(spread_scores(at)):
            next(last_head)
            if step == 1 and at + 1 < heads:
                rise(at + 1)
    gone = fetch(
        ((gq_ref, gq_any), (gk_ref, gk_any), (gv_ref, gv_any), (keep_ref, keep_any)), out_sems
    )
    for copy in loads[5 + heads :]:
        copy.wait()
    total = None
    for which, ref in enumerate((wq_ref, wk_ref, wv_ref)):
        part = dot_t(all_ref[which], ref[...])
        total = part if total is None else total + part
    x = joined(me, own_ref[0], got_ref[0]).astype(f32)
    grad = gy_ref[...].astype(f32) + norm_back(x, row_of(gain_ref), total)
    middle = seq // 2
    gradkeep_ref[...] = jnp.where(me == 0, grad[:middle], grad[middle:])
    gradaway_ref[...] = jnp.where(me == 0, grad[middle:], grad[:middle])
    sums = joined(me, sums_ref[8:], sums_ref[:8])
    spots = lax.broadcasted_iota(jnp.int32, (sums.shape[1], tile), 0)
    offsets = tile - jnp.where(spots < 3 * tile, spots, spots - 4 * tile)
    kinds = jnp.where(spots < 4 * tile, bucket_of(offsets), jnp.where(spots < 5 * tile, 15, 31))
    lanes = lax.broadcasted_iota(jnp.int32, kinds.shape, 1)
    one_hot = jnp.where(kinds == lanes, 1.0, 0.0).astype(f32)
    table = lax.dot_general(
        sums, one_hot, (((1,), (0,)), ((), ())), precision=lax.Precision.HIGHEST,
        preferred_element_type=f32,
    )
    table_ref[:, :tile] = table.astype(bf16)
    table_ref[:, tile:] = jnp.zeros((16, 2 * tile), bf16)
    for copy in gone:
        copy.wait()


def attention_back(chain, info, scale, gain, enc_in, got, qt, k, v, ctx, gctx, e, wq, wk, wv, gy):
    seq, width = k.shape
    heads = e.shape[0]
    block = pl.BlockSpec((1, seq // 2, width), lambda i, info: (info[0], 0, 0))
    side, part = shape((seq, 3 * width // 2), bf16), shape((seq // 2, width), f32)
    narrow = shape((seq, width // 2), bf16)
    near = (part, part, shape((16, 3 * tile), bf16))
    leaving = (narrow, narrow, narrow, side)
    far = (qt, k, v, ctx, gctx, e, wq, wk, wv, gy)
    return chain.run(
        functools.partial(attention_back_kernel, heads=heads),
        "attention_back",
        (1,),
        (scale, gain, enc_in, got) + far,
        [whole(scale), whole(gain), block, block] + [any_space] * len(far),
        near + leaving,
        tuple(whole(a) for a in near) + (any_space,) * 4,
        scalars=(info,),
        scratch=tuple(pltpu.VMEM(a.shape, bf16) for a in leaving + far)
        + (
            pltpu.VMEM((2, seq, seq), f32), pltpu.VMEM((2, seq, seq), bf16),
            pltpu.VMEM((16, 6 * tile), f32), pltpu.VMEM((3, seq, width), bf16), dma((9 + heads,)), dma((4,)),
        ),
        flops=6 * seq * width * width + 16 * seq * seq * width,
    )


def spot_in(me, relative, stages):
    spot = 0
    for k in range(stages):
        bit = jnp.where(me == 0, k, 1 - k) if k < 2 <= stages else k
        spot = spot | (((relative >> bit) & 1) << (stages - 1 - k))
    return spot


def store(info, base, low, rows, held_ref, slots, line):
    stages = slots.bit_length() - 1
    span = held_ref.shape[0] // slots
    wide = held_ref.shape[1]
    for at in range(low.shape[0] // rows):
        spot = spot_in(info[0], info[1] ^ (base + at), stages)
        for piece in range(low.shape[1] // wide):
            start = pl.multiple_of(spot * span + line + piece * rows, 16)
            held_ref[pl.ds(start, rows), :] = low[
                at * rows : (at + 1) * rows, piece * wide : (piece + 1) * wide
            ]


def release(held_ref, keep_any, send_any, sems, extra=None):
    middle = held_ref.shape[0] // 2
    pairs = [
        (held_ref.at[pl.ds(middle, middle), :], send_any.at[pl.ds(0, middle), :]),
        (held_ref.at[pl.ds(0, middle), :], keep_any),
    ]
    if extra is not None:
        pairs.append((extra, send_any.at[pl.ds(middle, extra.shape[0]), :]))
    for copy in fetch(pairs, sems):
        copy.wait()


def tall_kernel(
    info, r0_any, r1_any, extra_any, l0_any, l1_any, keep_any, send_any,
    r0_ref, r1_ref, extra_ref, l0_ref, l1_ref, held_ref, sems, out_sems, *, rows, slots
):
    parts, seq, width = l0_ref.shape
    wide = r0_ref.shape[1]
    loads = [
        (r0_any.at[:, pl.ds(pl.multiple_of(info[0] * wide, wide), wide)], r0_ref), (r1_any, r1_ref)
    ]
    for at in range(parts):
        spot = pl.ds(at * width, width)
        loads += [(l0_any.at[:, spot], l0_ref.at[at]), (l1_any.at[:, spot], l1_ref.at[at])]
    loads.append((extra_any, extra_ref))
    loads = fetch(loads, sems, 6)
    loads[0].wait()
    loads[1].wait()
    for at in range(parts):
        loads[2 * at + 2].wait()
        loads[2 * at + 3].wait()
        for copy in loads[2 * at + 6 : 2 * at + 8 + at // (parts - 2)]:
            copy.start()
        low = (t_dot(l0_ref[at], r0_ref[...]) + t_dot(l1_ref[at], r1_ref[...])).astype(bf16)
        store(info, at * (width // rows), low, rows, held_ref, slots, 0)
    loads[-1].wait()
    release(held_ref, keep_any, send_any, out_sems, extra_ref)


def tall_grad(chain, info, slots, left, left_got, right, right_got, extra):
    seq, tall = left.shape
    wide = right_got.shape[1]
    rows = tall // slots
    parts = 4
    middle = slots // 2 * rows
    outs = (shape((middle, wide), bf16), shape((middle + extra.shape[0], wide), bf16))
    far = pltpu.VMEM((parts, seq, tall // parts), bf16)
    return chain.run(
        functools.partial(tall_kernel, rows=rows, slots=slots), "grad_ff_out", (1,),
        (right, right_got, extra, left, left_got),
        [any_space] * 5,
        outs, (any_space, any_space), scalars=(info,),
        scratch=(
            pltpu.VMEM(right_got.shape, bf16), pltpu.VMEM(right_got.shape, bf16),
            pltpu.VMEM(extra.shape, bf16), far, far, pltpu.VMEM((tall, wide), bf16),
            dma((2 * parts + 3,)), dma((3,)),
        ),
        flops=4 * seq * tall * wide,
    )


def mixed_kernel(
    info, n0_any, n1_any, a0_any, c0_any, c1_any, g0_any, g1_any, *refs, rows, slots
):
    steps = len(refs) - 13
    a1_anys, (keep_any, send_any) = refs[:steps], refs[steps : steps + 2]
    n0_ref, n1_ref, a0_ref, a1_ref, c0_ref, c1_ref, g0_ref, g1_ref, held_ref, sems, out_sems = refs[steps + 2 :]
    seq, width = n0_ref.shape
    wide = held_ref.shape[1]
    loads = fetch(
        (
            (n0_any, n0_ref), (a0_any, a0_ref), (n1_any, n1_ref),
            (c0_any, c0_ref), (c1_any, c1_ref),
            (g0_any.at[:, pl.ds(pl.multiple_of(info[0] * wide, wide), wide)], g0_ref),
            (g1_any, g1_ref),
        )
        + tuple((part, a1_ref.at[at]) for at, part in enumerate(a1_anys)),
        sems,
        2,
    )
    loads[0].wait()
    loads[1].wait()
    for at in (2, *range(7, 7 + steps), 3, 4, 5, 6):
        loads[at].start()
    lines = width // wide * rows
    middle = slots // 2
    span = held_ref.shape[0] // slots
    held = held_ref.reshape(slots, span, wide)
    saved = []

    def leave(at, first, count):
        here = pl.ds(first, count)
        for which, (target, start) in enumerate(((send_any, middle), (keep_any, 0))):
            copy = pltpu.make_async_copy(
                held.at[pl.ds(start, middle), here, :],
                target.at[:, here, :],
                out_sems.at[2 * at + which],
            )
            copy.start()
            saved.append(copy)

    for at in range(steps):
        spot = slice(at * width, (at + 1) * width)
        low = t_dot(n0_ref[...], a0_ref[:, spot])
        if at == 0:
            loads[2].wait()
        loads[7 + at].wait()
        low = low + t_dot(n1_ref[...], a1_ref[at])
        store(info, 0, low.astype(bf16), rows, held_ref, slots, at * lines)
        leave(at, at * lines, lines)
    for copy in loads[3:7]:
        copy.wait()
    low = (dot(c0_ref[...], g0_ref[...]) + dot(c1_ref[...], g1_ref[...])).astype(bf16)
    store(info, 0, low, rows, held_ref, slots, steps * lines)
    leave(steps, steps * lines, rows)
    for copy in saved:
        copy.wait()


def mixed_grad(chain, info, slots, n2, n2_got, ctx, ctx_got, keep, got, gy, gy_got):
    seq, width = n2.shape
    wide = gy_got.shape[1]
    rows = width // slots
    lines = (keep.shape[1] // wide + 1) * rows
    outs = (shape((slots // 2, lines, wide), bf16),) * 2
    args = (n2, n2_got, keep, ctx, ctx_got, gy, gy_got) + got
    dims = [n2.shape, n2.shape, keep.shape, (len(got),) + n2.shape, ctx.shape, ctx.shape]
    dims += [gy_got.shape, gy_got.shape]
    done = chain.run(
        functools.partial(mixed_kernel, rows=rows, slots=slots), "grad_ff_in", (1,), args,
        [any_space] * len(args), outs, (any_space, any_space), scalars=(info,),
        scratch=tuple(pltpu.VMEM(d, bf16) for d in dims + [(slots * lines, wide)])
        + (dma((len(args),)), dma((2 * len(got) + 2,))),
        flops=4 * seq * width * (keep.shape[1] + wide),
    )
    return tuple(part.reshape(-1, wide) for part in done)


def heads_kernel(
    info, table_ref, n0_any, n1_any, g0_any, gq_any, gk_any, gv_any, keep_any, send_any,
    n0_ref, n1_ref, g0_ref, g1_ref, held_ref, sems, out_sems, *, rows, slots,
):
    loads = fetch(
        ((n0_any, n0_ref), (g0_any, g0_ref), (n1_any, n1_ref))
        + tuple(
            (part, g1_ref.at[:, pl.ds(at * held_ref.shape[1], held_ref.shape[1])])
            for at, part in enumerate((gq_any, gk_any, gv_any))
        ),
        sems,
    )
    wide = held_ref.shape[1]
    for copy in loads:
        copy.wait()
    for first, count in ((0, 2), (2, 1)):
        spot = slice(first * wide, (first + count) * wide)
        low = t_dot(n0_ref[...], g0_ref[:, spot]) + t_dot(n1_ref[...], g1_ref[:, spot])
        store(info, 0, low.astype(bf16), rows, held_ref, slots, first * rows)
    release(held_ref, keep_any, send_any, out_sems, table_ref)


def heads_grad(chain, info, slots, n1, n1_got, keep, got, table):
    seq, width = n1.shape
    wide = width // 2
    rows = width // slots
    lines = keep.shape[1] // wide * rows
    outs = (
        shape((slots // 2 * lines, wide), bf16), shape((slots // 2 * lines + 16, wide), bf16),
    )
    args = (n1, n1_got, keep) + got
    dims = (n1.shape, n1.shape, keep.shape, keep.shape)
    return chain.run(
        functools.partial(heads_kernel, rows=rows, slots=slots), "grad_heads", (1,), (table,) + args,
        [whole(table)] + [any_space] * 6, outs, (any_space, any_space), scalars=(info,),
        scratch=tuple(pltpu.VMEM(d, bf16) for d in dims)
        + (pltpu.VMEM((slots * lines, wide), bf16), dma((6,)), dma((3,))),
        flops=4 * seq * width * keep.shape[1],
    )


def stage_kernel(*refs, half, table):
    keep_ref, got_ref = refs[:2]
    outs = refs[3:] if table else refs[2:]
    outs[0][:half, :] = keep_ref[:half, :] + got_ref[:half, :]
    if len(outs) > 1:
        outs[1][:half, :] = keep_ref[half:, :] + got_ref[half : 2 * half, :]
    if table:
        total = refs[2][...] + got_ref[keep_ref.shape[0] :, :]
        if len(outs) > 1:
            outs[1][half:, :] = total
            outs[2][...] = total
        else:
            outs[0][half:, :] = total


def stage(chain, keep, got, last, table, flops, limit):
    count, wide = keep.shape
    extra = 0 if table is None else table.shape[0]
    args = (keep, got) if table is None else (keep, got, table)
    half = count if last else count // 2
    outs = (shape((half + extra, wide), bf16),)
    if not last:
        outs = (shape((half, wide), bf16), shape((half + extra, wide), bf16))
        outs += () if table is None else (shape(table.shape, bf16),)
    return chain.run(
        functools.partial(stage_kernel, half=half, table=table is not None), "sum_stage", (1,),
        args, [whole(a) for a in args], outs, tuple(whole(a) for a in outs), limit=limit, flops=flops,
    )


def split_kernel(*refs, rows, table):
    keep_ref, got_ref = refs[:2]
    outs = refs[3:] if table else refs[2:]
    for at in range(4):
        here = slice(at * rows, (at + 1) * rows)
        outs[at][:rows, :] = keep_ref[here, :] + got_ref[here, :]
    if table:
        total = refs[2][...] + got_ref[4 * rows :, :]
        for out in outs[1:4]:
            out[rows:, :] = total
        outs[4][...] = total


def split(chain, keep, got, table, limit, flops):
    rows, wide = keep.shape[0] // 4, keep.shape[1]
    extra = 0 if table is None else table.shape[0]
    args = (keep, got) if table is None else (keep, got, table)
    outs = (shape((rows, wide), bf16),) + (shape((rows + extra, wide), bf16),) * 3
    outs += () if table is None else (shape(table.shape, bf16),)
    return chain.run(
        functools.partial(split_kernel, rows=rows, table=table is not None), "sum_split", (1,),
        args, [whole(a) for a in args], outs, tuple(whole(a) for a in outs), limit=limit, flops=flops,
    )


def four_kernel(*refs, rows, table):
    keep_ref, *got = refs[:4]
    done_ref = refs[-1]
    total = keep_ref[...].astype(f32)
    for ref in got:
        total = total + ref[:rows, :].astype(f32)
    done_ref[:rows, :] = total.astype(bf16)
    if table:
        total = refs[4][...].astype(f32)
        for ref in got:
            total = total + ref[rows:, :].astype(f32)
        done_ref[rows:, :] = total.astype(bf16)


def four(chain, keep, got, table, limit, flops):
    args = (keep,) + got + (() if table is None else (table,))
    outs = (shape(got[0].shape, bf16),)
    return chain.run(
        functools.partial(four_kernel, rows=keep.shape[0], table=table is not None), "sum_four", (1,),
        args, [whole(a) for a in args], outs, tuple(whole(a) for a in outs), limit=limit, flops=flops,
    )


def factor_stage_kernel(keep_ref, got_ref, left_ref, right_ref, *refs, slots, pairs, rows):
    half = slots // 2
    block = 16 * pairs
    after = slots * rows
    got_right = after + slots * block
    if slots == 1:
        done_ref, = refs
        done_ref[:rows, :] = keep_ref[...] + got_ref[:rows, :]
        done_ref[rows : rows + block, :] = left_ref[...]
        done_ref[rows + block : rows + 2 * block, :] = got_ref[after:got_right, :]
        done_ref[rows + 2 * block : rows + 3 * block, :] = right_ref[...]
        done_ref[rows + 3 * block :, :] = got_ref[got_right:, :]
        return
    keep_out, send_out, left_out, right_out = refs
    middle = half * rows
    keep_out[...] = keep_ref[:middle, :] + got_ref[:middle, :]
    send_out[:middle, :] = keep_ref[middle:, :] + got_ref[middle:after, :]
    for slot in range(slots):
        target, first = (left_out, 0) if slot < half else (send_out, middle)
        first += slot % half * 2 * block
        target[first : first + block, :] = left_ref[slot * block : (slot + 1) * block, :]
        target[first + block : first + 2 * block, :] = got_ref[
            after + slot * block : after + (slot + 1) * block, :
        ]
    right_out[:block, :] = right_ref[...]
    right_out[block:, :] = got_ref[got_right:, :]
    first = middle + half * 2 * block
    send_out[first : first + block, :] = right_ref[...]
    send_out[first + block :, :] = got_ref[got_right:, :]


def factor_stage(chain, keep, got, left, right, limit, flops):
    wide = keep.shape[1]
    pairs = right.shape[0] // 16
    slots = left.shape[0] // (16 * pairs)
    rows = keep.shape[0] // slots
    if slots == 1:
        lines = (rows + 64 * pairs,)
    else:
        half = slots // 2
        lines = (half * rows, half * rows + 32 * half * pairs + 32 * pairs, 32 * half * pairs, 32 * pairs)
    outs = tuple(shape((count, wide), bf16) for count in lines)
    args = (keep, got, left, right)
    return chain.run(
        functools.partial(factor_stage_kernel, slots=slots, pairs=pairs, rows=rows), "sum_stage",
        (1,), args, [whole(a) for a in args], outs, tuple(whole(a) for a in outs), limit=limit,
        flops=flops,
    )


def two_stages(chain, keep, got, left, right, other_keep, other_got, limit, flops):
    wide = keep.shape[1]
    pairs = right.shape[0] // 16
    slots = left.shape[0] // (16 * pairs)
    rows = keep.shape[0] // slots
    half, other = slots // 2, other_keep.shape[0] // 2
    lines = (half * rows, half * rows + 32 * half * pairs + 32 * pairs, 32 * half * pairs, 32 * pairs)
    outs = tuple(shape((count, wide), bf16) for count in lines + (other, other))
    args = (keep, got, left, right, other_keep, other_got)

    def kernel(*refs):
        factor_stage_kernel(*refs[:4], *refs[6:10], slots=slots, pairs=pairs, rows=rows)
        stage_kernel(*refs[4:6], *refs[10:], half=other, table=False)

    done = chain.run(
        kernel, "sum_two_stages", (1,), args, [whole(a) for a in args], outs,
        tuple(whole(a) for a in outs), limit=limit, flops=flops,
    )
    return done[:4], done[4:]


def gain_of(weight, grad):
    return jnp.sum(weight[...].astype(f32) * grad, axis=1, keepdims=True)


def gain_line(total, gain_ref, chip):
    rows = total.shape[0]
    turned = jnp.broadcast_to(total, (rows, tile)).T[0:1]
    gain = row_of(gain_ref)
    width = gain.shape[1]
    mine = pltpu.roll(gain, lax.rem(width - chip * rows, width), 1)[:, :rows]
    return (turned / mine).reshape(rows)


def decoder_kernel(
    info, own_ref, got_ref, wso_ref, wsv_ref, wcq_ref, win_ref, wk_ref, wv_ref,
    gself_ref, gcross_ref, gffn_ref, gfinal_ref,
    sv_ref, so_ref, cq_ref, co_ref, in_ref, out_ref, ck_ref, cv_ref,
    dself_ref, dcross_ref, dffn_ref, dfinal_ref, left_ref, right_ref, *, heads,
):
    chip = info[1]
    count = left_ref.shape[0]
    each = count // 2
    tall, width = out_ref.shape
    rows, hidden = in_ref.shape
    head_dim = width // heads
    half = width // 2
    middle = tall + 16 * each
    for at, ref in enumerate((own_ref, got_ref)):
        here = slice(at * each, (at + 1) * each)
        left_ref[here] = ref[tall:middle, :].astype(f32).reshape(each, 16, half)
        right_ref[here] = ref[middle:, :].astype(f32).reshape(each, 16, half)

    def right(at):
        return jnp.concatenate([right_ref[:, at, :], right_ref[:, 8 + at, :]], axis=1).astype(bf16)

    def left(at):
        lane = at // 16 * tile
        return left_ref[:, at % 16, lane : lane + tile].astype(bf16)[:, :rows]

    pieces = width // tile
    early = [
        jnp.concatenate(
            [left_ref[:, 2 + which * pieces + at, 2 * tile :] for at in range(pieces)], axis=1
        ).astype(bf16)
        for which in range(2)
    ]
    r_z1, r_cq, r_z2, r_cctx = [right(at) for at in range(4)]
    r_sv = dot_t(r_z1, wso_ref[...]).astype(bf16)
    r = [r_sv, r_z1, r_cq, r_z2, early[0], r_cctx, early[1]]
    r_hid = jnp.concatenate([right(4 + at) for at in range(hidden // width)], axis=1)
    l_hid = jnp.concatenate(
        [left_ref[:, 0, 2 * tile :], left_ref[:, 1, 2 * tile :]], axis=1
    ).astype(bf16)[:, :tall]
    sv_ref[...] = t_dot(left(0), r[0])
    dself_ref[...] = gain_line(gain_of(wsv_ref, sv_ref[...]), gself_ref, chip)
    so_ref[...] = t_dot(left(1), r[1])
    cq_ref[...] = t_dot(left(2), r[2])
    dcross_ref[...] = gain_line(gain_of(wcq_ref, cq_ref[...]), gcross_ref, chip)
    co_ref[...] = t_dot(left(3), r[3])
    in_ref[...] = t_dot(left(4), r_hid)
    dffn_ref[...] = gain_line(gain_of(win_ref, in_ref[...]), gffn_ref, chip)
    out_ref[...] = t_dot(l_hid, r[6])
    for head in range(heads):
        spot = slice(head * head_dim, (head + 1) * head_dim)
        ck_ref[:, spot] = t_dot(left(8 + head), r[4][:, spot])
        cv_ref[:, spot] = t_dot(left(8 + heads + head), r[5][:, spot])
    total = gain_of(wk_ref, ck_ref[...]) + gain_of(wv_ref, cv_ref[...])
    dfinal_ref[...] = gain_line(total, gfinal_ref, chip)


def decoder_grads(chain, info, own, got, wso, weights, gains, rows, heads):
    width, hidden = weights[0].shape[0], weights[2].shape[1]
    tall = hidden * rows // width
    each = (own.shape[0] - tall) // 32
    line = shape((rows,), f32)
    flat = shape((rows, width), f32)
    outs = (flat, flat, flat, flat, shape((rows, hidden), f32), shape((tall, width), f32), flat, flat)
    outs += (line,) * 4

    def sliced(array):
        return pl.BlockSpec((rows, array.shape[1]), lambda i, info: (info[1], 0))

    return chain.run(
        functools.partial(decoder_kernel, heads=heads), "decoder_grads",
        (1,), (own, got, wso) + weights + gains,
        [whole(own), whole(got), whole(wso)] + [sliced(a) for a in weights] + [whole(a) for a in gains],
        outs, tuple(whole(a) for a in outs), scalars=(info,), limit=40, free=True,
        scratch=(
            pltpu.VMEM((2 * each, 16, width // 2), f32), pltpu.VMEM((2 * each, 16, width // 2), f32),
        ),
    )


def sides(me, own_ref, got_ref, first, rows):
    own, got = own_ref[first : first + rows, :], got_ref[first : first + rows, :]
    low = jnp.where(me == 0, own, got).astype(f32)
    high = jnp.where(me == 0, got, own).astype(f32)
    return low, high


def finish_kernel(
    info, out_ref, out_got, keep_ref, away_ref, grad_ref, grad_got, row_ref, row_got,
    fout_ref, enc_ref, back_ref, dec_ref, decback_ref,
):
    me = info[0]
    wide = out_ref.shape[1]
    low, high = sides(me, out_ref, out_got, 0, fout_ref.shape[0])
    fout_ref[:, :wide] = low
    fout_ref[:, wide:] = high
    enc_ref[me] = keep_ref[...]
    enc_ref[1 - me] = away_ref[...]
    back_ref[me] = grad_ref[...]
    back_ref[1 - me] = grad_got[...]
    rows_two = lax.broadcasted_iota(jnp.int32, (2, row_ref.shape[1]), 0)
    both = jnp.where(rows_two == me, row_ref[0:1], row_got[0:1])
    dec_ref[...] = both.astype(bf16)
    decback_ref[...] = jnp.where(rows_two == me, row_ref[1:2], row_got[1:2])


def finish(chain, info, tall, out, out_got, keep, away, grad, grad_got, row, row_got):
    width = keep.shape[1]
    half = away.shape[0]
    args = (out, out_got, keep, away, grad, grad_got, row, row_got)
    outs = (
        shape((tall, width), f32), shape((2, half, width), bf16),
        shape((2, half, width), f32), shape((2, width), bf16), shape((2, width), f32),
    )
    specs = [whole(a) for a in args]
    specs[0] = specs[1] = pl.BlockSpec((tall, out.shape[1]), lambda i, info: (0, 0))
    specs[2] = pl.BlockSpec((half, width), lambda i, info: (info[0], 0))
    return chain.run(
        finish_kernel, "finish_activations", (1,),
        args, specs, outs, tuple(whole(a) for a in outs), scalars=(info,), limit=40, free=True,
    )


def finish_mix_kernel(
    info, mix_ref, mix_got, win_ref, gain_ref, fin_ref, o_ref, dffn_ref, *, rows, steps
):
    me = info[0]
    wide = mix_ref.shape[1]
    for at in range(steps):
        low, high = sides(me, mix_ref, mix_got, at * rows, rows)
        fin_ref[:, at * wide : (at + 1) * wide] = low
        fin_ref[:, (steps + at) * wide : (steps + at + 1) * wide] = high
    low, high = sides(me, mix_ref, mix_got, steps * rows, rows)
    o_ref[:, :wide] = low
    o_ref[:, wide:] = high
    dffn_ref[...] = gain_line(gain_of(win_ref, fin_ref[...]), gain_ref, info[1])


def finish_mix(chain, info, mix, mix_got, win, gain, rows):
    width, hidden = win.shape
    args = (mix, mix_got, win, gain)
    outs = (shape((rows, hidden), f32), shape((rows, width), f32), shape((rows,), f32))
    specs = [whole(a) for a in args]
    specs[2] = pl.BlockSpec((rows, hidden), lambda i, info: (info[1], 0))
    return chain.run(
        functools.partial(finish_mix_kernel, rows=rows, steps=hidden // 2 // mix.shape[1]),
        "finish_mixed", (1,),
        args, specs, outs, tuple(whole(a) for a in outs), scalars=(info,), limit=40, free=True,
    )


def last_kernel(
    info, sum_ref, got_ref, wq_ref, wk_ref, wv_ref, gain_ref,
    q_ref, k_ref, v_ref, d_ref, table_ref, *, rows, heads,
):
    me = info[0]
    wide = sum_ref.shape[1]
    outs = (q_ref, k_ref, v_ref)
    for at, ref in enumerate(outs):
        low, high = sides(me, sum_ref, got_ref, at * rows, rows)
        ref[:, :wide] = low
        ref[:, wide:] = high
    total = sum(gain_of(w, ref[...]) for w, ref in zip((wq_ref, wk_ref, wv_ref), outs))
    d_ref[...] = gain_line(total, gain_ref, info[1])
    first = 3 * rows
    table = sum_ref[first:, :tile].astype(f32) + got_ref[first:, :tile].astype(f32)
    part = heads // 2
    table_ref[:part, :] = table[:part, : table_ref.shape[1]]
    table_ref[part:, :] = table[8 : 8 + part, : table_ref.shape[1]]


def last(chain, info, done, got, wq, wk, wv, gain, rows, buckets, heads):
    width = wq.shape[0]
    flat = shape((rows, width), f32)
    args = (done, got, wq, wk, wv, gain)
    outs = (flat, flat, flat, shape((rows,), f32), shape((heads, buckets), f32))
    specs = [whole(a) for a in args]
    for at in (2, 3, 4):
        specs[at] = pl.BlockSpec((rows, args[at].shape[1]), lambda i, info: (info[1], 0))
    return chain.run(
        functools.partial(last_kernel, rows=rows, heads=heads), "finish_last", (1,), args, specs,
        outs, tuple(whole(a) for a in outs), scalars=(info,), limit=40, free=True,
    )


def plain_grad(me, place, pieces, tall):
    parts = []
    for left, left_got, right, right_got, offset in pieces:
        wide = right_got.shape[1]
        keep = lax.dynamic_slice_in_dim(right, me * wide, wide, 1) if offset else right
        total = t_dot(
            jnp.concatenate([left, left_got]), jnp.concatenate([keep, right_got])
        ).astype(bf16)
        slots = place.shape[0]
        if tall:
            parts.append(total.reshape(slots, -1, wide))
        else:
            half = left.shape[1] // 2
            for at in range(0, wide, half):
                parts.append(total[:, at : at + half].reshape(slots, -1, half))
    total = jnp.concatenate(parts, axis=1)
    order = jnp.zeros_like(place).at[place].set(jnp.arange(place.shape[0], dtype=jnp.int32))
    return jnp.take(total, order, axis=0)


def plain_sides(me, done, got):
    low = jnp.where(me == 0, done, got).astype(f32)
    high = jnp.where(me == 0, got, done).astype(f32)
    return low, high


def body(
    enc_in,
    dec_in,
    lengths,
    cot_enc,
    cot_dec,
    enc_gain_attn,
    enc_query,
    enc_key,
    enc_value,
    enc_output,
    relative_bias_table,
    enc_gain_ffn,
    enc_ff_in,
    enc_ff_out,
    enc_gain_final,
    dec_gain_self,
    dec_self_value,
    dec_self_output,
    dec_gain_cross,
    dec_cross_query,
    dec_cross_key,
    dec_cross_value,
    dec_cross_output,
    dec_gain_ffn,
    dec_ff_in,
    dec_ff_out,
):
    pair_count, seq_dev, width = enc_in.shape
    seq_all = 2 * seq_dev
    bucket_count, heads = relative_bias_table.shape
    head_dim = width // heads
    hidden = enc_ff_in.shape[1]
    slots = lax.axis_size("batch")
    me = lax.axis_index("blk")
    chip = lax.axis_index("batch")
    stages = slots.bit_length() - 1
    rows = width // slots
    aligned = rows % 16 == 0
    chain = Chain()

    def across(array):
        return lax.ppermute(array, "blk", [(0, 1), (1, 0)])

    info = jnp.stack([me, chip]).astype(jnp.int32)
    order = list(range(stages))
    crossed = order if stages < 2 else [1, 0] + order[2:]
    def hop(array, *steps):
        pairs = []
        for which in range(slots):
            for core in range(2):
                mask = sum(1 << (order, crossed)[core][step] for step in steps)
                pairs.append((which * 2 + core, (which ^ mask) * 2 + core))
        return lax.ppermute(array, ("batch", "blk"), pairs)

    class Sum:
        def __init__(self, keep, send, table=None, factors=None):
            self.keep, self.table, self.at = keep, table, 0
            self.direct = aligned and table is not None and stages >= 4
            self.total = stages - 1 if self.direct else stages
            self.factors = factors
            self.got = hop(send, 0)

        def step(self, limit=24, flops=0):
            if self.at == self.total:
                return
            self.at += 1
            last = self.at == self.total
            apart = self.direct and self.at == stages - 2
            if self.factors is not None:
                outs = factor_stage(chain, self.keep, self.got, *self.factors, limit, flops)
                self.factors = outs[2:]
            elif apart:
                outs = split(chain, self.keep, self.got, self.table, limit, flops)
            elif last and self.direct:
                outs = four(chain, self.keep, self.got, self.table, limit, flops)
            elif aligned:
                outs = list(stage(chain, self.keep, self.got, last, self.table, flops, limit))
            else:
                total = self.keep + self.got
                half = total.shape[0] // 2
                outs = [total] if last else [total[:half], total[half:]]
            self.take(outs)

        def take(self, outs):
            last = self.at == self.total
            apart = self.direct and self.at == stages - 2
            self.keep = outs[0]
            if self.table is not None and not last and aligned:
                self.table = outs[-1]
            if last:
                self.done = self.keep
                self.other = across(self.done)
            elif apart:
                first, then = self.at, self.at + 1
                self.got = (hop(outs[1], then), hop(outs[2], first), hop(outs[3], first, then))
            else:
                self.got = hop(outs[1], self.at)

        def rest(self):
            while self.at < self.total:
                self.step()

    def plain_sum(pieces, tall):
        relative = chip ^ jnp.arange(slots, dtype=jnp.int32)
        total = plain_grad(me, spot_in(me, relative, stages).astype(jnp.int32), pieces, tall)
        total = total.reshape(-1, total.shape[-1])
        half = total.shape[0] // 2
        return Sum(total[:half], total[half:])

    enc_got = across(enc_in)
    cot_got = across(cot_enc)
    state, key_query = before(
        chain, info, dec_in, dec_gain_self, dec_gain_cross, dec_self_value, dec_self_output,
        dec_cross_query, dec_cross_key, head_dim,
    )

    (
        scale, ge_low, ge_away, dec_lines, dec_long, key_mix, mix,
        n1, q_turned, k, v, weights, context, y1, n2, hid, slope, result_low, out_away,
    ) = encoder(
        chain, info, lengths, enc_in, enc_got, enc_gain_attn, enc_query, enc_key, enc_value,
        relative_bias_table.T, enc_gain_ffn, enc_gain_final, enc_output, enc_ff_in, enc_ff_out, heads,
        cot_enc, cot_got, (key_query, state, cot_dec, dec_gain_ffn),
        (dec_cross_value, dec_cross_output, dec_ff_in, dec_ff_out),
    )
    ge_got = across(ge_away)
    hid_got, n2_got, ctx_got, n1_got = (across(part) for part in (hid, n2, context, n1))
    out_got = across(out_away)

    dec_rows, *packed = after(
        chain, info, key_mix, state, dec_lines, dec_long, mix, dec_gain_self, dec_gain_cross,
        (dec_cross_key, dec_cross_query, dec_self_output, dec_self_value, dec_ff_out),
        head_dim, heads, slots if aligned else 0,
    )
    dec_got = across(dec_rows)

    if aligned:
        left_send, left_keep, right = packed
        sum_out = Sum(
            *tall_grad(chain, info, slots, hid, hid_got, ge_low, ge_got, left_send),
            factors=(left_keep, right),
        )
    else:
        sum_out = plain_sum([(hid, hid_got, ge_low, ge_got, True)], True)
    *ga_away, ga_keep, gy_low, gy_away, g_ctx = backward(
        chain, info, ge_low, slope, enc_ff_out, enc_ff_in, y1, enc_gain_ffn, enc_output
    )
    ga_got, gy_got = tuple(across(part) for part in ga_away), across(gy_away)
    sum_out.step(64)
    if aligned:
        sum_mix = Sum(
            *mixed_grad(
                chain, info, slots, n2, n2_got, context, ctx_got, ga_keep, ga_got, gy_low, gy_got
            ),
        )
    else:
        sum_mix = plain_sum(
            [(n2, n2_got, ga_keep, jnp.concatenate(ga_got, axis=1), False), (context.T, ctx_got.T, gy_low, gy_got, True)], False
        )
    sum_out.step(64)
    grad_keep, grad_away, table_term, *g_away, g_keep = attention_back(
        chain, info, scale, enc_gain_attn, enc_in, enc_got, q_turned, k, v, context, g_ctx, weights,
        enc_query, enc_key, enc_value, gy_low,
    )
    g_got = tuple(across(part) for part in g_away)
    grad_got = across(grad_away)
    if aligned:
        sum_out.at, sum_mix.at = sum_out.at + 1, sum_mix.at + 1
        for_out, for_mix = two_stages(
            chain, sum_out.keep, sum_out.got, *sum_out.factors, sum_mix.keep, sum_mix.got, 64, large
        )
        sum_out.factors = for_out[2:]
        sum_out.take(for_out)
        sum_mix.take(for_mix)
    else:
        sum_out.step()
        sum_mix.step()
    if aligned:
        sum_heads = Sum(
            *heads_grad(chain, info, slots, n1, n1_got, g_keep, g_got, table_term), table_term
        )
    else:
        sum_heads = plain_sum([(n1, n1_got, g_keep, jnp.concatenate(g_got, axis=1), False)], False)
        table_sum = lax.psum(table_term.astype(f32), ("batch", "blk"))

    dec_weights = (dec_self_value, dec_cross_query, dec_ff_in, dec_cross_key, dec_cross_value)
    dec_gains = (dec_gain_self, dec_gain_cross, dec_gain_ffn, enc_gain_final)

    def mine(array):
        return lax.dynamic_slice_in_dim(array, chip * (array.shape[0] // slots), array.shape[0] // slots, 0)

    sum_mix.step()
    sum_out.step(24, large)
    sum_heads.step()
    sum_out.rest()
    if aligned:
        sum_mix.step(24, large)
        sum_heads.step()
        grad_ff_out, encoder_output, grad_in, dec_out, grad_dec = finish(
            chain, info, hidden // slots, sum_out.done, sum_out.other, result_low, out_got, grad_keep,
            grad_got, dec_rows, dec_got,
        )
        dec_outs = decoder_grads(
            chain, info, sum_out.done, sum_out.other, dec_self_output, dec_weights, dec_gains, rows, heads
        )
        (grad_self_value, grad_self_output, grad_cross_query, grad_cross_output) = dec_outs[:4]
        (grad_dec_ff_in, grad_dec_ff_out, grad_cross_key, grad_cross_value) = dec_outs[4:8]
        gain_self, gain_cross, gain_dec_ffn, gain_final = dec_outs[8:]
        sum_heads.rest()
        sum_mix.rest()
        grad_ff_in, grad_output, gain_ffn = finish_mix(
            chain, info, sum_mix.done, sum_mix.other, enc_ff_in, enc_gain_ffn, rows
        )
        sum_heads.rest()
        grad_query, grad_key, grad_value, gain_attn, grad_rel_table = last(
            chain, info, sum_heads.done, sum_heads.other, enc_query, enc_key, enc_value,
            enc_gain_attn, rows, bucket_count, heads,
        )
        grad_rel_table = grad_rel_table.T
    else:
        sum_mix.rest()
        sum_heads.rest()
        table = lax.all_gather(packed[0], ("batch", "blk"), axis=0, tiled=False)
        count = hidden // width
        tall = hidden // slots
        r = [table[:, at] for at in range(4)]
        r = [dot_t(r[0], dec_self_output).astype(bf16)] + r[:3] + [table[:, 8], r[3], table[:, 9]]
        r_hid = table[:, 4 : 4 + count].reshape(-1, hidden)
        chosen = lax.dynamic_slice_in_dim(table[:, 16:48], chip * rows, rows, 2)
        l = [chosen[:, at] for at in range(5)]
        l_hid = table[:, 48 : 48 + count].reshape(-1, hidden)
        l_hid = lax.dynamic_slice_in_dim(l_hid, chip * tall, tall, 1)
        grad_self_value, grad_self_output = t_dot(l[0], r[0]), t_dot(l[1], r[1])
        grad_cross_query, grad_cross_output = t_dot(l[2], r[2]), t_dot(l[3], r[3])
        grad_dec_ff_in = t_dot(l[4], r_hid)
        grad_dec_ff_out = t_dot(l_hid, r[6])
        many = chosen[:, 8 : 8 + 2 * heads].reshape(-1, 2, heads, rows)
        grad_cross_key, grad_cross_value = (
            jnp.einsum(
                "phd,phe->dhe", many[:, at], r[4 + at].reshape(-1, heads, head_dim),
                preferred_element_type=f32,
            ).reshape(rows, width)
            for at in range(2)
        )

        def gain_plain(gain, *terms):
            return sum(jnp.sum(mine(w).astype(f32) * g, axis=1) for w, g in terms) / mine(gain)

        gain_self = gain_plain(dec_gain_self, (dec_self_value, grad_self_value))
        gain_cross = gain_plain(dec_gain_cross, (dec_cross_query, grad_cross_query))
        gain_dec_ffn = gain_plain(dec_gain_ffn, (dec_ff_in, grad_dec_ff_in))
        gain_final = gain_plain(
            enc_gain_final, (dec_cross_key, grad_cross_key), (dec_cross_value, grad_cross_value)
        )
        sum_mix.rest()
        sum_heads.rest()
        grad_ff_out = jnp.concatenate(plain_sides(me, sum_out.done, sum_out.other), axis=1)
        low, high = plain_sides(me, sum_mix.done, sum_mix.other)

        def pick(side, at):
            return side[at * rows : (at + 1) * rows]

        grad_ff_in = jnp.concatenate(
            [pick(side, at) for side in (low, high) for at in range(low.shape[0] // rows - 1)], axis=1
        )
        spot = low.shape[0] // rows - 1
        grad_output = jnp.concatenate([pick(low, spot), pick(high, spot)], axis=1)
        low, high = plain_sides(me, sum_heads.done, sum_heads.other)
        grad_query, grad_key, grad_value = (
            jnp.concatenate([pick(low, at), pick(high, at)], axis=1) for at in range(3)
        )
        gain_ffn = gain_plain(enc_gain_ffn, (enc_ff_in, grad_ff_in))
        gain_attn = gain_plain(
            enc_gain_attn, (enc_query, grad_query), (enc_key, grad_key), (enc_value, grad_value)
        )
        turned = table_sum.T[:bucket_count]
        grad_rel_table = jnp.concatenate([turned[:, : heads // 2], turned[:, 8 : 8 + heads // 2]], axis=1)

        def stacked(own, got):
            return jnp.where(me == 0, jnp.stack([own, got]), jnp.stack([got, own]))

        out_keep = lax.dynamic_slice_in_dim(result_low, me * seq_dev, seq_dev, 0)
        encoder_output, grad_in = stacked(out_keep, out_got), stacked(grad_keep, grad_got)
        dec_out = stacked(dec_rows[0], dec_got[0]).astype(bf16)
        grad_dec = stacked(dec_rows[1], dec_got[1])

    return (
        encoder_output,
        dec_out,
        grad_in,
        grad_dec,
        gain_attn,
        grad_query,
        grad_key,
        grad_value,
        grad_output,
        grad_rel_table,
        gain_ffn,
        grad_ff_in,
        grad_ff_out,
        gain_final,
        gain_self,
        grad_self_value,
        grad_self_output,
        gain_cross,
        grad_cross_query,
        grad_cross_key,
        grad_cross_value,
        grad_cross_output,
        gain_dec_ffn,
        grad_dec_ff_in,
        grad_dec_ff_out,
    )


def solution(mesh):
    split = P("batch", "blk", None)
    rows = P("batch", None)
    line = P("batch")
    placed = (split, rows, line, split, rows) + (P(),) * 21
    return jax.shard_map(
        body,
        mesh=mesh,
        in_specs=placed,
        out_specs=(
            (split, rows, split, rows, line, rows, rows, rows, rows, P(), line, rows, rows, line)
            + (line, rows, rows, line, rows, rows, rows, rows, line, rows, rows)
        ),
        check_vma=False,
    )
```

```python
import functools

import jax
import jax.numpy as jnp
from jax import lax
from jax.experimental import pallas as pl
from jax.experimental.pallas import tpu as pltpu
from jax.sharding import PartitionSpec as P

epsilon = 1e-06
masked_score = -1e30
thresholds = (12, 16, 23, 32, 46, 64, 91)
bf16 = jnp.bfloat16
f32 = jnp.float32
tile = 128
chunk = 32
mib = 1 << 20
large = 5 * 10**9


def bucket_of(offset):
    distance = jnp.abs(offset)
    larger = jnp.full(offset.shape, 8, jnp.int32)
    for limit in thresholds:
        larger = larger + jnp.where(distance >= limit, 1, 0)
    inner = jnp.where(distance < 8, distance, larger)
    return jnp.where(offset > 0, 16, 0) + inner


def norm_scale(values):
    return lax.rsqrt(jnp.mean(values * values, axis=-1, keepdims=True) + epsilon)


def norm_apply(values, gain):
    return values * norm_scale(values) * gain


def norm_back(values, gain, upstream):
    scale = norm_scale(values)
    weighted = upstream * gain
    inner = jnp.mean(weighted * values, axis=-1, keepdims=True)
    return scale * weighted - values * (scale * scale * scale * inner)


def gelu_parts(a):
    root = 0.7978845608028654
    square = a * a
    t = jnp.tanh(root * a * (1.0 + 0.044715 * square))
    half = 0.5 + 0.5 * t
    slope = half + (half * (1.0 - t)) * (a * (root + (3 * 0.044715 * root) * square))
    return a * half, slope


def dot(left, right, dims=((1,), (0,))):
    return lax.dot_general(left, right, (dims, ((), ())), preferred_element_type=f32)


def dot_t(left, right):
    return dot(left, right, ((1,), (1,)))


def t_dot(left, right):
    return dot(left, right, ((0,), (0,)))


def shape(dims, kind):
    return jax.ShapeDtypeStruct(dims, kind)


def whole(array, buffers=None):
    zeros = (0,) * array.ndim
    if buffers is None:
        return pl.BlockSpec(array.shape, lambda *at: zeros)
    return pl.BlockSpec(array.shape, lambda *at: zeros, pipeline_mode=pl.Buffered(buffers))


class Chain:
    def __init__(self):
        self.last = ()

    def run(
        self, kernel, name, grid, args, in_specs, outs, out_specs, scalars=(), scratch=(),
        flops=0, limit=64, also=(), free=False,
    ):
        size = 0 if free else sum(a.size * a.dtype.itemsize for a in list(args) + list(outs))
        last = self.last + also
        skip = len(scalars) + len(args)

        def inner(*refs):
            kernel(*refs[:skip], *refs[skip + len(last) :])

        done = pl.pallas_call(
            inner,
            out_shape=outs,
            grid_spec=pltpu.PrefetchScalarGridSpec(
                num_scalar_prefetch=len(scalars),
                grid=grid,
                in_specs=list(in_specs) + [pl.BlockSpec(memory_space=pl.ANY)] * len(last),
                out_specs=out_specs,
                scratch_shapes=scratch,
            ),
            compiler_params=pltpu.CompilerParams(
                vmem_limit_bytes=limit * mib, dimension_semantics=("arbitrary",) * len(grid)
            ),
            cost_estimate=pl.CostEstimate(
                flops=int(4 * flops), bytes_accessed=int(size), transcendentals=0
            ),
            name=name,
        )(*scalars, *args, *last)
        self.last = (done[0],)
        return done


any_space = pl.BlockSpec(memory_space=pl.ANY)
dma = pltpu.SemaphoreType.DMA


def row_of(gain_ref):
    return gain_ref[...].reshape(1, -1)


def fetch(pairs, sems, first=None):
    copies = [
        pltpu.make_async_copy(source, target, sems.at[at])
        for at, (source, target) in enumerate(pairs)
    ]
    for copy in copies[:first]:
        copy.start()
    return copies


def picked(me, ref):
    rows = ref[...].astype(f32)
    return jnp.where(me == 0, rows[0:1], rows[1:2])


def joined(me, own, got):
    first = jnp.where(me == 0, own, got)
    last = jnp.where(me == 0, got, own)
    return jnp.concatenate([first, last], axis=0)


def wide_row(row):
    return jnp.broadcast_to(row.astype(bf16), (16, row.shape[1]))


def row_dot(row, weight):
    return dot(wide_row(row), weight)[0:1]


def row_dot_t(row, weight):
    return dot_t(wide_row(row), weight)[0:1]


def head_mask(width, head_dim):
    rows = lax.broadcasted_iota(jnp.int32, (16, width), 0)
    lanes = lax.broadcasted_iota(jnp.int32, (16, width), 1)
    return (lanes >= rows * head_dim) & (lanes < (rows + 1) * head_dim)


def spread(row, mask):
    return jnp.where(mask, jnp.broadcast_to(row, mask.shape), 0.0).astype(bf16)


def encoder_kernel(
    info, lens, gain_ref, table_ref, ffn_ref, final_ref,
    kq_ref, state_ref, cot_ref, dec_gain_ref,
    own_any, got_any, wq_any, wk_any, wv_any, wo_any, win_any, wout_any,
    cot_own_any, cot_got_any, dec_wv_any, dec_wco_any, dec_win_any, dec_wout_any,
    scale_ref, ge_ref, geaway_ref, rows_ref, long_ref, keymix_ref, mix_ref,
    n1_any, qt_any, k_any, v_any, e_any, ctx_any, y1_any, n2_any, hid_any, slope_any, low_any, away_any,
    x_ref, n1_ref, qt_ref, k_ref, v_ref, e_ref, ctx_ref, y1_ref, n2_ref, hid_ref, slope_ref,
    acc_ref, low_ref, away_ref, bias_ref, s_ref, wq_ref, wk_ref, wv_ref, wo_ref, win_ref, wout_ref, cot_x_ref,
    dec_wv, dec_wco, dec_win, dec_wout, sems, out_sems, x_sems, dec_sems, up_sems,
    *, heads, group,
):
    me = info[0]
    seq, width = x_ref.shape
    head_dim = width // heads
    blocks = seq // tile
    parts, _, piece = win_ref.shape
    many = parts * piece // width
    wide = group * head_dim
    rounds = heads // group

    loads = []
    for at in range(rounds):
        spot = pl.ds(at * wide, wide)
        for any_ref, ref in ((wq_any, wq_ref), (wk_any, wk_ref), (wv_any, wv_ref)):
            loads.append((any_ref.at[:, spot], ref.at[at]))
    loads.append((wo_any, wo_ref))
    for at in range(parts):
        spot = pl.ds(at * piece, piece)
        loads.append((win_any.at[:, spot], win_ref.at[at]))
        loads.append((wout_any.at[spot, :], wout_ref.at[at]))
    loads = [
        pltpu.make_async_copy(source, target, sems.at[at])
        for at, (source, target) in enumerate(loads)
    ]
    first = fetch(
        ((own_any.at[me], x_ref.at[pl.ds(me * (seq // 2), seq // 2), :]),
         (got_any.at[me], x_ref.at[pl.ds((1 - me) * (seq // 2), seq // 2), :])), x_sems
    )
    for copy in loads[: 3 * rounds]:
        copy.start()
    saved = []

    def save(source, target):
        copy = pltpu.make_async_copy(source, target, out_sems.at[len(saved)])
        copy.start()
        saved.append(copy)

    tables = jnp.concatenate(
        [table_ref[...], jnp.zeros((heads, tile - table_ref.shape[1]), f32)], axis=1
    )
    rows = lax.broadcasted_iota(jnp.int32, (tile, tile), 0)
    lanes = lax.broadcasted_iota(jnp.int32, (tile, tile), 1)
    kinds = [bucket_of((gap - 1) * tile + rows - lanes) for gap in range(3)]
    for head in range(heads):
        line = jnp.broadcast_to(tables[head : head + 1, :], (tile, tile))
        for gap in range(3):
            bias_ref[head, gap] = jnp.take_along_axis(line, kinds[gap], axis=1)

    for copy in first:
        copy.wait()
    n1_ref[...] = norm_apply(x_ref[...].astype(f32), row_of(gain_ref)).astype(bf16)
    save(n1_ref, n1_any)

    pair_rows = lax.broadcasted_iota(jnp.int32, (2 * head_dim, seq), 0)
    pair_lanes = lax.broadcasted_iota(jnp.int32, (seq, 2 * head_dim), 1)
    key_at = lax.broadcasted_iota(jnp.int32, (seq, 2 * head_dim), 0)
    gone = jnp.where(key_at < lens[me], 0.0, masked_score).astype(bf16)
    ones = jnp.ones((16, seq), bf16)
    vts = {}

    def project(at):
        n1 = n1_ref[...]
        for copy in loads[3 * at : 3 * at + 3]:
            copy.wait()
        for copy in loads[3 * rounds + 3 * at : 3 * rounds + 3 * at + 3]:
            copy.start()
        spot = slice(at * wide, (at + 1) * wide)
        qt_ref[spot, :] = dot(n1, wq_ref[at]).T.astype(bf16)
        k_ref[:, spot] = dot(n1, wk_ref[at]).astype(bf16)
        v = dot(n1, wv_ref[at])
        v_ref[:, spot] = v.astype(bf16)
        vts[at] = v.T.astype(bf16)

    def scores(head):
        pair = slice(head // 2 * 2 * head_dim, (head // 2 + 1) * 2 * head_dim)
        k2, q2 = k_ref[:, pair], qt_ref[pair, :]
        zero = jnp.zeros((), bf16)
        if head % 2 == 0:
            k2 = jnp.where(pair_lanes < head_dim, k2, jnp.where(pair_lanes == head_dim, gone, zero))
            q2 = jnp.where(pair_rows < head_dim, q2, jnp.ones((), bf16))
        else:
            k2 = jnp.where(pair_lanes >= head_dim, k2, jnp.where(pair_lanes == 0, gone, zero))
            q2 = jnp.where(pair_rows >= head_dim, q2, jnp.ones((), bf16))
        middle = seq // 2
        s_ref[head % 2, :, :middle] = dot(k2, q2[:, :middle])
        yield
        s_ref[head % 2, :, middle:] = dot(k2, q2[:, middle:])
        yield

    def weigh(head):
        slot = head % 2
        before = tables[head : head + 1, 15:16]
        after = tables[head : head + 1, 31:32]
        for query in range(blocks):
            yield
            across = slice(query * tile, (query + 1) * tile)
            tops = None
            for key in range(blocks):
                gap = key - query
                bias = before if gap < -1 else after if gap > 1 else bias_ref[head, gap + 1]
                down = slice(key * tile, (key + 1) * tile)
                value = s_ref[slot, down, across] + bias
                s_ref[slot, down, across] = value
                top = jnp.max(value.reshape(tile // 8, 8, tile), axis=0)
                tops = top if tops is None else jnp.maximum(tops, top)
            peak = jnp.max(tops, axis=0, keepdims=True)
            for key in range(blocks):
                down = slice(key * tile, (key + 1) * tile)
                e_ref[head, down, across] = jnp.exp(s_ref[slot, down, across] - peak).astype(bf16)
        save(e_ref.at[head], e_any.at[head])

    def mix(head):
        at, inner = divmod(head, group)
        vt = vts[at][inner * head_dim : (inner + 1) * head_dim]
        full = dot(jnp.concatenate([vt, ones], axis=0), e_ref[head])
        scale = 1.0 / full[head_dim : head_dim + 1]
        scale_ref[head : head + 1, :] = scale
        ctx_ref[head * head_dim : (head + 1) * head_dim, :] = (full[:head_dim] * scale).astype(bf16)

    project(0)
    wide_loads = fetch(
        tuple((dec_wout_any.at[pl.ds(at * width, width), :], dec_wout.at[at]) for at in range(many)),
        up_sems,
    )
    cot = picked(me, cot_ref)
    ups = []
    for _ in scores(0):
        pass
    for head in range(heads):
        if head % group == 0 and head // group + 1 < rounds:
            project(head // group + 1)
        ahead = scores(head + 1) if head + 1 < heads else iter(())
        for step, _ in enumerate(weigh(head)):
            if step == 1 and head:
                mix(head - 1)
            elif step > 1:
                next(ahead, None)
        for _ in ahead:
            pass
        if head % 2 and len(ups) < many:
            wide_loads[len(ups)].wait()
            ups.append(row_dot_t(cot, dec_wout[len(ups)]))
    mix(heads - 1)
    scale_ref[heads:, :] = jnp.zeros((16 - heads, seq), f32)
    save(qt_ref, qt_any)
    save(k_ref, k_any)
    save(v_ref, v_any)
    save(ctx_ref, ctx_any)

    loads[3 * rounds].wait()
    y1 = x_ref[...].astype(f32) + t_dot(ctx_ref[...], wo_ref[...])
    acc_ref[...] = y1
    y1_ref[...] = y1.astype(bf16)
    n2_ref[...] = norm_apply(y1, row_of(ffn_ref)).astype(bf16)
    save(y1_ref, y1_any)
    save(n2_ref, n2_any)
    for at in range(parts):
        spot = pl.ds(at * piece, piece)
        loads[3 * rounds + 1 + 2 * at].wait()
        if at == 1:
            late = fetch(
                (
                    (dec_wv_any, dec_wv), (dec_wco_any, dec_wco), (dec_win_any, dec_win),
                    (cot_own_any.at[me], cot_x_ref.at[pl.ds(me * (seq // 2), seq // 2), :]),
                    (cot_got_any.at[me], cot_x_ref.at[pl.ds((1 - me) * (seq // 2), seq // 2), :]),
                ),
                dec_sems,
            )
        value, slope = gelu_parts(dot(n2_ref[...], win_ref[at]))
        hid_ref[at] = value.astype(bf16)
        slope_ref[at] = slope.astype(bf16)
        save(hid_ref.at[at], hid_any.at[:, spot])
        save(slope_ref.at[at], slope_any.at[:, spot])
        loads[3 * rounds + 2 + 2 * at].wait()
        acc_ref[...] += dot(hid_ref[at], wout_ref[at])
    result = acc_ref[...]
    low = result.astype(bf16)
    low_ref[...] = low
    half = seq // 2
    away_ref[...] = jnp.where(me == 0, low[half:], low[:half])
    save(away_ref, away_any)
    save(low_ref, low_any)
    src = norm_apply(result, row_of(final_ref)).astype(bf16)

    gain = row_of(dec_gain_ref)
    mask = head_mask(width, head_dim)
    lanes = lax.broadcasted_iota(jnp.int32, (16, seq), 1)
    c = jnp.where(lanes < lens[me], dot_t(kq_ref[...], src), masked_score)
    c = jnp.exp(c - jnp.max(c, axis=-1, keepdims=True))
    c = c * (1.0 / jnp.sum(c, axis=-1, keepdims=True))
    c_low = c.astype(bf16)
    mixed = dot(c_low, src).astype(bf16)
    mix_ref[...] = mixed
    late[0].wait()
    cctx = jnp.sum(jnp.where(mask, dot(mixed, dec_wv[...]), 0.0), axis=0, keepdims=True)
    cctx = cctx.astype(bf16).astype(f32)
    late[1].wait()
    z2 = state_ref[3:4, :] + row_dot(cctx, dec_wco[...])
    m3 = norm_apply(z2, gain).astype(bf16).astype(f32)
    late[2].wait()
    dh, slope = gelu_parts(row_dot(m3, dec_win[...]))
    g_b = (slope * jnp.concatenate(ups, axis=1)).astype(bf16).astype(f32)
    gz2 = cot + norm_back(z2, gain, row_dot_t(g_b, dec_win[...]))
    g_cctx = row_dot_t(gz2, dec_wco[...]).astype(bf16).astype(f32)
    up = dot_t(spread(g_cctx, mask), dec_wv[...]).astype(bf16)
    d_c = dot_t(up, src)
    g_c = (c * (d_c - jnp.sum(c * d_c, axis=-1, keepdims=True))).astype(bf16)
    src_up = t_dot(
        jnp.concatenate([g_c, c_low], axis=0), jnp.concatenate([kq_ref[...], up], axis=0)
    )
    late[3].wait()
    late[4].wait()
    back = norm_back(acc_ref[...], row_of(final_ref), src_up)
    ge = (cot_x_ref[...].astype(f32) + back).astype(bf16)
    ge_ref[...] = ge
    middle = width // 2
    geaway_ref[...] = jnp.where(me == 0, ge[:, middle:], ge[:, :middle])
    keymix_ref[...] = dot(g_c, src).astype(bf16)
    for at, row in enumerate((cctx, z2, m3, gz2, g_cctx, cot)):
        rows_ref[at : at + 1, :] = row
    rows_ref[6:8, :] = jnp.zeros((2, width), f32)
    long_ref[0:1, :] = dh
    long_ref[1:2, :] = g_b
    for copy in saved:
        copy.wait()


def encoder(
    chain, info, lens, enc_in, got, gain, wq, wk, wv, table, ffn, final, wo, win, wout, heads,
    cot_enc, cot_got, decoder, dec_weights,
):
    pairs, seq_dev, width = enc_in.shape
    seq = 2 * seq_dev
    hidden = win.shape[1]
    group = 4
    rounds = heads // group
    wide = width // rounds
    piece = 2 * width
    parts, many = hidden // piece, hidden // width
    act, turned = shape((seq, width), bf16), shape((width, seq), bf16)
    part, tall = shape((seq_dev, width), bf16), shape((seq, hidden), bf16)
    few, hat = shape((16, width), bf16), shape((seq, width // 2), bf16)
    near = (shape((16, seq), f32), act, hat)
    near += (shape((8, width), f32), shape((2, hidden), f32), few, few)
    far = (act, turned, act, act, shape((heads, seq, seq), bf16), turned, act, act, tall, tall, act, part)
    small = (gain, table, ffn, final) + decoder

    def vmem(dims, kind=bf16):
        return pltpu.VMEM(dims, kind)

    return chain.run(
        functools.partial(encoder_kernel, heads=heads, group=group),
        "encoder_forward",
        (1,),
        small + (enc_in, got, wq, wk, wv, wo, win, wout, cot_enc, cot_got) + dec_weights,
        [whole(a) for a in small] + [any_space] * 14,
        near + far,
        tuple(whole(a) for a in near) + (any_space,) * len(far),
        scalars=(info, lens),
        scratch=(
            vmem((seq, width)), vmem((seq, width)), vmem((width, seq)), vmem((seq, width)),
            vmem((seq, width)), vmem((heads, seq, seq)), vmem((width, seq)), vmem((seq, width)),
            vmem((seq, width)), vmem((parts, seq, piece)), vmem((parts, seq, piece)),
            vmem((seq, width), f32), vmem((seq, width)), vmem((seq_dev, width)),
            vmem((heads, 3, tile, tile), f32), vmem((2, seq, seq), f32),
            vmem((rounds, width, wide)), vmem((rounds, width, wide)), vmem((rounds, width, wide)),
            vmem((width, width)), vmem((parts, width, piece)), vmem((parts, piece, width)),
            vmem((seq, width)),
        )
        + tuple(vmem(w.shape) for w in dec_weights[:3])
        + (
            vmem((many, width, width)),
            dma((3 * rounds + 1 + 2 * parts,)), dma((9 + heads + 2 * parts,)), dma((2,)), dma((5,)), dma((many,)),
        ),
        flops=2 * seq * width * (4 * width + 2 * hidden) + 16 * seq * seq * width,
    )


def before_kernel(
    info, dec_ref, self_ref, cross_ref, wsv_any, wso_any, wcq_any, wk_any,
    state_ref, kq_ref, wsv, wso, wcq, wk, sems, *, head_dim,
):
    copies = fetch(((wsv_any, wsv), (wso_any, wso), (wcq_any, wcq), (wk_any, wk)), sems)
    x = picked(info[0], dec_ref)
    m1 = norm_apply(x, row_of(self_ref)).astype(bf16).astype(f32)
    copies[0].wait()
    sv = row_dot(m1, wsv[...]).astype(bf16).astype(f32)
    copies[1].wait()
    z1 = x + row_dot(sv, wso[...])
    m2 = norm_apply(z1, row_of(cross_ref)).astype(bf16).astype(f32)
    copies[2].wait()
    cq = row_dot(m2, wcq[...]).astype(bf16).astype(f32)
    copies[3].wait()
    kq_ref[...] = dot_t(spread(cq, head_mask(x.shape[1], head_dim)), wk[...]).astype(bf16)
    for at, row in enumerate((x, m1, sv, z1, m2, cq)):
        state_ref[at : at + 1, :] = row
    state_ref[6:8, :] = jnp.zeros((2, x.shape[1]), f32)


def before(chain, info, dec, gain_self, gain_cross, wsv, wso, wcq, wk, head_dim):
    width = dec.shape[1]
    weights = (wsv, wso, wcq, wk)
    small = (dec, gain_self, gain_cross)
    outs = (shape((8, width), f32), shape((16, width), bf16))
    return chain.run(
        functools.partial(before_kernel, head_dim=head_dim), "decoder_before", (1,),
        small + weights, [whole(a) for a in small] + [any_space] * 4, outs,
        tuple(whole(a) for a in outs), scalars=(info,),
        scratch=tuple(pltpu.VMEM(w.shape, bf16) for w in weights) + (dma((4,)),),
        flops=64 * wk.size,
    )


def after_kernel(
    info, keymix_ref, state_ref, rows_ref, long_ref, mix_ref, self_ref, cross_ref,
    wk_any, wcq_any, wso_any, wsv_any, wout_any, both_ref, *refs, head_dim, heads, slots,
):
    packs = 3 if slots else 1
    wk, wcq, wso, wsv, wout, pad_ref, sems = refs[packs : packs + 7]
    refs = refs[:packs] + refs[packs + 7 :]
    width = state_ref.shape[1]
    pieces = [pl.ds(at, width) for at in range(0, wout.shape[0], width)]
    copies = fetch(
        ((wk_any, wk), (wcq_any, wcq), (wso_any, wso), (wsv_any, wsv))
        + tuple((wout_any.at[piece, :], wout.at[piece, :]) for piece in pieces),
        sems,
        4,
    )
    x, z1 = state_ref[0:1, :], state_ref[3:4, :]
    z2, gz2 = rows_ref[1:2, :], rows_ref[3:4, :]
    dh, g_b = long_ref[0:1, :], long_ref[1:2, :]
    width = x.shape[1]
    mask = head_mask(width, head_dim)
    mix = keymix_ref[...]
    copies[0].wait()
    for copy in copies[4:]:
        copy.start()
    g_cq = jnp.sum(jnp.where(mask, dot(mix, wk[...]), 0.0), axis=0, keepdims=True)
    g_cq = g_cq.astype(bf16).astype(f32)
    copies[1].wait()
    gz1 = gz2 + norm_back(z1, row_of(cross_ref), row_dot_t(g_cq, wcq[...]))
    count = dh.shape[1] // width
    g_bs = [g_b[:, at * width : (at + 1) * width] for at in range(count)]
    dhs = [dh[:, at * width : (at + 1) * width] for at in range(count)]
    right = [gz1, g_cq, gz2, rows_ref[4:5, :]] + g_bs
    left = [state_ref[1:2, :], state_ref[2:3, :], state_ref[4:5, :], rows_ref[0:1, :], rows_ref[2:3, :]]
    pad_ref[...] = jnp.zeros(pad_ref.shape, f32)
    for first, group in ((0, right), (16, left), (48, dhs)):
        for at, row in enumerate(group):
            pad_ref[first + at : first + at + 1, :] = row
    pad_ref[24 : 24 + heads, :] = mix[:heads].astype(f32)
    pad_ref[24 + heads : 24 + 2 * heads, :] = mix_ref[:heads].astype(f32)
    if not slots:
        pad_ref[8:9, :] = state_ref[5:6, :]
        pad_ref[9:10, :] = rows_ref[5:6, :]
        refs[0][...] = pad_ref[...].astype(bf16)
    else:
        send_factors(info, pad_ref, state_ref[5:6, :], rows_ref[5:6, :], refs, slots, width, count * width)
    copies[2].wait()
    g_sv = row_dot_t(gz1, wso[...]).astype(bf16).astype(f32)
    copies[3].wait()
    both_ref[1:2, :] = gz1 + norm_back(x, row_of(self_ref), row_dot_t(g_sv, wsv[...]))
    total = z2
    for at, piece in enumerate(pieces):
        copies[4 + at].wait()
        total = total + row_dot(dhs[at], wout[piece, :])
    both_ref[0:1, :] = total


def send_factors(info, pad_ref, query, cot, refs, slots, width, hidden):
    send_ref, keep_ref, right_ref, held_ref = refs
    half = width // 2
    both = jnp.concatenate([pad_ref[:8, :half], pad_ref[:8, half:]], axis=0).astype(bf16)
    right_ref[...] = both
    stages = slots.bit_length() - 1
    rows, tall = width // slots, hidden // slots
    per = width // tall
    many = pad_ref[16:48, :]
    two = lax.broadcasted_iota(jnp.int32, (16, tile), 0)
    count = width // tile
    fixed = jnp.zeros((16, tile), f32)
    for first, row in ((2, query), (2 + count, cot)):
        for at in range(count):
            fixed = jnp.where(two == first + at, row[:, at * tile : (at + 1) * tile], fixed)
    for slot in range(slots):
        mine = pltpu.roll(many, (width - slot * rows) % width, 1)[:, :tile]
        hid = pad_ref[48 + slot // per : 49 + slot // per, :]
        hid = pltpu.roll(hid, (width - slot % per * tall) % width, 1)
        hid = jnp.where(two == 0, hid[:, :tile], jnp.where(two == 1, hid[:, tile : 2 * tile], fixed))
        spot = spot_in(info[0], info[1] ^ slot, stages)
        held_ref[pl.ds(pl.multiple_of(spot * 16, 16), 16), :] = jnp.concatenate(
            [mine[:16], mine[16:], hid], axis=1
        ).astype(bf16)
    middle = slots // 2 * 16
    keep_ref[...] = held_ref[:middle, :]
    send_ref[:middle, :] = held_ref[middle:, :]
    send_ref[middle:, :] = both


def after(
    chain, info, key_mix, state, rows, long, mix, gain_self, gain_cross, weights, head_dim, heads, slots
):
    width = key_mix.shape[1]
    small = (key_mix, state, rows, long, mix, gain_self, gain_cross)
    half = slots // 2 * 16
    if slots:
        outs = tuple(shape((lines, width // 2), bf16) for lines in (half + 16, half, 16))
    else:
        outs = (shape((64, width), bf16),)
    outs = (shape((2, width), f32),) + outs
    return chain.run(
        functools.partial(after_kernel, head_dim=head_dim, heads=heads, slots=slots),
        "decoder_after", (1,),
        small + weights, [whole(a) for a in small] + [any_space] * 5, outs,
        tuple(whole(a) for a in outs), scalars=(info,),
        scratch=tuple(pltpu.VMEM(w.shape, bf16) for w in weights)
        + (pltpu.VMEM((64, width), f32), dma((4 + long.shape[1] // width,)))
        + ((pltpu.VMEM((2 * half, width // 2), bf16),) if slots else ()),
        flops=32 * weights[4].size,
    )


def backward_kernel(
    info, gain_ref, low_any, slope_any, wout_any, win_any, y1_any, wo_any,
    *refs,
):
    (low_ref, slope_ref, wout_ref, win_ref, y1_ref, wo_ref, ga_ref, gylow_ref, acc_ref) = refs[-11:-2]
    sems, out_sems = refs[-2:]
    me = info[0]
    parts, seq, width = slope_ref.shape
    part = parts // 2
    away_anys, (keep_any, gylow_any, gyaway_ref, gctx_ref) = refs[:part], refs[part : part + 4]
    chunks = [(1 - me) * part + at for at in range(part)] + [me * part + at for at in range(part)]
    loads = [(low_any, low_ref)]
    for at, chunk_at in enumerate(chunks):
        spot = pl.ds(pl.multiple_of(chunk_at * width, width), width)
        loads.append((wout_any.at[spot, :], wout_ref.at[at]))
        loads.append((slope_any.at[:, spot], slope_ref.at[at]))
        loads.append((win_any.at[:, spot], win_ref.at[at]))
    loads += [(y1_any, y1_ref), (wo_any, wo_ref)]
    loads = fetch(loads, sems, 7)
    saved = []
    loads[0].wait()
    for at in range(parts):
        for copy in loads[7 + 3 * at : 10 + 3 * at]:
            copy.start()
        loads[1 + 3 * at].wait()
        rise = dot_t(low_ref[...], wout_ref[at])
        loads[2 + 3 * at].wait()
        ga_ref[at] = (slope_ref[at].astype(f32) * rise).astype(bf16)
        if at < part:
            target = away_anys[at]
        else:
            target = keep_any.at[:, pl.ds(at % part * width, width)]
        copy = pltpu.make_async_copy(ga_ref.at[at], target, out_sems.at[at])
        copy.start()
        saved.append(copy)
        loads[3 + 3 * at].wait()
        if at == 0:
            acc_ref[...] = dot_t(ga_ref[at], win_ref[at])
        else:
            acc_ref[...] += dot_t(ga_ref[at], win_ref[at])
    loads[-2].wait()
    y1 = y1_ref[...].astype(f32)
    low = (low_ref[...].astype(f32) + norm_back(y1, row_of(gain_ref), acc_ref[...])).astype(bf16)
    gylow_ref[...] = low
    copy = pltpu.make_async_copy(gylow_ref, gylow_any, out_sems.at[parts])
    copy.start()
    saved.append(copy)
    half = width // 2
    gyaway_ref[...] = jnp.where(me == 0, low[:, half:], low[:, :half])
    loads[-1].wait()
    gctx_ref[...] = dot_t(wo_ref[...], low).astype(bf16)
    for copy in saved:
        copy.wait()


def backward(chain, info, low, slope, wout, win, y1, gain, wo):
    seq, width = low.shape
    hidden = win.shape[1]
    parts = hidden // width
    act, tall = shape((seq, width), bf16), shape((seq, hidden // 2), bf16)
    side, turned = shape((seq, width // 2), bf16), shape((width, seq), bf16)

    def vmem(*dims):
        return pltpu.VMEM(dims, bf16)

    return chain.run(
        backward_kernel,
        "feed_forward_back",
        (1,),
        (gain, low, slope, wout, win, y1, wo),
        [whole(gain)] + [any_space] * 6,
        (act,) * (parts // 2) + (tall, act, side, turned),
        (any_space,) * (parts // 2) + (any_space, any_space, whole(side), whole(turned)),
        scalars=(info,),
        scratch=(
            vmem(seq, width), vmem(parts, seq, width), vmem(parts, width, width),
            vmem(parts, width, width), vmem(seq, width), vmem(width, width),
            vmem(parts, seq, width), vmem(seq, width), pltpu.VMEM((seq, width), f32),
            dma((3 + 3 * parts,)), dma((parts + 1,)),
        ),
        flops=2 * seq * width * (width + 2 * hidden),
    )


def attention_back_kernel(
    info, scale_ref, gain_ref, own_ref, got_ref, qt_any, k_any, v_any, ctx_any, gctx_any, e_any,
    wq_any, wk_any, wv_any, gy_any,
    gradkeep_ref, gradaway_ref, table_ref, gq_any, gk_any, gv_any, keep_any,
    gq_ref, gk_ref, gv_ref, keep_ref, qt_ref, k_ref, v_ref, ctx_ref, gctx_ref, e_ref, wq_ref, wk_ref, wv_ref, gy_ref,
    rise_ref, gs_ref, sums_ref, all_ref, sems, out_sems, *, heads,
):
    me = info[0]
    seq, width = k_ref.shape
    head_dim = width // heads
    blocks = seq // tile
    half = width // 2
    side = heads // 2
    pair = 2 * head_dim
    loads = fetch(
        ((k_any, k_ref), (v_any, v_ref), (qt_any, qt_ref), (gctx_any, gctx_ref), (ctx_any, ctx_ref))
        + tuple(
            (e_any.at[(1 - me) * side + at if at < side else me * side + at - side], e_ref.at[at])
            for at in range(heads)
        )
        + ((wq_any, wq_ref), (wk_any, wk_ref), (wv_any, wv_ref), (gy_any, gy_ref)),
        sems,
        7,
    )
    for copy in (loads[1], loads[3], loads[4]):
        copy.wait()
    for copy in loads[7:11]:
        copy.start()
    pair_lanes = lax.broadcasted_iota(jnp.int32, (seq, pair), 1)
    ones = [
        jnp.where((pair_lanes == start) | (pair_lanes == start + 1), 1.0, 0.0).astype(bf16)
        for start in (head_dim, 0)
    ]
    low_half = pair_lanes < head_dim
    none = jnp.zeros((head_dim - 16, seq), bf16)
    line_rows = lax.broadcasted_iota(jnp.int32, (16, seq), 0)
    sums_ref[...] = jnp.zeros(sums_ref.shape, f32)

    def first_of(at):
        base = (1 - me if at < side else me) * half
        return pl.multiple_of(base + at % side // 2 * pair, pair)

    def prepare(at):
        rows = pl.ds(first_of(at), pair)
        g2 = gctx_ref[rows, :].astype(f32)
        head = lax.div(first_of(at), head_dim)
        g2 = jnp.concatenate(
            [
                g2[:head_dim] * scale_ref[pl.ds(head, 1), :],
                g2[head_dim:] * scale_ref[pl.ds(head + 1, 1), :],
            ],
            axis=0,
        )
        both = g2 * ctx_ref[rows, :].astype(f32)
        g2 = g2.astype(bf16)
        g_ext = []
        for inner in range(2):
            here = slice(inner * head_dim, (inner + 1) * head_dim)
            delta = -jnp.sum(both[here], axis=0, keepdims=True)
            high = delta.astype(bf16).astype(f32)
            extra = jnp.where(line_rows == 0, high, jnp.where(line_rows == 1, delta - high, 0.0))
            extra = extra.astype(bf16)
            if inner == 0:
                g_ext.append(jnp.concatenate([g2[here], extra, none], axis=0))
            else:
                g_ext.append(jnp.concatenate([extra, none, g2[here]], axis=0))
        return g2, g_ext

    pairs = {}

    def rise(at):
        upper = at % 2
        if not upper:
            pairs[at // 2] = prepare(at)
        v2 = v_ref[:, pl.ds(first_of(at), pair)]
        v_ext = jnp.where(low_half, ones[1], v2) if upper else jnp.where(low_half, v2, ones[0])
        rise_ref[upper] = dot(v_ext, pairs[at // 2][1][upper])

    def spread_scores(at):
        slot = at % 2
        near, outer = [], [None, None]
        for sub in range(tile // chunk):
            sums = [None] * 5
            for key in range(blocks):
                start = key * tile + sub * chunk
                down = slice(start, start + chunk)
                for query in range(blocks):
                    across = slice(query * tile, (query + 1) * tile)
                    g = e_ref[at, down, across].astype(f32) * rise_ref[slot, down, across]
                    gs_ref[slot, down, across] = g.astype(bf16)
                    kind = min(max(query - key, -2), 2) + 2
                    sums[kind] = g if sums[kind] is None else sums[kind] + g
            near.append(jnp.concatenate(sums[1:4] + [jnp.zeros((chunk, tile), f32)], axis=1))
            outer = [a if b is None else a + b for a, b in zip((sums[4], sums[0]), outer)]
            yield
        folded = jnp.concatenate(near, axis=0)
        lanes = 4 * tile
        while folded.shape[0] > 8:
            rest = folded.shape[0] // 2
            folded = folded[:rest] + pltpu.roll(folded[rest:], lanes - rest, 1)
        rows = lax.broadcasted_iota(jnp.int32, folded.shape, 0)
        for bit in (4, 2, 1):
            moved = pltpu.roll(folded, lanes - bit, 1)
            folded = jnp.where((rows & bit) != 0, moved, folded)
        line = jnp.sum(folded, axis=0, keepdims=True)
        outer = [jnp.sum(part, axis=0, keepdims=True) for part in outer]
        row = (8 if at >= side else 0) + at % side
        sums_ref[row : row + 1, :] = jnp.concatenate([line] + outer, axis=1)

    parts = {}
    rise(0)
    for copy in (loads[0], loads[2]):
        copy.wait()
    turned = {}

    def close(at):
        if at < 0:
            yield from [None] * 4
            return
        first = first_of(at)
        upper = at % 2
        here = slice(upper * head_dim, (upper + 1) * head_dim)
        q_mine = qt_ref[pl.ds(pl.multiple_of(first + upper * head_dim, head_dim), head_dim), :]
        g_q = dot(turned[at // 2][here], gs_ref[upper])
        yield
        g_k = dot_t(q_mine, gs_ref[upper])
        yield
        g_v = dot_t(pairs[at // 2][0][here], e_ref[at])
        yield
        parts[upper] = (g_q, g_k, g_v)
        if upper:
            for which, gone_ref in enumerate((gq_ref, gk_ref, gv_ref)):
                both = jnp.concatenate([parts[0][which], parts[1][which]], axis=0).astype(bf16).T
                all_ref[which, :, pl.ds(first, pair)] = both
                start = at % side // 2 * pair
                if at < side:
                    gone_ref[:, start : start + pair] = both
                else:
                    keep_ref[:, which * half + start : which * half + start + pair] = both
        yield

    for at in range(heads + 1):
        last_head = close(at - 1)
        if at == heads:
            for _ in last_head:
                pass
            break
        for copy in loads[11 + at : 12 + at]:
            copy.start()
        if at % 2 == 0:
            turned[at // 2] = k_ref[:, pl.ds(first_of(at), pair)].T
        loads[5 + at].wait()
        for step, _ in enumerate(spread_scores(at)):
            next(last_head)
            if step == 1 and at + 1 < heads:
                rise(at + 1)
    gone = fetch(
        ((gq_ref, gq_any), (gk_ref, gk_any), (gv_ref, gv_any), (keep_ref, keep_any)), out_sems
    )
    for copy in loads[5 + heads :]:
        copy.wait()
    total = None
    for which, ref in enumerate((wq_ref, wk_ref, wv_ref)):
        part = dot_t(all_ref[which], ref[...])
        total = part if total is None else total + part
    x = joined(me, own_ref[0], got_ref[0]).astype(f32)
    grad = gy_ref[...].astype(f32) + norm_back(x, row_of(gain_ref), total)
    middle = seq // 2
    gradkeep_ref[...] = jnp.where(me == 0, grad[:middle], grad[middle:])
    gradaway_ref[...] = jnp.where(me == 0, grad[middle:], grad[:middle])
    sums = joined(me, sums_ref[8:], sums_ref[:8])
    spots = lax.broadcasted_iota(jnp.int32, (sums.shape[1], tile), 0)
    offsets = tile - jnp.where(spots < 3 * tile, spots, spots - 4 * tile)
    kinds = jnp.where(spots < 4 * tile, bucket_of(offsets), jnp.where(spots < 5 * tile, 15, 31))
    lanes = lax.broadcasted_iota(jnp.int32, kinds.shape, 1)
    one_hot = jnp.where(kinds == lanes, 1.0, 0.0).astype(f32)
    table = lax.dot_general(
        sums, one_hot, (((1,), (0,)), ((), ())), precision=lax.Precision.HIGHEST,
        preferred_element_type=f32,
    )
    table_ref[:, :tile] = table.astype(bf16)
    table_ref[:, tile:] = jnp.zeros((16, 2 * tile), bf16)
    for copy in gone:
        copy.wait()


def attention_back(chain, info, scale, gain, enc_in, got, qt, k, v, ctx, gctx, e, wq, wk, wv, gy):
    seq, width = k.shape
    heads = e.shape[0]
    block = pl.BlockSpec((1, seq // 2, width), lambda i, info: (info[0], 0, 0))
    side, part = shape((seq, 3 * width // 2), bf16), shape((seq // 2, width), f32)
    narrow = shape((seq, width // 2), bf16)
    near = (part, part, shape((16, 3 * tile), bf16))
    leaving = (narrow, narrow, narrow, side)
    far = (qt, k, v, ctx, gctx, e, wq, wk, wv, gy)
    return chain.run(
        functools.partial(attention_back_kernel, heads=heads),
        "attention_back",
        (1,),
        (scale, gain, enc_in, got) + far,
        [whole(scale), whole(gain), block, block] + [any_space] * len(far),
        near + leaving,
        tuple(whole(a) for a in near) + (any_space,) * 4,
        scalars=(info,),
        scratch=tuple(pltpu.VMEM(a.shape, bf16) for a in leaving + far)
        + (
            pltpu.VMEM((2, seq, seq), f32), pltpu.VMEM((2, seq, seq), bf16),
            pltpu.VMEM((16, 6 * tile), f32), pltpu.VMEM((3, seq, width), bf16), dma((9 + heads,)), dma((4,)),
        ),
        flops=6 * seq * width * width + 16 * seq * seq * width,
    )


def spot_in(me, relative, stages):
    spot = 0
    for k in range(stages):
        bit = jnp.where(me == 0, k, 1 - k) if k < 2 <= stages else k
        spot = spot | (((relative >> bit) & 1) << (stages - 1 - k))
    return spot


def store(info, base, low, rows, held_ref, slots, line):
    stages = slots.bit_length() - 1
    span = held_ref.shape[0] // slots
    wide = held_ref.shape[1]
    for at in range(low.shape[0] // rows):
        spot = spot_in(info[0], info[1] ^ (base + at), stages)
        for piece in range(low.shape[1] // wide):
            start = pl.multiple_of(spot * span + line + piece * rows, 16)
            held_ref[pl.ds(start, rows), :] = low[
                at * rows : (at + 1) * rows, piece * wide : (piece + 1) * wide
            ]


def release(held_ref, keep_any, send_any, sems, extra=None):
    middle = held_ref.shape[0] // 2
    pairs = [
        (held_ref.at[pl.ds(middle, middle), :], send_any.at[pl.ds(0, middle), :]),
        (held_ref.at[pl.ds(0, middle), :], keep_any),
    ]
    if extra is not None:
        pairs.append((extra, send_any.at[pl.ds(middle, extra.shape[0]), :]))
    for copy in fetch(pairs, sems):
        copy.wait()


def tall_kernel(
    info, r0_any, r1_any, extra_any, l0_any, l1_any, keep_any, send_any,
    r0_ref, r1_ref, extra_ref, l0_ref, l1_ref, held_ref, sems, out_sems, *, rows, slots
):
    parts, seq, width = l0_ref.shape
    wide = r0_ref.shape[1]
    loads = [
        (r0_any.at[:, pl.ds(pl.multiple_of(info[0] * wide, wide), wide)], r0_ref), (r1_any, r1_ref)
    ]
    for at in range(parts):
        spot = pl.ds(at * width, width)
        loads += [(l0_any.at[:, spot], l0_ref.at[at]), (l1_any.at[:, spot], l1_ref.at[at])]
    loads.append((extra_any, extra_ref))
    loads = fetch(loads, sems, 6)
    loads[0].wait()
    loads[1].wait()
    for at in range(parts):
        loads[2 * at + 2].wait()
        loads[2 * at + 3].wait()
        for copy in loads[2 * at + 6 : 2 * at + 8 + at // (parts - 2)]:
            copy.start()
        low = (t_dot(l0_ref[at], r0_ref[...]) + t_dot(l1_ref[at], r1_ref[...])).astype(bf16)
        store(info, at * (width // rows), low, rows, held_ref, slots, 0)
    loads[-1].wait()
    release(held_ref, keep_any, send_any, out_sems, extra_ref)


def tall_grad(chain, info, slots, left, left_got, right, right_got, extra):
    seq, tall = left.shape
    wide = right_got.shape[1]
    rows = tall // slots
    parts = 4
    middle = slots // 2 * rows
    outs = (shape((middle, wide), bf16), shape((middle + extra.shape[0], wide), bf16))
    far = pltpu.VMEM((parts, seq, tall // parts), bf16)
    return chain.run(
        functools.partial(tall_kernel, rows=rows, slots=slots), "grad_ff_out", (1,),
        (right, right_got, extra, left, left_got),
        [any_space] * 5,
        outs, (any_space, any_space), scalars=(info,),
        scratch=(
            pltpu.VMEM(right_got.shape, bf16), pltpu.VMEM(right_got.shape, bf16),
            pltpu.VMEM(extra.shape, bf16), far, far, pltpu.VMEM((tall, wide), bf16),
            dma((2 * parts + 3,)), dma((3,)),
        ),
        flops=4 * seq * tall * wide,
    )


def mixed_kernel(
    info, n0_any, n1_any, a0_any, c0_any, c1_any, g0_any, g1_any, *refs, rows, slots
):
    steps = len(refs) - 13
    a1_anys, (keep_any, send_any) = refs[:steps], refs[steps : steps + 2]
    n0_ref, n1_ref, a0_ref, a1_ref, c0_ref, c1_ref, g0_ref, g1_ref, held_ref, sems, out_sems = refs[steps + 2 :]
    seq, width = n0_ref.shape
    wide = held_ref.shape[1]
    loads = fetch(
        (
            (n0_any, n0_ref), (a0_any, a0_ref), (n1_any, n1_ref),
            (c0_any, c0_ref), (c1_any, c1_ref),
            (g0_any.at[:, pl.ds(pl.multiple_of(info[0] * wide, wide), wide)], g0_ref),
            (g1_any, g1_ref),
        )
        + tuple((part, a1_ref.at[at]) for at, part in enumerate(a1_anys)),
        sems,
        2,
    )
    loads[0].wait()
    loads[1].wait()
    for at in (2, *range(7, 7 + steps), 3, 4, 5, 6):
        loads[at].start()
    lines = width // wide * rows
    middle = slots // 2
    span = held_ref.shape[0] // slots
    held = held_ref.reshape(slots, span, wide)
    saved = []

    def leave(at, first, count):
        here = pl.ds(first, count)
        for which, (target, start) in enumerate(((send_any, middle), (keep_any, 0))):
            copy = pltpu.make_async_copy(
                held.at[pl.ds(start, middle), here, :],
                target.at[:, here, :],
                out_sems.at[2 * at + which],
            )
            copy.start()
            saved.append(copy)

    for at in range(steps):
        spot = slice(at * width, (at + 1) * width)
        low = t_dot(n0_ref[...], a0_ref[:, spot])
        if at == 0:
            loads[2].wait()
        loads[7 + at].wait()
        low = low + t_dot(n1_ref[...], a1_ref[at])
        store(info, 0, low.astype(bf16), rows, held_ref, slots, at * lines)
        leave(at, at * lines, lines)
    for copy in loads[3:7]:
        copy.wait()
    low = (dot(c0_ref[...], g0_ref[...]) + dot(c1_ref[...], g1_ref[...])).astype(bf16)
    store(info, 0, low, rows, held_ref, slots, steps * lines)
    leave(steps, steps * lines, rows)
    for copy in saved:
        copy.wait()


def mixed_grad(chain, info, slots, n2, n2_got, ctx, ctx_got, keep, got, gy, gy_got):
    seq, width = n2.shape
    wide = gy_got.shape[1]
    rows = width // slots
    lines = (keep.shape[1] // wide + 1) * rows
    outs = (shape((slots // 2, lines, wide), bf16),) * 2
    args = (n2, n2_got, keep, ctx, ctx_got, gy, gy_got) + got
    dims = [n2.shape, n2.shape, keep.shape, (len(got),) + n2.shape, ctx.shape, ctx.shape]
    dims += [gy_got.shape, gy_got.shape]
    done = chain.run(
        functools.partial(mixed_kernel, rows=rows, slots=slots), "grad_ff_in", (1,), args,
        [any_space] * len(args), outs, (any_space, any_space), scalars=(info,),
        scratch=tuple(pltpu.VMEM(d, bf16) for d in dims + [(slots * lines, wide)])
        + (dma((len(args),)), dma((2 * len(got) + 2,))),
        flops=4 * seq * width * (keep.shape[1] + wide),
    )
    return tuple(part.reshape(-1, wide) for part in done)


def heads_kernel(
    info, table_ref, n0_any, n1_any, g0_any, gq_any, gk_any, gv_any, keep_any, send_any,
    n0_ref, n1_ref, g0_ref, g1_ref, held_ref, sems, out_sems, *, rows, slots,
):
    loads = fetch(
        ((n0_any, n0_ref), (g0_any, g0_ref), (n1_any, n1_ref))
        + tuple(
            (part, g1_ref.at[:, pl.ds(at * held_ref.shape[1], held_ref.shape[1])])
            for at, part in enumerate((gq_any, gk_any, gv_any))
        ),
        sems,
    )
    wide = held_ref.shape[1]
    for copy in loads:
        copy.wait()
    for first, count in ((0, 2), (2, 1)):
        spot = slice(first * wide, (first + count) * wide)
        low = t_dot(n0_ref[...], g0_ref[:, spot]) + t_dot(n1_ref[...], g1_ref[:, spot])
        store(info, 0, low.astype(bf16), rows, held_ref, slots, first * rows)
    release(held_ref, keep_any, send_any, out_sems, table_ref)


def heads_grad(chain, info, slots, n1, n1_got, keep, got, table):
    seq, width = n1.shape
    wide = width // 2
    rows = width // slots
    lines = keep.shape[1] // wide * rows
    outs = (
        shape((slots // 2 * lines, wide), bf16), shape((slots // 2 * lines + 16, wide), bf16),
    )
    args = (n1, n1_got, keep) + got
    dims = (n1.shape, n1.shape, keep.shape, keep.shape)
    return chain.run(
        functools.partial(heads_kernel, rows=rows, slots=slots), "grad_heads", (1,), (table,) + args,
        [whole(table)] + [any_space] * 6, outs, (any_space, any_space), scalars=(info,),
        scratch=tuple(pltpu.VMEM(d, bf16) for d in dims)
        + (pltpu.VMEM((slots * lines, wide), bf16), dma((6,)), dma((3,))),
        flops=4 * seq * width * keep.shape[1],
    )


def stage_kernel(*refs, half, table):
    keep_ref, got_ref = refs[:2]
    outs = refs[3:] if table else refs[2:]
    outs[0][:half, :] = keep_ref[:half, :] + got_ref[:half, :]
    if len(outs) > 1:
        outs[1][:half, :] = keep_ref[half:, :] + got_ref[half : 2 * half, :]
    if table:
        total = refs[2][...] + got_ref[keep_ref.shape[0] :, :]
        if len(outs) > 1:
            outs[1][half:, :] = total
            outs[2][...] = total
        else:
            outs[0][half:, :] = total


def stage(chain, keep, got, last, table, flops, limit):
    count, wide = keep.shape
    extra = 0 if table is None else table.shape[0]
    args = (keep, got) if table is None else (keep, got, table)
    half = count if last else count // 2
    outs = (shape((half + extra, wide), bf16),)
    if not last:
        outs = (shape((half, wide), bf16), shape((half + extra, wide), bf16))
        outs += () if table is None else (shape(table.shape, bf16),)
    return chain.run(
        functools.partial(stage_kernel, half=half, table=table is not None), "sum_stage", (1,),
        args, [whole(a) for a in args], outs, tuple(whole(a) for a in outs), limit=limit, flops=flops,
    )


def split_kernel(*refs, rows, table):
    keep_ref, got_ref = refs[:2]
    outs = refs[3:] if table else refs[2:]
    for at in range(4):
        here = slice(at * rows, (at + 1) * rows)
        outs[at][:rows, :] = keep_ref[here, :] + got_ref[here, :]
    if table:
        total = refs[2][...] + got_ref[4 * rows :, :]
        for out in outs[1:4]:
            out[rows:, :] = total
        outs[4][...] = total


def split(chain, keep, got, table, limit, flops):
    rows, wide = keep.shape[0] // 4, keep.shape[1]
    extra = 0 if table is None else table.shape[0]
    args = (keep, got) if table is None else (keep, got, table)
    outs = (shape((rows, wide), bf16),) + (shape((rows + extra, wide), bf16),) * 3
    outs += () if table is None else (shape(table.shape, bf16),)
    return chain.run(
        functools.partial(split_kernel, rows=rows, table=table is not None), "sum_split", (1,),
        args, [whole(a) for a in args], outs, tuple(whole(a) for a in outs), limit=limit, flops=flops,
    )


def four_kernel(*refs, rows, table):
    keep_ref, *got = refs[:4]
    done_ref = refs[-1]
    total = keep_ref[...].astype(f32)
    for ref in got:
        total = total + ref[:rows, :].astype(f32)
    done_ref[:rows, :] = total.astype(bf16)
    if table:
        total = refs[4][...].astype(f32)
        for ref in got:
            total = total + ref[rows:, :].astype(f32)
        done_ref[rows:, :] = total.astype(bf16)


def four(chain, keep, got, table, limit, flops):
    args = (keep,) + got + (() if table is None else (table,))
    outs = (shape(got[0].shape, bf16),)
    return chain.run(
        functools.partial(four_kernel, rows=keep.shape[0], table=table is not None), "sum_four", (1,),
        args, [whole(a) for a in args], outs, tuple(whole(a) for a in outs), limit=limit, flops=flops,
    )


def factor_stage_kernel(keep_ref, got_ref, left_ref, right_ref, *refs, slots, pairs, rows):
    half = slots // 2
    block = 16 * pairs
    after = slots * rows
    got_right = after + slots * block
    if slots == 1:
        done_ref, = refs
        done_ref[:rows, :] = keep_ref[...] + got_ref[:rows, :]
        done_ref[rows : rows + block, :] = left_ref[...]
        done_ref[rows + block : rows + 2 * block, :] = got_ref[after:got_right, :]
        done_ref[rows + 2 * block : rows + 3 * block, :] = right_ref[...]
        done_ref[rows + 3 * block :, :] = got_ref[got_right:, :]
        return
    keep_out, send_out, left_out, right_out = refs
    middle = half * rows
    keep_out[...] = keep_ref[:middle, :] + got_ref[:middle, :]
    send_out[:middle, :] = keep_ref[middle:, :] + got_ref[middle:after, :]
    for slot in range(slots):
        target, first = (left_out, 0) if slot < half else (send_out, middle)
        first += slot % half * 2 * block
        target[first : first + block, :] = left_ref[slot * block : (slot + 1) * block, :]
        target[first + block : first + 2 * block, :] = got_ref[
            after + slot * block : after + (slot + 1) * block, :
        ]
    right_out[:block, :] = right_ref[...]
    right_out[block:, :] = got_ref[got_right:, :]
    first = middle + half * 2 * block
    send_out[first : first + block, :] = right_ref[...]
    send_out[first + block :, :] = got_ref[got_right:, :]


def factor_stage(chain, keep, got, left, right, limit, flops):
    wide = keep.shape[1]
    pairs = right.shape[0] // 16
    slots = left.shape[0] // (16 * pairs)
    rows = keep.shape[0] // slots
    if slots == 1:
        lines = (rows + 64 * pairs,)
    else:
        half = slots // 2
        lines = (half * rows, half * rows + 32 * half * pairs + 32 * pairs, 32 * half * pairs, 32 * pairs)
    outs = tuple(shape((count, wide), bf16) for count in lines)
    args = (keep, got, left, right)
    return chain.run(
        functools.partial(factor_stage_kernel, slots=slots, pairs=pairs, rows=rows), "sum_stage",
        (1,), args, [whole(a) for a in args], outs, tuple(whole(a) for a in outs), limit=limit,
        flops=flops,
    )


def two_stages(chain, keep, got, left, right, other_keep, other_got, limit, flops):
    wide = keep.shape[1]
    pairs = right.shape[0] // 16
    slots = left.shape[0] // (16 * pairs)
    rows = keep.shape[0] // slots
    half, other = slots // 2, other_keep.shape[0] // 2
    lines = (half * rows, half * rows + 32 * half * pairs + 32 * pairs, 32 * half * pairs, 32 * pairs)
    outs = tuple(shape((count, wide), bf16) for count in lines + (other, other))
    args = (keep, got, left, right, other_keep, other_got)

    def kernel(*refs):
        factor_stage_kernel(*refs[:4], *refs[6:10], slots=slots, pairs=pairs, rows=rows)
        stage_kernel(*refs[4:6], *refs[10:], half=other, table=False)

    done = chain.run(
        kernel, "sum_two_stages", (1,), args, [whole(a) for a in args], outs,
        tuple(whole(a) for a in outs), limit=limit, flops=flops,
    )
    return done[:4], done[4:]


def gain_of(weight, grad):
    return jnp.sum(weight[...].astype(f32) * grad, axis=1, keepdims=True)


def gain_line(total, gain_ref, chip):
    rows = total.shape[0]
    turned = jnp.broadcast_to(total, (rows, tile)).T[0:1]
    gain = row_of(gain_ref)
    width = gain.shape[1]
    mine = pltpu.roll(gain, lax.rem(width - chip * rows, width), 1)[:, :rows]
    return (turned / mine).reshape(rows)


def decoder_kernel(
    info, own_ref, got_ref, wso_ref, wsv_ref, wcq_ref, win_ref, wk_ref, wv_ref,
    gself_ref, gcross_ref, gffn_ref, gfinal_ref,
    sv_ref, so_ref, cq_ref, co_ref, in_ref, out_ref, ck_ref, cv_ref,
    dself_ref, dcross_ref, dffn_ref, dfinal_ref, left_ref, right_ref, *, heads,
):
    chip = info[1]
    count = left_ref.shape[0]
    each = count // 2
    tall, width = out_ref.shape
    rows, hidden = in_ref.shape
    head_dim = width // heads
    half = width // 2
    middle = tall + 16 * each
    for at, ref in enumerate((own_ref, got_ref)):
        here = slice(at * each, (at + 1) * each)
        left_ref[here] = ref[tall:middle, :].astype(f32).reshape(each, 16, half)
        right_ref[here] = ref[middle:, :].astype(f32).reshape(each, 16, half)

    def right(at):
        return jnp.concatenate([right_ref[:, at, :], right_ref[:, 8 + at, :]], axis=1).astype(bf16)

    def left(at):
        lane = at // 16 * tile
        return left_ref[:, at % 16, lane : lane + tile].astype(bf16)[:, :rows]

    pieces = width // tile
    early = [
        jnp.concatenate(
            [left_ref[:, 2 + which * pieces + at, 2 * tile :] for at in range(pieces)], axis=1
        ).astype(bf16)
        for which in range(2)
    ]
    r_z1, r_cq, r_z2, r_cctx = [right(at) for at in range(4)]
    r_sv = dot_t(r_z1, wso_ref[...]).astype(bf16)
    r = [r_sv, r_z1, r_cq, r_z2, early[0], r_cctx, early[1]]
    r_hid = jnp.concatenate([right(4 + at) for at in range(hidden // width)], axis=1)
    l_hid = jnp.concatenate(
        [left_ref[:, 0, 2 * tile :], left_ref[:, 1, 2 * tile :]], axis=1
    ).astype(bf16)[:, :tall]
    sv_ref[...] = t_dot(left(0), r[0])
    dself_ref[...] = gain_line(gain_of(wsv_ref, sv_ref[...]), gself_ref, chip)
    so_ref[...] = t_dot(left(1), r[1])
    cq_ref[...] = t_dot(left(2), r[2])
    dcross_ref[...] = gain_line(gain_of(wcq_ref, cq_ref[...]), gcross_ref, chip)
    co_ref[...] = t_dot(left(3), r[3])
    in_ref[...] = t_dot(left(4), r_hid)
    dffn_ref[...] = gain_line(gain_of(win_ref, in_ref[...]), gffn_ref, chip)
    out_ref[...] = t_dot(l_hid, r[6])
    for head in range(heads):
        spot = slice(head * head_dim, (head + 1) * head_dim)
        ck_ref[:, spot] = t_dot(left(8 + head), r[4][:, spot])
        cv_ref[:, spot] = t_dot(left(8 + heads + head), r[5][:, spot])
    total = gain_of(wk_ref, ck_ref[...]) + gain_of(wv_ref, cv_ref[...])
    dfinal_ref[...] = gain_line(total, gfinal_ref, chip)


def decoder_grads(chain, info, own, got, wso, weights, gains, rows, heads):
    width, hidden = weights[0].shape[0], weights[2].shape[1]
    tall = hidden * rows // width
    each = (own.shape[0] - tall) // 32
    line = shape((rows,), f32)
    flat = shape((rows, width), f32)
    outs = (flat, flat, flat, flat, shape((rows, hidden), f32), shape((tall, width), f32), flat, flat)
    outs += (line,) * 4

    def sliced(array):
        return pl.BlockSpec((rows, array.shape[1]), lambda i, info: (info[1], 0))

    return chain.run(
        functools.partial(decoder_kernel, heads=heads), "decoder_grads",
        (1,), (own, got, wso) + weights + gains,
        [whole(own), whole(got), whole(wso)] + [sliced(a) for a in weights] + [whole(a) for a in gains],
        outs, tuple(whole(a) for a in outs), scalars=(info,), limit=40, free=True,
        scratch=(
            pltpu.VMEM((2 * each, 16, width // 2), f32), pltpu.VMEM((2 * each, 16, width // 2), f32),
        ),
    )


def sides(me, own_ref, got_ref, first, rows):
    own, got = own_ref[first : first + rows, :], got_ref[first : first + rows, :]
    low = jnp.where(me == 0, own, got).astype(f32)
    high = jnp.where(me == 0, got, own).astype(f32)
    return low, high


def finish_kernel(
    info, out_ref, out_got, keep_ref, away_ref, grad_ref, grad_got, row_ref, row_got,
    fout_ref, enc_ref, back_ref, dec_ref, decback_ref,
):
    me = info[0]
    wide = out_ref.shape[1]
    low, high = sides(me, out_ref, out_got, 0, fout_ref.shape[0])
    fout_ref[:, :wide] = low
    fout_ref[:, wide:] = high
    enc_ref[me] = keep_ref[...]
    enc_ref[1 - me] = away_ref[...]
    back_ref[me] = grad_ref[...]
    back_ref[1 - me] = grad_got[...]
    rows_two = lax.broadcasted_iota(jnp.int32, (2, row_ref.shape[1]), 0)
    both = jnp.where(rows_two == me, row_ref[0:1], row_got[0:1])
    dec_ref[...] = both.astype(bf16)
    decback_ref[...] = jnp.where(rows_two == me, row_ref[1:2], row_got[1:2])


def finish(chain, info, tall, out, out_got, keep, away, grad, grad_got, row, row_got):
    width = keep.shape[1]
    half = away.shape[0]
    args = (out, out_got, keep, away, grad, grad_got, row, row_got)
    outs = (
        shape((tall, width), f32), shape((2, half, width), bf16),
        shape((2, half, width), f32), shape((2, width), bf16), shape((2, width), f32),
    )
    specs = [whole(a) for a in args]
    specs[0] = specs[1] = pl.BlockSpec((tall, out.shape[1]), lambda i, info: (0, 0))
    specs[2] = pl.BlockSpec((half, width), lambda i, info: (info[0], 0))
    return chain.run(
        finish_kernel, "finish_activations", (1,),
        args, specs, outs, tuple(whole(a) for a in outs), scalars=(info,), limit=40, free=True,
    )


def finish_mix_kernel(
    info, mix_ref, mix_got, win_ref, gain_ref, fin_ref, o_ref, dffn_ref, *, rows, steps
):
    me = info[0]
    wide = mix_ref.shape[1]
    for at in range(steps):
        low, high = sides(me, mix_ref, mix_got, at * rows, rows)
        fin_ref[:, at * wide : (at + 1) * wide] = low
        fin_ref[:, (steps + at) * wide : (steps + at + 1) * wide] = high
    low, high = sides(me, mix_ref, mix_got, steps * rows, rows)
    o_ref[:, :wide] = low
    o_ref[:, wide:] = high
    dffn_ref[...] = gain_line(gain_of(win_ref, fin_ref[...]), gain_ref, info[1])


def finish_mix(chain, info, mix, mix_got, win, gain, rows):
    width, hidden = win.shape
    args = (mix, mix_got, win, gain)
    outs = (shape((rows, hidden), f32), shape((rows, width), f32), shape((rows,), f32))
    specs = [whole(a) for a in args]
    specs[2] = pl.BlockSpec((rows, hidden), lambda i, info: (info[1], 0))
    return chain.run(
        functools.partial(finish_mix_kernel, rows=rows, steps=hidden // 2 // mix.shape[1]),
        "finish_mixed", (1,),
        args, specs, outs, tuple(whole(a) for a in outs), scalars=(info,), limit=40, free=True,
    )


def last_kernel(
    info, sum_ref, got_ref, wq_ref, wk_ref, wv_ref, gain_ref,
    q_ref, k_ref, v_ref, d_ref, table_ref, *, rows, heads,
):
    me = info[0]
    wide = sum_ref.shape[1]
    outs = (q_ref, k_ref, v_ref)
    for at, ref in enumerate(outs):
        low, high = sides(me, sum_ref, got_ref, at * rows, rows)
        ref[:, :wide] = low
        ref[:, wide:] = high
    total = sum(gain_of(w, ref[...]) for w, ref in zip((wq_ref, wk_ref, wv_ref), outs))
    d_ref[...] = gain_line(total, gain_ref, info[1])
    first = 3 * rows
    table = sum_ref[first:, :tile].astype(f32) + got_ref[first:, :tile].astype(f32)
    part = heads // 2
    table_ref[:part, :] = table[:part, : table_ref.shape[1]]
    table_ref[part:, :] = table[8 : 8 + part, : table_ref.shape[1]]


def last(chain, info, done, got, wq, wk, wv, gain, rows, buckets, heads):
    width = wq.shape[0]
    flat = shape((rows, width), f32)
    args = (done, got, wq, wk, wv, gain)
    outs = (flat, flat, flat, shape((rows,), f32), shape((heads, buckets), f32))
    specs = [whole(a) for a in args]
    for at in (2, 3, 4):
        specs[at] = pl.BlockSpec((rows, args[at].shape[1]), lambda i, info: (info[1], 0))
    return chain.run(
        functools.partial(last_kernel, rows=rows, heads=heads), "finish_last", (1,), args, specs,
        outs, tuple(whole(a) for a in outs), scalars=(info,), limit=40, free=True,
    )


def plain_grad(me, place, pieces, tall):
    parts = []
    for left, left_got, right, right_got, offset in pieces:
        wide = right_got.shape[1]
        keep = lax.dynamic_slice_in_dim(right, me * wide, wide, 1) if offset else right
        total = t_dot(
            jnp.concatenate([left, left_got]), jnp.concatenate([keep, right_got])
        ).astype(bf16)
        slots = place.shape[0]
        if tall:
            parts.append(total.reshape(slots, -1, wide))
        else:
            half = left.shape[1] // 2
            for at in range(0, wide, half):
                parts.append(total[:, at : at + half].reshape(slots, -1, half))
    total = jnp.concatenate(parts, axis=1)
    order = jnp.zeros_like(place).at[place].set(jnp.arange(place.shape[0], dtype=jnp.int32))
    return jnp.take(total, order, axis=0)


def plain_sides(me, done, got):
    low = jnp.where(me == 0, done, got).astype(f32)
    high = jnp.where(me == 0, got, done).astype(f32)
    return low, high


def body(
    enc_in,
    dec_in,
    lengths,
    cot_enc,
    cot_dec,
    enc_gain_attn,
    enc_query,
    enc_key,
    enc_value,
    enc_output,
    relative_bias_table,
    enc_gain_ffn,
    enc_ff_in,
    enc_ff_out,
    enc_gain_final,
    dec_gain_self,
    dec_self_value,
    dec_self_output,
    dec_gain_cross,
    dec_cross_query,
    dec_cross_key,
    dec_cross_value,
    dec_cross_output,
    dec_gain_ffn,
    dec_ff_in,
    dec_ff_out,
):
    pair_count, seq_dev, width = enc_in.shape
    seq_all = 2 * seq_dev
    bucket_count, heads = relative_bias_table.shape
    head_dim = width // heads
    hidden = enc_ff_in.shape[1]
    slots = lax.axis_size("batch")
    me = lax.axis_index("blk")
    chip = lax.axis_index("batch")
    stages = slots.bit_length() - 1
    rows = width // slots
    aligned = rows % 16 == 0
    chain = Chain()

    def across(array):
        return lax.ppermute(array, "blk", [(0, 1), (1, 0)])

    info = jnp.stack([me, chip]).astype(jnp.int32)
    order = list(range(stages))
    crossed = order if stages < 2 else [1, 0] + order[2:]
    def hop(array, *steps):
        pairs = []
        for which in range(slots):
            for core in range(2):
                mask = sum(1 << (order, crossed)[core][step] for step in steps)
                pairs.append((which * 2 + core, (which ^ mask) * 2 + core))
        return lax.ppermute(array, ("batch", "blk"), pairs)

    class Sum:
        def __init__(self, keep, send, table=None, factors=None):
            self.keep, self.table, self.at = keep, table, 0
            self.direct = aligned and table is not None and stages >= 4
            self.total = stages - 1 if self.direct else stages
            self.factors = factors
            self.got = hop(send, 0)

        def step(self, limit=24, flops=0):
            if self.at == self.total:
                return
            self.at += 1
            last = self.at == self.total
            apart = self.direct and self.at == stages - 2
            if self.factors is not None:
                outs = factor_stage(chain, self.keep, self.got, *self.factors, limit, flops)
                self.factors = outs[2:]
            elif apart:
                outs = split(chain, self.keep, self.got, self.table, limit, flops)
            elif last and self.direct:
                outs = four(chain, self.keep, self.got, self.table, limit, flops)
            elif aligned:
                outs = list(stage(chain, self.keep, self.got, last, self.table, flops, limit))
            else:
                total = self.keep + self.got
                half = total.shape[0] // 2
                outs = [total] if last else [total[:half], total[half:]]
            self.take(outs)

        def take(self, outs):
            last = self.at == self.total
            apart = self.direct and self.at == stages - 2
            self.keep = outs[0]
            if self.table is not None and not last and aligned:
                self.table = outs[-1]
            if last:
                self.done = self.keep
                self.other = across(self.done)
            elif apart:
                first, then = self.at, self.at + 1
                self.got = (hop(outs[1], then), hop(outs[2], first), hop(outs[3], first, then))
            else:
                self.got = hop(outs[1], self.at)

        def rest(self):
            while self.at < self.total:
                self.step()

    def plain_sum(pieces, tall):
        relative = chip ^ jnp.arange(slots, dtype=jnp.int32)
        total = plain_grad(me, spot_in(me, relative, stages).astype(jnp.int32), pieces, tall)
        total = total.reshape(-1, total.shape[-1])
        half = total.shape[0] // 2
        return Sum(total[:half], total[half:])

    enc_got = across(enc_in)
    cot_got = across(cot_enc)
    state, key_query = before(
        chain, info, dec_in, dec_gain_self, dec_gain_cross, dec_self_value, dec_self_output,
        dec_cross_query, dec_cross_key, head_dim,
    )

    (
        scale, ge_low, ge_away, dec_lines, dec_long, key_mix, mix,
        n1, q_turned, k, v, weights, context, y1, n2, hid, slope, result_low, out_away,
    ) = encoder(
        chain, info, lengths, enc_in, enc_got, enc_gain_attn, enc_query, enc_key, enc_value,
        relative_bias_table.T, enc_gain_ffn, enc_gain_final, enc_output, enc_ff_in, enc_ff_out, heads,
        cot_enc, cot_got, (key_query, state, cot_dec, dec_gain_ffn),
        (dec_cross_value, dec_cross_output, dec_ff_in, dec_ff_out),
    )
    ge_got = across(ge_away)
    hid_got, n2_got, ctx_got, n1_got = (across(part) for part in (hid, n2, context, n1))
    out_got = across(out_away)

    dec_rows, *packed = after(
        chain, info, key_mix, state, dec_lines, dec_long, mix, dec_gain_self, dec_gain_cross,
        (dec_cross_key, dec_cross_query, dec_self_output, dec_self_value, dec_ff_out),
        head_dim, heads, slots if aligned else 0,
    )
    dec_got = across(dec_rows)

    if aligned:
        left_send, left_keep, right = packed
        sum_out = Sum(
            *tall_grad(chain, info, slots, hid, hid_got, ge_low, ge_got, left_send),
            factors=(left_keep, right),
        )
    else:
        sum_out = plain_sum([(hid, hid_got, ge_low, ge_got, True)], True)
    *ga_away, ga_keep, gy_low, gy_away, g_ctx = backward(
        chain, info, ge_low, slope, enc_ff_out, enc_ff_in, y1, enc_gain_ffn, enc_output
    )
    ga_got, gy_got = tuple(across(part) for part in ga_away), across(gy_away)
    sum_out.step(64)
    if aligned:
        sum_mix = Sum(
            *mixed_grad(
                chain, info, slots, n2, n2_got, context, ctx_got, ga_keep, ga_got, gy_low, gy_got
            ),
        )
    else:
        sum_mix = plain_sum(
            [(n2, n2_got, ga_keep, jnp.concatenate(ga_got, axis=1), False), (context.T, ctx_got.T, gy_low, gy_got, True)], False
        )
    sum_out.step(64)
    grad_keep, grad_away, table_term, *g_away, g_keep = attention_back(
        chain, info, scale, enc_gain_attn, enc_in, enc_got, q_turned, k, v, context, g_ctx, weights,
        enc_query, enc_key, enc_value, gy_low,
    )
    g_got = tuple(across(part) for part in g_away)
    grad_got = across(grad_away)
    if aligned:
        sum_out.at, sum_mix.at = sum_out.at + 1, sum_mix.at + 1
        for_out, for_mix = two_stages(
            chain, sum_out.keep, sum_out.got, *sum_out.factors, sum_mix.keep, sum_mix.got, 64, large
        )
        sum_out.factors = for_out[2:]
        sum_out.take(for_out)
        sum_mix.take(for_mix)
    else:
        sum_out.step()
        sum_mix.step()
    if aligned:
        sum_heads = Sum(
            *heads_grad(chain, info, slots, n1, n1_got, g_keep, g_got, table_term), table_term
        )
    else:
        sum_heads = plain_sum([(n1, n1_got, g_keep, jnp.concatenate(g_got, axis=1), False)], False)
        table_sum = lax.psum(table_term.astype(f32), ("batch", "blk"))

    dec_weights = (dec_self_value, dec_cross_query, dec_ff_in, dec_cross_key, dec_cross_value)
    dec_gains = (dec_gain_self, dec_gain_cross, dec_gain_ffn, enc_gain_final)

    def mine(array):
        return lax.dynamic_slice_in_dim(array, chip * (array.shape[0] // slots), array.shape[0] // slots, 0)

    sum_mix.step()
    sum_out.step(24, large)
    sum_heads.step()
    sum_out.rest()
    if aligned:
        sum_mix.step(24, large)
        sum_heads.step()
        grad_ff_out, encoder_output, grad_in, dec_out, grad_dec = finish(
            chain, info, hidden // slots, sum_out.done, sum_out.other, result_low, out_got, grad_keep,
            grad_got, dec_rows, dec_got,
        )
        dec_outs = decoder_grads(
            chain, info, sum_out.done, sum_out.other, dec_self_output, dec_weights, dec_gains, rows, heads
        )
        (grad_self_value, grad_self_output, grad_cross_query, grad_cross_output) = dec_outs[:4]
        (grad_dec_ff_in, grad_dec_ff_out, grad_cross_key, grad_cross_value) = dec_outs[4:8]
        gain_self, gain_cross, gain_dec_ffn, gain_final = dec_outs[8:]
        sum_heads.rest()
        sum_mix.rest()
        grad_ff_in, grad_output, gain_ffn = finish_mix(
            chain, info, sum_mix.done, sum_mix.other, enc_ff_in, enc_gain_ffn, rows
        )
        sum_heads.rest()
        grad_query, grad_key, grad_value, gain_attn, grad_rel_table = last(
            chain, info, sum_heads.done, sum_heads.other, enc_query, enc_key, enc_value,
            enc_gain_attn, rows, bucket_count, heads,
        )
        grad_rel_table = grad_rel_table.T
    else:
        sum_mix.rest()
        sum_heads.rest()
        table = lax.all_gather(packed[0], ("batch", "blk"), axis=0, tiled=False)
        count = hidden // width
        tall = hidden // slots
        r = [table[:, at] for at in range(4)]
        r = [dot_t(r[0], dec_self_output).astype(bf16)] + r[:3] + [table[:, 8], r[3], table[:, 9]]
        r_hid = table[:, 4 : 4 + count].reshape(-1, hidden)
        chosen = lax.dynamic_slice_in_dim(table[:, 16:48], chip * rows, rows, 2)
        l = [chosen[:, at] for at in range(5)]
        l_hid = table[:, 48 : 48 + count].reshape(-1, hidden)
        l_hid = lax.dynamic_slice_in_dim(l_hid, chip * tall, tall, 1)
        grad_self_value, grad_self_output = t_dot(l[0], r[0]), t_dot(l[1], r[1])
        grad_cross_query, grad_cross_output = t_dot(l[2], r[2]), t_dot(l[3], r[3])
        grad_dec_ff_in = t_dot(l[4], r_hid)
        grad_dec_ff_out = t_dot(l_hid, r[6])
        many = chosen[:, 8 : 8 + 2 * heads].reshape(-1, 2, heads, rows)
        grad_cross_key, grad_cross_value = (
            jnp.einsum(
                "phd,phe->dhe", many[:, at], r[4 + at].reshape(-1, heads, head_dim),
                preferred_element_type=f32,
            ).reshape(rows, width)
            for at in range(2)
        )

        def gain_plain(gain, *terms):
            return sum(jnp.sum(mine(w).astype(f32) * g, axis=1) for w, g in terms) / mine(gain)

        gain_self = gain_plain(dec_gain_self, (dec_self_value, grad_self_value))
        gain_cross = gain_plain(dec_gain_cross, (dec_cross_query, grad_cross_query))
        gain_dec_ffn = gain_plain(dec_gain_ffn, (dec_ff_in, grad_dec_ff_in))
        gain_final = gain_plain(
            enc_gain_final, (dec_cross_key, grad_cross_key), (dec_cross_value, grad_cross_value)
        )
        sum_mix.rest()
        sum_heads.rest()
        grad_ff_out = jnp.concatenate(plain_sides(me, sum_out.done, sum_out.other), axis=1)
        low, high = plain_sides(me, sum_mix.done, sum_mix.other)

        def pick(side, at):
            return side[at * rows : (at + 1) * rows]

        grad_ff_in = jnp.concatenate(
            [pick(side, at) for side in (low, high) for at in range(low.shape[0] // rows - 1)], axis=1
        )
        spot = low.shape[0] // rows - 1
        grad_output = jnp.concatenate([pick(low, spot), pick(high, spot)], axis=1)
        low, high = plain_sides(me, sum_heads.done, sum_heads.other)
        grad_query, grad_key, grad_value = (
            jnp.concatenate([pick(low, at), pick(high, at)], axis=1) for at in range(3)
        )
        gain_ffn = gain_plain(enc_gain_ffn, (enc_ff_in, grad_ff_in))
        gain_attn = gain_plain(
            enc_gain_attn, (enc_query, grad_query), (enc_key, grad_key), (enc_value, grad_value)
        )
        turned = table_sum.T[:bucket_count]
        grad_rel_table = jnp.concatenate([turned[:, : heads // 2], turned[:, 8 : 8 + heads // 2]], axis=1)

        def stacked(own, got):
            return jnp.where(me == 0, jnp.stack([own, got]), jnp.stack([got, own]))

        out_keep = lax.dynamic_slice_in_dim(result_low, me * seq_dev, seq_dev, 0)
        encoder_output, grad_in = stacked(out_keep, out_got), stacked(grad_keep, grad_got)
        dec_out = stacked(dec_rows[0], dec_got[0]).astype(bf16)
        grad_dec = stacked(dec_rows[1], dec_got[1])

    return (
        encoder_output,
        dec_out,
        grad_in,
        grad_dec,
        gain_attn,
        grad_query,
        grad_key,
        grad_value,
        grad_output,
        grad_rel_table,
        gain_ffn,
        grad_ff_in,
        grad_ff_out,
        gain_final,
        gain_self,
        grad_self_value,
        grad_self_output,
        gain_cross,
        grad_cross_query,
        grad_cross_key,
        grad_cross_value,
        grad_cross_output,
        gain_dec_ffn,
        grad_dec_ff_in,
        grad_dec_ff_out,
    )


def solution(mesh):
    split = P("batch", "blk", None)
    rows = P("batch", None)
    line = P("batch")
    placed = (split, rows, line, split, rows) + (P(),) * 21
    return jax.shard_map(
        body,
        mesh=mesh,
        in_specs=placed,
        out_specs=(
            (split, rows, split, rows, line, rows, rows, rows, rows, P(), line, rows, rows, line)
            + (line, rows, rows, line, rows, rows, rows, rows, line, rows, rows)
        ),
        check_vma=False,
    )
```
